32 devices in a mesh: row: 8 (over z, core), chan: 4 (over y, x).
Axes of the slice: x: 2, y: 2, z: 4, core: 2. Of those that a mesh axis runs over, the one named last changes fastest.
Arguments:
- image: bfloat16 [4, 64, 64, 512], P(None, 'row', None, 'chan'), may hold values from -31 to 31
- target: bfloat16 [4, 64, 64, 512], P(None, 'row', None, 'chan'), may hold values from -6 to 6
- time_index: int32 [4], replicated, may hold values from 0 to 999
- loss_weight: float32 [4], replicated, may hold values from 0.5 to 2
- clip_embed: bfloat16 [4, 2048], replicated, may hold values from -6 to 6
- clip_tokens: bfloat16 [4, 4, 2048], replicated, may hold values from -6 to 6
- norm_gain: float32 [3, 512], P(None, 'chan'), may hold values from 0.5 to 1.5
- norm_bias: float32 [3, 512], P(None, 'chan'), may hold values from -3 to 3
- conv1_w: bfloat16 [3, 3, 512, 512], P(None, None, 'chan'), may hold values from -0.09375 to 0.09375
- conv2_w: bfloat16 [3, 3, 512, 512], P(None, None, 'chan'), may hold values from -0.09375 to 0.09375
- conv_bias: float32 [2, 512], P(None, 'chan'), may hold values from -3 to 3
- emb_w: bfloat16 [2, 512, 2048], P(None, 'chan'), may hold values from -0.125 to 0.125
- emb_b: float32 [2, 512], P(None, 'chan'), may hold values from -3 to 3
- qkv_w: bfloat16 [3, 512, 512], P(None, 'chan'), may hold values from -0.25 to 0.25
- qv_bias: float32 [2, 512], P(None, 'chan'), may hold values from -3 to 3
- ctx_w: bfloat16 [2, 512, 2048], P(None, 'chan'), may hold values from -0.125 to 0.125
- ctx_b: float32 [2, 512], P(None, 'chan'), may hold values from -3 to 3
- out_w: bfloat16 [512, 512], P('chan'), may hold values from -6 to 6
- out_b: float32 [512], P('chan'), may hold values from -3 to 3
Outputs:
- output: float32 [4, 64, 64, 512], P(None, 'row', None, 'chan')
- grad_image: float32 [4, 64, 64, 512], P(None, 'row', None, 'chan')
- grad_norm_gain: float32 [3, 512], P(None, 'chan')
- grad_norm_bias: float32 [3, 512], P(None, 'chan')
- grad_conv1_w: float32 [3, 3, 512, 512], P(None, None, 'chan')
- grad_conv2_w: float32 [3, 3, 512, 512], P(None, None, 'chan')
- grad_conv_bias: float32 [2, 512], P(None, 'chan')
- grad_emb_w: float32 [2, 512, 2048], P(None, 'chan')
- grad_emb_b: float32 [2, 512], P(None, 'chan')
- grad_qkv_w: float32 [3, 512, 512], P(None, 'chan')
- grad_qv_bias: float32 [2, 512], P(None, 'chan')
- grad_ctx_w: float32 [2, 512, 2048], P(None, 'chan')
- grad_ctx_b: float32 [2, 512], P(None, 'chan')
- grad_out_w: float32 [512, 512], P('chan')
- grad_out_b: float32 [512], P('chan')
The draws below stay inside these ranges and needn't reach their ends.
All inputs are finite; a program needn't handle non-finite values.
Results may differ from the reference program's by a relative error of at most 0.018.
Values may be sent and summed in bfloat16 or wider, within the bound.
A program may use at most 192 MiB of HBM per device.

```python
import math
import jax
import jax.numpy as jnp
from jax import lax

C = 512
GROUPS = 32
HEADS = 8
HEAD = 64
EMB = 2048
CTXW = 2048
CTX = 4
H = 64
W = 64
STEPS = 1000
IMAGES = 4


def draw_image(key, part):
    base_key, chan_key = jax.random.split(key, 2)
    row_place = jnp.arange(H, dtype=jnp.float32)
    rising = 1.0 + 2.0 * row_place / max(H - 1, 1)
    chan_scale = jnp.exp(jax.random.uniform(chan_key, (C,), minval=-0.7, maxval=0.7))
    base = jnp.clip(jax.random.normal(base_key, (IMAGES, H, W, C)), -5.0, 5.0)
    return (base * rising[None, :, None, None] * chan_scale).astype(jnp.bfloat16)


def touch_ends(values, rng, low, top_value):
    longest = values.shape.index(max(values.shape))
    spots = []
    for shift in (0, 1):
        where = [jax.random.randint(jax.random.fold_in(rng, axis), (), 0, length) for axis, length in enumerate(values.shape)]
        where[longest] = (where[longest] + shift) % values.shape[longest]
        spots.append(tuple(where))
    return values.at[spots[0]].set(low).at[spots[1]].set(top_value)


def block_levels(stream_key, dims, cuts, smallest, largest):
    loudness, own = 1.0, jax.random.fold_in(stream_key, 6)
    for position, shards_of in cuts:
        draws = jnp.exp(jax.random.uniform(jax.random.fold_in(own, position), (shards_of,), jnp.float32, smallest / len(cuts), largest / len(cuts)))
        loudness = loudness * jnp.repeat(draws, dims[position] // shards_of).reshape([-1 if axis == position else 1 for axis in range(len(dims))])
    return loudness


def noise(key, dims, scale, reach, shards=(), kind=jnp.bfloat16):
    values = jax.random.normal(key, dims, jnp.float32) * scale
    if len(shards) > 0:
        values = block_levels(key, dims, shards, -0.22, 0.18) * values
    return jnp.clip(values, min=-reach, max=reach).astype(kind)


def setup_inputs(seed: int = 0) -> dict:
    keys = jax.random.split(jax.random.key(seed), 20)
    return {
        "image": draw_image(jax.random.fold_in(keys[19], 71), 0),
        "target": noise(keys[1], (IMAGES, H, W, C), 1.0, 6.0, ((1, 8), (3, 4))),
        "time_index": touch_ends(jax.random.randint(keys[2], (IMAGES,), 0, STEPS), jax.random.fold_in(keys[2], 1), 0, STEPS - 1).astype(jnp.int32),
        "loss_weight": jnp.clip(jnp.exp(jax.random.uniform(keys[3], (IMAGES,), jnp.float32, math.log(0.5), math.log(2.0))), 0.5, 2.0),
        "clip_embed": noise(keys[4], (IMAGES, EMB), 1.0, 6.0),
        "clip_tokens": noise(keys[5], (IMAGES, CTX, CTXW), 1.0, 6.0),
        "norm_gain": jnp.clip(1.0 + 0.1 * jax.random.normal(keys[6], (3, C), jnp.float32), 0.5, 1.5),
        "norm_bias": noise(keys[7], (3, C), 0.5, 3.0, ((1, 4),), jnp.float32),
        "conv1_w": noise(keys[8], (3, 3, C, C), (9 * C) ** -0.5, 0.09375, ((2, 4),)),
        "conv2_w": noise(keys[9], (3, 3, C, C), (9 * C) ** -0.5, 0.09375, ((2, 4),)),
        "conv_bias": noise(keys[10], (2, C), 0.5, 3.0, ((1, 4),), jnp.float32),
        "emb_w": noise(keys[11], (2, C, EMB), EMB ** -0.5, 0.125, ((1, 4),)),
        "emb_b": noise(keys[12], (2, C), 0.5, 3.0, ((1, 4),), jnp.float32),
        "qkv_w": noise(keys[13], (3, C, C), C ** -0.5, 0.25, ((1, 4),)),
        "qv_bias": noise(keys[14], (2, C), 0.5, 3.0, ((1, 4),), jnp.float32),
        "ctx_w": noise(keys[15], (2, C, CTXW), CTXW ** -0.5, 0.125, ((1, 4),)),
        "ctx_b": noise(keys[16], (2, C), 0.5, 3.0, ((1, 4),), jnp.float32),
        "out_w": noise(keys[17], (C, C), (0.6 * (H * W // C) ** 0.5), 6.0, ((0, 4),)),
        "out_b": noise(keys[18], (C,), 0.5, 3.0, ((0, 4),), jnp.float32),
    }


HIGH = lax.Precision.HIGHEST
EPSILON = 1e-05

@jax.custom_vjp
def low(v):
    return lax.optimization_barrier(v.astype(jnp.bfloat16)).astype(jnp.float32)

@jax.custom_vjp
def low_back(v):
    return v

def low_keep(v):
    return (low(v), None)

def low_pass(kept, grad):
    return (grad,)

def back_keep(v):
    return (v, None)

def back_low(kept, grad):
    return (low(grad),)
low.defvjp(low_keep, low_pass)
low_back.defvjp(back_keep, back_low)

def swish(source):
    return source * jax.nn.sigmoid(source)

def time_features(time_index, width_all):
    half_width = width_all // 2
    frequency = jnp.exp(-math.log(10000.0) * jnp.arange(half_width, dtype=jnp.float32) / half_width)
    angles = time_index.astype(jnp.float32)[:, None] * frequency[None, :]
    return jnp.concatenate([jnp.cos(angles), jnp.sin(angles)], axis=1)

def group_norm(source, gain, bias):
    layout = source.shape
    grouped = source.reshape(layout[0], layout[1], layout[2], GROUPS, layout[3] // GROUPS)
    center = lax.optimization_barrier(jnp.mean(grouped, axis=(1, 2, 4), keepdims=True))
    spread = lax.optimization_barrier(jnp.mean(grouped * grouped, axis=(1, 2, 4), keepdims=True)) - center * center
    scaled = (grouped - center) * lax.rsqrt(spread + EPSILON)
    return scaled.reshape(layout) * gain + bias

def conv_apply(source, weight):
    return lax.conv_general_dilated(source, weight, (1, 1), 'SAME', dimension_numbers=('NHWC', 'HWIO', 'NHWC'), precision=HIGH)

def attend(query, keys_all, values_all):
    block_rows = min(512, query.shape[0])
    blocks = query.reshape(-1, block_rows, HEADS, HEAD)

    def one_block(query_block):
        scores = low_back(jnp.einsum('qhd,khd->hqk', query_block, keys_all, precision=HIGH) * HEAD ** (-0.5))
        top_score = lax.optimization_barrier(jnp.max(scores, axis=-1, keepdims=True))
        expo = jnp.exp(scores - top_score)
        probs = expo / lax.optimization_barrier(jnp.sum(expo, axis=-1, keepdims=True))
        return jnp.einsum('hqk,khd->qhd', low(probs), values_all, precision=HIGH)
    return lax.map(jax.checkpoint(one_block), blocks).reshape(query.shape)

def forward(picture, feat_row, tokens_row, norm_gain, norm_bias, conv1_w, conv2_w, conv_bias, emb_w, emb_b, qkv_w, qv_bias, ctx_w, ctx_b, out_w, out_b):
    conv_one = jnp.transpose(conv1_w, (0, 1, 3, 2))
    conv_two = jnp.transpose(conv2_w, (0, 1, 3, 2))
    emb_mat = jnp.transpose(emb_w, (2, 0, 1))
    qkv_mat = jnp.transpose(qkv_w, (2, 0, 1))
    ctx_mat = jnp.transpose(ctx_w, (2, 0, 1))
    out_mat = jnp.transpose(out_w)
    cond = jnp.dot(low(swish(feat_row)), emb_mat.reshape(EMB, 2 * C), precision=HIGH).reshape(-1, 2, C) + emb_b
    scale_term = cond[:, 0][:, None, None, :]
    shift_term = cond[:, 1][:, None, None, :]
    act_one = low(swish(group_norm(picture, norm_gain[0], norm_bias[0])))
    hidden = low_back(conv_apply(act_one, conv_one) + conv_bias[0])
    modded = group_norm(hidden, norm_gain[1], norm_bias[1]) * (1.0 + scale_term) + shift_term
    act_two = low(swish(modded))
    resid = picture + low_back(conv_apply(act_two, conv_two) + conv_bias[1])
    normed = low(group_norm(resid, norm_gain[2], norm_bias[2]))
    projected = jnp.einsum('nhwc,cte->nhwte', normed, qkv_mat, precision=HIGH)
    query = low(low_back(projected[..., 0, :] + qv_bias[0])).reshape(-1, HEADS, HEAD)
    keys_image = low(low_back(projected[..., 1, :])).reshape(-1, HEADS, HEAD)
    values_image = low(low_back(projected[..., 2, :] + qv_bias[1])).reshape(-1, HEADS, HEAD)
    context = jnp.einsum('nte,ejc->ntjc', tokens_row, ctx_mat, precision=HIGH) + ctx_b
    keys_all = jnp.concatenate([low(context[0, :, 0]).reshape(CTX, HEADS, HEAD), keys_image], axis=0)
    values_all = jnp.concatenate([low(context[0, :, 1]).reshape(CTX, HEADS, HEAD), values_image], axis=0)
    attended = low(low_back(attend(query, keys_all, values_all))).reshape(-1, C)
    projected_out = low_back(jnp.dot(attended, out_mat, precision=HIGH) + out_b)
    return resid + projected_out.reshape(picture.shape)

def reference(image, target, time_index, loss_weight, clip_embed, clip_tokens, norm_gain, norm_bias, conv1_w, conv2_w, conv_bias, emb_w, emb_b, qkv_w, qv_bias, ctx_w, ctx_b, out_w, out_b):
    params = (norm_gain.astype(jnp.float32), norm_bias.astype(jnp.float32), conv1_w.astype(jnp.float32), conv2_w.astype(jnp.float32), conv_bias.astype(jnp.float32), emb_w.astype(jnp.float32), emb_b.astype(jnp.float32), qkv_w.astype(jnp.float32), qv_bias.astype(jnp.float32), ctx_w.astype(jnp.float32), ctx_b.astype(jnp.float32), out_w.astype(jnp.float32), out_b.astype(jnp.float32))
    feats = time_features(time_index, EMB) + clip_embed.astype(jnp.float32)

    def one_image(carry, items):
        picture, goal_image, feat_row, tokens_row, weight_row = items

        def wrapped(picture_in, *weights):
            return forward(picture_in, feat_row, tokens_row, *weights)
        result, pullback = jax.vjp(wrapped, picture, *params)
        grads = pullback(weight_row * (result - goal_image))
        updated = tuple((running + update for running, update in zip(carry, grads[1:])))
        return (updated, (result, grads[0]))
    start = tuple((jnp.zeros_like(weight) for weight in params))
    items = (image.astype(jnp.float32)[:, None], target.astype(jnp.float32)[:, None], feats[:, None], clip_tokens.astype(jnp.float32)[:, None], loss_weight.astype(jnp.float32))
    totals, (results, image_grads) = lax.scan(one_image, start, items)
    return (results.reshape(image.shape), image_grads.reshape(image.shape), totals[0], totals[1], totals[2], totals[3], totals[4], totals[5], totals[6], totals[7], totals[8], totals[9], totals[10], totals[11], totals[12])
```

```python
import math

import jax
import jax.numpy as jnp
from jax import lax
from jax.experimental import pallas as pl
from jax.experimental.pallas import tpu as pltpu
from jax.sharding import PartitionSpec as P

C = 512
GROUPS = 32
HEAD = 64
EMB = 2048
CTXW = 2048
CTX = 4
H = 64
W = 64
MB_IMG = 2


HIGH = lax.Precision.HIGHEST
EPSILON = 1e-05


def with_halo(cells, sides, width):
    for axis, dim in sides:
        count = lax.axis_size(axis)
        ends = count - 1
        head = lax.slice_in_dim(cells, 0, width, axis=dim)
        tail = lax.slice_in_dim(cells, cells.shape[dim] - width, cells.shape[dim], axis=dim)
        cells = jnp.concatenate(
            [
                lax.ppermute(tail, axis, [(i, (i + 1) % count) for i in range(ends)]),
                cells,
                lax.ppermute(head, axis, [((i + 1) % count, i) for i in range(ends)]),
            ],
            axis=dim,
        )
    return cells


def swish(source):
    return source * jax.nn.sigmoid(source)


def swish_slope(source):
    sigma = jax.nn.sigmoid(source)
    return sigma * (1.0 + source * (1.0 - sigma))


def time_features(time_index, width_all):
    half_width = width_all // 2
    frequency = jnp.exp(-math.log(10000.0) * jnp.arange(half_width, dtype=jnp.float32) / half_width)
    angles = time_index.astype(jnp.float32)[:, None] * frequency[None, :]
    return jnp.concatenate([jnp.cos(angles), jnp.sin(angles)], axis=1)


def rows_around(source):
    return with_halo(source, (("row", 1),), 1)


def all_channels(source):
    return lax.all_gather(source, "chan", axis=3, tiled=True)


def channel_total(source):
    return lax.psum_scatter(
        source.astype(jnp.bfloat16), "chan", scatter_dimension=3, tiled=True
    ).astype(jnp.float32)


def norm_forward(source, group_width, members):
    layout = source.shape
    grouped = source.reshape(layout[0], layout[1], layout[2], layout[3] // group_width, group_width)
    first_sum = jnp.sum(grouped, axis=(1, 2, 4))
    square_sum = jnp.sum(grouped * grouped, axis=(1, 2, 4))
    first_sum, square_sum = lax.psum((first_sum, square_sum), "row")
    center = first_sum / members
    spread = square_sum / members - center * center
    inverse_std = lax.rsqrt(spread + EPSILON)
    scaled = (grouped - center[:, None, None, :, None]) * inverse_std[:, None, None, :, None]
    return (scaled.reshape(layout), inverse_std)


def norm_backward(upstream, scaled, inverse_std, gain, group_width, members):
    layout = upstream.shape
    grouped_grad = (upstream * gain).reshape(
        layout[0], layout[1], layout[2], layout[3] // group_width, group_width
    )
    grouped_norm = scaled.reshape(grouped_grad.shape)
    grad_sum = jnp.sum(grouped_grad, axis=(1, 2, 4))
    cross_sum = jnp.sum(grouped_grad * grouped_norm, axis=(1, 2, 4))
    grad_sum, cross_sum = lax.psum((grad_sum, cross_sum), "row")
    result = inverse_std[:, None, None, :, None] * (
        grouped_grad
        - grad_sum[:, None, None, :, None] / members
        - grouped_norm * (cross_sum[:, None, None, :, None] / members)
    )
    gain_grad = jnp.sum(upstream * scaled, axis=(0, 1, 2))
    bias_grad = jnp.sum(upstream, axis=(0, 1, 2))
    return (result.reshape(layout), gain_grad, bias_grad)


def conv_apply(padded, weight):
    height = padded.shape[1] - 2
    width = padded.shape[2]
    widened = jnp.pad(padded, ((0, 0), (0, 0), (1, 1), (0, 0)))
    result = None
    for row_step in range(3):
        for col_step in range(3):
            partial_term = jnp.einsum(
                "nhwc,dc->nhwd",
                widened[:, row_step : row_step + height, col_step : col_step + width],
                weight[row_step, col_step],
                preferred_element_type=jnp.float32,
            )
            result = partial_term if result is None else result + partial_term
    return result


def conv_weight_grad(padded, upstream_low):
    height = upstream_low.shape[1]
    width = upstream_low.shape[2]
    widened = jnp.pad(padded, ((0, 0), (0, 0), (1, 1), (0, 0)))
    stacked = []
    for row_step in range(3):
        row_terms = []
        for col_step in range(3):
            row_terms.append(
                jnp.einsum(
                    "nhwc,nhwd->dc",
                    widened[:, row_step : row_step + height, col_step : col_step + width],
                    upstream_low,
                    preferred_element_type=jnp.float32,
                )
            )
        stacked.append(jnp.stack(row_terms))
    return jnp.stack(stacked)


def conv_input_grad(upstream_low, weight):
    height = upstream_low.shape[1]
    width = upstream_low.shape[2]
    widened = jnp.pad(rows_around(upstream_low), ((0, 0), (0, 0), (1, 1), (0, 0)))
    result = None
    for row_step in range(3):
        for col_step in range(3):
            partial_term = jnp.einsum(
                "nhwd,dc->nhwc",
                widened[
                    :, 2 - row_step : 2 - row_step + height, 2 - col_step : 2 - col_step + width
                ],
                weight[row_step, col_step],
                preferred_element_type=jnp.float32,
            )
            result = partial_term if result is None else result + partial_term
    return channel_total(result)


def general_body(
    image,
    target,
    time_index,
    loss_weight,
    clip_embed,
    clip_tokens,
    norm_gain,
    norm_bias,
    conv1_w,
    conv2_w,
    conv_bias,
    emb_w,
    emb_b,
    qkv_w,
    qv_bias,
    ctx_w,
    ctx_b,
    out_w,
    out_b,
):
    local_chan = conv1_w.shape[2]
    group_width = C // GROUPS
    members = H * W * group_width
    head_count = local_chan // HEAD
    scaling = HEAD ** (-0.5)
    batches = image.shape[0] // MB_IMG
    band_rows = image.shape[1]
    image_cols = image.shape[2]

    def heads_of(source):
        return source.reshape(source.shape[0], -1, head_count, HEAD)

    def one_batch(carry, items):
        picture, target_in, steps_in, weight_in, embed_in, tokens_in = items
        feat_low = swish(time_features(steps_in, EMB) + embed_in.astype(jnp.float32)).astype(
            jnp.bfloat16
        )
        cond = (
            jnp.einsum("ne,jde->njd", feat_low, emb_w, preferred_element_type=jnp.float32) + emb_b
        )
        scale_term = cond[:, 0][:, None, None, :]
        shift_term = cond[:, 1][:, None, None, :]
        picture_f = picture.astype(jnp.float32)
        scaled_one, inverse_one = norm_forward(picture_f, group_width, members)
        pre_one = scaled_one * norm_gain[0] + norm_bias[0]
        padded_one = all_channels(rows_around(swish(pre_one).astype(jnp.bfloat16)))
        hidden = conv_apply(padded_one, conv1_w) + conv_bias[0]
        scaled_two, inverse_two = norm_forward(hidden, group_width, members)
        normal_two = scaled_two * norm_gain[1] + norm_bias[1]
        modded = normal_two * (1.0 + scale_term) + shift_term
        padded_two = all_channels(rows_around(swish(modded).astype(jnp.bfloat16)))
        resid = picture_f + conv_apply(padded_two, conv2_w) + conv_bias[1]
        scaled_three, inverse_three = norm_forward(resid, group_width, members)
        normed_full = all_channels(
            (scaled_three * norm_gain[2] + norm_bias[2]).astype(jnp.bfloat16)
        )
        projected = jnp.einsum(
            "nhwc,tdc->nhwtd", normed_full, qkv_w, preferred_element_type=jnp.float32
        )
        query_own = heads_of((projected[..., 0, :] + qv_bias[0]).astype(jnp.bfloat16))
        key_own = heads_of(projected[..., 1, :].astype(jnp.bfloat16))
        value_own = heads_of((projected[..., 2, :] + qv_bias[1]).astype(jnp.bfloat16))
        context = (
            jnp.einsum("nte,jde->ntjd", tokens_in, ctx_w, preferred_element_type=jnp.float32)
            + ctx_b
        )
        ctx_key = heads_of(context[:, :, 0].astype(jnp.bfloat16))
        ctx_value = heads_of(context[:, :, 1].astype(jnp.bfloat16))
        key_rows, value_rows = (
            lax.all_gather(key_own, "row", axis=1, tiled=True),
            lax.all_gather(value_own, "row", axis=1, tiled=True),
        )
        score_image = (
            jnp.einsum("nqhd,nkhd->nhqk", query_own, key_rows, preferred_element_type=jnp.float32)
            * scaling
        )
        score_context = (
            jnp.einsum("nqhd,nkhd->nhqk", query_own, ctx_key, preferred_element_type=jnp.float32)
            * scaling
        )
        top_score = jnp.maximum(jnp.max(score_image, axis=3), jnp.max(score_context, axis=3))
        expo_image = jnp.exp(score_image - top_score[..., None])
        expo_context = jnp.exp(score_context - top_score[..., None])
        denom = jnp.sum(expo_image, axis=3) + jnp.sum(expo_context, axis=3)
        prob_image = expo_image / denom[..., None]
        prob_context = expo_context / denom[..., None]
        attended = jnp.einsum(
            "nhqk,nkhd->nqhd",
            prob_image.astype(jnp.bfloat16),
            value_rows,
            preferred_element_type=jnp.float32,
        ) + jnp.einsum(
            "nhqk,nkhd->nqhd",
            prob_context.astype(jnp.bfloat16),
            ctx_value,
            preferred_element_type=jnp.float32,
        )
        attn_full = all_channels(attended.astype(jnp.bfloat16).reshape(picture.shape))
        result = (
            resid
            + jnp.einsum("nhwc,dc->nhwd", attn_full, out_w, preferred_element_type=jnp.float32)
            + out_b
        )
        cotangent = weight_in[:, None, None, None] * (result - target_in.astype(jnp.float32))
        grad_proj = cotangent.astype(jnp.bfloat16)
        grad_outw = jnp.einsum(
            "nhwc,nhwd->dc", attn_full, grad_proj, preferred_element_type=jnp.float32
        )
        grad_outb = jnp.sum(grad_proj.astype(jnp.float32), axis=(0, 1, 2))
        grad_attn = heads_of(
            channel_total(
                jnp.einsum("nhwd,dc->nhwc", grad_proj, out_w, preferred_element_type=jnp.float32)
            ).astype(jnp.bfloat16)
        )
        dprob_image = jnp.einsum(
            "nqhd,nkhd->nhqk", grad_attn, value_rows, preferred_element_type=jnp.float32
        )
        dprob_context = jnp.einsum(
            "nqhd,nkhd->nhqk", grad_attn, ctx_value, preferred_element_type=jnp.float32
        )
        delta = jnp.sum(prob_image * dprob_image, axis=3) + jnp.sum(
            prob_context * dprob_context, axis=3
        )
        dscore_image = (prob_image * (dprob_image - delta[..., None])).astype(jnp.bfloat16)
        dscore_context = (prob_context * (dprob_context - delta[..., None])).astype(jnp.bfloat16)
        grad_query = (
            jnp.einsum(
                "nhqk,nkhd->nqhd", dscore_image, key_rows, preferred_element_type=jnp.float32
            )
            + jnp.einsum(
                "nhqk,nkhd->nqhd", dscore_context, ctx_key, preferred_element_type=jnp.float32
            )
        ) * scaling
        grad_ctx_key = (
            jnp.einsum(
                "nhqk,nqhd->nkhd", dscore_context, query_own, preferred_element_type=jnp.float32
            )
            * scaling
        )
        grad_ctx_value = jnp.einsum(
            "nhqk,nqhd->nkhd",
            prob_context.astype(jnp.bfloat16),
            grad_attn,
            preferred_element_type=jnp.float32,
        )
        key_terms = (
            jnp.einsum(
                "nhqk,nqhd->nkhd", dscore_image, query_own, preferred_element_type=jnp.float32
            )
            * scaling
        )
        value_terms = jnp.einsum(
            "nhqk,nqhd->nkhd",
            prob_image.astype(jnp.bfloat16),
            grad_attn,
            preferred_element_type=jnp.float32,
        )
        grad_key, grad_value = (
            lax.psum_scatter(
                key_terms.astype(jnp.bfloat16), "row", scatter_dimension=1, tiled=True
            ).astype(jnp.float32),
            lax.psum_scatter(
                value_terms.astype(jnp.bfloat16), "row", scatter_dimension=1, tiled=True
            ).astype(jnp.float32),
        )
        grad_stack = (
            jnp.stack([grad_query, grad_key, grad_value], axis=2)
            .reshape(picture.shape[0], band_rows, image_cols, 3, local_chan)
            .astype(jnp.bfloat16)
        )
        grad_qkvw = jnp.einsum(
            "nhwc,nhwtd->tdc", normed_full, grad_stack, preferred_element_type=jnp.float32
        )
        stack_sums = jnp.sum(grad_stack.astype(jnp.float32), axis=(0, 1, 2))
        grad_qvb = jnp.stack([stack_sums[0], stack_sums[2]])
        grad_context = jnp.stack(
            [
                grad_ctx_key.reshape(picture.shape[0], CTX, local_chan),
                grad_ctx_value.reshape(picture.shape[0], CTX, local_chan),
            ],
            axis=2,
        )
        grad_ctxw = jnp.einsum(
            "nte,ntjd->jde", tokens_in.astype(jnp.float32), grad_context, precision=HIGH
        )
        grad_ctxb = jnp.sum(grad_context, axis=(0, 1))
        grad_normed = channel_total(
            jnp.einsum("nhwtd,tdc->nhwc", grad_stack, qkv_w, preferred_element_type=jnp.float32)
        )
        grad_resid, gain_three, bias_three = norm_backward(
            grad_normed, scaled_three, inverse_three, norm_gain[2], group_width, members
        )
        grad_resid = cotangent + grad_resid
        grad_conv_two = grad_resid.astype(jnp.bfloat16)
        grad_w_two = conv_weight_grad(padded_two, grad_conv_two)
        grad_b_two = jnp.sum(grad_conv_two.astype(jnp.float32), axis=(0, 1, 2))
        grad_modded = conv_input_grad(grad_conv_two, conv2_w) * swish_slope(modded)
        grad_cond = jnp.stack(
            [jnp.sum(grad_modded * normal_two, axis=(1, 2)), jnp.sum(grad_modded, axis=(1, 2))],
            axis=1,
        )
        grad_embw = jnp.einsum(
            "ne,njd->jde", feat_low.astype(jnp.float32), grad_cond, precision=HIGH
        )
        grad_embb = jnp.sum(grad_cond, axis=0)
        grad_hidden, gain_two, bias_two = norm_backward(
            grad_modded * (1.0 + scale_term),
            scaled_two,
            inverse_two,
            norm_gain[1],
            group_width,
            members,
        )
        grad_conv_one = grad_hidden.astype(jnp.bfloat16)
        grad_w_one = conv_weight_grad(padded_one, grad_conv_one)
        grad_b_one = jnp.sum(grad_conv_one.astype(jnp.float32), axis=(0, 1, 2))
        grad_pre_one = conv_input_grad(grad_conv_one, conv1_w) * swish_slope(pre_one)
        grad_input, gain_one, bias_one = norm_backward(
            grad_pre_one, scaled_one, inverse_one, norm_gain[0], group_width, members
        )
        grad_picture = grad_resid + grad_input
        grad_gains = jnp.stack([gain_one, gain_two, gain_three])
        grad_biases = jnp.stack([bias_one, bias_two, bias_three])
        grad_convb = jnp.stack([grad_b_one, grad_b_two])
        batch_grads = (
            grad_gains,
            grad_biases,
            grad_w_one,
            grad_w_two,
            grad_convb,
            grad_embw,
            grad_embb,
            grad_qkvw,
            grad_qvb,
            grad_ctxw,
            grad_ctxb,
            grad_outw,
            grad_outb,
        )
        updated = tuple((running + update for running, update in zip(carry, batch_grads)))
        return (updated, (result, grad_picture))

    start = (
        jnp.zeros(norm_gain.shape, jnp.float32),
        jnp.zeros(norm_bias.shape, jnp.float32),
        jnp.zeros(conv1_w.shape, jnp.float32),
        jnp.zeros(conv2_w.shape, jnp.float32),
        jnp.zeros(conv_bias.shape, jnp.float32),
        jnp.zeros(emb_w.shape, jnp.float32),
        jnp.zeros(emb_b.shape, jnp.float32),
        jnp.zeros(qkv_w.shape, jnp.float32),
        jnp.zeros(qv_bias.shape, jnp.float32),
        jnp.zeros(ctx_w.shape, jnp.float32),
        jnp.zeros(ctx_b.shape, jnp.float32),
        jnp.zeros(out_w.shape, jnp.float32),
        jnp.zeros(out_b.shape, jnp.float32),
    )
    items = (
        image.reshape(batches, MB_IMG, band_rows, image_cols, local_chan),
        target.reshape(batches, MB_IMG, band_rows, image_cols, local_chan),
        time_index.reshape(batches, MB_IMG),
        loss_weight.reshape(batches, MB_IMG),
        clip_embed.reshape(batches, MB_IMG, EMB),
        clip_tokens.reshape(batches, MB_IMG, CTX, CTXW),
    )
    totals, (results, picture_grads) = lax.scan(one_batch, start, items)
    (
        sum_gain,
        sum_bias,
        sum_conv_one,
        sum_conv_two,
        sum_conv_bias,
        sum_emb_w,
        sum_emb_b,
        sum_qkv_w,
        sum_qv_bias,
        sum_ctx_w,
        sum_ctx_b,
        sum_out_w,
        sum_out_b,
    ) = totals
    (
        sum_gain,
        sum_bias,
        sum_conv_one,
        sum_conv_two,
        sum_conv_bias,
        sum_emb_w,
        sum_emb_b,
        sum_qkv_w,
        sum_qv_bias,
        sum_ctx_w,
        sum_ctx_b,
        sum_out_w,
        sum_out_b,
    ) = (
        lax.psum(sum_gain.astype(jnp.bfloat16), "row").astype(jnp.float32),
        lax.psum(sum_bias.astype(jnp.bfloat16), "row").astype(jnp.float32),
        lax.psum(sum_conv_one.astype(jnp.bfloat16), "row").astype(jnp.float32),
        lax.psum(sum_conv_two.astype(jnp.bfloat16), "row").astype(jnp.float32),
        lax.psum(sum_conv_bias.astype(jnp.bfloat16), "row").astype(jnp.float32),
        lax.psum(sum_emb_w.astype(jnp.bfloat16), "row").astype(jnp.float32),
        lax.psum(sum_emb_b.astype(jnp.bfloat16), "row").astype(jnp.float32),
        lax.psum(sum_qkv_w.astype(jnp.bfloat16), "row").astype(jnp.float32),
        lax.psum(sum_qv_bias.astype(jnp.bfloat16), "row").astype(jnp.float32),
        lax.psum(sum_ctx_w.astype(jnp.bfloat16), "row").astype(jnp.float32),
        lax.psum(sum_ctx_b.astype(jnp.bfloat16), "row").astype(jnp.float32),
        lax.psum(sum_out_w.astype(jnp.bfloat16), "row").astype(jnp.float32),
        lax.psum(sum_out_b.astype(jnp.bfloat16), "row").astype(jnp.float32),
    )
    return (
        results.reshape(image.shape),
        picture_grads.reshape(image.shape),
        sum_gain,
        sum_bias,
        sum_conv_one,
        sum_conv_two,
        sum_conv_bias,
        sum_emb_w,
        sum_emb_b,
        sum_qkv_w,
        sum_qv_bias,
        sum_ctx_w,
        sum_ctx_b,
        sum_out_w,
        sum_out_b,
    )


BF = jnp.bfloat16
F32 = jnp.float32
MESH_ID = pl.DeviceIdType.MESH
NN = (((1,), (0,)), ((), ()))
NT = (((1,), (1,)), ((), ()))
ANY = pl.BlockSpec(memory_space=pl.ANY)
VMEM = pl.BlockSpec(memory_space=pltpu.VMEM)
PIX = 512
PAD = 640
CHUNKS = 8
VMEM_LIMIT = 60 * 2**20
DMA = pltpu.SemaphoreType.DMA


def mm(left, right, dims=NN):
    return lax.dot_general(left, right, dims, preferred_element_type=F32)


class Place:
    def __init__(self):
        self.r = lax.axis_index("row")
        self.c = lax.axis_index("chan")
        self.z = lax.div(self.r, 2)
        self.k = lax.rem(self.r, 2)
        self.d = 2 * self.c + self.k
        self.pair = lax.rem(self.c - self.z + 4, 4)
        self.band = 2 * self.pair + self.k

    def head_device(self, head):
        return (2 * self.z + lax.rem(head, 2), lax.div(head, 2))

    def band_device(self, band):
        return (2 * self.z + lax.rem(band, 2), lax.rem(lax.div(band, 2) + self.z, 4))


def send(src, dst, send_sem, recv_sem, device):
    copy = pltpu.make_async_remote_copy(
        src_ref=src,
        dst_ref=dst,
        send_sem=send_sem,
        recv_sem=recv_sem,
        device_id=device,
        device_id_type=MESH_ID,
    )
    copy.start()
    return copy


def local(src, dst, sem):
    copy = pltpu.make_async_copy(src, dst, sem)
    copy.start()
    return copy


def greet_plane(me, barrier):
    for step in range(1, 8):
        pl.semaphore_signal(
            barrier,
            inc=1,
            device_id=me.head_device(lax.rem(me.d + step, 8)),
            device_id_type=MESH_ID,
        )


def group_matrix(ref):
    rows = lax.broadcasted_iota(jnp.int32, (C, C), 0)
    cols = lax.broadcasted_iota(jnp.int32, (C, C), 1)
    ref[...] = jnp.where(lax.div(rows, 16) == lax.div(cols, 16), 1.0, 0.0).astype(BF)


def group_total(rows, groups_ref):
    top = rows.astype(BF)
    rest = rows - top.astype(F32)
    mid = rest.astype(BF)
    low = (rest - mid.astype(F32)).astype(BF)
    stacked = jnp.concatenate([top, mid, low, jnp.zeros_like(low)], axis=0)
    sums = mm(stacked, groups_ref[...])
    return sums[0:8] + sums[8:16] + sums[16:24]


def plane_exchange(me, slots, ssem, rsem):
    copies = []
    for step in range(1, 8):
        copies.append(
            send(
                slots.at[me.d],
                slots.at[me.d],
                ssem.at[step],
                rsem.at[step],
                me.head_device(lax.rem(me.d + step, 8)),
            )
        )
    return copies


def slots_total(slots):
    total = slots[0]
    for slot in range(1, 8):
        total = total + slots[slot]
    return total


def fold(value):
    return value.reshape(value.shape[0] // 8, 8, value.shape[1]).sum(axis=0)


def as_row(value):
    return jnp.sum(value, axis=0, keepdims=True)


def store_rows(slots, index, rows):
    filled = rows + [jnp.zeros((1, C), F32)] * (8 - len(rows))
    slots[index] = jnp.concatenate(filled, axis=0)


def chunk_of(i):
    return pl.ds(pl.multiple_of(i * 64, 64), 64)


def put_shifted(dst, start, value):
    col = lax.broadcasted_iota(jnp.int32, (64, C), 0)
    where = pl.ds(pl.multiple_of(start, 64), 64)
    dst[1, where, :] = value.astype(BF)
    dst[0, where, :] = jnp.where(col == 0, 0.0, pltpu.roll(value, 1, 0)).astype(BF)
    dst[2, where, :] = jnp.where(col == 63, 0.0, pltpu.roll(value, 63, 0)).astype(BF)


def halo_send(me, cat, halo, ssem, rsem):
    @pl.when(me.band > 0)
    def _():
        send(cat.at[1, pl.ds(64, 64), :], halo.at[1], ssem.at[0], rsem.at[1],
             me.band_device(me.band - 1))

    @pl.when(me.band < 7)
    def _():
        send(cat.at[1, pl.ds(512, 64), :], halo.at[0], ssem.at[1], rsem.at[0],
             me.band_device(me.band + 1))


def halo_wait(me, cat, halo, ssem, rsem):
    def pair(slot, ahead):
        return pltpu.make_async_remote_copy(
            src_ref=cat.at[1, pl.ds(64, 64), :], dst_ref=halo.at[slot],
            send_sem=ssem.at[slot], recv_sem=rsem.at[slot],
            device_id=me.band_device(ahead), device_id_type=MESH_ID)

    zero = jnp.zeros((64, C), F32)

    @pl.when(me.band > 0)
    def _():
        both = pair(0, me.band - 1)
        both.wait_send()
        both.wait_recv()
        put_shifted(cat, 0, halo[0].astype(F32))

    @pl.when(me.band == 0)
    def _():
        put_shifted(cat, 0, zero)

    @pl.when(me.band < 7)
    def _():
        both = pair(1, me.band + 1)
        both.wait_send()
        both.wait_recv()
        put_shifted(cat, 576, halo[1].astype(F32))

    @pl.when(me.band == 7)
    def _():
        put_shifted(cat, 576, zero)


def conv_taps(acc, cat, weight, order, flip, dims):
    @pl.loop(0, 3 * len(order))
    def _(i):
        step = lax.div(i, 3)
        col = lax.rem(i, 3)
        row = order[0] if len(order) == 1 else order[0] + step * (order[1] - order[0])
        tap = (2 - row) * 3 + (2 - col) if flip else row * 3 + col
        start = pl.multiple_of(row * 64, 64)
        acc[...] += mm(cat[col, pl.ds(start, PIX), :], weight[tap], dims)


def image_targets(me):
    return [(n, (2 * n + me.k, lax.rem(me.z + n, 4))) for n in range(4)]


def front_kernel(
    img, tgt, vec, w1, w2, wq, wo,
    x_o, t_o, vec_o, st_o, a1_o, hid_o, a2_o, res_o, nrm_o, w1_o, w2_o, wq_o, wo_o, qkv_o,
    x_v, t_v, vec_v, st_v, a1_v, hid_v, a2_v, res_v, nrm_v, w1_v, w2_v, wq_v, wo_v, qkv_v,
    msg, groups, slots, halo,
    vs, vr, ims, imr, tgs, tgr, ws, wr, fs, fr, wl, sts, str_, hs, hr, qs, qr, lsem, osem,
):
    me = Place()
    barrier = pltpu.get_barrier_semaphore()
    greet_plane(me, barrier)
    own_block = jnp.logical_and(me.c == lax.rem(2 * me.z, 4), True)
    for chan in range(4):
        itself = jnp.logical_and(me.pair == me.z, me.c == chan)

        @pl.when(jnp.logical_not(itself))
        def _():
            pl.semaphore_signal(
                barrier, inc=1, device_id=(2 * me.pair + me.k, chan), device_id_type=MESH_ID
            )

    pl.semaphore_wait(barrier, 7 + 4 - jnp.where(own_block, 1, 0))
    own_cols = pl.ds(pl.multiple_of(me.c * 128, 128), 128)
    half = pl.ds(pl.multiple_of(me.c * 128 + me.k * 64, 64), 64)
    my_half = pl.ds(pl.multiple_of(me.k * 64, 64), 64)

    vec_v[:, own_cols] = vec[...]
    vec_copies = [
        send(vec, vec_v.at[:, own_cols], vs.at[t], vr.at[t], (me.r, lax.rem(me.c + t, 4)))
        for t in range(1, 4)
    ]

    def image_send(src, dst, ssem, rsem):
        for n, device in image_targets(me):
            itself = jnp.logical_and(own_block, me.z == n)

            @pl.when(jnp.logical_not(itself))
            def _():
                send(src.at[n], dst.at[:, own_cols], ssem.at[n], rsem.at[me.c], device)

            @pl.when(itself)
            def _():
                local(src.at[n], dst.at[:, own_cols], rsem.at[me.c])

    def image_wait(src, dst, ssem, rsem):
        for chan in range(4):
            pltpu.make_async_copy(
                src.at[0], dst.at[:, pl.ds(chan * 128, 128)], rsem.at[chan]
            ).wait()

    def image_drain(src, dst, ssem, rsem):
        for n, device in image_targets(me):
            itself = jnp.logical_and(own_block, me.z == n)

            @pl.when(jnp.logical_not(itself))
            def _():
                pltpu.make_async_remote_copy(
                    src_ref=src.at[n], dst_ref=dst.at[:, own_cols], send_sem=ssem.at[n],
                    recv_sem=rsem.at[me.c], device_id=device, device_id_type=MESH_ID,
                ).wait_send()

    def weight_send(index, src, dst):
        local(src, dst.at[:, own_cols, :], wl.at[index])
        return [
            send(src.at[:, my_half, :], dst.at[:, half, :], ws.at[index, t], wr.at[index, t],
                 (me.r, lax.rem(me.c + t, 4)))
            for t in range(1, 4)
        ]

    def weight_forward(index, dst, copies):
        out = []
        for t in range(1, 4):
            copies[t - 1].wait_recv()
            origin = lax.rem(me.c - t + 4, 4)
            rows = pl.ds(pl.multiple_of(origin * 128 + me.k * 64, 64), 64)
            out.append(
                send(dst.at[:, rows, :], dst.at[:, rows, :], fs.at[index, t], fr.at[index, t],
                     (me.r + 1 - 2 * me.k, me.c))
            )
        return out

    def weight_wait(index, src, dst, copies, forwards):
        for copy in copies:
            copy.wait_send()
        for copy in forwards:
            copy.wait()
        pltpu.make_async_copy(src, dst.at[:, own_cols, :], wl.at[index]).wait()

    image_send(img, x_v, ims, imr)
    w1_copies = weight_send(0, w1, w1_v)
    group_matrix(groups)
    col_zero = jnp.zeros((8, C), F32)
    for copy in vec_copies:
        copy.wait()
    image_wait(img, x_v, ims, imr)
    outs = []

    def save(index, src, dst):
        outs.append(local(src, dst, osem.at[index]))

    save(0, x_v, x_o)
    save(2, vec_v, vec_o)

    def statistics(number, ref):
        def add(i, carry):
            value = ref[chunk_of(i), :].astype(F32)
            return (carry[0] + fold(value), carry[1] + fold(value * value))

        first, square = lax.fori_loop(0, CHUNKS, add, (col_zero, col_zero))
        store_rows(slots.at[number], me.d, [as_row(first), as_row(square)])
        return plane_exchange(me, slots.at[number], sts.at[number], str_.at[number])

    def finish_statistics(number, copies):
        for copy in copies:
            copy.wait()
        means = group_total(slots_total(slots.at[number]), groups) * (1.0 / (H * W * 16))
        center = means[0:1]
        inverse = lax.rsqrt(means[1:2] - center * center + EPSILON)
        st_v[2 * number : 2 * number + 1, :] = center
        st_v[2 * number + 1 : 2 * number + 2, :] = inverse
        return center, inverse

    copies = statistics(0, x_v)
    w2_copies = weight_send(1, w2, w2_v)
    center, inverse = finish_statistics(0, copies)
    gain, bias = vec_v[0:1, :], vec_v[3:4, :]

    @pl.loop(0, CHUNKS)
    def _(i):
        value = (x_v[chunk_of(i), :].astype(F32) - center) * inverse
        put_shifted(a1_v, 64 + i * 64, swish(value * gain + bias))

    halo_send(me, a1_v, halo.at[0], hs.at[0], hr.at[0])
    hid_v[...] = jnp.broadcast_to(vec_v[6:7, :], (PIX, C))
    w1_forward = weight_forward(0, w1_v, w1_copies)
    weight_wait(0, w1, w1_v, w1_copies, w1_forward)
    save(9, w1_v, w1_o)
    wq_copies = weight_send(2, wq, wq_v)
    conv_taps(hid_v, a1_v, w1_v, (1,), False, NT)
    halo_wait(me, a1_v, halo.at[0], hs.at[0], hr.at[0])
    save(4, a1_v, a1_o)
    conv_taps(hid_v, a1_v, w1_v, (0, 2), False, NT)
    save(5, hid_v, hid_o)
    copies = statistics(1, hid_v)
    wo_copies = weight_send(3, wo, wo_v)
    image_send(tgt, t_v, tgs, tgr)
    center, inverse = finish_statistics(1, copies)
    gain, bias = vec_v[1:2, :], vec_v[4:5, :]
    scale, shift = 1.0 + vec_v[11:12, :], vec_v[12:13, :]

    @pl.loop(0, CHUNKS)
    def _(i):
        value = (hid_v[chunk_of(i), :] - center) * inverse
        put_shifted(a2_v, 64 + i * 64, swish((value * gain + bias) * scale + shift))

    halo_send(me, a2_v, halo.at[1], hs.at[1], hr.at[1])
    res_v[...] = x_v[...].astype(F32) + vec_v[7:8, :]
    w2_forward = weight_forward(1, w2_v, w2_copies)
    weight_wait(1, w2, w2_v, w2_copies, w2_forward)
    save(10, w2_v, w2_o)
    conv_taps(res_v, a2_v, w2_v, (1,), False, NT)
    halo_wait(me, a2_v, halo.at[1], hs.at[1], hr.at[1])
    save(6, a2_v, a2_o)
    conv_taps(res_v, a2_v, w2_v, (0, 2), False, NT)
    save(7, res_v, res_o)
    copies = statistics(2, res_v)
    wq_forward = weight_forward(2, wq_v, wq_copies)
    wo_forward = weight_forward(3, wo_v, wo_copies)
    weight_wait(2, wq, wq_v, wq_copies, wq_forward)
    save(11, wq_v, wq_o)
    center, inverse = finish_statistics(2, copies)
    gain, bias = vec_v[2:3, :], vec_v[5:6, :]
    normed = ((res_v[...] - center) * inverse * gain + bias)
    nrm_v[...] = normed.astype(BF)
    save(8, nrm_v, nrm_o)
    save(3, st_v, st_o)
    turned = jnp.transpose(normed).astype(BF)
    for j, row in ((0, 8), (1, None), (2, 9)):
        value = mm(wq_v[j], turned)
        if row is not None:
            wide = jnp.transpose(jnp.broadcast_to(vec_v[row : row + 1, :], (128, C)))
            value = value + jnp.concatenate([wide] * 4, axis=1)
        msg[j] = value.astype(BF)

    band_cols = pl.ds(pl.multiple_of(me.band * PIX, PIX), PIX)

    def head_rows(head):
        return pl.ds(pl.multiple_of(head * HEAD, HEAD), HEAD)

    own = local(msg.at[:, head_rows(me.d), :], qkv_v.at[:, :, band_cols], lsem.at[0])
    copies = []
    for step in range(1, 8):
        head = lax.rem(me.d + step, 8)
        copies.append(
            send(msg.at[:, head_rows(head), :], qkv_v.at[:, :, band_cols], qs.at[step],
                 qr.at[step], me.head_device(head))
        )
    weight_wait(3, wo, wo_v, wo_copies, wo_forward)
    save(12, wo_v, wo_o)
    image_wait(tgt, t_v, tgs, tgr)
    save(1, t_v, t_o)
    image_drain(img, x_v, ims, imr)
    image_drain(tgt, t_v, tgs, tgr)
    own.wait()
    for copy in copies:
        copy.wait()
    save(13, qkv_v, qkv_o)
    for copy in outs:
        copy.wait()


def front(img, tgt, vec, w1, w2, wq, wo):
    saved = [
        ((PIX, C), BF), ((PIX, C), BF), ((16, C), F32), ((8, C), F32), ((3, PAD, C), BF),
        ((PIX, C), F32), ((3, PAD, C), BF), ((PIX, C), F32), ((PIX, C), BF), ((9, C, C), BF),
        ((9, C, C), BF), ((3, C, C), BF), ((1, C, C), BF), ((3, HEAD, H * W), BF),
    ]
    return pl.pallas_call(
        front_kernel,
        name="front",
        out_shape=[jax.ShapeDtypeStruct(*one) for one in saved],
        in_specs=[ANY, ANY, VMEM, ANY, ANY, ANY, ANY],
        out_specs=[ANY] * len(saved),
        scratch_shapes=[pltpu.VMEM(*one) for one in saved]
        + [
            pltpu.VMEM((3, C, C), BF), pltpu.VMEM((C, C), BF), pltpu.VMEM((3, 8, 8, C), F32),
            pltpu.VMEM((2, 2, 64, C), BF),
            DMA((4,)), DMA((4,)), DMA((4,)), DMA((4,)), DMA((4,)), DMA((4,)),
            DMA((4, 4)), DMA((4, 4)), DMA((4, 4)), DMA((4, 4)), DMA((4,)),
            DMA((3, 8)), DMA((3, 8)), DMA((2, 2)), DMA((2, 2)), DMA((8,)), DMA((8,)),
            DMA((1,)), DMA((14,)),
        ],
        compiler_params=pltpu.CompilerParams(
            collective_id=1, has_side_effects=True, vmem_limit_bytes=VMEM_LIMIT
        ),
    )(img, tgt, vec, w1, w2, wq, wo)


LOG2E = 1.4426950408889634
QBLOCK = 256
VROWS = 80


def attend_kernel(qkv, ctx, p_o, pc_o, o_o, ot_o, linv_o, keys, ckeys, qs, vext, cvext):
    pixels = H * W
    i = pl.program_id(0)

    @pl.when(i == 0)
    def _():
        both = jnp.concatenate([qkv[1], qkv[1]], axis=0).astype(F32)
        keys[...] = jnp.transpose(both).astype(BF)
        cboth = jnp.concatenate([ctx[0], ctx[0]], axis=0).astype(F32)
        ckeys[...] = jnp.transpose(cboth)[0:16].astype(BF)
        scaled = qkv[0].astype(F32) * (HEAD ** (-0.5) * LOG2E)
        top = scaled.astype(BF)
        qs[0:HEAD, :] = top
        qs[HEAD:, :] = (scaled - top.astype(F32)).astype(BF)
        row = lax.broadcasted_iota(jnp.int32, (16, pixels), 0)
        vext[0:HEAD, :] = qkv[2]
        vext[HEAD:, :] = jnp.where(row == 0, 1.0, 0.0).astype(BF)
        cvext[0:HEAD, :] = ctx[1]
        cvext[HEAD:, :] = jnp.where(row[:, 0:128] == 0, 1.0, 0.0).astype(BF)

    cols = pl.ds(pl.multiple_of(i * QBLOCK, QBLOCK), QBLOCK)
    query = qs[:, cols]
    score = mm(keys[...], query)
    cscore = mm(ckeys[...], query)
    token = lax.broadcasted_iota(jnp.int32, (16, QBLOCK), 0)
    cscore = jnp.where(token < CTX, cscore, -1e30)
    top = jnp.maximum(
        jnp.max(score, axis=0, keepdims=True), jnp.max(cscore, axis=0, keepdims=True)
    )
    p_o[...] = jnp.exp2(score - top).astype(BF)
    pc = jnp.exp2(cscore - top).astype(BF)
    pc_o[...] = pc
    out = mm(vext[...], p_o[...]) + mm(cvext[:, 0:16], pc)
    linv = 1.0 / out[HEAD : HEAD + 1]
    out = out[0:HEAD] * linv
    o_o[...] = out
    ot_o[...] = out.astype(BF)
    linv_o[...] = jnp.broadcast_to(linv, (8, QBLOCK))


def attend(qkv, ctx):
    pixels = H * W
    whole = lambda *shape: pl.BlockSpec(shape, lambda i: (0,) * len(shape))
    cols = lambda rows: pl.BlockSpec((rows, QBLOCK), lambda i: (0, i))
    return pl.pallas_call(
        attend_kernel,
        name="attend",
        grid=(pixels // QBLOCK,),
        out_shape=[
            jax.ShapeDtypeStruct((pixels, pixels), BF),
            jax.ShapeDtypeStruct((16, pixels), BF),
            jax.ShapeDtypeStruct((HEAD, pixels), F32),
            jax.ShapeDtypeStruct((HEAD, pixels), BF),
            jax.ShapeDtypeStruct((8, pixels), F32),
        ],
        in_specs=[whole(3, HEAD, pixels), whole(2, HEAD, 128)],
        out_specs=[cols(pixels), cols(16), cols(HEAD), cols(HEAD), cols(8)],
        scratch_shapes=[
            pltpu.VMEM((pixels, 128), BF), pltpu.VMEM((16, 128), BF),
            pltpu.VMEM((128, pixels), BF), pltpu.VMEM((VROWS, pixels), BF),
            pltpu.VMEM((VROWS, 128), BF),
        ],
        compiler_params=pltpu.CompilerParams(vmem_limit_bytes=VMEM_LIMIT),
    )(qkv, ctx)


def band_back_send(me, src, dst, ssem, rsem):
    for chan in range(4):
        cols = pl.ds(chan * 128, 128)
        itself = jnp.logical_and(me.band == me.r, me.c == chan)

        @pl.when(jnp.logical_not(itself))
        def _():
            send(src.at[:, cols], dst.at[me.z], ssem.at[chan], rsem.at[me.z], (me.band, chan))

        @pl.when(itself)
        def _():
            local(src.at[:, cols], dst.at[me.z], rsem.at[me.z])


def band_back_wait(me, src, dst, ssem, rsem):
    for n in range(4):
        pltpu.make_async_copy(src.at[:, pl.ds(0, 128)], dst.at[n], rsem.at[n]).wait()
    for chan in range(4):
        itself = jnp.logical_and(me.band == me.r, me.c == chan)

        @pl.when(jnp.logical_not(itself))
        def _():
            pltpu.make_async_remote_copy(
                src_ref=src.at[:, pl.ds(chan * 128, 128)], dst_ref=dst.at[me.z],
                send_sem=ssem.at[chan], recv_sem=rsem.at[me.z], device_id=(me.band, chan),
                device_id_type=MESH_ID,
            ).wait_send()


def greet_back(me, barrier):
    own_block = me.c == lax.rem(2 * me.z, 4)
    for n in range(4):
        itself = jnp.logical_and(own_block, me.z == n)

        @pl.when(jnp.logical_not(itself))
        def _():
            pl.semaphore_signal(
                barrier, inc=1, device_id=(2 * n + me.k, lax.rem(me.z + n, 4)),
                device_id_type=MESH_ID,
            )

    return 4 - jnp.where(own_block, 1, 0)


def middle_kernel(
    ot, res, tgt, wo, vec,
    out_o, cot_o, gwo_o, gob_o, dot_o,
    attn_t, res_v, tgt_v, wo_v, out_b, back, cot_v, dat, dot_v,
    as_, ar, bs, br, ds_, dr, lsem, osem,
):
    me = Place()
    barrier = pltpu.get_barrier_semaphore()
    greet_plane(me, barrier)
    others = greet_back(me, barrier)
    loads = [local(a, b, lsem.at[j]) for j, (a, b) in enumerate(
        ((res, res_v), (tgt, tgt_v), (wo.at[0], wo_v)))]
    pl.semaphore_wait(barrier, 7 + others)
    mine = pl.ds(pl.multiple_of(me.d * HEAD, HEAD), HEAD)

    def band_cols(band):
        return pl.ds(pl.multiple_of(band * PIX, PIX), PIX)

    own = local(ot.at[:, band_cols(me.band)], attn_t.at[mine, :], lsem.at[3])
    copies = []
    for step in range(1, 8):
        band = lax.rem(me.band + step, 8)
        copies.append(
            send(ot.at[:, band_cols(band)], attn_t.at[mine, :], as_.at[step], ar.at[me.d],
                 me.band_device(band))
        )
    for load in loads:
        load.wait()
    own.wait()
    for copy in copies:
        copy.wait_send()
    for step in range(1, 8):
        head = lax.rem(me.d + step, 8)
        pltpu.make_async_copy(
            ot.at[:, band_cols(0)],
            attn_t.at[pl.ds(pl.multiple_of(head * HEAD, HEAD), HEAD), :],
            ar.at[head],
        ).wait()
    attn = jnp.transpose(attn_t[...].astype(F32)).astype(BF)
    result = res_v[...] + mm(attn, wo_v[...], NT) + vec[10:11, :]
    out_b[...] = result.astype(BF)
    band_back_send(me, out_b, back, bs, br)
    cot = vec[13:14, :] * (result - tgt_v[...].astype(F32))
    cot_v[...] = cot
    saves = [local(cot_v, cot_o, osem.at[0])]
    low = cot.astype(BF)
    dat[...] = jnp.transpose(mm(low, wo_v[...])).astype(BF)
    own = local(dat.at[mine, :], dot_v.at[:, band_cols(me.band)], lsem.at[4])
    copies = []
    for step in range(1, 8):
        head = lax.rem(me.d + step, 8)
        rows = pl.ds(pl.multiple_of(head * HEAD, HEAD), HEAD)
        copies.append(
            send(dat.at[rows, :], dot_v.at[:, band_cols(me.band)], ds_.at[step], dr.at[step],
                 me.head_device(head))
        )
    lowf = low.astype(F32)
    gwo_o[...] = mm(jnp.transpose(lowf).astype(BF), attn).astype(BF)
    gob_o[...] = jnp.broadcast_to(as_row(lowf), (8, C))
    band_back_wait(me, out_b, back, bs, br)
    out_o[...] = back[...].astype(F32)
    own.wait()
    for copy in copies:
        copy.wait()
    saves.append(local(dot_v, dot_o, osem.at[1]))
    for copy in saves:
        copy.wait()


def middle(ot, res, tgt, wo, vec):
    return pl.pallas_call(
        middle_kernel,
        name="middle",
        out_shape=[
            jax.ShapeDtypeStruct((4, PIX, 128), F32),
            jax.ShapeDtypeStruct((PIX, C), F32),
            jax.ShapeDtypeStruct((C, C), BF),
            jax.ShapeDtypeStruct((8, C), F32),
            jax.ShapeDtypeStruct((HEAD, H * W), BF),
        ],
        in_specs=[ANY, ANY, ANY, ANY, VMEM],
        out_specs=[VMEM, ANY, VMEM, VMEM, ANY],
        scratch_shapes=[
            pltpu.VMEM((C, PIX), BF), pltpu.VMEM((PIX, C), F32), pltpu.VMEM((PIX, C), BF),
            pltpu.VMEM((C, C), BF), pltpu.VMEM((PIX, C), BF), pltpu.VMEM((4, PIX, 128), BF),
            pltpu.VMEM((PIX, C), F32), pltpu.VMEM((C, PIX), BF), pltpu.VMEM((HEAD, H * W), BF),
            DMA((8,)), DMA((8,)), DMA((4,)), DMA((4,)), DMA((8,)), DMA((8,)), DMA((5,)),
            DMA((2,)),
        ],
        compiler_params=pltpu.CompilerParams(
            collective_id=2, has_side_effects=True, vmem_limit_bytes=VMEM_LIMIT
        ),
    )(ot, res, tgt, wo, vec)


KBLOCK = 256


def attend_back_kernel(
    qkv, ctx, p, pc, o, linv, dot_, dqkv_o, dctx_o, vext, cvext, dos, dor, qrow, dq
):
    pixels = H * W
    i = pl.program_id(0)
    scaling = HEAD ** (-0.5)

    def score_grads(values, probs):
        return (probs.astype(F32) * mm(values, dos[...])).astype(BF)

    @pl.when(i == 0)
    def _():
        row = lax.broadcasted_iota(jnp.int32, (HEAD, pixels), 0)
        ones = jnp.where(row < 3, 1.0, 0.0)
        vext[...] = jnp.transpose(
            jnp.concatenate([qkv[2].astype(F32), ones], axis=0)
        ).astype(BF)
        cvext[...] = jnp.transpose(
            jnp.concatenate([ctx[1].astype(F32), ones[:, 0:128]], axis=0)
        )[0:16].astype(BF)
        grad = (dot_[...].astype(F32) * linv[0:1, :]).astype(BF)
        gradf = grad.astype(F32)
        delta = -jnp.sum(gradf * o[...], axis=0, keepdims=True)
        top = delta.astype(BF).astype(F32)
        mid = (delta - top).astype(BF).astype(F32)
        low = delta - top - mid
        dos[0:HEAD, :] = grad
        dos[HEAD:, :] = jnp.where(
            row == 0, top, jnp.where(row == 1, mid, jnp.where(row == 2, low, 0.0))
        ).astype(BF)
        dor[...] = jnp.transpose(jnp.concatenate([gradf, jnp.zeros_like(gradf)], axis=0)).astype(BF)
        qf = qkv[0].astype(F32) * scaling
        qrow[...] = jnp.transpose(jnp.concatenate([qf, jnp.zeros_like(qf)], axis=0)).astype(BF)
        probs = pc[...]
        dsc = score_grads(cvext[...], probs)
        dctx_o[0] = mm(dsc, qrow[...])
        dctx_o[1] = mm(probs, dor[...])
        dq[...] = mm(ctx[0][:, 0:16], dsc)

    cols = pl.ds(pl.multiple_of(i * KBLOCK, KBLOCK), KBLOCK)
    probs = p[...]
    ds = score_grads(vext[cols, :], probs)
    dqkv_o[2, :, cols] = jnp.transpose(mm(probs, dor[...]))[0:HEAD].astype(BF)
    dqkv_o[1, :, cols] = jnp.transpose(mm(ds, qrow[...]))[0:HEAD].astype(BF)
    dq[...] += mm(qkv[1, :, cols], ds)

    @pl.when(i == pixels // KBLOCK - 1)
    def _():
        dqkv_o[0] = (dq[...] * scaling).astype(BF)


def attend_back(qkv, ctx, p, pc, o, linv, dot_):
    pixels = H * W
    whole = lambda *shape: pl.BlockSpec(shape, lambda i: (0,) * len(shape))
    return pl.pallas_call(
        attend_back_kernel,
        name="attend_back",
        grid=(pixels // KBLOCK,),
        out_shape=[
            jax.ShapeDtypeStruct((3, HEAD, pixels), BF),
            jax.ShapeDtypeStruct((2, 16, 128), F32),
        ],
        in_specs=[
            whole(3, HEAD, pixels), whole(2, HEAD, 128),
            pl.BlockSpec((KBLOCK, pixels), lambda i: (i, 0)),
            whole(16, pixels), whole(HEAD, pixels), whole(8, pixels), whole(HEAD, pixels),
        ],
        out_specs=[whole(3, HEAD, pixels), whole(2, 16, 128)],
        scratch_shapes=[
            pltpu.VMEM((pixels, 128), BF), pltpu.VMEM((16, 128), BF),
            pltpu.VMEM((128, pixels), BF), pltpu.VMEM((pixels, 128), BF),
            pltpu.VMEM((pixels, 128), BF), pltpu.VMEM((HEAD, pixels), F32),
        ],
        compiler_params=pltpu.CompilerParams(vmem_limit_bytes=VMEM_LIMIT),
    )(qkv, ctx, p, pc, o, linv, dot_)


TAPS = 22
GROUP_TAPS = ((0, 1), (1, 3), (4, 3), (7, 3), (10, 3), (13, 3), (16, 3), (19, 3))


class Reduce:
    def __init__(self, me, part, from_core, from_chan, plane, from_plane, total, sems):
        self.me = me
        self.part, self.from_core, self.from_chan = part, from_core, from_chan
        self.plane, self.from_plane, self.total = plane, from_plane, total
        self.sems = sems
        self.copies = {}

    def advance(self, group):
        stage = self.copies.get(group, (0, []))[0]
        for copy in self.copies.get(group, (0, []))[1]:
            copy.wait()
        step = (self.core_send, self.chan_send, self.plane_send, self.plane_gather,
                self.core_gather, lambda group, taps: [])[stage]
        start, count = GROUP_TAPS[group]
        self.copies[group] = (stage + 1, step(group, pl.ds(start, count)))

    def core_send(self, group, taps):
        me = self.me
        s, r = self.sems[0], self.sems[1]
        return [
            send(self.part.at[taps, :, 1 - me.k], self.from_core.at[taps], s.at[group],
                 r.at[group], (me.r + 1 - 2 * me.k, me.c))
        ]

    def chan_send(self, group, taps):
        me = self.me
        start, count = GROUP_TAPS[group]

        @pl.loop(start, start + count)
        def _(tap):
            own = self.part[tap, :, me.k].astype(F32) + self.from_core[tap].astype(F32)
            self.part[tap, :, me.k] = own.astype(BF)

        s, r = self.sems[2], self.sems[3]
        out = []
        for t in range(1, 4):
            chan = lax.rem(me.c + t, 4)
            out.append(
                send(self.part.at[taps, chan, me.k], self.from_chan.at[t - 1, taps],
                     s.at[group, t], r.at[group, t], (me.r, chan))
            )
        return out

    def plane_send(self, group, taps):
        me = self.me
        start, count = GROUP_TAPS[group]

        @pl.loop(start, start + count)
        def _(tap):
            value = self.part[tap, me.c, me.k].astype(F32)
            for t in range(3):
                value = value + self.from_chan[t, tap].astype(F32)
            self.plane[tap] = value.astype(BF)

        s, r = self.sems[4], self.sems[5]
        out = []
        for t in range(1, 4):
            z = lax.rem(me.z + t, 4)
            rows = pl.ds(pl.multiple_of(z * 16, 16), 16)
            out.append(
                send(self.plane.at[taps, rows, :], self.from_plane.at[t - 1, taps],
                     s.at[group, t], r.at[group, t], (2 * z + me.k, me.c))
            )
        return out

    def plane_gather(self, group, taps):
        me = self.me
        start, count = GROUP_TAPS[group]
        rows = pl.ds(pl.multiple_of(me.z * 16, 16), 16)

        @pl.loop(start, start + count)
        def _(tap):
            value = self.plane[tap, rows, :].astype(F32)
            for t in range(3):
                value = value + self.from_plane[t, tap].astype(F32)
            self.total[tap, me.k, me.z] = value.astype(BF)

        s, r = self.sems[6], self.sems[7]
        out = []
        for t in range(1, 4):
            z = lax.rem(me.z + t, 4)
            piece = self.total.at[taps, me.k, me.z]
            out.append(send(piece, piece, s.at[group, t], r.at[group, t], (2 * z + me.k, me.c)))
        return out

    def core_gather(self, group, taps):
        me = self.me
        s, r = self.sems[8], self.sems[9]
        piece = self.total.at[taps, me.k]
        return [send(piece, piece, s.at[group], r.at[group], (me.r + 1 - 2 * me.k, me.c))]


def back_kernel(
    dqkv, vec, st, x, a1, hid, a2, res, nrm, cot, w1, w2, wq, gwo, gob,
    gimg_o, zv_o, fin_o,
    dt_v, x_v, a1_v, hid_v, a2_v, res_v, nrm_v, drs_v, w1_v, w2_v, wq_v,
    cat, turned, acc, groups, slots, halo, keep, img_b, back, zsl,
    part, from_core, from_chan, plane, from_plane, total,
    as_, ar, ss, sr, hs, hr, bs, br, zs, zr, c1s, c1r, c2s, c2r, p1s, p1r, p2s, p2r, c3s, c3r,
    lsem, osem,
):
    me = Place()
    barrier = pltpu.get_barrier_semaphore()
    greet_plane(me, barrier)
    others = greet_back(me, barrier)
    for t in range(1, 4):
        pl.semaphore_signal(
            barrier, inc=1, device_id=(2 * lax.rem(me.z + t, 4) + me.k, me.c),
            device_id_type=MESH_ID,
        )
    loads = [local(a, b, lsem.at[j]) for j, (a, b) in enumerate((
        (gwo, part.at[0]), (nrm, nrm_v), (wq, wq_v), (res, res_v), (cot, drs_v), (a2, a2_v),
        (w2, w2_v), (hid, hid_v), (a1, a1_v), (w1, w1_v), (x, x_v)))]
    pl.semaphore_wait(barrier, 10 + others)
    reduce = Reduce(me, part, from_core, from_chan, plane, from_plane, total,
                    (c1s, c1r, c2s, c2r, p1s, p1r, p2s, p2r, c3s, c3r))
    mine = pl.ds(pl.multiple_of(me.d * HEAD, HEAD), HEAD)

    def band_cols(band):
        return pl.ds(pl.multiple_of(band * PIX, PIX), PIX)

    own = local(dqkv.at[:, :, band_cols(me.band)], dt_v.at[:, mine, :], lsem.at[11])
    copies = []
    for step in range(1, 8):
        band = lax.rem(me.band + step, 8)
        copies.append(
            send(dqkv.at[:, :, band_cols(band)], dt_v.at[:, mine, :], as_.at[step], ar.at[me.d],
                 me.band_device(band))
        )
    group_matrix(groups)
    zero8 = jnp.zeros((8, C), F32)
    members = 1.0 / (H * W * 16)
    loads[0].wait()
    reduce.advance(0)
    loads[1].wait()
    loads[2].wait()
    own.wait()
    for copy in copies:
        copy.wait_send()
    for step in range(1, 8):
        head = lax.rem(me.d + step, 8)
        pltpu.make_async_copy(
            dqkv.at[:, :, band_cols(0)],
            dt_v.at[:, pl.ds(pl.multiple_of(head * HEAD, HEAD), HEAD), :],
            ar.at[head],
        ).wait()

    @pl.loop(0, 3)
    def _(j):
        part[1 + j] = mm(dt_v[j], nrm_v[...]).astype(BF).reshape(4, 2, 64, C)

    reduce.advance(1)
    reduce.advance(0)
    for j in range(3):
        rows = jnp.transpose(dt_v[j].astype(F32))
        if j != 1:
            keep[j : j + 1, :] = as_row(rows)
        value = mm(rows.astype(BF), wq_v[j])
        if j == 0:
            acc[...] = value
        else:
            acc[...] += value
    loads[3].wait()

    def sums(scaled_of, upstream_of):
        def add(i, carry):
            upstream = upstream_of(i)
            return (carry[0] + fold(upstream), carry[1] + fold(upstream * scaled_of(i)))

        first, cross = lax.fori_loop(0, CHUNKS, add, (zero8, zero8))
        return [as_row(first), as_row(cross)]

    def scaled(ref, number):
        return lambda i: (ref[chunk_of(i), :].astype(F32) - st[2 * number : 2 * number + 1, :]) * st[
            2 * number + 1 : 2 * number + 2, :]

    def exchange(number, rows):
        store_rows(slots.at[number], me.d, rows)
        return plane_exchange(me, slots.at[number], ss.at[number], sr.at[number])

    scaled3, scaled2, scaled1 = scaled(res_v, 2), scaled(hid_v, 1), scaled(x_v, 0)
    copies = exchange(0, sums(scaled3, lambda i: acc[chunk_of(i), :]))
    reduce.advance(1)
    for load in loads[4:]:
        load.wait()
    for copy in copies:
        copy.wait()

    def group_means(total_rows, factor):
        return group_total(total_rows * factor, groups) * members

    total3 = slots_total(slots.at[0])
    gain = vec[2:3, :]
    means = group_means(total3, gain)
    keep[8:16, :] = total3
    inverse = st[5:6, :]

    def resid_grad(i, carry):
        where = chunk_of(i)
        value = drs_v[where, :] + inverse * (
            acc[where, :] * gain - means[0:1] - scaled3(i) * means[1:2])
        drs_v[where, :] = value
        put_shifted(cat, 64 + i * 64, value)
        return carry + fold(value.astype(BF).astype(F32))

    keep[3:4, :] = as_row(lax.fori_loop(0, CHUNKS, resid_grad, zero8))
    halo_send(me, cat, halo.at[0], hs.at[0], hr.at[0])
    reduce.advance(0)
    turned[...] = jnp.transpose(drs_v[...]).astype(BF)

    def weight_grads(group, source):
        start = GROUP_TAPS[group][0]
        row = (group - 2) % 3

        @pl.loop(0, 3)
        def _(col):
            part[start + col] = mm(turned[...], source[col, row * 64 : row * 64 + PIX, :]).astype(
                BF).reshape(4, 2, 64, C)

        reduce.advance(group)

    weight_grads(2, a2_v)
    reduce.advance(1)
    weight_grads(3, a2_v)
    reduce.advance(2)
    weight_grads(4, a2_v)
    reduce.advance(0)
    reduce.advance(3)
    acc[...] = jnp.zeros((PIX, C), F32)
    conv_taps(acc, cat, w2_v, (1,), True, NN)
    halo_wait(me, cat, halo.at[0], hs.at[0], hr.at[0])
    reduce.advance(1)
    reduce.advance(4)
    conv_taps(acc, cat, w2_v, (0, 2), True, NN)
    reduce.advance(2)
    gain2, bias2 = vec[1:2, :], vec[4:5, :]
    scale, shift = 1.0 + vec[11:12, :], vec[12:13, :]

    def mod_grad(i):
        where = chunk_of(i)
        mod = (scaled2(i) * gain2 + bias2) * scale + shift
        value = acc[where, :] * swish_slope(mod)
        acc[where, :] = value
        return value

    copies = exchange(1, sums(scaled2, mod_grad))
    reduce.advance(0)
    reduce.advance(3)
    for copy in copies:
        copy.wait()
    total2 = slots_total(slots.at[1])
    means2 = group_means(total2, gain2 * scale)
    keep[16:24, :] = total2
    inverse2 = st[3:4, :]

    def hidden_grad(i, carry):
        where = chunk_of(i)
        value = inverse2 * (
            acc[where, :] * (gain2 * scale) - means2[0:1] - scaled2(i) * means2[1:2])
        acc[where, :] = value
        put_shifted(cat, 64 + i * 64, value)
        return carry + fold(value.astype(BF).astype(F32))

    keep[1:2, :] = as_row(lax.fori_loop(0, CHUNKS, hidden_grad, zero8))
    halo_send(me, cat, halo.at[1], hs.at[1], hr.at[1])
    turned[...] = jnp.transpose(acc[...]).astype(BF)
    reduce.advance(1)
    weight_grads(5, a1_v)
    reduce.advance(4)
    reduce.advance(2)
    weight_grads(6, a1_v)
    reduce.advance(5)
    reduce.advance(3)
    weight_grads(7, a1_v)
    reduce.advance(6)
    reduce.advance(1)
    acc[...] = jnp.zeros((PIX, C), F32)
    conv_taps(acc, cat, w1_v, (1,), True, NN)
    halo_wait(me, cat, halo.at[1], hs.at[1], hr.at[1])
    reduce.advance(7)
    conv_taps(acc, cat, w1_v, (0, 2), True, NN)
    gain1, bias1 = vec[0:1, :], vec[3:4, :]

    def pre_grad(i):
        where = chunk_of(i)
        value = acc[where, :] * swish_slope(scaled1(i) * gain1 + bias1)
        acc[where, :] = value
        return value

    first, cross = sums(scaled1, pre_grad)
    copies = exchange(2, [first, cross, keep[1:2, :], keep[3:4, :], keep[0:1, :], keep[2:3, :],
                          gob[0:1, :]])
    reduce.advance(4)
    reduce.advance(2)
    reduce.advance(5)
    for copy in copies:
        copy.wait()
    total1 = slots_total(slots.at[2])
    means1 = group_means(total1, gain1)
    inverse1 = st[1:2, :]

    @pl.loop(0, CHUNKS)
    def _(i):
        where = chunk_of(i)
        value = drs_v[where, :] + inverse1 * (
            acc[where, :] * gain1 - means1[0:1] - scaled1(i) * means1[1:2])
        img_b[where, :] = value.astype(BF)

    band_back_send(me, img_b, back, bs, br)
    u2, v2 = keep[16:17, :], keep[17:18, :]
    keep[24:40, :] = jnp.concatenate(
        [total1[1:2], total1[0:1], scale * v2, scale * u2, keep[9:10, :], keep[8:9, :],
         total1[2:7], gain2 * v2 + bias2 * u2, u2, jnp.zeros((3, C), F32)], axis=0)
    own_cols = pl.ds(pl.multiple_of(me.c * 128, 128), 128)
    zsl[me.z] = keep[24:40, own_cols]
    zcopies = [
        send(zsl.at[me.z], zsl.at[me.z], zs.at[t], zr.at[t],
             (2 * lax.rem(me.z + t, 4) + me.k, me.c))
        for t in range(1, 4)
    ]
    for group in (3, 6, 7, 4, 2, 5, 3, 6, 7, 4, 2, 5, 3, 6, 7, 4, 5, 6, 7, 5, 6, 7, 6, 7):
        if reduce.copies[group][0] < 6:
            reduce.advance(group)
    band_back_wait(me, img_b, back, bs, br)
    gimg_o[...] = back[...].astype(F32)
    for copy in zcopies:
        copy.wait()
    zv_o[...] = zsl[...]
    for group in range(8):
        while reduce.copies[group][0] < 6:
            reduce.advance(group)
    local(total, fin_o, osem.at[0]).wait()


def back(*args):
    shared = [
        ((3, C, PIX), BF), ((PIX, C), BF), ((3, PAD, C), BF), ((PIX, C), F32), ((3, PAD, C), BF),
        ((PIX, C), F32), ((PIX, C), BF), ((PIX, C), F32), ((9, C, C), BF), ((9, C, C), BF),
        ((3, C, C), BF), ((3, PAD, C), BF), ((C, PIX), BF), ((PIX, C), F32), ((C, C), BF),
        ((3, 8, 8, C), F32), ((2, 2, 64, C), BF), ((40, C), F32), ((PIX, C), BF),
        ((4, PIX, 128), BF), ((4, 16, 128), F32),
        ((TAPS, 4, 2, 64, C), BF), ((TAPS, 4, 64, C), BF), ((3, TAPS, 64, C), BF),
        ((TAPS, 64, C), BF), ((3, TAPS, 16, C), BF), ((TAPS, 2, 4, 16, C), BF),
    ]
    return pl.pallas_call(
        back_kernel,
        name="back",
        out_shape=[
            jax.ShapeDtypeStruct((4, PIX, 128), F32),
            jax.ShapeDtypeStruct((4, 16, 128), F32),
            jax.ShapeDtypeStruct((TAPS, 2, 4, 16, C), BF),
        ],
        in_specs=[ANY, VMEM, VMEM] + [ANY] * 11 + [VMEM],
        out_specs=[VMEM, VMEM, ANY],
        scratch_shapes=[pltpu.VMEM(*one) for one in shared]
        + [
            DMA((8,)), DMA((8,)), DMA((3, 8)), DMA((3, 8)), DMA((2, 2)), DMA((2, 2)),
            DMA((4,)), DMA((4,)), DMA((4,)), DMA((4,)), DMA((8,)), DMA((8,)), DMA((8, 4)),
            DMA((8, 4)), DMA((8, 4)), DMA((8, 4)), DMA((8, 4)), DMA((8, 4)), DMA((8,)),
            DMA((8,)), DMA((12,)), DMA((1,)),
        ],
        compiler_params=pltpu.CompilerParams(
            collective_id=3, has_side_effects=True, vmem_limit_bytes=VMEM_LIMIT
        ),
    )(*args)


def plane_body(
    image, target, time_index, loss_weight, clip_embed, clip_tokens, norm_gain, norm_bias,
    conv1_w, conv2_w, conv_bias, emb_w, emb_b, qkv_w, qv_bias, ctx_w, ctx_b, out_w, out_b,
):
    row = lax.axis_index("row")
    z, k = row // 2, row % 2
    feat = swish(time_features(time_index, EMB) + clip_embed.astype(F32)).astype(BF)
    cond = jnp.einsum("ne,jde->njd", feat, emb_w, preferred_element_type=F32) + emb_b
    weight_row = jnp.broadcast_to(lax.dynamic_slice_in_dim(loss_weight, z, 1), (1, 128))
    vec = jnp.concatenate([
        norm_gain, norm_bias, conv_bias, qv_bias, out_b[None],
        lax.dynamic_index_in_dim(cond, z, 0, False), weight_row, jnp.zeros((2, 128), F32)])
    tokens = lax.dynamic_index_in_dim(clip_tokens, z, 0, False)
    ctx = jnp.einsum("jde,te->jdt", ctx_w, tokens, preferred_element_type=F32) + ctx_b[:, :, None]
    ctx = lax.dynamic_slice_in_dim(ctx, k * HEAD, HEAD, 1).astype(BF)
    ctx = jnp.pad(ctx, ((0, 0), (0, 0), (0, 128 - CTX)))
    x, tgt, vec_all, st, a1, hid, a2, res, nrm, w1, w2, wq, wo, qkv = front(
        image.reshape(4, PIX, 128), target.reshape(4, PIX, 128), vec,
        conv1_w.reshape(9, 128, C), conv2_w.reshape(9, 128, C), qkv_w, out_w[None])
    p, pc, o, ot, linv = attend(qkv, ctx)
    result, cot, gwo, gob, dot_ = middle(ot, res, tgt, wo, vec_all)
    dqkv, dctx = attend_back(qkv, ctx, p, pc, o, linv, dot_)
    dctx = lax.all_gather(dctx[:, :CTX, :HEAD], "row", axis=0, tiled=False)
    gimg, zv, fin = back(dqkv, vec_all, st, x, a1, hid, a2, res, nrm, cot, w1, w2, wq,
                         gwo.reshape(4, 2, 64, C), gob)
    dctx = dctx.reshape(4, 2, 2, CTX, HEAD)
    dctx = jnp.transpose(dctx, (0, 3, 2, 1, 4)).reshape(4, CTX, 2, 128)
    grad_ctx_w = jnp.einsum("nte,ntjd->jde", clip_tokens.astype(F32), dctx, precision=HIGH)
    sums = jnp.sum(zv, axis=0)
    dcond = zv[:, 11:13]
    grad_emb_w = jnp.einsum("ne,njd->jde", feat.astype(F32), dcond, precision=HIGH)
    fin = fin.reshape(TAPS, 128, C).astype(F32)
    return (
        result.reshape(image.shape),
        gimg.reshape(image.shape),
        jnp.stack([sums[0], sums[2], sums[4]]),
        jnp.stack([sums[1], sums[3], sums[5]]),
        fin[13:22].reshape(3, 3, 128, C),
        fin[4:13].reshape(3, 3, 128, C),
        sums[6:8],
        grad_emb_w,
        jnp.sum(dcond, axis=0),
        fin[1:4],
        sums[8:10],
        grad_ctx_w,
        jnp.sum(dctx, axis=(0, 1)),
        fin[0],
        sums[10],
    )


def solution(mesh):
    sizes = dict(mesh.shape)
    planes = sizes["row"] == 8 and sizes["chan"] == 4
    return jax.shard_map(
        plane_body if planes else general_body,
        mesh=mesh,
        in_specs=(
            P(None, "row", None, "chan"), P(None, "row", None, "chan"), P(), P(), P(), P(),
            P(None, "chan"), P(None, "chan"), P(None, None, "chan", None),
            P(None, None, "chan", None), P(None, "chan"), P(None, "chan", None),
            P(None, "chan"), P(None, "chan", None), P(None, "chan"), P(None, "chan", None),
            P(None, "chan"), P("chan", None), P("chan"),
        ),
        out_specs=(
            P(None, "row", None, "chan"), P(None, "row", None, "chan"), P(None, "chan"),
            P(None, "chan"), P(None, None, "chan", None), P(None, None, "chan", None),
            P(None, "chan"), P(None, "chan", None), P(None, "chan"), P(None, "chan", None),
            P(None, "chan"), P(None, "chan", None), P(None, "chan"), P("chan", None), P("chan"),
        ),
        check_vma=False,
    )
```

```python
import math

import jax
import jax.numpy as jnp
from jax import lax
from jax.experimental import pallas as pl
from jax.experimental.pallas import tpu as pltpu
from jax.sharding import PartitionSpec as P

C = 512
GROUPS = 32
HEAD = 64
EMB = 2048
CTXW = 2048
CTX = 4
H = 64
W = 64
MB_IMG = 2


HIGH = lax.Precision.HIGHEST
EPSILON = 1e-05


def with_halo(cells, sides, width):
    for axis, dim in sides:
        count = lax.axis_size(axis)
        ends = count - 1
        head = lax.slice_in_dim(cells, 0, width, axis=dim)
        tail = lax.slice_in_dim(cells, cells.shape[dim] - width, cells.shape[dim], axis=dim)
        cells = jnp.concatenate(
            [
                lax.ppermute(tail, axis, [(i, (i + 1) % count) for i in range(ends)]),
                cells,
                lax.ppermute(head, axis, [((i + 1) % count, i) for i in range(ends)]),
            ],
            axis=dim,
        )
    return cells


def swish(source):
    return source * jax.nn.sigmoid(source)


def swish_slope(source):
    sigma = jax.nn.sigmoid(source)
    return sigma * (1.0 + source * (1.0 - sigma))


def time_features(time_index, width_all):
    half_width = width_all // 2
    frequency = jnp.exp(-math.log(10000.0) * jnp.arange(half_width, dtype=jnp.float32) / half_width)
    angles = time_index.astype(jnp.float32)[:, None] * frequency[None, :]
    return jnp.concatenate([jnp.cos(angles), jnp.sin(angles)], axis=1)


def rows_around(source):
    return with_halo(source, (("row", 1),), 1)


def all_channels(source):
    return lax.all_gather(source, "chan", axis=3, tiled=True)


def channel_total(source):
    return lax.psum_scatter(
        source.astype(jnp.bfloat16), "chan", scatter_dimension=3, tiled=True
    ).astype(jnp.float32)


def norm_forward(source, group_width, members):
    layout = source.shape
    grouped = source.reshape(layout[0], layout[1], layout[2], layout[3] // group_width, group_width)
    first_sum = jnp.sum(grouped, axis=(1, 2, 4))
    square_sum = jnp.sum(grouped * grouped, axis=(1, 2, 4))
    first_sum, square_sum = lax.psum((first_sum, square_sum), "row")
    center = first_sum / members
    spread = square_sum / members - center * center
    inverse_std = lax.rsqrt(spread + EPSILON)
    scaled = (grouped - center[:, None, None, :, None]) * inverse_std[:, None, None, :, None]
    return (scaled.reshape(layout), inverse_std)


def norm_backward(upstream, scaled, inverse_std, gain, group_width, members):
    layout = upstream.shape
    grouped_grad = (upstream * gain).reshape(
        layout[0], layout[1], layout[2], layout[3] // group_width, group_width
    )
    grouped_norm = scaled.reshape(grouped_grad.shape)
    grad_sum = jnp.sum(grouped_grad, axis=(1, 2, 4))
    cross_sum = jnp.sum(grouped_grad * grouped_norm, axis=(1, 2, 4))
    grad_sum, cross_sum = lax.psum((grad_sum, cross_sum), "row")
    result = inverse_std[:, None, None, :, None] * (
        grouped_grad
        - grad_sum[:, None, None, :, None] / members
        - grouped_norm * (cross_sum[:, None, None, :, None] / members)
    )
    gain_grad = jnp.sum(upstream * scaled, axis=(0, 1, 2))
    bias_grad = jnp.sum(upstream, axis=(0, 1, 2))
    return (result.reshape(layout), gain_grad, bias_grad)


def conv_apply(padded, weight):
    height = padded.shape[1] - 2
    width = padded.shape[2]
    widened = jnp.pad(padded, ((0, 0), (0, 0), (1, 1), (0, 0)))
    result = None
    for row_step in range(3):
        for col_step in range(3):
            partial_term = jnp.einsum(
                "nhwc,dc->nhwd",
                widened[:, row_step : row_step + height, col_step : col_step + width],
                weight[row_step, col_step],
                preferred_element_type=jnp.float32,
            )
            result = partial_term if result is None else result + partial_term
    return result


def conv_weight_grad(padded, upstream_low):
    height = upstream_low.shape[1]
    width = upstream_low.shape[2]
    widened = jnp.pad(padded, ((0, 0), (0, 0), (1, 1), (0, 0)))
    stacked = []
    for row_step in range(3):
        row_terms = []
        for col_step in range(3):
            row_terms.append(
                jnp.einsum(
                    "nhwc,nhwd->dc",
                    widened[:, row_step : row_step + height, col_step : col_step + width],
                    upstream_low,
                    preferred_element_type=jnp.float32,
                )
            )
        stacked.append(jnp.stack(row_terms))
    return jnp.stack(stacked)


def conv_input_grad(upstream_low, weight):
    height = upstream_low.shape[1]
    width = upstream_low.shape[2]
    widened = jnp.pad(rows_around(upstream_low), ((0, 0), (0, 0), (1, 1), (0, 0)))
    result = None
    for row_step in range(3):
        for col_step in range(3):
            partial_term = jnp.einsum(
                "nhwd,dc->nhwc",
                widened[
                    :, 2 - row_step : 2 - row_step + height, 2 - col_step : 2 - col_step + width
                ],
                weight[row_step, col_step],
                preferred_element_type=jnp.float32,
            )
            result = partial_term if result is None else result + partial_term
    return channel_total(result)


def general_body(
    image,
    target,
    time_index,
    loss_weight,
    clip_embed,
    clip_tokens,
    norm_gain,
    norm_bias,
    conv1_w,
    conv2_w,
    conv_bias,
    emb_w,
    emb_b,
    qkv_w,
    qv_bias,
    ctx_w,
    ctx_b,
    out_w,
    out_b,
):
    local_chan = conv1_w.shape[2]
    group_width = C // GROUPS
    members = H * W * group_width
    head_count = local_chan // HEAD
    scaling = HEAD ** (-0.5)
    batches = image.shape[0] // MB_IMG
    band_rows = image.shape[1]
    image_cols = image.shape[2]

    def heads_of(source):
        return source.reshape(source.shape[0], -1, head_count, HEAD)

    def one_batch(carry, items):
        picture, target_in, steps_in, weight_in, embed_in, tokens_in = items
        feat_low = swish(time_features(steps_in, EMB) + embed_in.astype(jnp.float32)).astype(
            jnp.bfloat16
        )
        cond = (
            jnp.einsum("ne,jde->njd", feat_low, emb_w, preferred_element_type=jnp.float32) + emb_b
        )
        scale_term = cond[:, 0][:, None, None, :]
        shift_term = cond[:, 1][:, None, None, :]
        picture_f = picture.astype(jnp.float32)
        scaled_one, inverse_one = norm_forward(picture_f, group_width, members)
        pre_one = scaled_one * norm_gain[0] + norm_bias[0]
        padded_one = all_channels(rows_around(swish(pre_one).astype(jnp.bfloat16)))
        hidden = conv_apply(padded_one, conv1_w) + conv_bias[0]
        scaled_two, inverse_two = norm_forward(hidden, group_width, members)
        normal_two = scaled_two * norm_gain[1] + norm_bias[1]
        modded = normal_two * (1.0 + scale_term) + shift_term
        padded_two = all_channels(rows_around(swish(modded).astype(jnp.bfloat16)))
        resid = picture_f + conv_apply(padded_two, conv2_w) + conv_bias[1]
        scaled_three, inverse_three = norm_forward(resid, group_width, members)
        normed_full = all_channels(
            (scaled_three * norm_gain[2] + norm_bias[2]).astype(jnp.bfloat16)
        )
        projected = jnp.einsum(
            "nhwc,tdc->nhwtd", normed_full, qkv_w, preferred_element_type=jnp.float32
        )
        query_own = heads_of((projected[..., 0, :] + qv_bias[0]).astype(jnp.bfloat16))
        key_own = heads_of(projected[..., 1, :].astype(jnp.bfloat16))
        value_own = heads_of((projected[..., 2, :] + qv_bias[1]).astype(jnp.bfloat16))
        context = (
            jnp.einsum("nte,jde->ntjd", tokens_in, ctx_w, preferred_element_type=jnp.float32)
            + ctx_b
        )
        ctx_key = heads_of(context[:, :, 0].astype(jnp.bfloat16))
        ctx_value = heads_of(context[:, :, 1].astype(jnp.bfloat16))
        key_rows, value_rows = (
            lax.all_gather(key_own, "row", axis=1, tiled=True),
            lax.all_gather(value_own, "row", axis=1, tiled=True),
        )
        score_image = (
            jnp.einsum("nqhd,nkhd->nhqk", query_own, key_rows, preferred_element_type=jnp.float32)
            * scaling
        )
        score_context = (
            jnp.einsum("nqhd,nkhd->nhqk", query_own, ctx_key, preferred_element_type=jnp.float32)
            * scaling
        )
        top_score = jnp.maximum(jnp.max(score_image, axis=3), jnp.max(score_context, axis=3))
        expo_image = jnp.exp(score_image - top_score[..., None])
        expo_context = jnp.exp(score_context - top_score[..., None])
        denom = jnp.sum(expo_image, axis=3) + jnp.sum(expo_context, axis=3)
        prob_image = expo_image / denom[..., None]
        prob_context = expo_context / denom[..., None]
        attended = jnp.einsum(
            "nhqk,nkhd->nqhd",
            prob_image.astype(jnp.bfloat16),
            value_rows,
            preferred_element_type=jnp.float32,
        ) + jnp.einsum(
            "nhqk,nkhd->nqhd",
            prob_context.astype(jnp.bfloat16),
            ctx_value,
            preferred_element_type=jnp.float32,
        )
        attn_full = all_channels(attended.astype(jnp.bfloat16).reshape(picture.shape))
        result = (
            resid
            + jnp.einsum("nhwc,dc->nhwd", attn_full, out_w, preferred_element_type=jnp.float32)
            + out_b
        )
        cotangent = weight_in[:, None, None, None] * (result - target_in.astype(jnp.float32))
        grad_proj = cotangent.astype(jnp.bfloat16)
        grad_outw = jnp.einsum(
            "nhwc,nhwd->dc", attn_full, grad_proj, preferred_element_type=jnp.float32
        )
        grad_outb = jnp.sum(grad_proj.astype(jnp.float32), axis=(0, 1, 2))
        grad_attn = heads_of(
            channel_total(
                jnp.einsum("nhwd,dc->nhwc", grad_proj, out_w, preferred_element_type=jnp.float32)
            ).astype(jnp.bfloat16)
        )
        dprob_image = jnp.einsum(
            "nqhd,nkhd->nhqk", grad_attn, value_rows, preferred_element_type=jnp.float32
        )
        dprob_context = jnp.einsum(
            "nqhd,nkhd->nhqk", grad_attn, ctx_value, preferred_element_type=jnp.float32
        )
        delta = jnp.sum(prob_image * dprob_image, axis=3) + jnp.sum(
            prob_context * dprob_context, axis=3
        )
        dscore_image = (prob_image * (dprob_image - delta[..., None])).astype(jnp.bfloat16)
        dscore_context = (prob_context * (dprob_context - delta[..., None])).astype(jnp.bfloat16)
        grad_query = (
            jnp.einsum(
                "nhqk,nkhd->nqhd", dscore_image, key_rows, preferred_element_type=jnp.float32
            )
            + jnp.einsum(
                "nhqk,nkhd->nqhd", dscore_context, ctx_key, preferred_element_type=jnp.float32
            )
        ) * scaling
        grad_ctx_key = (
            jnp.einsum(
                "nhqk,nqhd->nkhd", dscore_context, query_own, preferred_element_type=jnp.float32
            )
            * scaling
        )
        grad_ctx_value = jnp.einsum(
            "nhqk,nqhd->nkhd",
            prob_context.astype(jnp.bfloat16),
            grad_attn,
            preferred_element_type=jnp.float32,
        )
        key_terms = (
            jnp.einsum(
                "nhqk,nqhd->nkhd", dscore_image, query_own, preferred_element_type=jnp.float32
            )
            * scaling
        )
        value_terms = jnp.einsum(
            "nhqk,nqhd->nkhd",
            prob_image.astype(jnp.bfloat16),
            grad_attn,
            preferred_element_type=jnp.float32,
        )
        grad_key, grad_value = (
            lax.psum_scatter(
                key_terms.astype(jnp.bfloat16), "row", scatter_dimension=1, tiled=True
            ).astype(jnp.float32),
            lax.psum_scatter(
                value_terms.astype(jnp.bfloat16), "row", scatter_dimension=1, tiled=True
            ).astype(jnp.float32),
        )
        grad_stack = (
            jnp.stack([grad_query, grad_key, grad_value], axis=2)
            .reshape(picture.shape[0], band_rows, image_cols, 3, local_chan)
            .astype(jnp.bfloat16)
        )
        grad_qkvw = jnp.einsum(
            "nhwc,nhwtd->tdc", normed_full, grad_stack, preferred_element_type=jnp.float32
        )
        stack_sums = jnp.sum(grad_stack.astype(jnp.float32), axis=(0, 1, 2))
        grad_qvb = jnp.stack([stack_sums[0], stack_sums[2]])
        grad_context = jnp.stack(
            [
                grad_ctx_key.reshape(picture.shape[0], CTX, local_chan),
                grad_ctx_value.reshape(picture.shape[0], CTX, local_chan),
            ],
            axis=2,
        )
        grad_ctxw = jnp.einsum(
            "nte,ntjd->jde", tokens_in.astype(jnp.float32), grad_context, precision=HIGH
        )
        grad_ctxb = jnp.sum(grad_context, axis=(0, 1))
        grad_normed = channel_total(
            jnp.einsum("nhwtd,tdc->nhwc", grad_stack, qkv_w, preferred_element_type=jnp.float32)
        )
        grad_resid, gain_three, bias_three = norm_backward(
            grad_normed, scaled_three, inverse_three, norm_gain[2], group_width, members
        )
        grad_resid = cotangent + grad_resid
        grad_conv_two = grad_resid.astype(jnp.bfloat16)
        grad_w_two = conv_weight_grad(padded_two, grad_conv_two)
        grad_b_two = jnp.sum(grad_conv_two.astype(jnp.float32), axis=(0, 1, 2))
        grad_modded = conv_input_grad(grad_conv_two, conv2_w) * swish_slope(modded)
        grad_cond = jnp.stack(
            [jnp.sum(grad_modded * normal_two, axis=(1, 2)), jnp.sum(grad_modded, axis=(1, 2))],
            axis=1,
        )
        grad_embw = jnp.einsum(
            "ne,njd->jde", feat_low.astype(jnp.float32), grad_cond, precision=HIGH
        )
        grad_embb = jnp.sum(grad_cond, axis=0)
        grad_hidden, gain_two, bias_two = norm_backward(
            grad_modded * (1.0 + scale_term),
            scaled_two,
            inverse_two,
            norm_gain[1],
            group_width,
            members,
        )
        grad_conv_one = grad_hidden.astype(jnp.bfloat16)
        grad_w_one = conv_weight_grad(padded_one, grad_conv_one)
        grad_b_one = jnp.sum(grad_conv_one.astype(jnp.float32), axis=(0, 1, 2))
        grad_pre_one = conv_input_grad(grad_conv_one, conv1_w) * swish_slope(pre_one)
        grad_input, gain_one, bias_one = norm_backward(
            grad_pre_one, scaled_one, inverse_one, norm_gain[0], group_width, members
        )
        grad_picture = grad_resid + grad_input
        grad_gains = jnp.stack([gain_one, gain_two, gain_three])
        grad_biases = jnp.stack([bias_one, bias_two, bias_three])
        grad_convb = jnp.stack([grad_b_one, grad_b_two])
        batch_grads = (
            grad_gains,
            grad_biases,
            grad_w_one,
            grad_w_two,
            grad_convb,
            grad_embw,
            grad_embb,
            grad_qkvw,
            grad_qvb,
            grad_ctxw,
            grad_ctxb,
            grad_outw,
            grad_outb,
        )
        updated = tuple((running + update for running, update in zip(carry, batch_grads)))
        return (updated, (result, grad_picture))

    start = (
        jnp.zeros(norm_gain.shape, jnp.float32),
        jnp.zeros(norm_bias.shape, jnp.float32),
        jnp.zeros(conv1_w.shape, jnp.float32),
        jnp.zeros(conv2_w.shape, jnp.float32),
        jnp.zeros(conv_bias.shape, jnp.float32),
        jnp.zeros(emb_w.shape, jnp.float32),
        jnp.zeros(emb_b.shape, jnp.float32),
        jnp.zeros(qkv_w.shape, jnp.float32),
        jnp.zeros(qv_bias.shape, jnp.float32),
        jnp.zeros(ctx_w.shape, jnp.float32),
        jnp.zeros(ctx_b.shape, jnp.float32),
        jnp.zeros(out_w.shape, jnp.float32),
        jnp.zeros(out_b.shape, jnp.float32),
    )
    items = (
        image.reshape(batches, MB_IMG, band_rows, image_cols, local_chan),
        target.reshape(batches, MB_IMG, band_rows, image_cols, local_chan),
        time_index.reshape(batches, MB_IMG),
        loss_weight.reshape(batches, MB_IMG),
        clip_embed.reshape(batches, MB_IMG, EMB),
        clip_tokens.reshape(batches, MB_IMG, CTX, CTXW),
    )
    totals, (results, picture_grads) = lax.scan(one_batch, start, items)
    (
        sum_gain,
        sum_bias,
        sum_conv_one,
        sum_conv_two,
        sum_conv_bias,
        sum_emb_w,
        sum_emb_b,
        sum_qkv_w,
        sum_qv_bias,
        sum_ctx_w,
        sum_ctx_b,
        sum_out_w,
        sum_out_b,
    ) = totals
    (
        sum_gain,
        sum_bias,
        sum_conv_one,
        sum_conv_two,
        sum_conv_bias,
        sum_emb_w,
        sum_emb_b,
        sum_qkv_w,
        sum_qv_bias,
        sum_ctx_w,
        sum_ctx_b,
        sum_out_w,
        sum_out_b,
    ) = (
        lax.psum(sum_gain.astype(jnp.bfloat16), "row").astype(jnp.float32),
        lax.psum(sum_bias.astype(jnp.bfloat16), "row").astype(jnp.float32),
        lax.psum(sum_conv_one.astype(jnp.bfloat16), "row").astype(jnp.float32),
        lax.psum(sum_conv_two.astype(jnp.bfloat16), "row").astype(jnp.float32),
        lax.psum(sum_conv_bias.astype(jnp.bfloat16), "row").astype(jnp.float32),
        lax.psum(sum_emb_w.astype(jnp.bfloat16), "row").astype(jnp.float32),
        lax.psum(sum_emb_b.astype(jnp.bfloat16), "row").astype(jnp.float32),
        lax.psum(sum_qkv_w.astype(jnp.bfloat16), "row").astype(jnp.float32),
        lax.psum(sum_qv_bias.astype(jnp.bfloat16), "row").astype(jnp.float32),
        lax.psum(sum_ctx_w.astype(jnp.bfloat16), "row").astype(jnp.float32),
        lax.psum(sum_ctx_b.astype(jnp.bfloat16), "row").astype(jnp.float32),
        lax.psum(sum_out_w.astype(jnp.bfloat16), "row").astype(jnp.float32),
        lax.psum(sum_out_b.astype(jnp.bfloat16), "row").astype(jnp.float32),
    )
    return (
        results.reshape(image.shape),
        picture_grads.reshape(image.shape),
        sum_gain,
        sum_bias,
        sum_conv_one,
        sum_conv_two,
        sum_conv_bias,
        sum_emb_w,
        sum_emb_b,
        sum_qkv_w,
        sum_qv_bias,
        sum_ctx_w,
        sum_ctx_b,
        sum_out_w,
        sum_out_b,
    )


BF = jnp.bfloat16
F32 = jnp.float32
MESH_ID = pl.DeviceIdType.MESH
NN = (((1,), (0,)), ((), ()))
NT = (((1,), (1,)), ((), ()))
ANY = pl.BlockSpec(memory_space=pl.ANY)
VMEM = pl.BlockSpec(memory_space=pltpu.VMEM)
PIX = 512
PAD = 640
CHUNKS = 8
VMEM_LIMIT = 60 * 2**20
DMA = pltpu.SemaphoreType.DMA


def mm(left, right, dims=NN):
    return lax.dot_general(left, right, dims, preferred_element_type=F32)


class Place:
    def __init__(self):
        self.r = lax.axis_index("row")
        self.c = lax.axis_index("chan")
        self.z = lax.div(self.r, 2)
        self.k = lax.rem(self.r, 2)
        self.d = 2 * self.c + self.k
        self.pair = lax.rem(self.c - self.z + 4, 4)
        self.band = 2 * self.pair + self.k

    def head_device(self, head):
        return (2 * self.z + lax.rem(head, 2), lax.div(head, 2))

    def band_device(self, band):
        return (2 * self.z + lax.rem(band, 2), lax.rem(lax.div(band, 2) + self.z, 4))


def send(src, dst, send_sem, recv_sem, device):
    copy = pltpu.make_async_remote_copy(
        src_ref=src,
        dst_ref=dst,
        send_sem=send_sem,
        recv_sem=recv_sem,
        device_id=device,
        device_id_type=MESH_ID,
    )
    copy.start()
    return copy


def local(src, dst, sem):
    copy = pltpu.make_async_copy(src, dst, sem)
    copy.start()
    return copy


def greet_plane(me, barrier):
    for step in range(1, 8):
        pl.semaphore_signal(
            barrier,
            inc=1,
            device_id=me.head_device(lax.rem(me.d + step, 8)),
            device_id_type=MESH_ID,
        )


def group_matrix(ref):
    rows = lax.broadcasted_iota(jnp.int32, (C, C), 0)
    cols = lax.broadcasted_iota(jnp.int32, (C, C), 1)
    ref[...] = jnp.where(lax.div(rows, 16) == lax.div(cols, 16), 1.0, 0.0).astype(BF)


def group_total(rows, groups_ref):
    top = rows.astype(BF)
    rest = rows - top.astype(F32)
    mid = rest.astype(BF)
    low = (rest - mid.astype(F32)).astype(BF)
    stacked = jnp.concatenate([top, mid, low, jnp.zeros_like(low)], axis=0)
    sums = mm(stacked, groups_ref[...])
    return sums[0:8] + sums[8:16] + sums[16:24]


def plane_exchange(me, slots, ssem, rsem):
    copies = []
    for step in range(1, 8):
        copies.append(
            send(
                slots.at[me.d],
                slots.at[me.d],
                ssem.at[step],
                rsem.at[step],
                me.head_device(lax.rem(me.d + step, 8)),
            )
        )
    return copies


def slots_total(slots):
    total = slots[0]
    for slot in range(1, 8):
        total = total + slots[slot]
    return total


def fold(value):
    return value.reshape(value.shape[0] // 8, 8, value.shape[1]).sum(axis=0)


def as_row(value):
    return jnp.sum(value, axis=0, keepdims=True)


def store_rows(slots, index, rows):
    filled = rows + [jnp.zeros((1, C), F32)] * (8 - len(rows))
    slots[index] = jnp.concatenate(filled, axis=0)


def chunk_of(i):
    return pl.ds(pl.multiple_of(i * 64, 64), 64)


def put_shifted(dst, start, value):
    col = lax.broadcasted_iota(jnp.int32, (64, C), 0)
    where = pl.ds(pl.multiple_of(start, 64), 64)
    dst[1, where, :] = value.astype(BF)
    dst[0, where, :] = jnp.where(col == 0, 0.0, pltpu.roll(value, 1, 0)).astype(BF)
    dst[2, where, :] = jnp.where(col == 63, 0.0, pltpu.roll(value, 63, 0)).astype(BF)


def halo_send(me, cat, halo, ssem, rsem):
    @pl.when(me.band > 0)
    def _():
        send(cat.at[1, pl.ds(64, 64), :], halo.at[1], ssem.at[0], rsem.at[1],
             me.band_device(me.band - 1))

    @pl.when(me.band < 7)
    def _():
        send(cat.at[1, pl.ds(512, 64), :], halo.at[0], ssem.at[1], rsem.at[0],
             me.band_device(me.band + 1))


def halo_wait(me, cat, halo, ssem, rsem):
    def pair(slot, ahead):
        return pltpu.make_async_remote_copy(
            src_ref=cat.at[1, pl.ds(64, 64), :], dst_ref=halo.at[slot],
            send_sem=ssem.at[slot], recv_sem=rsem.at[slot],
            device_id=me.band_device(ahead), device_id_type=MESH_ID)

    zero = jnp.zeros((64, C), F32)

    @pl.when(me.band > 0)
    def _():
        both = pair(0, me.band - 1)
        both.wait_send()
        both.wait_recv()
        put_shifted(cat, 0, halo[0].astype(F32))

    @pl.when(me.band == 0)
    def _():
        put_shifted(cat, 0, zero)

    @pl.when(me.band < 7)
    def _():
        both = pair(1, me.band + 1)
        both.wait_send()
        both.wait_recv()
        put_shifted(cat, 576, halo[1].astype(F32))

    @pl.when(me.band == 7)
    def _():
        put_shifted(cat, 576, zero)


def conv_taps(acc, cat, weight, order, flip, dims):
    @pl.loop(0, 3 * len(order))
    def _(i):
        step = lax.div(i, 3)
        col = lax.rem(i, 3)
        row = order[0] if len(order) == 1 else order[0] + step * (order[1] - order[0])
        tap = (2 - row) * 3 + (2 - col) if flip else row * 3 + col
        start = pl.multiple_of(row * 64, 64)
        acc[...] += mm(cat[col, pl.ds(start, PIX), :], weight[tap], dims)


LOG2E = 1.4426950408889634
VROWS = 80
SUB = 256
KEYS = 512


def image_targets(me):
    return [(n, (2 * n + me.k, lax.rem(me.z + n, 4))) for n in range(4)]


class Gather:
    def __init__(self, me, index, src, dst, sems):
        self.me, self.src, self.dst = me, src, dst
        third = src.shape[0] // 3
        odd = lax.rem(me.z, 2)
        self.plane_taps = pl.ds(third * odd, 2 * third)
        self.give_taps = pl.ds(2 * third * odd, third)
        self.take_taps = pl.ds(2 * third * (1 - odd), third)
        self.x = me.c + 1 - 2 * lax.rem(me.c, 2)
        self.y = lax.rem(me.c + 2, 4)
        self.far = lax.rem(self.x + 2, 4)
        self.core = (me.r + 1 - 2 * me.k, me.c)
        self.over = (2 * (me.z + 1 - 2 * odd) + me.k, me.c)
        (self.own, self.first_s, self.first_r, self.relay_s, self.relay_r, self.give_s,
         self.give_r, self.core_s, self.core_r) = [sem.at[index] for sem in sems]
        self.started = []
        self.core_plane = []
        self.core_take = []
        self.gives = []

    def rows(self, chan, start=0, size=64):
        return pl.ds(pl.multiple_of(chan * 128 + self.me.k * 64 + start, size), size)

    def move(self, taps, rows, s, r, device):
        piece = self.dst.at[taps, rows, :]
        return send(piece, piece, s, r, device)

    def start(self):
        me = self.me
        half = pl.ds(pl.multiple_of(me.k * 64, 64), 64)
        quarter = pl.ds(pl.multiple_of(me.c * 128, 128), 128)
        for j, chan in enumerate((self.x, self.y)):
            self.started.append(
                send(self.src.at[self.plane_taps, half, :],
                     self.dst.at[self.plane_taps, self.rows(me.c), :],
                     self.first_s.at[j], self.first_r.at[j], (me.r, chan)))
        self.kept = local(self.src, self.dst.at[:, quarter, :], self.own.at[0])

    def spread(self, slot, chan):
        self.core_plane.append(
            self.move(self.plane_taps, self.rows(chan), self.core_s.at[slot], self.core_r.at[slot],
                      self.core))
        self.gives.append(
            self.move(self.give_taps, self.rows(chan), self.give_s.at[slot], self.give_r.at[slot],
                      self.over))

    def relay(self):
        self.relays = []
        for j, (chan, onward) in enumerate(((self.x, self.y), (self.y, self.x))):
            self.started[j].wait_recv()
            self.relays.append(
                self.move(self.plane_taps, self.rows(chan, 32 * j, 32), self.relay_s.at[j],
                          self.relay_r.at[j], (self.me.r, onward)))
            self.spread(j, chan)

    def relayed(self):
        for copy in self.relays:
            copy.wait_recv()
        self.spread(2, self.far)

    def plane_done(self):
        self.kept.wait()
        for copy in self.core_plane:
            copy.wait_recv()

    def take(self):
        for slot, chan in enumerate((self.x, self.y, self.far)):
            self.gives[slot].wait_recv()
            self.core_take.append(
                self.move(self.take_taps, self.rows(chan), self.core_s.at[3 + slot],
                          self.core_r.at[3 + slot], self.core))

    def take_done(self):
        for copy in self.core_take:
            copy.wait_recv()

    def drain(self):
        for copy in self.started + self.relays + self.gives + self.core_plane + self.core_take:
            copy.wait_send()


def front_kernel(
    img, tgt, vec, feat, tokens, emb_w, emb_b, ctx_w, ctx_b, w1, w2, wq, wo,
    x_o, t_o, vec_o, st_o, a1_o, hid_o, a2_o, res_o, nrm_o, w1_o, w2_o, wq_o, wo_o, qkv_o,
    attn_o, p_o, ctx_o, pc_o, o_o, linv_o,
    x_v, t_v, vec_v, st_v, a1_v, hid_v, a2_v, res_v, nrm_v, w1_v, w2_v, wq_v, wo_v, qkv_v,
    attn_v,
    msg, groups, slots, halo, vsrc, cond, keys, ckeys, qs, vext, cvext, sbuf, mbuf, cbuf, pb, ob,
    vs, vr, ims, imr, tgs, tgr, own_sem, first_s, first_r, relay_s, relay_r, give_s, give_r,
    core_s, core_r, wos, wor, wofs, wofr, wol, sts, str_, hs, hr, qs_s, qs_r, lsem, osem, psem,
    as_, ar,
):
    me = Place()
    barrier = pltpu.get_barrier_semaphore()
    greet_plane(me, barrier)
    own_block = me.c == lax.rem(2 * me.z, 4)
    for chan in range(4):
        itself = jnp.logical_and(me.pair == me.z, me.c == chan)

        @pl.when(jnp.logical_not(itself))
        def _():
            pl.semaphore_signal(
                barrier, inc=1, device_id=(2 * me.pair + me.k, chan), device_id_type=MESH_ID
            )

    odd = lax.rem(me.z, 2)
    pl.semaphore_signal(
        barrier, inc=1, device_id=(2 * (me.z + 1 - 2 * odd) + me.k, me.c), device_id_type=MESH_ID
    )
    for j in range(2):
        cond[j] = mm(feat[...], emb_w[j], NT) + emb_b[j : j + 1, :]
    vsrc[0:11, :] = vec[0:11, :]
    vsrc[11:12, :] = cond[0, pl.ds(me.z, 1), :]
    vsrc[12:13, :] = cond[1, pl.ds(me.z, 1), :]
    vsrc[13:16, :] = vec[13:16, :]
    lane = lax.broadcasted_iota(jnp.int32, (16, 128), 1)
    for j in range(2):
        value = mm(tokens[...], ctx_w[j], NT) + ctx_b[j : j + 1, :]
        turned = pltpu.roll(value, HEAD, 1)
        first = lax.div(lane, HEAD) == me.k
        both = jnp.where(first, value, turned)
        ctx_o[j] = both.astype(BF)
        if j == 0:
            ckeys[...] = both.astype(BF)
        else:
            wide = jnp.concatenate([both, jnp.zeros((112, 128), F32)], axis=0)
            cvext[0:HEAD, :] = jnp.transpose(wide)[0:HEAD].astype(BF)
    row = lax.broadcasted_iota(jnp.int32, (16, H * W), 0)
    vext[HEAD:, :] = jnp.where(row == 0, 1.0, 0.0).astype(BF)
    cvext[HEAD:, :] = jnp.where(row[:, 0:128] == 0, 1.0, 0.0).astype(BF)
    pl.semaphore_wait(barrier, 8 + 4 - jnp.where(own_block, 1, 0))
    own_cols = pl.ds(pl.multiple_of(me.c * 128, 128), 128)

    vec_v[:, own_cols] = vsrc[...]
    vec_copies = [
        send(vsrc, vec_v.at[:, own_cols], vs.at[t], vr.at[t], (me.r, lax.rem(me.c + t, 4)))
        for t in range(1, 4)
    ]

    def image_send(src, dst, ssem, rsem):
        for n, device in image_targets(me):
            itself = jnp.logical_and(own_block, me.z == n)

            @pl.when(jnp.logical_not(itself))
            def _():
                send(src.at[n], dst.at[:, own_cols], ssem.at[n], rsem.at[me.c], device)

            @pl.when(itself)
            def _():
                local(src.at[n], dst.at[:, own_cols], rsem.at[me.c])

    def image_wait(src, dst, ssem, rsem):
        for chan in range(4):
            pltpu.make_async_copy(
                src.at[0], dst.at[:, pl.ds(chan * 128, 128)], rsem.at[chan]
            ).wait()

    def image_drain(src, dst, ssem, rsem):
        for n, device in image_targets(me):
            itself = jnp.logical_and(own_block, me.z == n)

            @pl.when(jnp.logical_not(itself))
            def _():
                pltpu.make_async_remote_copy(
                    src_ref=src.at[n], dst_ref=dst.at[:, own_cols], send_sem=ssem.at[n],
                    recv_sem=rsem.at[me.c], device_id=device, device_id_type=MESH_ID,
                ).wait_send()

    gather_sems = (own_sem, first_s, first_r, relay_s, relay_r, give_s, give_r, core_s, core_r)
    gather1 = Gather(me, 0, w1, w1_v, gather_sems)
    gather2 = Gather(me, 1, w2, w2_v, gather_sems)
    gather3 = Gather(me, 2, wq, wq_v, gather_sems)

    image_send(img, x_v, ims, imr)
    gather1.start()
    group_matrix(groups)
    col_zero = jnp.zeros((8, C), F32)
    for copy in vec_copies:
        copy.wait()
    outs = []

    def save(index, src, dst):
        outs.append(local(src, dst, osem.at[index]))

    def statistics(number, ref):
        def add(i, carry):
            value = ref[chunk_of(i), :].astype(F32)
            return (carry[0] + fold(value), carry[1] + fold(value * value))

        first, square = lax.fori_loop(0, CHUNKS, add, (col_zero, col_zero))
        store_rows(slots.at[number], me.d, [as_row(first), as_row(square)])
        return plane_exchange(me, slots.at[number], sts.at[number], str_.at[number])

    def finish_statistics(number, copies):
        for copy in copies:
            copy.wait()
        means = group_total(slots_total(slots.at[number]), groups) * (1.0 / (H * W * 16))
        center = means[0:1]
        inverse = lax.rsqrt(means[1:2] - center * center + EPSILON)
        st_v[2 * number : 2 * number + 1, :] = center
        st_v[2 * number + 1 : 2 * number + 2, :] = inverse
        return center, inverse

    image_wait(img, x_v, ims, imr)
    copies = statistics(0, x_v)
    save(0, x_v, x_o)
    save(2, vec_v, vec_o)
    gather1.relay()
    center, inverse = finish_statistics(0, copies)
    gain, bias = vec_v[0:1, :], vec_v[3:4, :]

    @pl.loop(0, CHUNKS)
    def _(i):
        value = (x_v[chunk_of(i), :].astype(F32) - center) * inverse
        put_shifted(a1_v, 64 + i * 64, swish(value * gain + bias))

    halo_send(me, a1_v, halo.at[0], hs.at[0], hr.at[0])
    gather1.relayed()
    gather2.start()
    hid_v[...] = jnp.broadcast_to(vec_v[6:7, :], (PIX, C))
    gather1.plane_done()
    conv_taps(hid_v, a1_v, w1_v, (1,), False, NT)
    halo_wait(me, a1_v, halo.at[0], hs.at[0], hr.at[0])
    save(4, a1_v, a1_o)
    gather1.take()
    conv_taps(hid_v, a1_v, w1_v, (2 * odd,), False, NT)
    gather1.take_done()
    conv_taps(hid_v, a1_v, w1_v, (2 - 2 * odd,), False, NT)
    copies = statistics(1, hid_v)
    save(9, w1_v, w1_o)
    save(5, hid_v, hid_o)
    gather2.relay()
    center, inverse = finish_statistics(1, copies)
    gain, bias = vec_v[1:2, :], vec_v[4:5, :]
    scale, shift = 1.0 + vec_v[11:12, :], vec_v[12:13, :]

    @pl.loop(0, CHUNKS)
    def _(i):
        value = (hid_v[chunk_of(i), :] - center) * inverse
        put_shifted(a2_v, 64 + i * 64, swish((value * gain + bias) * scale + shift))

    halo_send(me, a2_v, halo.at[1], hs.at[1], hr.at[1])
    gather2.relayed()
    gather3.start()
    res_v[...] = x_v[...].astype(F32) + vec_v[7:8, :]
    gather2.plane_done()
    conv_taps(res_v, a2_v, w2_v, (1,), False, NT)
    halo_wait(me, a2_v, halo.at[1], hs.at[1], hr.at[1])
    save(6, a2_v, a2_o)
    gather2.take()
    gather3.relay()
    conv_taps(res_v, a2_v, w2_v, (2 * odd,), False, NT)
    gather2.take_done()
    gather3.relayed()
    conv_taps(res_v, a2_v, w2_v, (2 - 2 * odd,), False, NT)
    copies = statistics(2, res_v)
    save(10, w2_v, w2_o)
    save(7, res_v, res_o)
    gather3.take()
    center, inverse = finish_statistics(2, copies)
    gain, bias = vec_v[2:3, :], vec_v[5:6, :]
    normed = (res_v[...] - center) * inverse * gain + bias
    nrm_v[...] = normed.astype(BF)
    st_v[6:8, :] = jnp.zeros((2, C), F32)
    save(8, nrm_v, nrm_o)
    save(3, st_v, st_o)
    turned = jnp.transpose(normed).astype(BF)
    gather3.plane_done()
    gather3.take_done()
    save(11, wq_v, wq_o)
    band_cols = pl.ds(pl.multiple_of(me.band * PIX, PIX), PIX)

    def head_rows(head):
        return pl.ds(pl.multiple_of(head * HEAD, HEAD), HEAD)

    owns = []
    qkv_copies = {}
    for j, bias_row in ((1, None), (0, 8), (2, 9)):
        value = mm(wq_v[j], turned)
        if bias_row is not None:
            wide = jnp.transpose(jnp.broadcast_to(vec_v[bias_row : bias_row + 1, :], (128, C)))
            value = value + jnp.concatenate([wide] * 4, axis=1)
        msg[j] = value.astype(BF)
        owns.append(local(msg.at[j, head_rows(me.d), :], qkv_v.at[j, :, band_cols], lsem.at[j]))
        qkv_copies[j] = []
        for step in range(1, 8):
            head = lax.rem(me.d + step, 8)
            qkv_copies[j].append(
                send(msg.at[j, head_rows(head), :], qkv_v.at[j, :, band_cols], qs_s.at[j, step],
                     qs_r.at[j, step], me.head_device(head)))

    for own in owns:
        own.wait()
    for copy in qkv_copies[1]:
        copy.wait()
    both = jnp.concatenate([qkv_v[1], qkv_v[1]], axis=0).astype(F32)
    keys[...] = jnp.transpose(both).astype(BF)
    for copy in qkv_copies[0]:
        copy.wait()
    scaled = qkv_v[0].astype(F32) * (HEAD ** (-0.5) * LOG2E)
    top = scaled.astype(BF)
    qs[0:HEAD, :] = top
    qs[HEAD:, :] = (scaled - top.astype(F32)).astype(BF)
    token = lax.broadcasted_iota(jnp.int32, (16, SUB), 0)
    valid = lax.div(token, CTX) == me.z
    chunks = H * W // KEYS

    def begin(slot, block):
        query = qs[:, pl.ds(pl.multiple_of(block * SUB, SUB), SUB)]
        score = jnp.where(valid, mm(ckeys[...], query), -1e30)
        cbuf[slot] = score
        return query, jnp.maximum(score[0:8], score[8:16])

    def score_chunk(slot, query, highest, chunk):
        value = mm(keys[chunk * KEYS : (chunk + 1) * KEYS, :], query)
        sbuf[slot, chunk * KEYS : (chunk + 1) * KEYS, :] = value
        return jnp.maximum(highest, jnp.max(value.reshape(KEYS // 8, 8, SUB), axis=0))

    query, highest = begin(0, 0)
    for chunk in range(chunks):
        highest = score_chunk(0, query, highest, chunk)
    mbuf[0] = highest
    for copy in qkv_copies[2]:
        copy.wait()
    vext[0:HEAD, :] = qkv_v[2]
    save(13, qkv_v, qkv_o)
    image_send(tgt, t_v, tgs, tgr)
    half = pl.ds(pl.multiple_of(me.c * 128 + me.k * 64, 64), 64)
    my_half = pl.ds(pl.multiple_of(me.k * 64, 64), 64)
    wo_own = local(wo, wo_v.at[:, own_cols, :], wol.at[0])
    wo_copies = [
        send(wo.at[:, my_half, :], wo_v.at[:, half, :], wos.at[t], wor.at[t],
             (me.r, lax.rem(me.c + t, 4)))
        for t in range(1, 4)
    ]
    attn_rows = head_rows(me.d)

    def p_copy(block, slot):
        return pltpu.make_async_copy(
            pb.at[slot], p_o.at[:, pl.ds(pl.multiple_of(block * PIX, PIX), PIX)], psem.at[slot])

    @pl.loop(0, 8)
    def _(block):
        slot = lax.rem(block, 2)

        @pl.when(block >= 2)
        def _():
            p_copy(block - 2, slot).wait()

        for sub in range(2):
            cols = pl.ds(sub * SUB, SUB)
            wide = pl.ds(pl.multiple_of(block * PIX + sub * SUB, SUB), SUB)
            following = jnp.minimum(2 * block + sub + 1, H * W // SUB - 1)
            top = jnp.max(mbuf[sub], axis=0, keepdims=True)
            pc = jnp.exp2(cbuf[sub] - top).astype(BF)
            pc_o[:, wide] = pc
            out = mm(cvext[:, 0:16], pc)
            query, highest = begin(1 - sub, following)
            for chunk in range(chunks):
                highest = score_chunk(1 - sub, query, highest, chunk)
                rows = slice(chunk * KEYS, (chunk + 1) * KEYS)
                probs = jnp.exp2(sbuf[sub, rows, :] - top).astype(BF)
                pb[slot, rows, cols] = probs
                out = out + mm(vext[:, rows], probs)
            mbuf[1 - sub] = highest
            linv = 1.0 / out[HEAD : HEAD + 1]
            out = out[0:HEAD] * linv
            o_o[:, wide] = out
            ob[block, :, cols] = out.astype(BF)
            linv_o[:, wide] = jnp.broadcast_to(linv, (8, SUB))
        p_copy(block, slot).start()

        @pl.when(block != me.band)
        def _():
            send(ob.at[block], attn_v.at[attn_rows, :], as_.at[block], ar.at[me.d],
                 me.band_device(block))

        @pl.when(block == me.band)
        def _():
            local(ob.at[block], attn_v.at[attn_rows, :], ar.at[me.d])

    wo_forward = []
    for t in range(1, 4):
        wo_copies[t - 1].wait()
        origin = lax.rem(me.c - t + 4, 4)
        rows = pl.ds(pl.multiple_of(origin * 128 + me.k * 64, 64), 64)
        wo_forward.append(
            send(wo_v.at[:, rows, :], wo_v.at[:, rows, :], wofs.at[t], wofr.at[t],
                 (me.r + 1 - 2 * me.k, me.c)))
    image_wait(tgt, t_v, tgs, tgr)
    save(1, t_v, t_o)
    for gather in (gather1, gather2, gather3):
        gather.drain()
    image_drain(img, x_v, ims, imr)
    image_drain(tgt, t_v, tgs, tgr)
    wo_own.wait()
    for copy in wo_forward:
        copy.wait()
    save(12, wo_v, wo_o)
    for block in range(8):

        @pl.when(block != me.band)
        def _():
            pltpu.make_async_remote_copy(
                src_ref=ob.at[block], dst_ref=attn_v.at[attn_rows, :], send_sem=as_.at[block],
                recv_sem=ar.at[me.d], device_id=me.band_device(block), device_id_type=MESH_ID,
            ).wait_send()

        pltpu.make_async_copy(
            ob.at[0], attn_v.at[pl.ds(block * HEAD, HEAD), :], ar.at[block]).wait()
    save(14, attn_v, attn_o)
    p_copy(6, 0).wait()
    p_copy(7, 1).wait()
    for copy in outs:
        copy.wait()


def front(*args):
    pixels = H * W
    saved = [
        ((PIX, C), BF), ((PIX, C), BF), ((16, C), F32), ((8, C), F32), ((3, PAD, C), BF),
        ((PIX, C), F32), ((3, PAD, C), BF), ((PIX, C), F32), ((PIX, C), BF), ((9, C, C), BF),
        ((9, C, C), BF), ((3, C, C), BF), ((1, C, C), BF), ((3, HEAD, pixels), BF), ((C, PIX), BF),
    ]
    more = [
        ((pixels, pixels), BF), ((2, 16, 128), BF), ((16, pixels), BF), ((HEAD, pixels), F32),
        ((8, pixels), F32),
    ]
    return pl.pallas_call(
        front_kernel,
        name="front",
        out_shape=[jax.ShapeDtypeStruct(*one) for one in saved + more],
        in_specs=[ANY, ANY] + [VMEM] * 7 + [ANY] * 4,
        out_specs=[ANY] * (len(saved) + 1) + [VMEM] * 4,
        scratch_shapes=[pltpu.VMEM(*one) for one in saved]
        + [
            pltpu.VMEM((3, C, C), BF), pltpu.VMEM((C, C), BF), pltpu.VMEM((3, 8, 8, C), F32),
            pltpu.VMEM((2, 2, 64, C), BF), pltpu.VMEM((16, 128), F32),
            pltpu.VMEM((2, 16, 128), F32), pltpu.VMEM((pixels, 128), BF),
            pltpu.VMEM((16, 128), BF), pltpu.VMEM((128, pixels), BF),
            pltpu.VMEM((VROWS, pixels), BF), pltpu.VMEM((VROWS, 128), BF),
            pltpu.VMEM((2, pixels, SUB), F32), pltpu.VMEM((2, 8, SUB), F32),
            pltpu.VMEM((2, 16, SUB), F32), pltpu.VMEM((2, pixels, PIX), BF),
            pltpu.VMEM((8, HEAD, PIX), BF),
            DMA((4,)), DMA((4,)), DMA((4,)), DMA((4,)), DMA((4,)), DMA((4,)),
            DMA((3, 1)), DMA((3, 2)), DMA((3, 2)), DMA((3, 2)), DMA((3, 2)), DMA((3, 3)),
            DMA((3, 3)), DMA((3, 6)), DMA((3, 6)), DMA((4,)), DMA((4,)), DMA((4,)), DMA((4,)),
            DMA((1,)), DMA((3, 8)), DMA((3, 8)), DMA((2, 2)), DMA((2, 2)), DMA((3, 8)),
            DMA((3, 8)), DMA((3,)), DMA((15,)), DMA((2,)), DMA((8,)), DMA((8,)),
        ],
        compiler_params=pltpu.CompilerParams(
            collective_id=1, has_side_effects=True, vmem_limit_bytes=VMEM_LIMIT
        ),
    )(*args)


def band_back_send(me, src, dst, ssem, rsem):
    for chan in range(4):
        cols = pl.ds(chan * 128, 128)
        itself = jnp.logical_and(me.band == me.r, me.c == chan)

        @pl.when(jnp.logical_not(itself))
        def _():
            send(src.at[:, cols], dst.at[me.z], ssem.at[chan], rsem.at[me.z], (me.band, chan))

        @pl.when(itself)
        def _():
            local(src.at[:, cols], dst.at[me.z], rsem.at[me.z])


def band_back_wait(me, src, dst, ssem, rsem):
    for n in range(4):
        pltpu.make_async_copy(src.at[:, pl.ds(0, 128)], dst.at[n], rsem.at[n]).wait()
    for chan in range(4):
        itself = jnp.logical_and(me.band == me.r, me.c == chan)

        @pl.when(jnp.logical_not(itself))
        def _():
            pltpu.make_async_remote_copy(
                src_ref=src.at[:, pl.ds(chan * 128, 128)], dst_ref=dst.at[me.z],
                send_sem=ssem.at[chan], recv_sem=rsem.at[me.z], device_id=(me.band, chan),
                device_id_type=MESH_ID,
            ).wait_send()


def greet_back(me, barrier):
    own_block = me.c == lax.rem(2 * me.z, 4)
    for n in range(4):
        itself = jnp.logical_and(own_block, me.z == n)

        @pl.when(jnp.logical_not(itself))
        def _():
            pl.semaphore_signal(
                barrier, inc=1, device_id=(2 * n + me.k, lax.rem(me.z + n, 4)),
                device_id_type=MESH_ID,
            )

    return 4 - jnp.where(own_block, 1, 0)


def middle_kernel(
    attn, res, tgt, wo, vec, qkv, ctx, p, pc, o, linv, tokens,
    out_o, cot_o, gwo_o, gob_o, dt_o, gcw_o, gcb_o,
    attn_v, res_v, tgt_v, wo_v, out_b, back, cot_v, dat, dot_v, qkv_v, o_v,
    vext, cvext, dos, dor, qrow, dq, pb, dkv, dqb, dt_v, dctx, cslots,
    bs, br, ds_, dr, cs, cr, ks, kr, q_s, q_r, lsem, osem, psem,
):
    me = Place()
    scaling = HEAD ** (-0.5)
    barrier = pltpu.get_barrier_semaphore()
    greet_plane(me, barrier)
    others = greet_back(me, barrier)
    for step in range(1, 8):
        pl.semaphore_signal(
            barrier, inc=1, device_id=(lax.rem(me.r + step, 8), me.c), device_id_type=MESH_ID
        )
    loads = [local(a, b, lsem.at[j]) for j, (a, b) in enumerate(
        ((attn, attn_v), (wo.at[0], wo_v), (res, res_v), (tgt, tgt_v), (qkv, qkv_v), (o, o_v)))]

    def p_copy(block, slot):
        return pltpu.make_async_copy(
            p.at[pl.ds(pl.multiple_of(block * PIX, PIX), PIX), :], pb.at[slot], psem.at[slot])

    p_copy(0, 0).start()

    def band_cols(band):
        return pl.ds(pl.multiple_of(band * PIX, PIX), PIX)

    def head_rows(head):
        return pl.ds(pl.multiple_of(head * HEAD, HEAD), HEAD)

    for load in loads[0:4]:
        load.wait()
    rows = jnp.transpose(attn_v[...].astype(F32)).astype(BF)
    result = res_v[...] + mm(rows, wo_v[...], NT) + vec[10:11, :]
    out_b[...] = result.astype(BF)
    cot = vec[13:14, :] * (result - tgt_v[...].astype(F32))
    cot_v[...] = cot
    low = cot.astype(BF)
    dat[...] = jnp.transpose(mm(low, wo_v[...])).astype(BF)
    pl.semaphore_wait(barrier, 14 + others)
    own = local(dat.at[head_rows(me.d), :], dot_v.at[:, band_cols(me.band)], lsem.at[6])
    copies = []
    for step in range(1, 8):
        head = lax.rem(me.d + step, 8)
        copies.append(
            send(dat.at[head_rows(head), :], dot_v.at[:, band_cols(me.band)], ds_.at[step],
                 dr.at[step], me.head_device(head)))
    saves = [local(cot_v, cot_o, osem.at[0])]
    lowf = low.astype(F32)
    gwo_o[...] = mm(jnp.transpose(lowf).astype(BF), rows).astype(BF)
    gob_o[...] = jnp.broadcast_to(as_row(lowf), (8, C))
    for load in loads[4:]:
        load.wait()
    row = lax.broadcasted_iota(jnp.int32, (HEAD, H * W), 0)
    ones = jnp.where(row < 3, 1.0, 0.0)
    vext[...] = jnp.transpose(jnp.concatenate([qkv_v[2].astype(F32), ones], axis=0)).astype(BF)
    lane = lax.broadcasted_iota(jnp.int32, (16, 128), 1)
    cvext[...] = jnp.where(
        lane < HEAD, ctx[1].astype(F32), jnp.where(lane < HEAD + 3, 1.0, 0.0)).astype(BF)
    queries = qkv_v[0].astype(F32) * scaling
    qrow[...] = jnp.transpose(
        jnp.concatenate([queries, jnp.zeros_like(queries)], axis=0)).astype(BF)
    own.wait()
    for copy in copies:
        copy.wait()
    band_back_send(me, out_b, back, bs, br)
    grad = (dot_v[...].astype(F32) * linv[0:1, :]).astype(BF)
    gradf = grad.astype(F32)
    delta = -jnp.sum(gradf * o_v[...], axis=0, keepdims=True)
    top = delta.astype(BF).astype(F32)
    mid = (delta - top).astype(BF).astype(F32)
    last = delta - top - mid
    dos[0:HEAD, :] = grad
    dos[HEAD:, :] = jnp.where(
        row == 0, top, jnp.where(row == 1, mid, jnp.where(row == 2, last, 0.0))).astype(BF)
    dor[...] = jnp.transpose(jnp.concatenate([gradf, jnp.zeros_like(gradf)], axis=0)).astype(BF)

    def score_grads(values, probs):
        return (probs.astype(F32) * mm(values, dos[...])).astype(BF)

    dsc = score_grads(cvext[...], pc[...])
    for j, (left, right) in enumerate(((dsc, qrow), (pc[...], dor))):
        value = mm(left, right[...])
        dctx[j] = jnp.where(me.k == 0, value, pltpu.roll(value, HEAD, 1))
    cslots[me.r] = dctx[...]
    ctx_copies = [
        send(cslots.at[me.r], cslots.at[me.r], cs.at[step], cr.at[step],
             (lax.rem(me.r + step, 8), me.c))
        for step in range(1, 8)
    ]
    wide = jnp.concatenate([ctx[0].astype(F32), jnp.zeros((112, 128), F32)], axis=0)
    dq[...] = mm(jnp.transpose(wide)[0:HEAD, 0:16].astype(BF), dsc)
    mine = head_rows(me.d)

    @pl.loop(0, 8)
    def _(block):
        slot = lax.rem(block, 2)

        @pl.when(block < 7)
        def _():
            p_copy(block + 1, 1 - slot).start()

        p_copy(block, slot).wait()
        grads = []
        for sub in range(2):
            part = pl.ds(pl.multiple_of(block * PIX + sub * SUB, SUB), SUB)
            probs = pb[slot, sub * SUB : (sub + 1) * SUB, :]
            grads.append(score_grads(vext[part, :], probs))
            dkv[block, 1, :, sub * SUB : (sub + 1) * SUB] = jnp.transpose(
                mm(probs, dor[...]))[0:HEAD].astype(BF)
        for sub in range(2):
            part = pl.ds(pl.multiple_of(block * PIX + sub * SUB, SUB), SUB)
            dkv[block, 0, :, sub * SUB : (sub + 1) * SUB] = jnp.transpose(
                mm(grads[sub], qrow[...]))[0:HEAD].astype(BF)
            dq[...] += mm(qkv_v[1, :, part], grads[sub])

        @pl.when(block != me.band)
        def _():
            send(dkv.at[block], dt_v.at[1:3, mine, :], ks.at[block], kr.at[me.d],
                 me.band_device(block))

        @pl.when(block == me.band)
        def _():
            local(dkv.at[block], dt_v.at[1:3, mine, :], kr.at[me.d])

    dqb[...] = (dq[...] * scaling).astype(BF)
    own = local(dqb.at[:, band_cols(me.band)], dt_v.at[0, mine, :], q_r.at[me.d])
    copies = []
    for step in range(1, 8):
        band = lax.rem(me.band + step, 8)
        copies.append(
            send(dqb.at[:, band_cols(band)], dt_v.at[0, mine, :], q_s.at[step], q_r.at[me.d],
                 me.band_device(band)))
    for copy in ctx_copies:
        copy.wait()
    for j in range(2):
        total = cslots[0, j]
        for slot in range(1, 8):
            total = total + cslots[slot, j]
        gcb_o[j : j + 1, :] = as_row(total)
        gcw_o[j] = sum(mm(term, tokens[...]) for term in split_rows(total))
    band_back_wait(me, out_b, back, bs, br)
    out_o[...] = back[...].astype(F32)
    for copy in copies:
        copy.wait_send()
    for block in range(8):

        @pl.when(block != me.band)
        def _():
            pltpu.make_async_remote_copy(
                src_ref=dkv.at[block], dst_ref=dt_v.at[1:3, mine, :], send_sem=ks.at[block],
                recv_sem=kr.at[me.d], device_id=me.band_device(block), device_id_type=MESH_ID,
            ).wait_send()

        pltpu.make_async_copy(
            dkv.at[0], dt_v.at[1:3, pl.ds(block * HEAD, HEAD), :], kr.at[block]).wait()
        pltpu.make_async_copy(
            dqb.at[:, pl.ds(0, PIX)], dt_v.at[0, pl.ds(block * HEAD, HEAD), :], q_r.at[block]
        ).wait()
    saves.append(local(dt_v, dt_o, osem.at[1]))
    for copy in saves:
        copy.wait()


def middle(*args):
    pixels = H * W
    return pl.pallas_call(
        middle_kernel,
        name="middle",
        out_shape=[
            jax.ShapeDtypeStruct((4, PIX, 128), F32),
            jax.ShapeDtypeStruct((PIX, C), F32),
            jax.ShapeDtypeStruct((C, C), BF),
            jax.ShapeDtypeStruct((8, C), F32),
            jax.ShapeDtypeStruct((3, C, PIX), BF),
            jax.ShapeDtypeStruct((2, 128, CTXW), F32),
            jax.ShapeDtypeStruct((2, 128), F32),
        ],
        in_specs=[ANY] * 4 + [VMEM, ANY, VMEM, ANY, VMEM, ANY, VMEM, VMEM],
        out_specs=[VMEM, ANY, VMEM, VMEM, ANY, VMEM, VMEM],
        scratch_shapes=[
            pltpu.VMEM((C, PIX), BF), pltpu.VMEM((PIX, C), F32), pltpu.VMEM((PIX, C), BF),
            pltpu.VMEM((C, C), BF), pltpu.VMEM((PIX, C), BF), pltpu.VMEM((4, PIX, 128), BF),
            pltpu.VMEM((PIX, C), F32), pltpu.VMEM((C, PIX), BF), pltpu.VMEM((HEAD, pixels), BF),
            pltpu.VMEM((3, HEAD, pixels), BF), pltpu.VMEM((HEAD, pixels), F32),
            pltpu.VMEM((pixels, 128), BF), pltpu.VMEM((16, 128), BF),
            pltpu.VMEM((128, pixels), BF), pltpu.VMEM((pixels, 128), BF),
            pltpu.VMEM((pixels, 128), BF), pltpu.VMEM((HEAD, pixels), F32),
            pltpu.VMEM((2, PIX, pixels), BF), pltpu.VMEM((8, 2, HEAD, PIX), BF),
            pltpu.VMEM((HEAD, pixels), BF), pltpu.VMEM((3, C, PIX), BF),
            pltpu.VMEM((2, 16, 128), F32), pltpu.VMEM((8, 2, 16, 128), F32),
            DMA((4,)), DMA((4,)), DMA((8,)), DMA((8,)), DMA((8,)), DMA((8,)), DMA((8,)),
            DMA((8,)), DMA((8,)), DMA((8,)), DMA((7,)), DMA((2,)), DMA((2,)),
        ],
        compiler_params=pltpu.CompilerParams(
            collective_id=2, has_side_effects=True, vmem_limit_bytes=VMEM_LIMIT
        ),
    )(*args)


TAPS = 22
GROUP_TAPS = ((0, 1), (1, 3), (4, 3), (7, 3), (10, 3), (13, 3), (16, 3), (19, 3))


class Reduce:
    def __init__(self, me, part, from_core, from_chan, plane, from_plane, total, sems):
        self.me = me
        self.part, self.from_core, self.from_chan = part, from_core, from_chan
        self.plane, self.from_plane, self.total = plane, from_plane, total
        self.sems = sems
        self.copies = {}

    def advance(self, group):
        stage = self.copies.get(group, (0, []))[0]
        for copy in self.copies.get(group, (0, []))[1]:
            copy.wait()
        step = (self.core_send, self.chan_send, self.plane_send, self.plane_gather,
                self.core_gather, lambda group, taps: [])[stage]
        start, count = GROUP_TAPS[group]
        self.copies[group] = (stage + 1, step(group, pl.ds(start, count)))

    def core_send(self, group, taps):
        me = self.me
        s, r = self.sems[0], self.sems[1]
        return [
            send(self.part.at[taps, :, 1 - me.k], self.from_core.at[taps], s.at[group],
                 r.at[group], (me.r + 1 - 2 * me.k, me.c))
        ]

    def chan_send(self, group, taps):
        me = self.me
        start, count = GROUP_TAPS[group]

        @pl.loop(start, start + count)
        def _(tap):
            own = self.part[tap, :, me.k].astype(F32) + self.from_core[tap].astype(F32)
            self.part[tap, :, me.k] = own.astype(BF)

        s, r = self.sems[2], self.sems[3]
        out = []
        for t in range(1, 4):
            chan = lax.rem(me.c + t, 4)
            out.append(
                send(self.part.at[taps, chan, me.k], self.from_chan.at[t - 1, taps],
                     s.at[group, t], r.at[group, t], (me.r, chan))
            )
        return out

    def plane_send(self, group, taps):
        me = self.me
        start, count = GROUP_TAPS[group]

        @pl.loop(start, start + count)
        def _(tap):
            value = self.part[tap, me.c, me.k].astype(F32)
            for t in range(3):
                value = value + self.from_chan[t, tap].astype(F32)
            self.plane[tap] = value.astype(BF)

        s, r = self.sems[4], self.sems[5]
        out = []
        for t in range(1, 4):
            z = lax.rem(me.z + t, 4)
            rows = pl.ds(pl.multiple_of(z * 16, 16), 16)
            out.append(
                send(self.plane.at[taps, rows, :], self.from_plane.at[t - 1, taps],
                     s.at[group, t], r.at[group, t], (2 * z + me.k, me.c))
            )
        return out

    def plane_gather(self, group, taps):
        me = self.me
        start, count = GROUP_TAPS[group]
        rows = pl.ds(pl.multiple_of(me.z * 16, 16), 16)

        @pl.loop(start, start + count)
        def _(tap):
            value = self.plane[tap, rows, :].astype(F32)
            for t in range(3):
                value = value + self.from_plane[t, tap].astype(F32)
            self.total[tap, me.k, me.z] = value.astype(BF)

        s, r = self.sems[6], self.sems[7]
        out = []
        for t in range(1, 4):
            z = lax.rem(me.z + t, 4)
            piece = self.total.at[taps, me.k, me.z]
            out.append(send(piece, piece, s.at[group, t], r.at[group, t], (2 * z + me.k, me.c)))
        return out

    def core_gather(self, group, taps):
        me = self.me
        s, r = self.sems[8], self.sems[9]
        piece = self.total.at[taps, me.k]
        return [send(piece, piece, s.at[group], r.at[group], (me.r + 1 - 2 * me.k, me.c))]


def split_rows(rows):
    first = rows.astype(BF).astype(F32)
    second = (rows - first).astype(BF).astype(F32)
    stacked = jnp.concatenate([first, second, rows - first - second, jnp.zeros((80, 128), F32)],
                              axis=0)
    left = jnp.transpose(stacked).astype(BF)
    return left[:, 0:16], left[:, 16:32], left[:, 32:48]


def back_kernel(
    dt, vec, st, x, a1, hid, a2, res, nrm, cot, w1, w2, wq, gwo, gob, feat,
    gimg_o, zv_o, fin_o, gemb_o,
    dt_v, x_v, a1_v, hid_v, a2_v, res_v, nrm_v, drs_v, w1_v, w2_v, wq_v,
    cat, turned, acc, groups, slots, halo, keep, img_b, back, zsl,
    part, from_core, from_chan, plane, from_plane, total,
    ss, sr, hs, hr, bs, br, zs, zr, c1s, c1r, c2s, c2r, p1s, p1r, p2s, p2r, c3s, c3r,
    lsem, osem,
):
    me = Place()
    barrier = pltpu.get_barrier_semaphore()
    greet_plane(me, barrier)
    others = greet_back(me, barrier)
    for t in range(1, 4):
        pl.semaphore_signal(
            barrier, inc=1, device_id=(2 * lax.rem(me.z + t, 4) + me.k, me.c),
            device_id_type=MESH_ID,
        )
    loads = [local(a, b, lsem.at[j]) for j, (a, b) in enumerate((
        (dt, dt_v), (wq, wq_v), (res, res_v), (gwo, part.at[0]), (nrm, nrm_v), (cot, drs_v),
        (a2, a2_v), (w2, w2_v), (hid, hid_v), (a1, a1_v), (w1, w1_v), (x, x_v)))]
    reduce = Reduce(me, part, from_core, from_chan, plane, from_plane, total,
                    (c1s, c1r, c2s, c2r, p1s, p1r, p2s, p2r, c3s, c3r))
    group_matrix(groups)
    zero8 = jnp.zeros((8, C), F32)
    members = 1.0 / (H * W * 16)
    loads[0].wait()
    loads[1].wait()
    for j in range(3):
        rows = jnp.transpose(dt_v[j].astype(F32))
        if j != 1:
            keep[j : j + 1, :] = as_row(rows)
        value = mm(rows.astype(BF), wq_v[j])
        if j == 0:
            acc[...] = value
        else:
            acc[...] += value
    loads[2].wait()

    def sums(scaled_of, upstream_of):
        def add(i, carry):
            upstream = upstream_of(i)
            return (carry[0] + fold(upstream), carry[1] + fold(upstream * scaled_of(i)))

        first, cross = lax.fori_loop(0, CHUNKS, add, (zero8, zero8))
        return [as_row(first), as_row(cross)]

    def scaled(ref, number):
        return lambda i: (ref[chunk_of(i), :].astype(F32) - st[2 * number : 2 * number + 1, :]) * st[
            2 * number + 1 : 2 * number + 2, :]

    def exchange(number, rows):
        store_rows(slots.at[number], me.d, rows)
        return plane_exchange(me, slots.at[number], ss.at[number], sr.at[number])

    scaled3, scaled2, scaled1 = scaled(res_v, 2), scaled(hid_v, 1), scaled(x_v, 0)
    rows3 = sums(scaled3, lambda i: acc[chunk_of(i), :])
    pl.semaphore_wait(barrier, 10 + others)
    copies = exchange(0, rows3)
    loads[3].wait()
    reduce.advance(0)
    loads[4].wait()

    @pl.loop(0, 3)
    def _(j):
        part[1 + j] = mm(dt_v[j], nrm_v[...]).astype(BF).reshape(4, 2, 64, C)

    reduce.advance(1)
    reduce.advance(0)
    for load in loads[5:]:
        load.wait()
    for copy in copies:
        copy.wait()

    def group_means(total_rows, factor):
        return group_total(total_rows * factor, groups) * members

    total3 = slots_total(slots.at[0])
    gain = vec[2:3, :]
    means = group_means(total3, gain)
    keep[8:16, :] = total3
    inverse = st[5:6, :]

    def resid_grad(i, carry):
        where = chunk_of(i)
        value = drs_v[where, :] + inverse * (
            acc[where, :] * gain - means[0:1] - scaled3(i) * means[1:2])
        drs_v[where, :] = value
        put_shifted(cat, 64 + i * 64, value)
        return carry + fold(value.astype(BF).astype(F32))

    keep[3:4, :] = as_row(lax.fori_loop(0, CHUNKS, resid_grad, zero8))
    halo_send(me, cat, halo.at[0], hs.at[0], hr.at[0])
    reduce.advance(1)
    turned[...] = jnp.transpose(drs_v[...]).astype(BF)

    def weight_grads(group, source):
        start = GROUP_TAPS[group][0]
        row = (group - 2) % 3

        @pl.loop(0, 3)
        def _(col):
            part[start + col] = mm(turned[...], source[col, row * 64 : row * 64 + PIX, :]).astype(
                BF).reshape(4, 2, 64, C)

        reduce.advance(group)

    weight_grads(2, a2_v)
    weight_grads(3, a2_v)
    weight_grads(4, a2_v)
    reduce.advance(0)
    acc[...] = jnp.zeros((PIX, C), F32)
    conv_taps(acc, cat, w2_v, (1,), True, NN)
    halo_wait(me, cat, halo.at[0], hs.at[0], hr.at[0])
    reduce.advance(2)
    conv_taps(acc, cat, w2_v, (0, 2), True, NN)
    gain2, bias2 = vec[1:2, :], vec[4:5, :]
    scale, shift = 1.0 + vec[11:12, :], vec[12:13, :]

    def mod_grad(i):
        where = chunk_of(i)
        mod = (scaled2(i) * gain2 + bias2) * scale + shift
        value = acc[where, :] * swish_slope(mod)
        acc[where, :] = value
        return value

    copies = exchange(1, sums(scaled2, mod_grad))
    reduce.advance(1)
    reduce.advance(0)
    for copy in copies:
        copy.wait()
    total2 = slots_total(slots.at[1])
    means2 = group_means(total2, gain2 * scale)
    keep[16:24, :] = total2
    inverse2 = st[3:4, :]

    def hidden_grad(i, carry):
        where = chunk_of(i)
        value = inverse2 * (
            acc[where, :] * (gain2 * scale) - means2[0:1] - scaled2(i) * means2[1:2])
        acc[where, :] = value
        put_shifted(cat, 64 + i * 64, value)
        return carry + fold(value.astype(BF).astype(F32))

    keep[1:2, :] = as_row(lax.fori_loop(0, CHUNKS, hidden_grad, zero8))
    halo_send(me, cat, halo.at[1], hs.at[1], hr.at[1])
    reduce.advance(3)
    turned[...] = jnp.transpose(acc[...]).astype(BF)
    weight_grads(5, a1_v)
    reduce.advance(2)
    weight_grads(6, a1_v)
    reduce.advance(1)
    weight_grads(7, a1_v)
    reduce.advance(0)
    reduce.advance(4)
    acc[...] = jnp.zeros((PIX, C), F32)
    conv_taps(acc, cat, w1_v, (1,), True, NN)
    halo_wait(me, cat, halo.at[1], hs.at[1], hr.at[1])
    conv_taps(acc, cat, w1_v, (0, 2), True, NN)
    gain1, bias1 = vec[0:1, :], vec[3:4, :]

    def pre_grad(i):
        where = chunk_of(i)
        value = acc[where, :] * swish_slope(scaled1(i) * gain1 + bias1)
        acc[where, :] = value
        return value

    first, cross = sums(scaled1, pre_grad)
    copies = exchange(2, [first, cross, keep[1:2, :], keep[3:4, :], keep[0:1, :], keep[2:3, :],
                          gob[0:1, :]])
    reduce.advance(5)
    reduce.advance(3)
    reduce.advance(2)
    reduce.advance(1)
    for copy in copies:
        copy.wait()
    total1 = slots_total(slots.at[2])
    means1 = group_means(total1, gain1)
    inverse1 = st[1:2, :]

    @pl.loop(0, CHUNKS)
    def _(i):
        where = chunk_of(i)
        value = drs_v[where, :] + inverse1 * (
            acc[where, :] * gain1 - means1[0:1] - scaled1(i) * means1[1:2])
        img_b[where, :] = value.astype(BF)

    band_back_send(me, img_b, back, bs, br)
    u2, v2 = keep[16:17, :], keep[17:18, :]
    keep[24:40, :] = jnp.concatenate(
        [total1[1:2], total1[0:1], scale * v2, scale * u2, keep[9:10, :], keep[8:9, :],
         total1[2:7], gain2 * v2 + bias2 * u2, u2, jnp.zeros((3, C), F32)], axis=0)
    own_cols = pl.ds(pl.multiple_of(me.c * 128, 128), 128)
    zsl[me.z] = keep[24:40, own_cols]
    zcopies = [
        send(zsl.at[me.z], zsl.at[me.z], zs.at[t], zr.at[t],
             (2 * lax.rem(me.z + t, 4) + me.k, me.c))
        for t in range(1, 4)
    ]
    for group in (6, 4, 7, 3, 2, 5, 4, 3):
        reduce.advance(group)
    for copy in zcopies:
        copy.wait()
    zv_o[...] = zsl[...]
    for j in range(2):
        rows = jnp.concatenate([zsl[n, 11 + j : 12 + j, :] for n in range(4)]
                               + [jnp.zeros((12, 128), F32)], axis=0)
        terms = split_rows(rows)
        gemb_o[j] = sum(mm(term, feat[...]) for term in terms)
    for group in (6, 5, 4):
        reduce.advance(group)
    band_back_wait(me, img_b, back, bs, br)
    gimg_o[...] = back[...].astype(F32)
    for group in (7, 6, 5, 7, 6, 7):
        reduce.advance(group)
    for group in range(8):
        while reduce.copies[group][0] < 6:
            reduce.advance(group)
    local(total, fin_o, osem.at[0]).wait()


def back(*args):
    shared = [
        ((3, C, PIX), BF), ((PIX, C), BF), ((3, PAD, C), BF), ((PIX, C), F32), ((3, PAD, C), BF),
        ((PIX, C), F32), ((PIX, C), BF), ((PIX, C), F32), ((9, C, C), BF), ((9, C, C), BF),
        ((3, C, C), BF), ((3, PAD, C), BF), ((C, PIX), BF), ((PIX, C), F32), ((C, C), BF),
        ((3, 8, 8, C), F32), ((2, 2, 64, C), BF), ((40, C), F32), ((PIX, C), BF),
        ((4, PIX, 128), BF), ((4, 16, 128), F32),
        ((TAPS, 4, 2, 64, C), BF), ((TAPS, 4, 64, C), BF), ((3, TAPS, 64, C), BF),
        ((TAPS, 64, C), BF), ((3, TAPS, 16, C), BF), ((TAPS, 2, 4, 16, C), BF),
    ]
    return pl.pallas_call(
        back_kernel,
        name="back",
        out_shape=[
            jax.ShapeDtypeStruct((4, PIX, 128), F32),
            jax.ShapeDtypeStruct((4, 16, 128), F32),
            jax.ShapeDtypeStruct((TAPS, 2, 4, 16, C), BF),
            jax.ShapeDtypeStruct((2, 128, EMB), F32),
        ],
        in_specs=[ANY, VMEM, VMEM] + [ANY] * 11 + [VMEM, VMEM],
        out_specs=[VMEM, VMEM, ANY, VMEM],
        scratch_shapes=[pltpu.VMEM(*one) for one in shared]
        + [
            DMA((3, 8)), DMA((3, 8)), DMA((2, 2)), DMA((2, 2)),
            DMA((4,)), DMA((4,)), DMA((4,)), DMA((4,)), DMA((8,)), DMA((8,)), DMA((8, 4)),
            DMA((8, 4)), DMA((8, 4)), DMA((8, 4)), DMA((8, 4)), DMA((8, 4)), DMA((8,)),
            DMA((8,)), DMA((12,)), DMA((1,)),
        ],
        compiler_params=pltpu.CompilerParams(
            collective_id=3, has_side_effects=True, vmem_limit_bytes=VMEM_LIMIT
        ),
    )(*args)


def plane_body(
    image, target, time_index, loss_weight, clip_embed, clip_tokens, norm_gain, norm_bias,
    conv1_w, conv2_w, conv_bias, emb_w, emb_b, qkv_w, qv_bias, ctx_w, ctx_b, out_w, out_b,
):
    z = lax.axis_index("row") // 2
    feat = swish(time_features(time_index, EMB) + clip_embed.astype(F32)).astype(BF)
    feat = jnp.pad(feat, ((0, 12), (0, 0)))
    tokens = clip_tokens.reshape(4 * CTX, CTXW)
    weight_row = jnp.broadcast_to(lax.dynamic_slice_in_dim(loss_weight, z, 1), (1, 128))
    vec = jnp.concatenate([
        norm_gain, norm_bias, conv_bias, qv_bias, out_b[None], jnp.zeros((2, 128), F32),
        weight_row, jnp.zeros((2, 128), F32)])
    (x, tgt, vec_all, st, a1, hid, a2, res, nrm, w1, w2, wq, wo, qkv, attn, p, ctx, pc, o,
     linv) = front(
        image.reshape(4, PIX, 128), target.reshape(4, PIX, 128), vec, feat, tokens, emb_w, emb_b,
        ctx_w, ctx_b, conv1_w.reshape(9, 128, C), conv2_w.reshape(9, 128, C), qkv_w, out_w[None])
    result, cot, gwo, gob, dt, grad_ctx_w, grad_ctx_b = middle(
        attn, res, tgt, wo, vec_all, qkv, ctx, p, pc, o, linv, tokens)
    gimg, zv, fin, grad_emb_w = back(
        dt, vec_all, st, x, a1, hid, a2, res, nrm, cot, w1, w2, wq, gwo.reshape(4, 2, 64, C), gob,
        feat)
    sums = jnp.sum(zv, axis=0)
    fin = fin.reshape(TAPS, 128, C).astype(F32)
    return (
        result.reshape(image.shape),
        gimg.reshape(image.shape),
        jnp.stack([sums[0], sums[2], sums[4]]),
        jnp.stack([sums[1], sums[3], sums[5]]),
        fin[13:22].reshape(3, 3, 128, C),
        fin[4:13].reshape(3, 3, 128, C),
        sums[6:8],
        grad_emb_w,
        sums[11:13],
        fin[1:4],
        sums[8:10],
        grad_ctx_w,
        grad_ctx_b,
        fin[0],
        sums[10],
    )


def solution(mesh):
    sizes = dict(mesh.shape)
    planes = sizes["row"] == 8 and sizes["chan"] == 4
    return jax.shard_map(
        plane_body if planes else general_body,
        mesh=mesh,
        in_specs=(
            P(None, "row", None, "chan"), P(None, "row", None, "chan"), P(), P(), P(), P(),
            P(None, "chan"), P(None, "chan"), P(None, None, "chan", None),
            P(None, None, "chan", None), P(None, "chan"), P(None, "chan", None),
            P(None, "chan"), P(None, "chan", None), P(None, "chan"), P(None, "chan", None),
            P(None, "chan"), P("chan", None), P("chan"),
        ),
        out_specs=(
            P(None, "row", None, "chan"), P(None, "row", None, "chan"), P(None, "chan"),
            P(None, "chan"), P(None, None, "chan", None), P(None, None, "chan", None),
            P(None, "chan"), P(None, "chan", None), P(None, "chan"), P(None, "chan", None),
            P(None, "chan"), P(None, "chan", None), P(None, "chan"), P("chan", None), P("chan"),
        ),
        check_vma=False,
    )
```

```python
import math

import jax
import jax.numpy as jnp
from jax import lax
from jax.experimental import pallas as pl
from jax.experimental.pallas import tpu as pltpu
from jax.sharding import PartitionSpec as P

C = 512
GROUPS = 32
HEAD = 64
EMB = 2048
CTXW = 2048
CTX = 4
H = 64
W = 64
MB_IMG = 2


HIGH = lax.Precision.HIGHEST
EPSILON = 1e-05


def with_halo(cells, sides, width):
    for axis, dim in sides:
        count = lax.axis_size(axis)
        ends = count - 1
        head = lax.slice_in_dim(cells, 0, width, axis=dim)
        tail = lax.slice_in_dim(cells, cells.shape[dim] - width, cells.shape[dim], axis=dim)
        cells = jnp.concatenate(
            [
                lax.ppermute(tail, axis, [(i, (i + 1) % count) for i in range(ends)]),
                cells,
                lax.ppermute(head, axis, [((i + 1) % count, i) for i in range(ends)]),
            ],
            axis=dim,
        )
    return cells


def swish(source):
    return source * jax.nn.sigmoid(source)


def swish_slope(source):
    sigma = jax.nn.sigmoid(source)
    return sigma * (1.0 + source * (1.0 - sigma))


def time_features(time_index, width_all):
    half_width = width_all // 2
    frequency = jnp.exp(-math.log(10000.0) * jnp.arange(half_width, dtype=jnp.float32) / half_width)
    angles = time_index.astype(jnp.float32)[:, None] * frequency[None, :]
    return jnp.concatenate([jnp.cos(angles), jnp.sin(angles)], axis=1)


def rows_around(source):
    return with_halo(source, (("row", 1),), 1)


def all_channels(source):
    return lax.all_gather(source, "chan", axis=3, tiled=True)


def channel_total(source):
    return lax.psum_scatter(
        source.astype(jnp.bfloat16), "chan", scatter_dimension=3, tiled=True
    ).astype(jnp.float32)


def norm_forward(source, group_width, members):
    layout = source.shape
    grouped = source.reshape(layout[0], layout[1], layout[2], layout[3] // group_width, group_width)
    first_sum = jnp.sum(grouped, axis=(1, 2, 4))
    square_sum = jnp.sum(grouped * grouped, axis=(1, 2, 4))
    first_sum, square_sum = lax.psum((first_sum, square_sum), "row")
    center = first_sum / members
    spread = square_sum / members - center * center
    inverse_std = lax.rsqrt(spread + EPSILON)
    scaled = (grouped - center[:, None, None, :, None]) * inverse_std[:, None, None, :, None]
    return (scaled.reshape(layout), inverse_std)


def norm_backward(upstream, scaled, inverse_std, gain, group_width, members):
    layout = upstream.shape
    grouped_grad = (upstream * gain).reshape(
        layout[0], layout[1], layout[2], layout[3] // group_width, group_width
    )
    grouped_norm = scaled.reshape(grouped_grad.shape)
    grad_sum = jnp.sum(grouped_grad, axis=(1, 2, 4))
    cross_sum = jnp.sum(grouped_grad * grouped_norm, axis=(1, 2, 4))
    grad_sum, cross_sum = lax.psum((grad_sum, cross_sum), "row")
    result = inverse_std[:, None, None, :, None] * (
        grouped_grad
        - grad_sum[:, None, None, :, None] / members
        - grouped_norm * (cross_sum[:, None, None, :, None] / members)
    )
    gain_grad = jnp.sum(upstream * scaled, axis=(0, 1, 2))
    bias_grad = jnp.sum(upstream, axis=(0, 1, 2))
    return (result.reshape(layout), gain_grad, bias_grad)


def conv_apply(padded, weight):
    height = padded.shape[1] - 2
    width = padded.shape[2]
    widened = jnp.pad(padded, ((0, 0), (0, 0), (1, 1), (0, 0)))
    result = None
    for row_step in range(3):
        for col_step in range(3):
            partial_term = jnp.einsum(
                "nhwc,dc->nhwd",
                widened[:, row_step : row_step + height, col_step : col_step + width],
                weight[row_step, col_step],
                preferred_element_type=jnp.float32,
            )
            result = partial_term if result is None else result + partial_term
    return result


def conv_weight_grad(padded, upstream_low):
    height = upstream_low.shape[1]
    width = upstream_low.shape[2]
    widened = jnp.pad(padded, ((0, 0), (0, 0), (1, 1), (0, 0)))
    stacked = []
    for row_step in range(3):
        row_terms = []
        for col_step in range(3):
            row_terms.append(
                jnp.einsum(
                    "nhwc,nhwd->dc",
                    widened[:, row_step : row_step + height, col_step : col_step + width],
                    upstream_low,
                    preferred_element_type=jnp.float32,
                )
            )
        stacked.append(jnp.stack(row_terms))
    return jnp.stack(stacked)


def conv_input_grad(upstream_low, weight):
    height = upstream_low.shape[1]
    width = upstream_low.shape[2]
    widened = jnp.pad(rows_around(upstream_low), ((0, 0), (0, 0), (1, 1), (0, 0)))
    result = None
    for row_step in range(3):
        for col_step in range(3):
            partial_term = jnp.einsum(
                "nhwd,dc->nhwc",
                widened[
                    :, 2 - row_step : 2 - row_step + height, 2 - col_step : 2 - col_step + width
                ],
                weight[row_step, col_step],
                preferred_element_type=jnp.float32,
            )
            result = partial_term if result is None else result + partial_term
    return channel_total(result)


def general_body(
    image,
    target,
    time_index,
    loss_weight,
    clip_embed,
    clip_tokens,
    norm_gain,
    norm_bias,
    conv1_w,
    conv2_w,
    conv_bias,
    emb_w,
    emb_b,
    qkv_w,
    qv_bias,
    ctx_w,
    ctx_b,
    out_w,
    out_b,
):
    local_chan = conv1_w.shape[2]
    group_width = C // GROUPS
    members = H * W * group_width
    head_count = local_chan // HEAD
    scaling = HEAD ** (-0.5)
    batches = image.shape[0] // MB_IMG
    band_rows = image.shape[1]
    image_cols = image.shape[2]

    def heads_of(source):
        return source.reshape(source.shape[0], -1, head_count, HEAD)

    def one_batch(carry, items):
        picture, target_in, steps_in, weight_in, embed_in, tokens_in = items
        feat_low = swish(time_features(steps_in, EMB) + embed_in.astype(jnp.float32)).astype(
            jnp.bfloat16
        )
        cond = (
            jnp.einsum("ne,jde->njd", feat_low, emb_w, preferred_element_type=jnp.float32) + emb_b
        )
        scale_term = cond[:, 0][:, None, None, :]
        shift_term = cond[:, 1][:, None, None, :]
        picture_f = picture.astype(jnp.float32)
        scaled_one, inverse_one = norm_forward(picture_f, group_width, members)
        pre_one = scaled_one * norm_gain[0] + norm_bias[0]
        padded_one = all_channels(rows_around(swish(pre_one).astype(jnp.bfloat16)))
        hidden = conv_apply(padded_one, conv1_w) + conv_bias[0]
        scaled_two, inverse_two = norm_forward(hidden, group_width, members)
        normal_two = scaled_two * norm_gain[1] + norm_bias[1]
        modded = normal_two * (1.0 + scale_term) + shift_term
        padded_two = all_channels(rows_around(swish(modded).astype(jnp.bfloat16)))
        resid = picture_f + conv_apply(padded_two, conv2_w) + conv_bias[1]
        scaled_three, inverse_three = norm_forward(resid, group_width, members)
        normed_full = all_channels(
            (scaled_three * norm_gain[2] + norm_bias[2]).astype(jnp.bfloat16)
        )
        projected = jnp.einsum(
            "nhwc,tdc->nhwtd", normed_full, qkv_w, preferred_element_type=jnp.float32
        )
        query_own = heads_of((projected[..., 0, :] + qv_bias[0]).astype(jnp.bfloat16))
        key_own = heads_of(projected[..., 1, :].astype(jnp.bfloat16))
        value_own = heads_of((projected[..., 2, :] + qv_bias[1]).astype(jnp.bfloat16))
        context = (
            jnp.einsum("nte,jde->ntjd", tokens_in, ctx_w, preferred_element_type=jnp.float32)
            + ctx_b
        )
        ctx_key = heads_of(context[:, :, 0].astype(jnp.bfloat16))
        ctx_value = heads_of(context[:, :, 1].astype(jnp.bfloat16))
        key_rows, value_rows = (
            lax.all_gather(key_own, "row", axis=1, tiled=True),
            lax.all_gather(value_own, "row", axis=1, tiled=True),
        )
        score_image = (
            jnp.einsum("nqhd,nkhd->nhqk", query_own, key_rows, preferred_element_type=jnp.float32)
            * scaling
        )
        score_context = (
            jnp.einsum("nqhd,nkhd->nhqk", query_own, ctx_key, preferred_element_type=jnp.float32)
            * scaling
        )
        top_score = jnp.maximum(jnp.max(score_image, axis=3), jnp.max(score_context, axis=3))
        expo_image = jnp.exp(score_image - top_score[..., None])
        expo_context = jnp.exp(score_context - top_score[..., None])
        denom = jnp.sum(expo_image, axis=3) + jnp.sum(expo_context, axis=3)
        prob_image = expo_image / denom[..., None]
        prob_context = expo_context / denom[..., None]
        attended = jnp.einsum(
            "nhqk,nkhd->nqhd",
            prob_image.astype(jnp.bfloat16),
            value_rows,
            preferred_element_type=jnp.float32,
        ) + jnp.einsum(
            "nhqk,nkhd->nqhd",
            prob_context.astype(jnp.bfloat16),
            ctx_value,
            preferred_element_type=jnp.float32,
        )
        attn_full = all_channels(attended.astype(jnp.bfloat16).reshape(picture.shape))
        result = (
            resid
            + jnp.einsum("nhwc,dc->nhwd", attn_full, out_w, preferred_element_type=jnp.float32)
            + out_b
        )
        cotangent = weight_in[:, None, None, None] * (result - target_in.astype(jnp.float32))
        grad_proj = cotangent.astype(jnp.bfloat16)
        grad_outw = jnp.einsum(
            "nhwc,nhwd->dc", attn_full, grad_proj, preferred_element_type=jnp.float32
        )
        grad_outb = jnp.sum(grad_proj.astype(jnp.float32), axis=(0, 1, 2))
        grad_attn = heads_of(
            channel_total(
                jnp.einsum("nhwd,dc->nhwc", grad_proj, out_w, preferred_element_type=jnp.float32)
            ).astype(jnp.bfloat16)
        )
        dprob_image = jnp.einsum(
            "nqhd,nkhd->nhqk", grad_attn, value_rows, preferred_element_type=jnp.float32
        )
        dprob_context = jnp.einsum(
            "nqhd,nkhd->nhqk", grad_attn, ctx_value, preferred_element_type=jnp.float32
        )
        delta = jnp.sum(prob_image * dprob_image, axis=3) + jnp.sum(
            prob_context * dprob_context, axis=3
        )
        dscore_image = (prob_image * (dprob_image - delta[..., None])).astype(jnp.bfloat16)
        dscore_context = (prob_context * (dprob_context - delta[..., None])).astype(jnp.bfloat16)
        grad_query = (
            jnp.einsum(
                "nhqk,nkhd->nqhd", dscore_image, key_rows, preferred_element_type=jnp.float32
            )
            + jnp.einsum(
                "nhqk,nkhd->nqhd", dscore_context, ctx_key, preferred_element_type=jnp.float32
            )
        ) * scaling
        grad_ctx_key = (
            jnp.einsum(
                "nhqk,nqhd->nkhd", dscore_context, query_own, preferred_element_type=jnp.float32
            )
            * scaling
        )
        grad_ctx_value = jnp.einsum(
            "nhqk,nqhd->nkhd",
            prob_context.astype(jnp.bfloat16),
            grad_attn,
            preferred_element_type=jnp.float32,
        )
        key_terms = (
            jnp.einsum(
                "nhqk,nqhd->nkhd", dscore_image, query_own, preferred_element_type=jnp.float32
            )
            * scaling
        )
        value_terms = jnp.einsum(
            "nhqk,nqhd->nkhd",
            prob_image.astype(jnp.bfloat16),
            grad_attn,
            preferred_element_type=jnp.float32,
        )
        grad_key, grad_value = (
            lax.psum_scatter(
                key_terms.astype(jnp.bfloat16), "row", scatter_dimension=1, tiled=True
            ).astype(jnp.float32),
            lax.psum_scatter(
                value_terms.astype(jnp.bfloat16), "row", scatter_dimension=1, tiled=True
            ).astype(jnp.float32),
        )
        grad_stack = (
            jnp.stack([grad_query, grad_key, grad_value], axis=2)
            .reshape(picture.shape[0], band_rows, image_cols, 3, local_chan)
            .astype(jnp.bfloat16)
        )
        grad_qkvw = jnp.einsum(
            "nhwc,nhwtd->tdc", normed_full, grad_stack, preferred_element_type=jnp.float32
        )
        stack_sums = jnp.sum(grad_stack.astype(jnp.float32), axis=(0, 1, 2))
        grad_qvb = jnp.stack([stack_sums[0], stack_sums[2]])
        grad_context = jnp.stack(
            [
                grad_ctx_key.reshape(picture.shape[0], CTX, local_chan),
                grad_ctx_value.reshape(picture.shape[0], CTX, local_chan),
            ],
            axis=2,
        )
        grad_ctxw = jnp.einsum(
            "nte,ntjd->jde", tokens_in.astype(jnp.float32), grad_context, precision=HIGH
        )
        grad_ctxb = jnp.sum(grad_context, axis=(0, 1))
        grad_normed = channel_total(
            jnp.einsum("nhwtd,tdc->nhwc", grad_stack, qkv_w, preferred_element_type=jnp.float32)
        )
        grad_resid, gain_three, bias_three = norm_backward(
            grad_normed, scaled_three, inverse_three, norm_gain[2], group_width, members
        )
        grad_resid = cotangent + grad_resid
        grad_conv_two = grad_resid.astype(jnp.bfloat16)
        grad_w_two = conv_weight_grad(padded_two, grad_conv_two)
        grad_b_two = jnp.sum(grad_conv_two.astype(jnp.float32), axis=(0, 1, 2))
        grad_modded = conv_input_grad(grad_conv_two, conv2_w) * swish_slope(modded)
        grad_cond = jnp.stack(
            [jnp.sum(grad_modded * normal_two, axis=(1, 2)), jnp.sum(grad_modded, axis=(1, 2))],
            axis=1,
        )
        grad_embw = jnp.einsum(
            "ne,njd->jde", feat_low.astype(jnp.float32), grad_cond, precision=HIGH
        )
        grad_embb = jnp.sum(grad_cond, axis=0)
        grad_hidden, gain_two, bias_two = norm_backward(
            grad_modded * (1.0 + scale_term),
            scaled_two,
            inverse_two,
            norm_gain[1],
            group_width,
            members,
        )
        grad_conv_one = grad_hidden.astype(jnp.bfloat16)
        grad_w_one = conv_weight_grad(padded_one, grad_conv_one)
        grad_b_one = jnp.sum(grad_conv_one.astype(jnp.float32), axis=(0, 1, 2))
        grad_pre_one = conv_input_grad(grad_conv_one, conv1_w) * swish_slope(pre_one)
        grad_input, gain_one, bias_one = norm_backward(
            grad_pre_one, scaled_one, inverse_one, norm_gain[0], group_width, members
        )
        grad_picture = grad_resid + grad_input
        grad_gains = jnp.stack([gain_one, gain_two, gain_three])
        grad_biases = jnp.stack([bias_one, bias_two, bias_three])
        grad_convb = jnp.stack([grad_b_one, grad_b_two])
        batch_grads = (
            grad_gains,
            grad_biases,
            grad_w_one,
            grad_w_two,
            grad_convb,
            grad_embw,
            grad_embb,
            grad_qkvw,
            grad_qvb,
            grad_ctxw,
            grad_ctxb,
            grad_outw,
            grad_outb,
        )
        updated = tuple((running + update for running, update in zip(carry, batch_grads)))
        return (updated, (result, grad_picture))

    start = (
        jnp.zeros(norm_gain.shape, jnp.float32),
        jnp.zeros(norm_bias.shape, jnp.float32),
        jnp.zeros(conv1_w.shape, jnp.float32),
        jnp.zeros(conv2_w.shape, jnp.float32),
        jnp.zeros(conv_bias.shape, jnp.float32),
        jnp.zeros(emb_w.shape, jnp.float32),
        jnp.zeros(emb_b.shape, jnp.float32),
        jnp.zeros(qkv_w.shape, jnp.float32),
        jnp.zeros(qv_bias.shape, jnp.float32),
        jnp.zeros(ctx_w.shape, jnp.float32),
        jnp.zeros(ctx_b.shape, jnp.float32),
        jnp.zeros(out_w.shape, jnp.float32),
        jnp.zeros(out_b.shape, jnp.float32),
    )
    items = (
        image.reshape(batches, MB_IMG, band_rows, image_cols, local_chan),
        target.reshape(batches, MB_IMG, band_rows, image_cols, local_chan),
        time_index.reshape(batches, MB_IMG),
        loss_weight.reshape(batches, MB_IMG),
        clip_embed.reshape(batches, MB_IMG, EMB),
        clip_tokens.reshape(batches, MB_IMG, CTX, CTXW),
    )
    totals, (results, picture_grads) = lax.scan(one_batch, start, items)
    (
        sum_gain,
        sum_bias,
        sum_conv_one,
        sum_conv_two,
        sum_conv_bias,
        sum_emb_w,
        sum_emb_b,
        sum_qkv_w,
        sum_qv_bias,
        sum_ctx_w,
        sum_ctx_b,
        sum_out_w,
        sum_out_b,
    ) = totals
    (
        sum_gain,
        sum_bias,
        sum_conv_one,
        sum_conv_two,
        sum_conv_bias,
        sum_emb_w,
        sum_emb_b,
        sum_qkv_w,
        sum_qv_bias,
        sum_ctx_w,
        sum_ctx_b,
        sum_out_w,
        sum_out_b,
    ) = (
        lax.psum(sum_gain.astype(jnp.bfloat16), "row").astype(jnp.float32),
        lax.psum(sum_bias.astype(jnp.bfloat16), "row").astype(jnp.float32),
        lax.psum(sum_conv_one.astype(jnp.bfloat16), "row").astype(jnp.float32),
        lax.psum(sum_conv_two.astype(jnp.bfloat16), "row").astype(jnp.float32),
        lax.psum(sum_conv_bias.astype(jnp.bfloat16), "row").astype(jnp.float32),
        lax.psum(sum_emb_w.astype(jnp.bfloat16), "row").astype(jnp.float32),
        lax.psum(sum_emb_b.astype(jnp.bfloat16), "row").astype(jnp.float32),
        lax.psum(sum_qkv_w.astype(jnp.bfloat16), "row").astype(jnp.float32),
        lax.psum(sum_qv_bias.astype(jnp.bfloat16), "row").astype(jnp.float32),
        lax.psum(sum_ctx_w.astype(jnp.bfloat16), "row").astype(jnp.float32),
        lax.psum(sum_ctx_b.astype(jnp.bfloat16), "row").astype(jnp.float32),
        lax.psum(sum_out_w.astype(jnp.bfloat16), "row").astype(jnp.float32),
        lax.psum(sum_out_b.astype(jnp.bfloat16), "row").astype(jnp.float32),
    )
    return (
        results.reshape(image.shape),
        picture_grads.reshape(image.shape),
        sum_gain,
        sum_bias,
        sum_conv_one,
        sum_conv_two,
        sum_conv_bias,
        sum_emb_w,
        sum_emb_b,
        sum_qkv_w,
        sum_qv_bias,
        sum_ctx_w,
        sum_ctx_b,
        sum_out_w,
        sum_out_b,
    )


BF = jnp.bfloat16
F32 = jnp.float32
MESH_ID = pl.DeviceIdType.MESH
NN = (((1,), (0,)), ((), ()))
NT = (((1,), (1,)), ((), ()))
ANY = pl.BlockSpec(memory_space=pl.ANY)
VMEM = pl.BlockSpec(memory_space=pltpu.VMEM)
SMEM = pl.BlockSpec(memory_space=pltpu.SMEM)
PIX = 512
PAD = 640
CHUNKS = 8
VMEM_LIMIT = 60 * 2**20
DMA = pltpu.SemaphoreType.DMA


def mm(left, right, dims=NN):
    return lax.dot_general(left, right, dims, preferred_element_type=F32)


def mixed(chan, z):
    low = lax.rem(chan + lax.div(z, 2), 2)
    return low + 2 * lax.rem(lax.div(chan, 2) + lax.rem(z, 2), 2)


class Place:
    def __init__(self):
        self.r = lax.axis_index("row")
        self.c = lax.axis_index("chan")
        self.z = lax.div(self.r, 2)
        self.k = lax.rem(self.r, 2)
        self.d = 2 * self.c + self.k
        self.pair = mixed(self.c, self.z)
        self.band = 2 * self.pair + self.k

    def head_device(self, head):
        return (2 * self.z + lax.rem(head, 2), lax.div(head, 2))

    def band_device(self, band):
        return (2 * self.z + lax.rem(band, 2), mixed(lax.div(band, 2), self.z))


def send(src, dst, send_sem, recv_sem, device):
    copy = pltpu.make_async_remote_copy(
        src_ref=src,
        dst_ref=dst,
        send_sem=send_sem,
        recv_sem=recv_sem,
        device_id=device,
        device_id_type=MESH_ID,
    )
    copy.start()
    return copy


def local(src, dst, sem):
    copy = pltpu.make_async_copy(src, dst, sem)
    copy.start()
    return copy


def greet_plane(me, barrier):
    for step in range(1, 8):
        pl.semaphore_signal(
            barrier,
            inc=1,
            device_id=me.head_device(lax.rem(me.d + step, 8)),
            device_id_type=MESH_ID,
        )


def group_matrix(ref):
    rows = lax.broadcasted_iota(jnp.int32, (C, C), 0)
    cols = lax.broadcasted_iota(jnp.int32, (C, C), 1)
    ref[...] = jnp.where(lax.div(rows, 16) == lax.div(cols, 16), 1.0, 0.0).astype(BF)


def group_total(rows, groups_ref):
    top = rows.astype(BF)
    rest = rows - top.astype(F32)
    mid = rest.astype(BF)
    low = (rest - mid.astype(F32)).astype(BF)
    stacked = jnp.concatenate([top, mid, low, jnp.zeros_like(low)], axis=0)
    sums = mm(stacked, groups_ref[...])
    return sums[0:8] + sums[8:16] + sums[16:24]


def plane_exchange(me, slots, ssem, rsem):
    copies = []
    for step in range(1, 8):
        copies.append(
            send(
                slots.at[me.d],
                slots.at[me.d],
                ssem.at[step],
                rsem.at[step],
                me.head_device(lax.rem(me.d + step, 8)),
            )
        )
    return copies


def slots_total(slots):
    total = slots[0]
    for slot in range(1, 8):
        total = total + slots[slot]
    return total


def fold(value):
    return value.reshape(value.shape[0] // 8, 8, value.shape[1]).sum(axis=0)


def as_row(value):
    return jnp.sum(value, axis=0, keepdims=True)


def store_rows(slots, index, rows):
    filled = rows + [jnp.zeros((1, C), F32)] * (8 - len(rows))
    slots[index] = jnp.concatenate(filled, axis=0)


def chunk_of(i):
    return pl.ds(pl.multiple_of(i * 64, 64), 64)


def put_shifted(dst, start, value):
    col = lax.broadcasted_iota(jnp.int32, (64, C), 0)
    where = pl.ds(pl.multiple_of(start, 64), 64)
    dst[1, where, :] = value.astype(BF)
    dst[0, where, :] = jnp.where(col == 0, 0.0, pltpu.roll(value, 1, 0)).astype(BF)
    dst[2, where, :] = jnp.where(col == 63, 0.0, pltpu.roll(value, 63, 0)).astype(BF)


def halo_send(me, cat, halo, ssem, rsem):
    @pl.when(me.band > 0)
    def _():
        send(cat.at[1, pl.ds(64, 64), :], halo.at[1], ssem.at[0], rsem.at[1],
             me.band_device(me.band - 1))

    @pl.when(me.band < 7)
    def _():
        send(cat.at[1, pl.ds(512, 64), :], halo.at[0], ssem.at[1], rsem.at[0],
             me.band_device(me.band + 1))


def halo_wait(me, cat, halo, ssem, rsem):
    def pair(slot, ahead):
        return pltpu.make_async_remote_copy(
            src_ref=cat.at[1, pl.ds(64, 64), :], dst_ref=halo.at[slot],
            send_sem=ssem.at[slot], recv_sem=rsem.at[slot],
            device_id=me.band_device(ahead), device_id_type=MESH_ID)

    zero = jnp.zeros((64, C), F32)

    @pl.when(me.band > 0)
    def _():
        both = pair(0, me.band - 1)
        both.wait_send()
        both.wait_recv()
        put_shifted(cat, 0, halo[0].astype(F32))

    @pl.when(me.band == 0)
    def _():
        put_shifted(cat, 0, zero)

    @pl.when(me.band < 7)
    def _():
        both = pair(1, me.band + 1)
        both.wait_send()
        both.wait_recv()
        put_shifted(cat, 576, halo[1].astype(F32))

    @pl.when(me.band == 7)
    def _():
        put_shifted(cat, 576, zero)


def conv_taps(acc, cat, weight, order, flip, dims):
    @pl.loop(0, 3 * len(order))
    def _(i):
        step = lax.div(i, 3)
        col = lax.rem(i, 3)
        row = order[0] if len(order) == 1 else order[0] + step * (order[1] - order[0])
        tap = (2 - row) * 3 + (2 - col) if flip else row * 3 + col
        start = pl.multiple_of(row * 64, 64)
        acc[...] += mm(cat[col, pl.ds(start, PIX), :], weight[tap], dims)


LOG2E = 1.4426950408889634
VROWS = 80
SUB = 256
KEYS = 512


def image_targets(me):
    return [(n, (2 * n + me.k, mixed(me.z, jnp.int32(n)))) for n in range(4)]


class Gather:
    def __init__(self, me, index, src, dst, sems):
        self.me, self.src, self.dst = me, src, dst
        third = src.shape[0] // 3
        odd = lax.rem(me.z, 2)
        self.plane_taps = pl.ds(third * odd, 2 * third)
        self.give_taps = pl.ds(2 * third * odd, third)
        self.take_taps = pl.ds(2 * third * (1 - odd), third)
        self.x = me.c + 1 - 2 * lax.rem(me.c, 2)
        self.y = lax.rem(me.c + 2, 4)
        self.far = lax.rem(self.x + 2, 4)
        self.core = (me.r + 1 - 2 * me.k, me.c)
        self.over = (2 * (me.z + 1 - 2 * odd) + me.k, me.c)
        (self.own, self.first_s, self.first_r, self.relay_s, self.relay_r, self.give_s,
         self.give_r, self.core_s, self.core_r) = [sem.at[index] for sem in sems]
        self.started = []
        self.core_plane = []
        self.core_take = []
        self.gives = []

    def rows(self, chan, start=0, size=64):
        return pl.ds(pl.multiple_of(chan * 128 + self.me.k * 64 + start, size), size)

    def move(self, taps, rows, s, r, device):
        piece = self.dst.at[taps, rows, :]
        return send(piece, piece, s, r, device)

    def start(self):
        me = self.me
        half = pl.ds(pl.multiple_of(me.k * 64, 64), 64)
        quarter = pl.ds(pl.multiple_of(me.c * 128, 128), 128)
        for j, chan in enumerate((self.x, self.y)):
            self.started.append(
                send(self.src.at[self.plane_taps, half, :],
                     self.dst.at[self.plane_taps, self.rows(me.c), :],
                     self.first_s.at[j], self.first_r.at[j], (me.r, chan)))
        self.kept = local(self.src, self.dst.at[:, quarter, :], self.own.at[0])

    def spread(self, slot, chan):
        self.core_plane.append(
            self.move(self.plane_taps, self.rows(chan), self.core_s.at[slot], self.core_r.at[slot],
                      self.core))
        self.gives.append(
            self.move(self.give_taps, self.rows(chan), self.give_s.at[slot], self.give_r.at[slot],
                      self.over))

    def relay(self):
        self.relays = []
        for j, (chan, onward) in enumerate(((self.x, self.y), (self.y, self.x))):
            self.started[j].wait_recv()
            self.relays.append(
                self.move(self.plane_taps, self.rows(chan, 32 * j, 32), self.relay_s.at[j],
                          self.relay_r.at[j], (self.me.r, onward)))
            self.spread(j, chan)

    def relayed(self):
        for copy in self.relays:
            copy.wait_recv()
        self.spread(2, self.far)

    def plane_done(self):
        self.kept.wait()
        for copy in self.core_plane:
            copy.wait_recv()

    def take(self):
        for slot, chan in enumerate((self.x, self.y, self.far)):
            self.gives[slot].wait_recv()
            self.core_take.append(
                self.move(self.take_taps, self.rows(chan), self.core_s.at[3 + slot],
                          self.core_r.at[3 + slot], self.core))

    def take_done(self):
        for copy in self.core_take:
            copy.wait_recv()

    def drain(self):
        for copy in self.started + self.relays + self.gives + self.core_plane + self.core_take:
            copy.wait_send()


def front_kernel(
    img, tgt, steps, loss, embed, words, norm_gain, norm_bias, conv_bias, qv_bias, out_b,
    emb_w, emb_b, ctx_w, ctx_b, w1, w2, wq, wo,
    x_o, t_o, vec_o, st_o, a1_o, hid_o, a2_o, res_o, nrm_o, w1_o, w2_o, wq_o, wo_o, qkv_o,
    attn_o, p_o, ctx_o, pc_o, o_o, linv_o, feat, tokens,
    x_v, t_v, vec_v, st_v, a1_v, hid_v, a2_v, res_v, nrm_v, w1_v, w2_v, wq_v, wo_v, qkv_v,
    attn_v,
    msg, groups, slots, halo, vsrc, wide, cond, keys, ckeys, qs, vext, cvext, sbuf, mbuf, cbuf, pb, ob,
    vs, vr, ims, imr, tgs, tgr, own_sem, first_s, first_r, relay_s, relay_r, give_s, give_r,
    core_s, core_r, wos, wor, wofs, wofr, wol, sts, str_, hs, hr, qs_s, qs_r, lsem, osem, psem,
    as_, ar,
):
    me = Place()
    barrier = pltpu.get_barrier_semaphore()
    greet_plane(me, barrier)
    own_block = me.pair == me.z
    for chan in range(4):
        itself = jnp.logical_and(me.pair == me.z, me.c == chan)

        @pl.when(jnp.logical_not(itself))
        def _():
            pl.semaphore_signal(
                barrier, inc=1, device_id=(2 * me.pair + me.k, chan), device_id_type=MESH_ID
            )

    odd = lax.rem(me.z, 2)
    pl.semaphore_signal(
        barrier, inc=1, device_id=(2 * (me.z + 1 - 2 * odd) + me.k, me.c), device_id_type=MESH_ID
    )
    wide[...] = jnp.zeros((16, EMB), F32)
    wide[0:4, :] = embed[...].astype(F32)
    row = lax.broadcasted_iota(jnp.int32, (16, EMB // 2), 0)
    column = lax.broadcasted_iota(jnp.int32, (16, EMB // 2), 1).astype(F32)
    frequency = jnp.exp(-math.log(10000.0) * column / (EMB // 2))
    angle = jnp.zeros((16, EMB // 2), F32)
    for n in range(4):
        angle = jnp.where(row == n, steps[n].astype(F32) * frequency, angle)
    for start, wave in ((0, jnp.cos), (EMB // 2, jnp.sin)):
        value = wave(angle) + wide[:, start : start + EMB // 2]
        feat[:, start : start + EMB // 2] = jnp.where(row < 4, swish(value), 0.0).astype(BF)
    for n in range(4):
        wide[4 * n : 4 * n + 4, :] = words[n].astype(F32)
    tokens[...] = wide[...].astype(BF)
    for j in range(2):
        cond[j] = mm(feat[...], emb_w[j], NT) + emb_b[j : j + 1, :]
    vsrc[0:3, :] = norm_gain[...]
    vsrc[3:6, :] = norm_bias[...]
    vsrc[6:8, :] = conv_bias[...]
    vsrc[8:10, :] = qv_bias[...]
    vsrc[10:11, :] = out_b[...]
    vsrc[11:12, :] = cond[0, pl.ds(me.z, 1), :]
    vsrc[12:13, :] = cond[1, pl.ds(me.z, 1), :]
    vsrc[13:14, :] = jnp.full((1, 128), loss[me.z], F32)
    vsrc[14:16, :] = jnp.zeros((2, 128), F32)
    lane = lax.broadcasted_iota(jnp.int32, (16, 128), 1)
    for j in range(2):
        value = mm(tokens[...], ctx_w[j], NT) + ctx_b[j : j + 1, :]
        turned = pltpu.roll(value, HEAD, 1)
        first = lax.div(lane, HEAD) == me.k
        both = jnp.where(first, value, turned)
        ctx_o[j] = both.astype(BF)
        if j == 0:
            ckeys[...] = both.astype(BF)
        else:
            tall = jnp.concatenate([both, jnp.zeros((112, 128), F32)], axis=0)
            cvext[0:HEAD, :] = jnp.transpose(tall)[0:HEAD].astype(BF)
    row = lax.broadcasted_iota(jnp.int32, (16, H * W), 0)
    vext[HEAD:, :] = jnp.where(row == 0, 1.0, 0.0).astype(BF)
    cvext[HEAD:, :] = jnp.where(row[:, 0:128] == 0, 1.0, 0.0).astype(BF)
    pl.semaphore_wait(barrier, 8 + 4 - jnp.where(own_block, 1, 0))
    own_cols = pl.ds(pl.multiple_of(me.c * 128, 128), 128)

    vec_v[:, own_cols] = vsrc[...]
    vec_copies = [
        send(vsrc, vec_v.at[:, own_cols], vs.at[t], vr.at[t], (me.r, lax.rem(me.c + t, 4)))
        for t in range(1, 4)
    ]

    def image_send(src, dst, ssem, rsem):
        for n, device in image_targets(me):
            itself = jnp.logical_and(own_block, me.z == n)

            @pl.when(jnp.logical_not(itself))
            def _():
                send(src.at[n], dst.at[:, own_cols], ssem.at[n], rsem.at[me.c], device)

            @pl.when(itself)
            def _():
                local(src.at[n], dst.at[:, own_cols], rsem.at[me.c])

    def image_wait(src, dst, ssem, rsem):
        for chan in range(4):
            pltpu.make_async_copy(
                src.at[0], dst.at[:, pl.ds(chan * 128, 128)], rsem.at[chan]
            ).wait()

    def image_drain(src, dst, ssem, rsem):
        for n, device in image_targets(me):
            itself = jnp.logical_and(own_block, me.z == n)

            @pl.when(jnp.logical_not(itself))
            def _():
                pltpu.make_async_remote_copy(
                    src_ref=src.at[n], dst_ref=dst.at[:, own_cols], send_sem=ssem.at[n],
                    recv_sem=rsem.at[me.c], device_id=device, device_id_type=MESH_ID,
                ).wait_send()

    gather_sems = (own_sem, first_s, first_r, relay_s, relay_r, give_s, give_r, core_s, core_r)
    gather1 = Gather(me, 0, w1, w1_v, gather_sems)
    gather2 = Gather(me, 1, w2, w2_v, gather_sems)
    gather3 = Gather(me, 2, wq, wq_v, gather_sems)

    image_send(img, x_v, ims, imr)
    gather1.start()
    group_matrix(groups)
    col_zero = jnp.zeros((8, C), F32)
    for copy in vec_copies:
        copy.wait()
    outs = []

    def save(index, src, dst):
        outs.append(local(src, dst, osem.at[index]))

    def statistics(number, ref):
        def add(i, carry):
            value = ref[chunk_of(i), :].astype(F32)
            return (carry[0] + fold(value), carry[1] + fold(value * value))

        first, square = lax.fori_loop(0, CHUNKS, add, (col_zero, col_zero))
        store_rows(slots.at[number], me.d, [as_row(first), as_row(square)])
        return plane_exchange(me, slots.at[number], sts.at[number], str_.at[number])

    def finish_statistics(number, copies):
        for copy in copies:
            copy.wait()
        means = group_total(slots_total(slots.at[number]), groups) * (1.0 / (H * W * 16))
        center = means[0:1]
        inverse = lax.rsqrt(means[1:2] - center * center + EPSILON)
        st_v[2 * number : 2 * number + 1, :] = center
        st_v[2 * number + 1 : 2 * number + 2, :] = inverse
        return center, inverse

    image_wait(img, x_v, ims, imr)
    copies = statistics(0, x_v)
    save(0, x_v, x_o)
    save(2, vec_v, vec_o)
    gather1.relay()
    center, inverse = finish_statistics(0, copies)
    gain, bias = vec_v[0:1, :], vec_v[3:4, :]

    @pl.loop(0, CHUNKS)
    def _(i):
        value = (x_v[chunk_of(i), :].astype(F32) - center) * inverse
        put_shifted(a1_v, 64 + i * 64, swish(value * gain + bias))

    halo_send(me, a1_v, halo.at[0], hs.at[0], hr.at[0])
    gather1.relayed()
    gather2.start()
    hid_v[...] = jnp.broadcast_to(vec_v[6:7, :], (PIX, C))
    gather1.plane_done()
    conv_taps(hid_v, a1_v, w1_v, (1,), False, NT)
    halo_wait(me, a1_v, halo.at[0], hs.at[0], hr.at[0])
    save(4, a1_v, a1_o)
    gather1.take()
    conv_taps(hid_v, a1_v, w1_v, (2 * odd,), False, NT)
    gather1.take_done()
    conv_taps(hid_v, a1_v, w1_v, (2 - 2 * odd,), False, NT)
    copies = statistics(1, hid_v)
    save(9, w1_v, w1_o)
    save(5, hid_v, hid_o)
    gather2.relay()
    center, inverse = finish_statistics(1, copies)
    gain, bias = vec_v[1:2, :], vec_v[4:5, :]
    scale, shift = 1.0 + vec_v[11:12, :], vec_v[12:13, :]

    @pl.loop(0, CHUNKS)
    def _(i):
        value = (hid_v[chunk_of(i), :] - center) * inverse
        put_shifted(a2_v, 64 + i * 64, swish((value * gain + bias) * scale + shift))

    halo_send(me, a2_v, halo.at[1], hs.at[1], hr.at[1])
    gather2.relayed()
    gather3.start()
    res_v[...] = x_v[...].astype(F32) + vec_v[7:8, :]
    gather2.plane_done()
    conv_taps(res_v, a2_v, w2_v, (1,), False, NT)
    halo_wait(me, a2_v, halo.at[1], hs.at[1], hr.at[1])
    save(6, a2_v, a2_o)
    gather2.take()
    gather3.relay()
    conv_taps(res_v, a2_v, w2_v, (2 * odd,), False, NT)
    gather2.take_done()
    gather3.relayed()
    conv_taps(res_v, a2_v, w2_v, (2 - 2 * odd,), False, NT)
    copies = statistics(2, res_v)
    save(10, w2_v, w2_o)
    save(7, res_v, res_o)
    gather3.take()
    center, inverse = finish_statistics(2, copies)
    gain, bias = vec_v[2:3, :], vec_v[5:6, :]
    normed = (res_v[...] - center) * inverse * gain + bias
    nrm_v[...] = normed.astype(BF)
    st_v[6:8, :] = jnp.zeros((2, C), F32)
    save(8, nrm_v, nrm_o)
    save(3, st_v, st_o)
    turned = jnp.transpose(normed).astype(BF)
    gather3.plane_done()
    gather3.take_done()
    save(11, wq_v, wq_o)
    band_cols = pl.ds(pl.multiple_of(me.band * PIX, PIX), PIX)

    def head_rows(head):
        return pl.ds(pl.multiple_of(head * HEAD, HEAD), HEAD)

    owns = []
    qkv_copies = {}
    for j, bias_row in ((1, None), (2, 9), (0, 8)):
        value = mm(wq_v[j], turned)
        if bias_row is not None:
            tall = jnp.transpose(jnp.broadcast_to(vec_v[bias_row : bias_row + 1, :], (128, C)))
            value = value + jnp.concatenate([tall] * 4, axis=1)
        msg[j] = value.astype(BF)
        owns.append(local(msg.at[j, head_rows(me.d), :], qkv_v.at[j, :, band_cols], lsem.at[j]))
        qkv_copies[j] = []
        for step in range(1, 8):
            head = lax.rem(me.d + step, 8)
            qkv_copies[j].append(
                send(msg.at[j, head_rows(head), :], qkv_v.at[j, :, band_cols], qs_s.at[j, step],
                     qs_r.at[j, step], me.head_device(head)))

    for own in owns:
        own.wait()
    for copy in qkv_copies[1]:
        copy.wait()
    both = jnp.concatenate([qkv_v[1], qkv_v[1]], axis=0).astype(F32)
    keys[...] = jnp.transpose(both).astype(BF)

    def scale_queries(where):
        scaled = qkv_v[0, :, where].astype(F32) * (HEAD ** (-0.5) * LOG2E)
        top = scaled.astype(BF)
        qs[0:HEAD, where] = top
        qs[HEAD:, where] = (scaled - top.astype(F32)).astype(BF)

    scale_queries(band_cols)
    token = lax.broadcasted_iota(jnp.int32, (16, SUB), 0)
    valid = lax.div(token, CTX) == me.z
    chunks = H * W // KEYS

    def begin(slot, block):
        query = qs[:, pl.ds(pl.multiple_of(block * SUB, SUB), SUB)]
        score = jnp.where(valid, mm(ckeys[...], query), -1e30)
        cbuf[slot] = score
        return query, jnp.maximum(score[0:8], score[8:16])

    def score_chunk(slot, query, highest, chunk):
        value = mm(keys[chunk * KEYS : (chunk + 1) * KEYS, :], query)
        sbuf[slot, chunk * KEYS : (chunk + 1) * KEYS, :] = value
        return jnp.maximum(highest, jnp.max(value.reshape(KEYS // 8, 8, SUB), axis=0))

    query, highest = begin(0, 2 * me.band)
    for chunk in range(chunks):
        highest = score_chunk(0, query, highest, chunk)
    mbuf[0] = highest
    for copy in qkv_copies[2]:
        copy.wait()
    vext[0:HEAD, :] = qkv_v[2]
    for copy in qkv_copies[0]:
        copy.wait()
    scale_queries(pl.ds(0, H * W))
    save(13, qkv_v, qkv_o)
    image_send(tgt, t_v, tgs, tgr)
    half = pl.ds(pl.multiple_of(me.c * 128 + me.k * 64, 64), 64)
    my_half = pl.ds(pl.multiple_of(me.k * 64, 64), 64)
    wo_own = local(wo, wo_v.at[:, own_cols, :], wol.at[0])
    wo_copies = [
        send(wo.at[:, my_half, :], wo_v.at[:, half, :], wos.at[t], wor.at[t],
             (me.r, lax.rem(me.c + t, 4)))
        for t in range(1, 4)
    ]
    attn_rows = head_rows(me.d)

    def p_copy(block, slot):
        return pltpu.make_async_copy(
            pb.at[slot], p_o.at[:, pl.ds(pl.multiple_of(block * PIX, PIX), PIX)], psem.at[slot])

    @pl.loop(0, 8)
    def _(turn):
        block = lax.rem(me.band + turn, 8)
        slot = lax.rem(turn, 2)

        @pl.when(turn >= 2)
        def _():
            p_copy(block, slot).wait()

        for sub in range(2):
            cols = pl.ds(sub * SUB, SUB)
            place = pl.ds(pl.multiple_of(block * PIX + sub * SUB, SUB), SUB)
            following = lax.rem(2 * block + sub + 1, H * W // SUB)
            top = jnp.max(mbuf[sub], axis=0, keepdims=True)
            pc = jnp.exp2(cbuf[sub] - top).astype(BF)
            pc_o[:, place] = pc
            out = mm(cvext[:, 0:16], pc)
            query, highest = begin(1 - sub, following)
            for chunk in range(chunks):
                highest = score_chunk(1 - sub, query, highest, chunk)
                rows = slice(chunk * KEYS, (chunk + 1) * KEYS)
                probs = jnp.exp2(sbuf[sub, rows, :] - top).astype(BF)
                pb[slot, rows, cols] = probs
                out = out + mm(vext[:, rows], probs)
            mbuf[1 - sub] = highest
            linv = 1.0 / out[HEAD : HEAD + 1]
            out = out[0:HEAD] * linv
            o_o[:, place] = out
            ob[block, :, cols] = out.astype(BF)
            linv_o[:, place] = jnp.broadcast_to(linv, (8, SUB))
        p_copy(block, slot).start()

        @pl.when(block != me.band)
        def _():
            send(ob.at[block], attn_v.at[attn_rows, :], as_.at[block], ar.at[me.d],
                 me.band_device(block))

        @pl.when(block == me.band)
        def _():
            local(ob.at[block], attn_v.at[attn_rows, :], ar.at[me.d])

    wo_forward = []
    for t in range(1, 4):
        wo_copies[t - 1].wait()
        origin = lax.rem(me.c - t + 4, 4)
        rows = pl.ds(pl.multiple_of(origin * 128 + me.k * 64, 64), 64)
        wo_forward.append(
            send(wo_v.at[:, rows, :], wo_v.at[:, rows, :], wofs.at[t], wofr.at[t],
                 (me.r + 1 - 2 * me.k, me.c)))
    image_wait(tgt, t_v, tgs, tgr)
    save(1, t_v, t_o)
    for gather in (gather1, gather2, gather3):
        gather.drain()
    image_drain(img, x_v, ims, imr)
    image_drain(tgt, t_v, tgs, tgr)
    wo_own.wait()
    for copy in wo_forward:
        copy.wait()
    save(12, wo_v, wo_o)
    for block in range(8):

        @pl.when(block != me.band)
        def _():
            pltpu.make_async_remote_copy(
                src_ref=ob.at[block], dst_ref=attn_v.at[attn_rows, :], send_sem=as_.at[block],
                recv_sem=ar.at[me.d], device_id=me.band_device(block), device_id_type=MESH_ID,
            ).wait_send()

        pltpu.make_async_copy(
            ob.at[0], attn_v.at[pl.ds(block * HEAD, HEAD), :], ar.at[block]).wait()
    save(14, attn_v, attn_o)
    p_copy(0, 0).wait()
    p_copy(0, 1).wait()
    for copy in outs:
        copy.wait()


def front(*args):
    pixels = H * W
    saved = [
        ((PIX, C), BF), ((PIX, C), BF), ((16, C), F32), ((8, C), F32), ((3, PAD, C), BF),
        ((PIX, C), F32), ((3, PAD, C), BF), ((PIX, C), F32), ((PIX, C), BF), ((9, C, C), BF),
        ((9, C, C), BF), ((3, C, C), BF), ((1, C, C), BF), ((3, HEAD, pixels), BF), ((C, PIX), BF),
    ]
    more = [
        ((pixels, pixels), BF), ((2, 16, 128), BF), ((16, pixels), BF), ((HEAD, pixels), F32),
        ((8, pixels), F32), ((16, EMB), BF), ((16, CTXW), BF),
    ]
    return pl.pallas_call(
        front_kernel,
        name="front",
        out_shape=[jax.ShapeDtypeStruct(*one) for one in saved + more],
        in_specs=[ANY, ANY] + [SMEM] * 2 + [VMEM] * 11 + [ANY] * 4,
        out_specs=[ANY] * (len(saved) + 1) + [VMEM] * 6,
        scratch_shapes=[pltpu.VMEM(*one) for one in saved]
        + [
            pltpu.VMEM((3, C, C), BF), pltpu.VMEM((C, C), BF), pltpu.VMEM((3, 8, 8, C), F32),
            pltpu.VMEM((2, 2, 64, C), BF), pltpu.VMEM((16, 128), F32),
            pltpu.VMEM((16, EMB), F32),
            pltpu.VMEM((2, 16, 128), F32), pltpu.VMEM((pixels, 128), BF),
            pltpu.VMEM((16, 128), BF), pltpu.VMEM((128, pixels), BF),
            pltpu.VMEM((VROWS, pixels), BF), pltpu.VMEM((VROWS, 128), BF),
            pltpu.VMEM((2, pixels, SUB), F32), pltpu.VMEM((2, 8, SUB), F32),
            pltpu.VMEM((2, 16, SUB), F32), pltpu.VMEM((2, pixels, PIX), BF),
            pltpu.VMEM((8, HEAD, PIX), BF),
            DMA((4,)), DMA((4,)), DMA((4,)), DMA((4,)), DMA((4,)), DMA((4,)),
            DMA((3, 1)), DMA((3, 2)), DMA((3, 2)), DMA((3, 2)), DMA((3, 2)), DMA((3, 3)),
            DMA((3, 3)), DMA((3, 6)), DMA((3, 6)), DMA((4,)), DMA((4,)), DMA((4,)), DMA((4,)),
            DMA((1,)), DMA((3, 8)), DMA((3, 8)), DMA((2, 2)), DMA((2, 2)), DMA((3, 8)),
            DMA((3, 8)), DMA((3,)), DMA((15,)), DMA((2,)), DMA((8,)), DMA((8,)),
        ],
        compiler_params=pltpu.CompilerParams(
            collective_id=1, has_side_effects=True, vmem_limit_bytes=VMEM_LIMIT
        ),
    )(*args)


def band_back_send(me, src, dst, ssem, rsem):
    for chan in range(4):
        cols = pl.ds(chan * 128, 128)
        itself = jnp.logical_and(me.band == me.r, me.c == chan)

        @pl.when(jnp.logical_not(itself))
        def _():
            send(src.at[:, cols], dst.at[me.z], ssem.at[chan], rsem.at[me.z], (me.band, chan))

        @pl.when(itself)
        def _():
            local(src.at[:, cols], dst.at[me.z], rsem.at[me.z])


def band_back_wait(me, src, dst, ssem, rsem):
    for n in range(4):
        pltpu.make_async_copy(src.at[:, pl.ds(0, 128)], dst.at[n], rsem.at[n]).wait()
    for chan in range(4):
        itself = jnp.logical_and(me.band == me.r, me.c == chan)

        @pl.when(jnp.logical_not(itself))
        def _():
            pltpu.make_async_remote_copy(
                src_ref=src.at[:, pl.ds(chan * 128, 128)], dst_ref=dst.at[me.z],
                send_sem=ssem.at[chan], recv_sem=rsem.at[me.z], device_id=(me.band, chan),
                device_id_type=MESH_ID,
            ).wait_send()


def greet_back(me, barrier):
    own_block = me.pair == me.z
    for n in range(4):
        itself = jnp.logical_and(own_block, me.z == n)

        @pl.when(jnp.logical_not(itself))
        def _():
            pl.semaphore_signal(
                barrier, inc=1, device_id=(2 * n + me.k, mixed(me.z, jnp.int32(n))),
                device_id_type=MESH_ID,
            )

    return 4 - jnp.where(own_block, 1, 0)


def middle_kernel(
    attn, res, tgt, wo, vec, qkv, ctx, p, pc, o, linv,
    out_o, cot_o, gwo_o, gob_o, dt_o, ctot_o,
    attn_v, res_v, tgt_v, wo_v, out_b, back, cot_v, dat, dot_v, qkv_v, o_v,
    vext, cvext, dos, dor, qrow, dq, pb, dkv, dqb, dt_v, dctx, cslots,
    bs, br, ds_, dr, cs, cr, ks, kr, q_s, q_r, lsem, osem, psem,
):
    me = Place()
    scaling = HEAD ** (-0.5)
    barrier = pltpu.get_barrier_semaphore()
    greet_plane(me, barrier)
    others = greet_back(me, barrier)
    for step in range(1, 8):
        pl.semaphore_signal(
            barrier, inc=1, device_id=(lax.rem(me.r + step, 8), me.c), device_id_type=MESH_ID
        )
    loads = [local(a, b, lsem.at[j]) for j, (a, b) in enumerate(
        ((attn, attn_v), (wo.at[0], wo_v), (res, res_v), (tgt, tgt_v), (qkv, qkv_v), (o, o_v)))]

    def p_copy(block, slot):
        return pltpu.make_async_copy(
            p.at[pl.ds(pl.multiple_of(block * PIX, PIX), PIX), :], pb.at[slot], psem.at[slot])

    p_copy(me.band, 0).start()

    def band_cols(band):
        return pl.ds(pl.multiple_of(band * PIX, PIX), PIX)

    def head_rows(head):
        return pl.ds(pl.multiple_of(head * HEAD, HEAD), HEAD)

    for load in loads[0:4]:
        load.wait()
    rows = jnp.transpose(attn_v[...].astype(F32)).astype(BF)
    result = res_v[...] + mm(rows, wo_v[...], NT) + vec[10:11, :]
    out_b[...] = result.astype(BF)
    cot = vec[13:14, :] * (result - tgt_v[...].astype(F32))
    cot_v[...] = cot
    low = cot.astype(BF)
    dat[...] = jnp.transpose(mm(low, wo_v[...])).astype(BF)
    pl.semaphore_wait(barrier, 14 + others)
    own = local(dat.at[head_rows(me.d), :], dot_v.at[:, band_cols(me.band)], lsem.at[6])
    copies = []
    for step in range(1, 8):
        head = lax.rem(me.d + step, 8)
        copies.append(
            send(dat.at[head_rows(head), :], dot_v.at[:, band_cols(me.band)], ds_.at[step],
                 dr.at[step], me.head_device(head)))
    saves = [local(cot_v, cot_o, osem.at[0])]
    lowf = low.astype(F32)
    gwo_o[...] = mm(jnp.transpose(lowf).astype(BF), rows).astype(BF)
    gob_o[...] = jnp.broadcast_to(as_row(lowf), (8, C))
    for load in loads[4:]:
        load.wait()
    row = lax.broadcasted_iota(jnp.int32, (HEAD, H * W), 0)
    ones = jnp.where(row < 3, 1.0, 0.0)
    vext[...] = jnp.transpose(jnp.concatenate([qkv_v[2].astype(F32), ones], axis=0)).astype(BF)
    lane = lax.broadcasted_iota(jnp.int32, (16, 128), 1)
    cvext[...] = jnp.where(
        lane < HEAD, ctx[1].astype(F32), jnp.where(lane < HEAD + 3, 1.0, 0.0)).astype(BF)
    queries = qkv_v[0].astype(F32) * scaling
    qrow[...] = jnp.transpose(
        jnp.concatenate([queries, jnp.zeros_like(queries)], axis=0)).astype(BF)
    own.wait()
    for copy in copies:
        copy.wait()
    band_back_send(me, out_b, back, bs, br)
    grad = (dot_v[...].astype(F32) * linv[0:1, :]).astype(BF)
    gradf = grad.astype(F32)
    delta = -jnp.sum(gradf * o_v[...], axis=0, keepdims=True)
    top = delta.astype(BF).astype(F32)
    mid = (delta - top).astype(BF).astype(F32)
    last = delta - top - mid
    dos[0:HEAD, :] = grad
    dos[HEAD:, :] = jnp.where(
        row == 0, top, jnp.where(row == 1, mid, jnp.where(row == 2, last, 0.0))).astype(BF)
    dor[...] = jnp.transpose(jnp.concatenate([gradf, jnp.zeros_like(gradf)], axis=0)).astype(BF)

    def score_grads(values, probs):
        return (probs.astype(F32) * mm(values, dos[...])).astype(BF)

    dsc = score_grads(cvext[...], pc[...])
    for j, (left, right) in enumerate(((dsc, qrow), (pc[...], dor))):
        value = mm(left, right[...])
        dctx[j] = jnp.where(me.k == 0, value, pltpu.roll(value, HEAD, 1))
    cslots[me.r] = dctx[...]
    ctx_copies = [
        send(cslots.at[me.r], cslots.at[me.r], cs.at[step], cr.at[step],
             (lax.rem(me.r + step, 8), me.c))
        for step in range(1, 8)
    ]
    wide = jnp.concatenate([ctx[0].astype(F32), jnp.zeros((112, 128), F32)], axis=0)
    dq[...] = mm(jnp.transpose(wide)[0:HEAD, 0:16].astype(BF), dsc)
    mine = head_rows(me.d)

    @pl.loop(0, 8)
    def _(turn):
        block = lax.rem(me.band + turn, 8)
        slot = lax.rem(turn, 2)

        @pl.when(turn < 7)
        def _():
            p_copy(lax.rem(block + 1, 8), 1 - slot).start()

        p_copy(block, slot).wait()
        grads = []
        for sub in range(2):
            part = pl.ds(pl.multiple_of(block * PIX + sub * SUB, SUB), SUB)
            probs = pb[slot, sub * SUB : (sub + 1) * SUB, :]
            grads.append(score_grads(vext[part, :], probs))
            dkv[block, 1, :, sub * SUB : (sub + 1) * SUB] = jnp.transpose(
                mm(probs, dor[...]))[0:HEAD].astype(BF)
        for sub in range(2):
            part = pl.ds(pl.multiple_of(block * PIX + sub * SUB, SUB), SUB)
            dkv[block, 0, :, sub * SUB : (sub + 1) * SUB] = jnp.transpose(
                mm(grads[sub], qrow[...]))[0:HEAD].astype(BF)
            dq[...] += mm(qkv_v[1, :, part], grads[sub])

        @pl.when(block != me.band)
        def _():
            send(dkv.at[block], dt_v.at[1:3, mine, :], ks.at[block], kr.at[me.d],
                 me.band_device(block))

        @pl.when(block == me.band)
        def _():
            local(dkv.at[block], dt_v.at[1:3, mine, :], kr.at[me.d])

    dqb[...] = (dq[...] * scaling).astype(BF)
    own = local(dqb.at[:, band_cols(me.band)], dt_v.at[0, mine, :], q_r.at[me.d])
    copies = []
    for step in range(1, 8):
        band = lax.rem(me.band + step, 8)
        copies.append(
            send(dqb.at[:, band_cols(band)], dt_v.at[0, mine, :], q_s.at[step], q_r.at[me.d],
                 me.band_device(band)))
    for copy in ctx_copies:
        copy.wait()
    for j in range(2):
        total = cslots[0, j]
        for slot in range(1, 8):
            total = total + cslots[slot, j]
        ctot_o[j] = total
    band_back_wait(me, out_b, back, bs, br)
    saves.append(local(back, out_o, osem.at[2]))
    for copy in copies:
        copy.wait_send()
    for block in range(8):

        @pl.when(block != me.band)
        def _():
            pltpu.make_async_remote_copy(
                src_ref=dkv.at[block], dst_ref=dt_v.at[1:3, mine, :], send_sem=ks.at[block],
                recv_sem=kr.at[me.d], device_id=me.band_device(block), device_id_type=MESH_ID,
            ).wait_send()

        pltpu.make_async_copy(
            dkv.at[0], dt_v.at[1:3, pl.ds(block * HEAD, HEAD), :], kr.at[block]).wait()
        pltpu.make_async_copy(
            dqb.at[:, pl.ds(0, PIX)], dt_v.at[0, pl.ds(block * HEAD, HEAD), :], q_r.at[block]
        ).wait()
    saves.append(local(dt_v, dt_o, osem.at[1]))
    for copy in saves:
        copy.wait()


def middle(*args):
    pixels = H * W
    return pl.pallas_call(
        middle_kernel,
        name="middle",
        out_shape=[
            jax.ShapeDtypeStruct((4, PIX, 128), BF),
            jax.ShapeDtypeStruct((PIX, C), F32),
            jax.ShapeDtypeStruct((C, C), BF),
            jax.ShapeDtypeStruct((8, C), F32),
            jax.ShapeDtypeStruct((3, C, PIX), BF),
            jax.ShapeDtypeStruct((2, 16, 128), F32),
        ],
        in_specs=[ANY] * 4 + [VMEM, ANY, VMEM, ANY, VMEM, ANY, VMEM],
        out_specs=[ANY, ANY, VMEM, VMEM, ANY, VMEM],
        scratch_shapes=[
            pltpu.VMEM((C, PIX), BF), pltpu.VMEM((PIX, C), F32), pltpu.VMEM((PIX, C), BF),
            pltpu.VMEM((C, C), BF), pltpu.VMEM((PIX, C), BF), pltpu.VMEM((4, PIX, 128), BF),
            pltpu.VMEM((PIX, C), F32), pltpu.VMEM((C, PIX), BF), pltpu.VMEM((HEAD, pixels), BF),
            pltpu.VMEM((3, HEAD, pixels), BF), pltpu.VMEM((HEAD, pixels), F32),
            pltpu.VMEM((pixels, 128), BF), pltpu.VMEM((16, 128), BF),
            pltpu.VMEM((128, pixels), BF), pltpu.VMEM((pixels, 128), BF),
            pltpu.VMEM((pixels, 128), BF), pltpu.VMEM((HEAD, pixels), F32),
            pltpu.VMEM((2, PIX, pixels), BF), pltpu.VMEM((8, 2, HEAD, PIX), BF),
            pltpu.VMEM((HEAD, pixels), BF), pltpu.VMEM((3, C, PIX), BF),
            pltpu.VMEM((2, 16, 128), F32), pltpu.VMEM((8, 2, 16, 128), F32),
            DMA((4,)), DMA((4,)), DMA((8,)), DMA((8,)), DMA((8,)), DMA((8,)), DMA((8,)),
            DMA((8,)), DMA((8,)), DMA((8,)), DMA((7,)), DMA((3,)), DMA((2,)),
        ],
        compiler_params=pltpu.CompilerParams(
            collective_id=2, has_side_effects=True, vmem_limit_bytes=VMEM_LIMIT
        ),
    )(*args)


TAPS = 22
GROUP_TAPS = ((0, 1), (1, 3), (4, 3), (7, 3), (10, 3), (13, 3), (16, 3), (19, 2), (21, 1))
GROUPS_SENT = len(GROUP_TAPS)
STAGES = 9


class Reduce:
    def __init__(self, me, part, bufs, total, sems):
        self.me, self.part, self.total = me, part, total
        (self.from_core, self.near_x, self.near_y, self.last_x, self.last_y, self.plane,
         self.plane_two, self.plane_one) = bufs
        self.s, self.r = sems
        odd = lax.rem(me.z, 2)
        self.x = me.c + 1 - 2 * lax.rem(me.c, 2)
        self.y = lax.rem(me.c + 2, 4)
        self.far = lax.rem(self.x + 2, 4)
        self.core = (me.r + 1 - 2 * me.k, me.c)
        self.z1 = me.z + 1 - 2 * odd
        self.z2 = lax.rem(me.z + 2, 4)
        self.z3 = lax.rem(self.z1 + 2, 4)
        self.copies = {}

    def plane_device(self, z):
        return (2 * z + self.me.k, self.me.c)

    def advance(self, group):
        stage, waiting = self.copies.get(group, (0, []))
        for copy in waiting:
            copy.wait()
        start, count = GROUP_TAPS[group]
        step = (self.core_send, self.first_send, self.second_send, self.halve_send,
                self.quarter_send, self.quarter_back, self.half_back, self.core_back,
                lambda *_: [])[stage]
        taps = pl.ds(start, count)
        moves = step(taps, lambda body: pl.loop(start, start + count)(body))
        copies = [
            send(src, dst, self.s.at[group, stage, j], self.r.at[group, stage, j], device)
            for j, (src, dst, device) in enumerate(moves)
        ]
        self.copies[group] = (stage + 1, copies)

    def core_send(self, taps, each):
        return [(self.part.at[taps, :, 1 - self.me.k], self.from_core.at[taps], self.core)]

    def first_send(self, taps, each):
        me, part = self.me, self.part

        @each
        def _(tap):
            own = part[tap, :, me.k].astype(F32) + self.from_core[tap].astype(F32)
            part[tap, :, me.k] = own.astype(BF)

        low, high = pl.ds(0, 32), pl.ds(32, 32)
        x, y = (me.r, self.x), (me.r, self.y)
        return [
            (part.at[taps, self.far, me.k, low, :], self.near_x.at[1, taps], x),
            (part.at[taps, self.far, me.k, high, :], self.near_y.at[1, taps], y),
            (part.at[taps, self.x, me.k, low, :], self.near_x.at[0, taps], x),
            (part.at[taps, self.y, me.k, high, :], self.near_y.at[0, taps], y),
        ]

    def second_send(self, taps, each):
        me, part = self.me, self.part
        low, high = pl.ds(0, 32), pl.ds(32, 32)

        @each
        def _(tap):
            for chan, rows, near in ((self.y, low, self.near_x), (self.x, high, self.near_y)):
                value = part[tap, chan, me.k, rows, :].astype(F32) + near[1, tap].astype(F32)
                part[tap, chan, me.k, rows, :] = value.astype(BF)

        return [
            (part.at[taps, self.y, me.k, low, :], self.last_y.at[taps], (me.r, self.y)),
            (part.at[taps, self.x, me.k, high, :], self.last_x.at[taps], (me.r, self.x)),
        ]

    def rows(self, z):
        return pl.ds(pl.multiple_of(z * 16, 16), 16)

    def halve_send(self, taps, each):
        me, part = self.me, self.part

        @each
        def _(tap):
            for start, near, last in ((0, self.near_x, self.last_y), (32, self.near_y, self.last_x)):
                rows = pl.ds(start, 32)
                value = (part[tap, me.c, me.k, rows, :].astype(F32) + near[0, tap].astype(F32)
                         + last[tap].astype(F32))
                self.plane[tap, rows, :] = value.astype(BF)

        device = self.plane_device(self.z1)
        return [
            (self.plane.at[taps, self.rows(self.z1), :], self.plane_two.at[0, taps], device),
            (self.plane.at[taps, self.rows(self.z3), :], self.plane_two.at[1, taps], device),
        ]

    def quarter_send(self, taps, each):
        @each
        def _(tap):
            for j, z in enumerate((self.me.z, self.z2)):
                value = (self.plane[tap, self.rows(z), :].astype(F32)
                         + self.plane_two[j, tap].astype(F32))
                self.plane[tap, self.rows(z), :] = value.astype(BF)

        return [(self.plane.at[taps, self.rows(self.z2), :], self.plane_one.at[taps],
                 self.plane_device(self.z2))]

    def quarter_back(self, taps, each):
        me = self.me

        @each
        def _(tap):
            value = (self.plane[tap, self.rows(me.z), :].astype(F32)
                     + self.plane_one[tap].astype(F32))
            self.total[tap, me.k, me.z] = value.astype(BF)

        piece = self.total.at[taps, me.k, me.z]
        return [(piece, piece, self.plane_device(self.z2))]

    def half_back(self, taps, each):
        device = self.plane_device(self.z1)
        pieces = [self.total.at[taps, self.me.k, z] for z in (self.me.z, self.z2)]
        return [(piece, piece, device) for piece in pieces]

    def core_back(self, taps, each):
        piece = self.total.at[taps, self.me.k]
        return [(piece, piece, self.core)]


def back_kernel(
    dt, vec, st, x, a1, hid, a2, res, nrm, cot, w1, w2, wq, gwo, gob,
    gimg_o, zs_o, gw1_o, gw2_o, gqkv_o, gwo_o,
    dt_v, x_v, a1_v, hid_v, a2_v, res_v, nrm_v, drs_v, w1_v, w2_v, wq_v,
    cat, turned, acc, groups, slots, halo, keep, img_b, back, zsl,
    part, from_core, near_x, near_y, last_x, last_y, plane, plane_two, plane_one, total,
    ss, sr, hs, hr, bs, br, zs, zr, red_s, red_r, lsem, osem,
):
    me = Place()
    barrier = pltpu.get_barrier_semaphore()
    greet_plane(me, barrier)
    others = greet_back(me, barrier)
    for t in range(1, 4):
        pl.semaphore_signal(
            barrier, inc=1, device_id=(2 * lax.rem(me.z + t, 4) + me.k, me.c),
            device_id_type=MESH_ID,
        )
    loads = [local(a, b, lsem.at[j]) for j, (a, b) in enumerate((
        (dt, dt_v), (wq, wq_v), (res, res_v), (gwo, part.at[0]), (nrm, nrm_v), (cot, drs_v),
        (a2, a2_v), (w2, w2_v), (hid, hid_v), (a1, a1_v), (w1, w1_v), (x, x_v)))]
    reduce = Reduce(
        me, part, (from_core, near_x, near_y, last_x, last_y, plane, plane_two, plane_one), total,
        (red_s, red_r))

    def advance(*groups):
        for group in groups:
            reduce.advance(group)

    group_matrix(groups)
    zero8 = jnp.zeros((8, C), F32)
    members = 1.0 / (H * W * 16)
    loads[0].wait()
    loads[1].wait()
    for j in range(3):
        rows = jnp.transpose(dt_v[j].astype(F32))
        if j != 1:
            keep[j : j + 1, :] = as_row(rows)
        value = mm(rows.astype(BF), wq_v[j])
        if j == 0:
            acc[...] = value
        else:
            acc[...] += value
    loads[2].wait()

    def sums(scaled_of, upstream_of):
        def add(i, carry):
            upstream = upstream_of(i)
            return (carry[0] + fold(upstream), carry[1] + fold(upstream * scaled_of(i)))

        first, cross = lax.fori_loop(0, CHUNKS, add, (zero8, zero8))
        return [as_row(first), as_row(cross)]

    def scaled(ref, number):
        return lambda i: (ref[chunk_of(i), :].astype(F32) - st[2 * number : 2 * number + 1, :]) * st[
            2 * number + 1 : 2 * number + 2, :]

    def exchange(number, rows):
        store_rows(slots.at[number], me.d, rows)
        return plane_exchange(me, slots.at[number], ss.at[number], sr.at[number])

    scaled3, scaled2, scaled1 = scaled(res_v, 2), scaled(hid_v, 1), scaled(x_v, 0)
    rows3 = sums(scaled3, lambda i: acc[chunk_of(i), :])
    pl.semaphore_wait(barrier, 10 + others)
    copies = exchange(0, rows3)
    loads[3].wait()
    advance(0)
    loads[4].wait()

    @pl.loop(0, 3)
    def _(j):
        part[1 + j] = mm(dt_v[j], nrm_v[...]).astype(BF).reshape(4, 2, 64, C)

    advance(1)
    loads[5].wait()
    for copy in copies:
        copy.wait()

    def group_means(total_rows, factor):
        return group_total(total_rows * factor, groups) * members

    total3 = slots_total(slots.at[0])
    gain = vec[2:3, :]
    means = group_means(total3, gain)
    keep[8:16, :] = total3
    inverse = st[5:6, :]

    def resid_grad(i, carry):
        where = chunk_of(i)
        value = drs_v[where, :] + inverse * (
            acc[where, :] * gain - means[0:1] - scaled3(i) * means[1:2])
        drs_v[where, :] = value
        put_shifted(cat, 64 + i * 64, value)
        return carry + fold(value.astype(BF).astype(F32))

    keep[3:4, :] = as_row(lax.fori_loop(0, CHUNKS, resid_grad, zero8))
    halo_send(me, cat, halo.at[0], hs.at[0], hr.at[0])
    advance(0, 1)
    turned[...] = jnp.transpose(drs_v[...]).astype(BF)

    def weight_grads(group, source, first):
        start, count = GROUP_TAPS[group]

        @pl.loop(0, count)
        def _(i):
            tap = start - first + i
            rows = pl.ds(pl.multiple_of(lax.div(tap, 3) * 64, 64), PIX)
            part[start + i] = mm(turned[...], source[lax.rem(tap, 3), rows, :]).astype(
                BF).reshape(4, 2, 64, C)

        advance(group)

    loads[6].wait()
    for group in (2, 3, 4):
        weight_grads(group, a2_v, 4)
    advance(0)
    acc[...] = jnp.zeros((PIX, C), F32)
    loads[7].wait()
    conv_taps(acc, cat, w2_v, (1,), True, NN)
    halo_wait(me, cat, halo.at[0], hs.at[0], hr.at[0])
    advance(2)
    conv_taps(acc, cat, w2_v, (0, 2), True, NN)
    advance(1)
    loads[8].wait()
    gain2, bias2 = vec[1:2, :], vec[4:5, :]
    scale, shift = 1.0 + vec[11:12, :], vec[12:13, :]

    def mod_grad(i):
        where = chunk_of(i)
        mod = (scaled2(i) * gain2 + bias2) * scale + shift
        value = acc[where, :] * swish_slope(mod)
        acc[where, :] = value
        return value

    copies = exchange(1, sums(scaled2, mod_grad))
    advance(0, 2)
    for copy in copies:
        copy.wait()
    total2 = slots_total(slots.at[1])
    means2 = group_means(total2, gain2 * scale)
    keep[16:24, :] = total2
    inverse2 = st[3:4, :]

    def hidden_grad(i, carry):
        where = chunk_of(i)
        value = inverse2 * (
            acc[where, :] * (gain2 * scale) - means2[0:1] - scaled2(i) * means2[1:2])
        acc[where, :] = value
        put_shifted(cat, 64 + i * 64, value)
        return carry + fold(value.astype(BF).astype(F32))

    keep[1:2, :] = as_row(lax.fori_loop(0, CHUNKS, hidden_grad, zero8))
    halo_send(me, cat, halo.at[1], hs.at[1], hr.at[1])
    advance(3, 1)
    turned[...] = jnp.transpose(acc[...]).astype(BF)
    loads[9].wait()
    for group in (5, 6, 7, 8):
        weight_grads(group, a1_v, 13)
    advance(0, 2)
    acc[...] = jnp.zeros((PIX, C), F32)
    loads[10].wait()
    conv_taps(acc, cat, w1_v, (1,), True, NN)
    halo_wait(me, cat, halo.at[1], hs.at[1], hr.at[1])
    advance(1, 3)
    conv_taps(acc, cat, w1_v, (0, 2), True, NN)
    loads[11].wait()
    gain1, bias1 = vec[0:1, :], vec[3:4, :]

    def pre_grad(i):
        where = chunk_of(i)
        value = acc[where, :] * swish_slope(scaled1(i) * gain1 + bias1)
        acc[where, :] = value
        return value

    first, cross = sums(scaled1, pre_grad)
    copies = exchange(2, [first, cross, keep[1:2, :], keep[3:4, :], keep[0:1, :], keep[2:3, :],
                          gob[0:1, :]])
    advance(4, 0, 2, 3, 1)
    for copy in copies:
        copy.wait()
    total1 = slots_total(slots.at[2])
    means1 = group_means(total1, gain1)
    inverse1 = st[1:2, :]

    @pl.loop(0, CHUNKS)
    def _(i):
        where = chunk_of(i)
        value = drs_v[where, :] + inverse1 * (
            acc[where, :] * gain1 - means1[0:1] - scaled1(i) * means1[1:2])
        img_b[where, :] = value.astype(BF)

    band_back_send(me, img_b, back, bs, br)
    u2, v2 = keep[16:17, :], keep[17:18, :]
    keep[24:40, :] = jnp.concatenate(
        [total1[1:2], scale * v2, keep[9:10, :], total1[0:1], scale * u2, keep[8:9, :],
         total1[2:7], gain2 * v2 + bias2 * u2, u2, jnp.zeros((3, C), F32)], axis=0)
    own_cols = pl.ds(pl.multiple_of(me.c * 128, 128), 128)
    zsl[me.z] = keep[24:40, own_cols]
    zcopies = [
        send(zsl.at[me.z], zsl.at[me.z], zs.at[t], zr.at[t],
             (2 * lax.rem(me.z + t, 4) + me.k, me.c))
        for t in range(1, 4)
    ]
    advance(4, 5, 2, 3, 1, 0, 6, 4, 5, 2, 3, 7, 1, 6, 4, 5, 8)
    for copy in zcopies:
        copy.wait()
    zs_o[...] = zsl[...]
    advance(7, 3, 4, 6, 5, 8, 7)
    band_back_wait(me, img_b, back, bs, br)
    saves = [local(back, gimg_o, osem.at[0])]
    for _ in range(STAGES):
        for group in range(GROUPS_SENT):
            if reduce.copies[group][0] < STAGES:
                reduce.advance(group)
    for j, (dst, start, count) in enumerate(
            ((gwo_o, 0, 1), (gqkv_o, 1, 3), (gw2_o, 4, 9), (gw1_o, 13, 9))):
        saves.append(local(total.at[pl.ds(start, count)], dst, osem.at[j + 1]))
    for copy in saves:
        copy.wait()


def back(*args):
    shared = [
        ((3, C, PIX), BF), ((PIX, C), BF), ((3, PAD, C), BF), ((PIX, C), F32), ((3, PAD, C), BF),
        ((PIX, C), F32), ((PIX, C), BF), ((PIX, C), F32), ((9, C, C), BF), ((9, C, C), BF),
        ((3, C, C), BF), ((3, PAD, C), BF), ((C, PIX), BF), ((PIX, C), F32), ((C, C), BF),
        ((3, 8, 8, C), F32), ((2, 2, 64, C), BF), ((40, C), F32), ((PIX, C), BF),
        ((4, PIX, 128), BF), ((4, 16, 128), F32),
        ((TAPS, 4, 2, 64, C), BF), ((TAPS, 4, 64, C), BF), ((2, TAPS, 32, C), BF),
        ((2, TAPS, 32, C), BF), ((TAPS, 32, C), BF), ((TAPS, 32, C), BF), ((TAPS, 64, C), BF),
        ((2, TAPS, 16, C), BF), ((TAPS, 16, C), BF), ((TAPS, 2, 4, 16, C), BF),
    ]
    return pl.pallas_call(
        back_kernel,
        name="back",
        out_shape=[
            jax.ShapeDtypeStruct((4, PIX, 128), BF),
            jax.ShapeDtypeStruct((4, 16, 128), F32),
            jax.ShapeDtypeStruct((9, 2, 4, 16, C), BF),
            jax.ShapeDtypeStruct((9, 2, 4, 16, C), BF),
            jax.ShapeDtypeStruct((3, 2, 4, 16, C), BF),
            jax.ShapeDtypeStruct((1, 2, 4, 16, C), BF),
        ],
        in_specs=[ANY, VMEM, VMEM] + [ANY] * 11 + [VMEM],
        out_specs=[ANY, VMEM, ANY, ANY, ANY, ANY],
        scratch_shapes=[pltpu.VMEM(*one) for one in shared]
        + [
            DMA((3, 8)), DMA((3, 8)), DMA((2, 2)), DMA((2, 2)), DMA((4,)), DMA((4,)), DMA((4,)),
            DMA((4,)), DMA((GROUPS_SENT, STAGES, 4)), DMA((GROUPS_SENT, STAGES, 4)), DMA((12,)),
            DMA((5,)),
        ],
        compiler_params=pltpu.CompilerParams(
            collective_id=3, has_side_effects=True, vmem_limit_bytes=VMEM_LIMIT
        ),
    )(*args)


def split_rows(rows):
    first = rows.astype(BF).astype(F32)
    second = (rows - first).astype(BF).astype(F32)
    stacked = jnp.concatenate([first, second, rows - first - second, jnp.zeros((80, 128), F32)],
                              axis=0)
    left = jnp.transpose(stacked).astype(BF)
    return left[:, 0:16], left[:, 16:32], left[:, 32:48]


def finish_kernel(
    res, gimg, gw1, gw2, gqkv, gwo, zs, ctot, feat, tokens,
    res_o, gimg_o, gain_o, bias_o, gw1_o, gw2_o, cb_o, gemb_o, gembb_o, gqkv_o, qvb_o, gctx_o,
    gctxb_o, gwo_o, ob_o,
    res_v, gimg_v, gw1_v, gw2_v, gqkv_v, gwo_v, res_f, gimg_f, gw1_f, gw2_f, gqkv_f, gwo_f,
    gemb_f, gctx_f, lsem, osem,
):
    pairs = (
        (gw1, gw1_v, gw1_f, gw1_o), (gw2, gw2_v, gw2_f, gw2_o), (res, res_v, res_f, res_o),
        (gimg, gimg_v, gimg_f, gimg_o), (gqkv, gqkv_v, gqkv_f, gqkv_o), (gwo, gwo_v, gwo_f, gwo_o))
    loads = [local(src, low, lsem.at[j]) for j, (src, low, _, _) in enumerate(pairs)]
    saves = []
    for j in range(2):
        rows = jnp.concatenate([zs[n, 11 + j : 12 + j, :] for n in range(4)]
                               + [jnp.zeros((12, 128), F32)], axis=0)
        gemb_f[j] = sum(mm(term, feat[...]) for term in split_rows(rows))
        saves.append(local(gemb_f.at[j], gemb_o.at[j], osem.at[6 + j]))
        gctx_f[j] = sum(mm(term, tokens[...]) for term in split_rows(ctot[j]))
        saves.append(local(gctx_f.at[j], gctx_o.at[j], osem.at[8 + j]))
        gctxb_o[j : j + 1, :] = as_row(ctot[j])
    total = (zs[0] + zs[1]) + (zs[2] + zs[3])
    gain_o[...] = total[0:3]
    bias_o[...] = total[3:6]
    cb_o[...] = total[6:8]
    qvb_o[...] = total[8:10]
    ob_o[...] = total[10:11]
    gembb_o[...] = total[11:13]
    for j, (_, low, high, dst) in enumerate(pairs):
        loads[j].wait()

        @pl.loop(0, high.shape[0])
        def _(i):
            high[i] = low[i].astype(F32)

        saves.append(local(high, dst, osem.at[j]))
    for copy in saves:
        copy.wait()


def finish(*args):
    wide = [((4, PIX, 128), F32)] * 2 + [((9, 128, C), F32)] * 2 + [((3, 128, C), F32),
                                                                    ((1, 128, C), F32)]
    res, gimg, gw1, gw2, gqkv, gwo = wide
    emb, ctx = ((2, 128, EMB), F32), ((2, 128, CTXW), F32)
    outs = [
        res, gimg, ((3, 128), F32), ((3, 128), F32), gw1, gw2, ((2, 128), F32), emb,
        ((2, 128), F32), gqkv, ((2, 128), F32), ctx, ((2, 128), F32), gwo, ((1, 128), F32)]
    return pl.pallas_call(
        finish_kernel,
        name="finish",
        out_shape=[jax.ShapeDtypeStruct(*one) for one in outs],
        in_specs=[ANY] * 6 + [VMEM] * 4,
        out_specs=[VMEM if len(one[0]) == 2 else ANY for one in outs],
        scratch_shapes=[pltpu.VMEM(shape, BF) for shape, _ in wide]
        + [pltpu.VMEM(*one) for one in wide + [emb, ctx]] + [DMA((6,)), DMA((10,))],
        compiler_params=pltpu.CompilerParams(vmem_limit_bytes=VMEM_LIMIT),
    )(*args)


def plane_body(
    image, target, time_index, loss_weight, clip_embed, clip_tokens, norm_gain, norm_bias,
    conv1_w, conv2_w, conv_bias, emb_w, emb_b, qkv_w, qv_bias, ctx_w, ctx_b, out_w, out_b,
):
    (x, tgt, vec, st, a1, hid, a2, res, nrm, w1, w2, wq, wo, qkv, attn, p, ctx, pc, o, linv, feat,
     tokens) = front(
        image.reshape(4, PIX, 128), target.reshape(4, PIX, 128), time_index, loss_weight,
        clip_embed, clip_tokens, norm_gain, norm_bias, conv_bias, qv_bias, out_b[None], emb_w,
        emb_b, ctx_w, ctx_b, conv1_w.reshape(9, 128, C), conv2_w.reshape(9, 128, C), qkv_w,
        out_w[None])
    result, cot, gwo, gob, dt, ctot = middle(
        attn, res, tgt, wo, vec, qkv, ctx, p, pc, o, linv)
    gimg, zs, gw1, gw2, gqkv, gwo = back(
        dt, vec, st, x, a1, hid, a2, res, nrm, cot, w1, w2, wq, gwo.reshape(4, 2, 64, C), gob)
    taps = lambda value: value.reshape(value.shape[0], 128, C)
    outs = finish(result, gimg, taps(gw1), taps(gw2), taps(gqkv), taps(gwo), zs, ctot, feat, tokens)
    shapes = (
        image, image, norm_gain, norm_bias, conv1_w, conv2_w, conv_bias, emb_w, emb_b, qkv_w,
        qv_bias, ctx_w, ctx_b, out_w, out_b)
    return tuple(out.reshape(like.shape) for out, like in zip(outs, shapes))


def solution(mesh):
    sizes = dict(mesh.shape)
    planes = sizes["row"] == 8 and sizes["chan"] == 4
    return jax.shard_map(
        plane_body if planes else general_body,
        mesh=mesh,
        in_specs=(
            P(None, "row", None, "chan"), P(None, "row", None, "chan"), P(), P(), P(), P(),
            P(None, "chan"), P(None, "chan"), P(None, None, "chan", None),
            P(None, None, "chan", None), P(None, "chan"), P(None, "chan", None),
            P(None, "chan"), P(None, "chan", None), P(None, "chan"), P(None, "chan", None),
            P(None, "chan"), P("chan", None), P("chan"),
        ),
        out_specs=(
            P(None, "row", None, "chan"), P(None, "row", None, "chan"), P(None, "chan"),
            P(None, "chan"), P(None, None, "chan", None), P(None, None, "chan", None),
            P(None, "chan"), P(None, "chan", None), P(None, "chan"), P(None, "chan", None),
            P(None, "chan"), P(None, "chan", None), P(None, "chan"), P("chan", None), P("chan"),
        ),
        check_vma=False,
    )
```

```python
import math

import jax
import jax.numpy as jnp
from jax import lax
from jax.experimental import pallas as pl
from jax.experimental.pallas import tpu as pltpu
from jax.sharding import PartitionSpec as P

C = 512
GROUPS = 32
HEAD = 64
EMB = 2048
CTXW = 2048
CTX = 4
H = 64
W = 64
MB_IMG = 2


HIGH = lax.Precision.HIGHEST
EPSILON = 1e-05


def with_halo(cells, sides, width):
    for axis, dim in sides:
        count = lax.axis_size(axis)
        ends = count - 1
        head = lax.slice_in_dim(cells, 0, width, axis=dim)
        tail = lax.slice_in_dim(cells, cells.shape[dim] - width, cells.shape[dim], axis=dim)
        cells = jnp.concatenate(
            [
                lax.ppermute(tail, axis, [(i, (i + 1) % count) for i in range(ends)]),
                cells,
                lax.ppermute(head, axis, [((i + 1) % count, i) for i in range(ends)]),
            ],
            axis=dim,
        )
    return cells


def swish(source):
    return source * jax.nn.sigmoid(source)


def swish_slope(source):
    sigma = jax.nn.sigmoid(source)
    return sigma * (1.0 + source * (1.0 - sigma))


def time_features(time_index, width_all):
    half_width = width_all // 2
    frequency = jnp.exp(-math.log(10000.0) * jnp.arange(half_width, dtype=jnp.float32) / half_width)
    angles = time_index.astype(jnp.float32)[:, None] * frequency[None, :]
    return jnp.concatenate([jnp.cos(angles), jnp.sin(angles)], axis=1)


def rows_around(source):
    return with_halo(source, (("row", 1),), 1)


def all_channels(source):
    return lax.all_gather(source, "chan", axis=3, tiled=True)


def channel_total(source):
    return lax.psum_scatter(
        source.astype(jnp.bfloat16), "chan", scatter_dimension=3, tiled=True
    ).astype(jnp.float32)


def norm_forward(source, group_width, members):
    layout = source.shape
    grouped = source.reshape(layout[0], layout[1], layout[2], layout[3] // group_width, group_width)
    first_sum = jnp.sum(grouped, axis=(1, 2, 4))
    square_sum = jnp.sum(grouped * grouped, axis=(1, 2, 4))
    first_sum, square_sum = lax.psum((first_sum, square_sum), "row")
    center = first_sum / members
    spread = square_sum / members - center * center
    inverse_std = lax.rsqrt(spread + EPSILON)
    scaled = (grouped - center[:, None, None, :, None]) * inverse_std[:, None, None, :, None]
    return (scaled.reshape(layout), inverse_std)


def norm_backward(upstream, scaled, inverse_std, gain, group_width, members):
    layout = upstream.shape
    grouped_grad = (upstream * gain).reshape(
        layout[0], layout[1], layout[2], layout[3] // group_width, group_width
    )
    grouped_norm = scaled.reshape(grouped_grad.shape)
    grad_sum = jnp.sum(grouped_grad, axis=(1, 2, 4))
    cross_sum = jnp.sum(grouped_grad * grouped_norm, axis=(1, 2, 4))
    grad_sum, cross_sum = lax.psum((grad_sum, cross_sum), "row")
    result = inverse_std[:, None, None, :, None] * (
        grouped_grad
        - grad_sum[:, None, None, :, None] / members
        - grouped_norm * (cross_sum[:, None, None, :, None] / members)
    )
    gain_grad = jnp.sum(upstream * scaled, axis=(0, 1, 2))
    bias_grad = jnp.sum(upstream, axis=(0, 1, 2))
    return (result.reshape(layout), gain_grad, bias_grad)


def conv_apply(padded, weight):
    height = padded.shape[1] - 2
    width = padded.shape[2]
    widened = jnp.pad(padded, ((0, 0), (0, 0), (1, 1), (0, 0)))
    result = None
    for row_step in range(3):
        for col_step in range(3):
            partial_term = jnp.einsum(
                "nhwc,dc->nhwd",
                widened[:, row_step : row_step + height, col_step : col_step + width],
                weight[row_step, col_step],
                preferred_element_type=jnp.float32,
            )
            result = partial_term if result is None else result + partial_term
    return result


def conv_weight_grad(padded, upstream_low):
    height = upstream_low.shape[1]
    width = upstream_low.shape[2]
    widened = jnp.pad(padded, ((0, 0), (0, 0), (1, 1), (0, 0)))
    stacked = []
    for row_step in range(3):
        row_terms = []
        for col_step in range(3):
            row_terms.append(
                jnp.einsum(
                    "nhwc,nhwd->dc",
                    widened[:, row_step : row_step + height, col_step : col_step + width],
                    upstream_low,
                    preferred_element_type=jnp.float32,
                )
            )
        stacked.append(jnp.stack(row_terms))
    return jnp.stack(stacked)


def conv_input_grad(upstream_low, weight):
    height = upstream_low.shape[1]
    width = upstream_low.shape[2]
    widened = jnp.pad(rows_around(upstream_low), ((0, 0), (0, 0), (1, 1), (0, 0)))
    result = None
    for row_step in range(3):
        for col_step in range(3):
            partial_term = jnp.einsum(
                "nhwd,dc->nhwc",
                widened[
                    :, 2 - row_step : 2 - row_step + height, 2 - col_step : 2 - col_step + width
                ],
                weight[row_step, col_step],
                preferred_element_type=jnp.float32,
            )
            result = partial_term if result is None else result + partial_term
    return channel_total(result)


def general_body(
    image,
    target,
    time_index,
    loss_weight,
    clip_embed,
    clip_tokens,
    norm_gain,
    norm_bias,
    conv1_w,
    conv2_w,
    conv_bias,
    emb_w,
    emb_b,
    qkv_w,
    qv_bias,
    ctx_w,
    ctx_b,
    out_w,
    out_b,
):
    local_chan = conv1_w.shape[2]
    group_width = C // GROUPS
    members = H * W * group_width
    head_count = local_chan // HEAD
    scaling = HEAD ** (-0.5)
    batches = image.shape[0] // MB_IMG
    band_rows = image.shape[1]
    image_cols = image.shape[2]

    def heads_of(source):
        return source.reshape(source.shape[0], -1, head_count, HEAD)

    def one_batch(carry, items):
        picture, target_in, steps_in, weight_in, embed_in, tokens_in = items
        feat_low = swish(time_features(steps_in, EMB) + embed_in.astype(jnp.float32)).astype(
            jnp.bfloat16
        )
        cond = (
            jnp.einsum("ne,jde->njd", feat_low, emb_w, preferred_element_type=jnp.float32) + emb_b
        )
        scale_term = cond[:, 0][:, None, None, :]
        shift_term = cond[:, 1][:, None, None, :]
        picture_f = picture.astype(jnp.float32)
        scaled_one, inverse_one = norm_forward(picture_f, group_width, members)
        pre_one = scaled_one * norm_gain[0] + norm_bias[0]
        padded_one = all_channels(rows_around(swish(pre_one).astype(jnp.bfloat16)))
        hidden = conv_apply(padded_one, conv1_w) + conv_bias[0]
        scaled_two, inverse_two = norm_forward(hidden, group_width, members)
        normal_two = scaled_two * norm_gain[1] + norm_bias[1]
        modded = normal_two * (1.0 + scale_term) + shift_term
        padded_two = all_channels(rows_around(swish(modded).astype(jnp.bfloat16)))
        resid = picture_f + conv_apply(padded_two, conv2_w) + conv_bias[1]
        scaled_three, inverse_three = norm_forward(resid, group_width, members)
        normed_full = all_channels(
            (scaled_three * norm_gain[2] + norm_bias[2]).astype(jnp.bfloat16)
        )
        projected = jnp.einsum(
            "nhwc,tdc->nhwtd", normed_full, qkv_w, preferred_element_type=jnp.float32
        )
        query_own = heads_of((projected[..., 0, :] + qv_bias[0]).astype(jnp.bfloat16))
        key_own = heads_of(projected[..., 1, :].astype(jnp.bfloat16))
        value_own = heads_of((projected[..., 2, :] + qv_bias[1]).astype(jnp.bfloat16))
        context = (
            jnp.einsum("nte,jde->ntjd", tokens_in, ctx_w, preferred_element_type=jnp.float32)
            + ctx_b
        )
        ctx_key = heads_of(context[:, :, 0].astype(jnp.bfloat16))
        ctx_value = heads_of(context[:, :, 1].astype(jnp.bfloat16))
        key_rows, value_rows = (
            lax.all_gather(key_own, "row", axis=1, tiled=True),
            lax.all_gather(value_own, "row", axis=1, tiled=True),
        )
        score_image = (
            jnp.einsum("nqhd,nkhd->nhqk", query_own, key_rows, preferred_element_type=jnp.float32)
            * scaling
        )
        score_context = (
            jnp.einsum("nqhd,nkhd->nhqk", query_own, ctx_key, preferred_element_type=jnp.float32)
            * scaling
        )
        top_score = jnp.maximum(jnp.max(score_image, axis=3), jnp.max(score_context, axis=3))
        expo_image = jnp.exp(score_image - top_score[..., None])
        expo_context = jnp.exp(score_context - top_score[..., None])
        denom = jnp.sum(expo_image, axis=3) + jnp.sum(expo_context, axis=3)
        prob_image = expo_image / denom[..., None]
        prob_context = expo_context / denom[..., None]
        attended = jnp.einsum(
            "nhqk,nkhd->nqhd",
            prob_image.astype(jnp.bfloat16),
            value_rows,
            preferred_element_type=jnp.float32,
        ) + jnp.einsum(
            "nhqk,nkhd->nqhd",
            prob_context.astype(jnp.bfloat16),
            ctx_value,
            preferred_element_type=jnp.float32,
        )
        attn_full = all_channels(attended.astype(jnp.bfloat16).reshape(picture.shape))
        result = (
            resid
            + jnp.einsum("nhwc,dc->nhwd", attn_full, out_w, preferred_element_type=jnp.float32)
            + out_b
        )
        cotangent = weight_in[:, None, None, None] * (result - target_in.astype(jnp.float32))
        grad_proj = cotangent.astype(jnp.bfloat16)
        grad_outw = jnp.einsum(
            "nhwc,nhwd->dc", attn_full, grad_proj, preferred_element_type=jnp.float32
        )
        grad_outb = jnp.sum(grad_proj.astype(jnp.float32), axis=(0, 1, 2))
        grad_attn = heads_of(
            channel_total(
                jnp.einsum("nhwd,dc->nhwc", grad_proj, out_w, preferred_element_type=jnp.float32)
            ).astype(jnp.bfloat16)
        )
        dprob_image = jnp.einsum(
            "nqhd,nkhd->nhqk", grad_attn, value_rows, preferred_element_type=jnp.float32
        )
        dprob_context = jnp.einsum(
            "nqhd,nkhd->nhqk", grad_attn, ctx_value, preferred_element_type=jnp.float32
        )
        delta = jnp.sum(prob_image * dprob_image, axis=3) + jnp.sum(
            prob_context * dprob_context, axis=3
        )
        dscore_image = (prob_image * (dprob_image - delta[..., None])).astype(jnp.bfloat16)
        dscore_context = (prob_context * (dprob_context - delta[..., None])).astype(jnp.bfloat16)
        grad_query = (
            jnp.einsum(
                "nhqk,nkhd->nqhd", dscore_image, key_rows, preferred_element_type=jnp.float32
            )
            + jnp.einsum(
                "nhqk,nkhd->nqhd", dscore_context, ctx_key, preferred_element_type=jnp.float32
            )
        ) * scaling
        grad_ctx_key = (
            jnp.einsum(
                "nhqk,nqhd->nkhd", dscore_context, query_own, preferred_element_type=jnp.float32
            )
            * scaling
        )
        grad_ctx_value = jnp.einsum(
            "nhqk,nqhd->nkhd",
            prob_context.astype(jnp.bfloat16),
            grad_attn,
            preferred_element_type=jnp.float32,
        )
        key_terms = (
            jnp.einsum(
                "nhqk,nqhd->nkhd", dscore_image, query_own, preferred_element_type=jnp.float32
            )
            * scaling
        )
        value_terms = jnp.einsum(
            "nhqk,nqhd->nkhd",
            prob_image.astype(jnp.bfloat16),
            grad_attn,
            preferred_element_type=jnp.float32,
        )
        grad_key, grad_value = (
            lax.psum_scatter(
                key_terms.astype(jnp.bfloat16), "row", scatter_dimension=1, tiled=True
            ).astype(jnp.float32),
            lax.psum_scatter(
                value_terms.astype(jnp.bfloat16), "row", scatter_dimension=1, tiled=True
            ).astype(jnp.float32),
        )
        grad_stack = (
            jnp.stack([grad_query, grad_key, grad_value], axis=2)
            .reshape(picture.shape[0], band_rows, image_cols, 3, local_chan)
            .astype(jnp.bfloat16)
        )
        grad_qkvw = jnp.einsum(
            "nhwc,nhwtd->tdc", normed_full, grad_stack, preferred_element_type=jnp.float32
        )
        stack_sums = jnp.sum(grad_stack.astype(jnp.float32), axis=(0, 1, 2))
        grad_qvb = jnp.stack([stack_sums[0], stack_sums[2]])
        grad_context = jnp.stack(
            [
                grad_ctx_key.reshape(picture.shape[0], CTX, local_chan),
                grad_ctx_value.reshape(picture.shape[0], CTX, local_chan),
            ],
            axis=2,
        )
        grad_ctxw = jnp.einsum(
            "nte,ntjd->jde", tokens_in.astype(jnp.float32), grad_context, precision=HIGH
        )
        grad_ctxb = jnp.sum(grad_context, axis=(0, 1))
        grad_normed = channel_total(
            jnp.einsum("nhwtd,tdc->nhwc", grad_stack, qkv_w, preferred_element_type=jnp.float32)
        )
        grad_resid, gain_three, bias_three = norm_backward(
            grad_normed, scaled_three, inverse_three, norm_gain[2], group_width, members
        )
        grad_resid = cotangent + grad_resid
        grad_conv_two = grad_resid.astype(jnp.bfloat16)
        grad_w_two = conv_weight_grad(padded_two, grad_conv_two)
        grad_b_two = jnp.sum(grad_conv_two.astype(jnp.float32), axis=(0, 1, 2))
        grad_modded = conv_input_grad(grad_conv_two, conv2_w) * swish_slope(modded)
        grad_cond = jnp.stack(
            [jnp.sum(grad_modded * normal_two, axis=(1, 2)), jnp.sum(grad_modded, axis=(1, 2))],
            axis=1,
        )
        grad_embw = jnp.einsum(
            "ne,njd->jde", feat_low.astype(jnp.float32), grad_cond, precision=HIGH
        )
        grad_embb = jnp.sum(grad_cond, axis=0)
        grad_hidden, gain_two, bias_two = norm_backward(
            grad_modded * (1.0 + scale_term),
            scaled_two,
            inverse_two,
            norm_gain[1],
            group_width,
            members,
        )
        grad_conv_one = grad_hidden.astype(jnp.bfloat16)
        grad_w_one = conv_weight_grad(padded_one, grad_conv_one)
        grad_b_one = jnp.sum(grad_conv_one.astype(jnp.float32), axis=(0, 1, 2))
        grad_pre_one = conv_input_grad(grad_conv_one, conv1_w) * swish_slope(pre_one)
        grad_input, gain_one, bias_one = norm_backward(
            grad_pre_one, scaled_one, inverse_one, norm_gain[0], group_width, members
        )
        grad_picture = grad_resid + grad_input
        grad_gains = jnp.stack([gain_one, gain_two, gain_three])
        grad_biases = jnp.stack([bias_one, bias_two, bias_three])
        grad_convb = jnp.stack([grad_b_one, grad_b_two])
        batch_grads = (
            grad_gains,
            grad_biases,
            grad_w_one,
            grad_w_two,
            grad_convb,
            grad_embw,
            grad_embb,
            grad_qkvw,
            grad_qvb,
            grad_ctxw,
            grad_ctxb,
            grad_outw,
            grad_outb,
        )
        updated = tuple((running + update for running, update in zip(carry, batch_grads)))
        return (updated, (result, grad_picture))

    start = (
        jnp.zeros(norm_gain.shape, jnp.float32),
        jnp.zeros(norm_bias.shape, jnp.float32),
        jnp.zeros(conv1_w.shape, jnp.float32),
        jnp.zeros(conv2_w.shape, jnp.float32),
        jnp.zeros(conv_bias.shape, jnp.float32),
        jnp.zeros(emb_w.shape, jnp.float32),
        jnp.zeros(emb_b.shape, jnp.float32),
        jnp.zeros(qkv_w.shape, jnp.float32),
        jnp.zeros(qv_bias.shape, jnp.float32),
        jnp.zeros(ctx_w.shape, jnp.float32),
        jnp.zeros(ctx_b.shape, jnp.float32),
        jnp.zeros(out_w.shape, jnp.float32),
        jnp.zeros(out_b.shape, jnp.float32),
    )
    items = (
        image.reshape(batches, MB_IMG, band_rows, image_cols, local_chan),
        target.reshape(batches, MB_IMG, band_rows, image_cols, local_chan),
        time_index.reshape(batches, MB_IMG),
        loss_weight.reshape(batches, MB_IMG),
        clip_embed.reshape(batches, MB_IMG, EMB),
        clip_tokens.reshape(batches, MB_IMG, CTX, CTXW),
    )
    totals, (results, picture_grads) = lax.scan(one_batch, start, items)
    (
        sum_gain,
        sum_bias,
        sum_conv_one,
        sum_conv_two,
        sum_conv_bias,
        sum_emb_w,
        sum_emb_b,
        sum_qkv_w,
        sum_qv_bias,
        sum_ctx_w,
        sum_ctx_b,
        sum_out_w,
        sum_out_b,
    ) = totals
    (
        sum_gain,
        sum_bias,
        sum_conv_one,
        sum_conv_two,
        sum_conv_bias,
        sum_emb_w,
        sum_emb_b,
        sum_qkv_w,
        sum_qv_bias,
        sum_ctx_w,
        sum_ctx_b,
        sum_out_w,
        sum_out_b,
    ) = (
        lax.psum(sum_gain.astype(jnp.bfloat16), "row").astype(jnp.float32),
        lax.psum(sum_bias.astype(jnp.bfloat16), "row").astype(jnp.float32),
        lax.psum(sum_conv_one.astype(jnp.bfloat16), "row").astype(jnp.float32),
        lax.psum(sum_conv_two.astype(jnp.bfloat16), "row").astype(jnp.float32),
        lax.psum(sum_conv_bias.astype(jnp.bfloat16), "row").astype(jnp.float32),
        lax.psum(sum_emb_w.astype(jnp.bfloat16), "row").astype(jnp.float32),
        lax.psum(sum_emb_b.astype(jnp.bfloat16), "row").astype(jnp.float32),
        lax.psum(sum_qkv_w.astype(jnp.bfloat16), "row").astype(jnp.float32),
        lax.psum(sum_qv_bias.astype(jnp.bfloat16), "row").astype(jnp.float32),
        lax.psum(sum_ctx_w.astype(jnp.bfloat16), "row").astype(jnp.float32),
        lax.psum(sum_ctx_b.astype(jnp.bfloat16), "row").astype(jnp.float32),
        lax.psum(sum_out_w.astype(jnp.bfloat16), "row").astype(jnp.float32),
        lax.psum(sum_out_b.astype(jnp.bfloat16), "row").astype(jnp.float32),
    )
    return (
        results.reshape(image.shape),
        picture_grads.reshape(image.shape),
        sum_gain,
        sum_bias,
        sum_conv_one,
        sum_conv_two,
        sum_conv_bias,
        sum_emb_w,
        sum_emb_b,
        sum_qkv_w,
        sum_qv_bias,
        sum_ctx_w,
        sum_ctx_b,
        sum_out_w,
        sum_out_b,
    )


BF = jnp.bfloat16
F32 = jnp.float32
MESH_ID = pl.DeviceIdType.MESH
NN = (((1,), (0,)), ((), ()))
NT = (((1,), (1,)), ((), ()))
ANY = pl.BlockSpec(memory_space=pl.ANY)
VMEM = pl.BlockSpec(memory_space=pltpu.VMEM)
SMEM = pl.BlockSpec(memory_space=pltpu.SMEM)
PIX = 512
PAD = 640
CHUNKS = 8
VMEM_LIMIT = 60 * 2**20
DMA = pltpu.SemaphoreType.DMA


def mm(left, right, dims=NN):
    return lax.dot_general(left, right, dims, preferred_element_type=F32)


def mixed(chan, z):
    low = lax.rem(chan + lax.div(z, 2), 2)
    return low + 2 * lax.rem(lax.div(chan, 2) + lax.rem(z, 2), 2)


class Place:
    def __init__(self):
        self.r = lax.axis_index("row")
        self.c = lax.axis_index("chan")
        self.z = lax.div(self.r, 2)
        self.k = lax.rem(self.r, 2)
        self.d = 2 * self.c + self.k
        self.pair = mixed(self.c, self.z)
        self.band = 2 * self.pair + self.k

    def head_device(self, head):
        return (2 * self.z + lax.rem(head, 2), lax.div(head, 2))

    def band_device(self, band):
        return (2 * self.z + lax.rem(band, 2), mixed(lax.div(band, 2), self.z))


def send(src, dst, send_sem, recv_sem, device):
    copy = pltpu.make_async_remote_copy(
        src_ref=src,
        dst_ref=dst,
        send_sem=send_sem,
        recv_sem=recv_sem,
        device_id=device,
        device_id_type=MESH_ID,
    )
    copy.start()
    return copy


def local(src, dst, sem):
    copy = pltpu.make_async_copy(src, dst, sem)
    copy.start()
    return copy


def greet_plane(me, barrier):
    for step in range(1, 8):
        pl.semaphore_signal(
            barrier,
            inc=1,
            device_id=me.head_device(lax.rem(me.d + step, 8)),
            device_id_type=MESH_ID,
        )


def group_matrix(ref):
    rows = lax.broadcasted_iota(jnp.int32, (C, C), 0)
    cols = lax.broadcasted_iota(jnp.int32, (C, C), 1)
    ref[...] = jnp.where(lax.div(rows, 16) == lax.div(cols, 16), 1.0, 0.0).astype(BF)


def group_total(rows, groups_ref):
    top = rows.astype(BF)
    rest = rows - top.astype(F32)
    mid = rest.astype(BF)
    low = (rest - mid.astype(F32)).astype(BF)
    stacked = jnp.concatenate([top, mid, low, jnp.zeros_like(low)], axis=0)
    sums = mm(stacked, groups_ref[...])
    return sums[0:8] + sums[8:16] + sums[16:24]


def plane_exchange(me, slots, ssem, rsem):
    copies = []
    for step in range(1, 8):
        copies.append(
            send(
                slots.at[me.d],
                slots.at[me.d],
                ssem.at[step],
                rsem.at[step],
                me.head_device(lax.rem(me.d + step, 8)),
            )
        )
    return copies


def slots_total(slots):
    total = slots[0]
    for slot in range(1, 8):
        total = total + slots[slot]
    return total


def fold(value):
    return value.reshape(value.shape[0] // 8, 8, value.shape[1]).sum(axis=0)


def as_row(value):
    return jnp.sum(value, axis=0, keepdims=True)


def store_rows(slots, index, rows):
    filled = rows + [jnp.zeros((1, C), F32)] * (8 - len(rows))
    slots[index] = jnp.concatenate(filled, axis=0)


def chunk_of(i):
    return pl.ds(pl.multiple_of(i * 64, 64), 64)


def put_shifted(dst, start, value):
    col = lax.broadcasted_iota(jnp.int32, (64, C), 0)
    where = pl.ds(pl.multiple_of(start, 64), 64)
    dst[1, where, :] = value.astype(BF)
    dst[0, where, :] = jnp.where(col == 0, 0.0, pltpu.roll(value, 1, 0)).astype(BF)
    dst[2, where, :] = jnp.where(col == 63, 0.0, pltpu.roll(value, 63, 0)).astype(BF)


def halo_send(me, cat, halo, ssem, rsem):
    @pl.when(me.band > 0)
    def _():
        send(cat.at[1, pl.ds(64, 64), :], halo.at[1], ssem.at[0], rsem.at[1],
             me.band_device(me.band - 1))

    @pl.when(me.band < 7)
    def _():
        send(cat.at[1, pl.ds(512, 64), :], halo.at[0], ssem.at[1], rsem.at[0],
             me.band_device(me.band + 1))


def halo_wait(me, cat, halo, ssem, rsem):
    def pair(slot, ahead):
        return pltpu.make_async_remote_copy(
            src_ref=cat.at[1, pl.ds(64, 64), :], dst_ref=halo.at[slot],
            send_sem=ssem.at[slot], recv_sem=rsem.at[slot],
            device_id=me.band_device(ahead), device_id_type=MESH_ID)

    zero = jnp.zeros((64, C), F32)

    @pl.when(me.band > 0)
    def _():
        both = pair(0, me.band - 1)
        both.wait_send()
        both.wait_recv()
        put_shifted(cat, 0, halo[0].astype(F32))

    @pl.when(me.band == 0)
    def _():
        put_shifted(cat, 0, zero)

    @pl.when(me.band < 7)
    def _():
        both = pair(1, me.band + 1)
        both.wait_send()
        both.wait_recv()
        put_shifted(cat, 576, halo[1].astype(F32))

    @pl.when(me.band == 7)
    def _():
        put_shifted(cat, 576, zero)


def conv_taps(acc, cat, weight, order, flip, dims):
    @pl.loop(0, 3 * len(order))
    def _(i):
        step = lax.div(i, 3)
        col = lax.rem(i, 3)
        row = order[0] if len(order) == 1 else order[0] + step * (order[1] - order[0])
        tap = (2 - row) * 3 + (2 - col) if flip else row * 3 + col
        start = pl.multiple_of(row * 64, 64)
        acc[...] += mm(cat[col, pl.ds(start, PIX), :], weight[tap], dims)


HALF_ROWS = 34 * 64
SPREAD = (1, 2, 3, 0)


def half_place(me):
    return lax.div(me.pair, 2), lax.rem(me.band, 4)


def spread_rows(me, src_of, dst, place_rows, ssem, rsem, steps):
    core, place = half_place(me)
    for step in steps:
        chan = lax.rem(me.c + step, 4)
        args = (src_of(chan), dst.at[place_rows(place), :])
        if step == 0:

            @pl.when(core == me.k)
            def _():
                local(*args, rsem.at[place])

            @pl.when(core != me.k)
            def _():
                send(*args, ssem.at[step], rsem.at[place], (2 * me.z + core, chan))

        else:
            send(*args, ssem.at[step], rsem.at[place], (2 * me.z + core, chan))


def spread_sent(me, src_of, dst, place_rows, ssem, rsem):
    core, place = half_place(me)
    for step in range(4):
        chan = lax.rem(me.c + step, 4)

        def done():
            pltpu.make_async_remote_copy(
                src_ref=src_of(chan), dst_ref=dst.at[place_rows(place), :],
                send_sem=ssem.at[step], recv_sem=rsem.at[place],
                device_id=(2 * me.z + core, chan), device_id_type=MESH_ID).wait_send()

        if step == 0:
            pl.when(core != me.k)(done)
        else:
            done()


def spread_received(src_of, dst, place_rows, rsem):
    for place in range(4):
        pltpu.make_async_copy(src_of(0), dst.at[place_rows(place), :], rsem.at[place]).wait()


def act_rows(place):
    return pl.ds(pl.multiple_of(64 + place * PIX, 64), PIX)


def grad_rows(place):
    return pl.ds(place * PIX, PIX)


def spread_edges(me, act, dst, ssem, rsem, finish=False):
    for band, core, start, to in ((3, 1, 512, 0), (4, 0, 64, HALF_ROWS - 64)):

        @pl.when(me.band == band)
        def _():
            piece, there = act.at[pl.ds(start, 64), :], dst.at[pl.ds(to, 64), :]
            for step in range(4):
                chan = lax.rem(me.c + step, 4)
                if step == 0:
                    if not finish:
                        local(piece, there, rsem.at[0])
                else:
                    copy = pltpu.make_async_remote_copy(
                        src_ref=piece, dst_ref=there, send_sem=ssem.at[step], recv_sem=rsem.at[0],
                        device_id=(2 * me.z + core, chan), device_id_type=MESH_ID)
                    if finish:
                        copy.wait_send()
                    else:
                        copy.start()

    if finish:
        pltpu.make_async_copy(act.at[pl.ds(0, 64), :], dst.at[pl.ds(0, 64), :], rsem.at[0]).wait()
    else:
        empty = jnp.zeros((64, C), BF)

        @pl.when(me.k == 0)
        def _():
            dst[0:64, :] = empty

        @pl.when(me.k == 1)
        def _():
            dst[HALF_ROWS - 64 :, :] = empty


LOG2E = 1.4426950408889634
VROWS = 80
SUB = 256
KEYS = 512


def image_targets(me):
    return [(n, (2 * n + me.k, mixed(me.z, jnp.int32(n)))) for n in range(4)]


class Gather:
    def __init__(self, me, index, src, dst, sems):
        self.me, self.src, self.dst = me, src, dst
        third = src.shape[0] // 3
        odd = lax.rem(me.z, 2)
        self.plane_taps = pl.ds(third * odd, 2 * third)
        self.give_taps = pl.ds(2 * third * odd, third)
        self.take_taps = pl.ds(2 * third * (1 - odd), third)
        self.x = me.c + 1 - 2 * lax.rem(me.c, 2)
        self.y = lax.rem(me.c + 2, 4)
        self.far = lax.rem(self.x + 2, 4)
        self.core = (me.r + 1 - 2 * me.k, me.c)
        self.over = (2 * (me.z + 1 - 2 * odd) + me.k, me.c)
        (self.own, self.first_s, self.first_r, self.relay_s, self.relay_r, self.give_s,
         self.give_r, self.core_s, self.core_r) = [sem.at[index] for sem in sems]
        self.started = []
        self.core_plane = []
        self.core_take = []
        self.gives = []

    def rows(self, chan, start=0, size=64):
        return pl.ds(pl.multiple_of(chan * 128 + self.me.k * 64 + start, size), size)

    def move(self, taps, rows, s, r, device):
        piece = self.dst.at[taps, rows, :]
        return send(piece, piece, s, r, device)

    def start(self):
        me = self.me
        half = pl.ds(pl.multiple_of(me.k * 64, 64), 64)
        quarter = pl.ds(pl.multiple_of(me.c * 128, 128), 128)
        for j, chan in enumerate((self.x, self.y)):
            self.started.append(
                send(self.src.at[self.plane_taps, half, :],
                     self.dst.at[self.plane_taps, self.rows(me.c), :],
                     self.first_s.at[j], self.first_r.at[j], (me.r, chan)))
        self.kept = local(self.src, self.dst.at[:, quarter, :], self.own.at[0])

    def spread(self, slot, chan):
        self.core_plane.append(
            self.move(self.plane_taps, self.rows(chan), self.core_s.at[slot], self.core_r.at[slot],
                      self.core))
        self.gives.append(
            self.move(self.give_taps, self.rows(chan), self.give_s.at[slot], self.give_r.at[slot],
                      self.over))

    def relay(self):
        self.relays = []
        for j, (chan, onward) in enumerate(((self.x, self.y), (self.y, self.x))):
            self.started[j].wait_recv()
            self.relays.append(
                self.move(self.plane_taps, self.rows(chan, 32 * j, 32), self.relay_s.at[j],
                          self.relay_r.at[j], (self.me.r, onward)))
            self.spread(j, chan)

    def relayed(self):
        for copy in self.relays:
            copy.wait_recv()
        self.spread(2, self.far)

    def plane_done(self):
        self.kept.wait()
        for copy in self.core_plane:
            copy.wait_recv()

    def take(self):
        for slot, chan in enumerate((self.x, self.y, self.far)):
            self.gives[slot].wait_recv()
            self.core_take.append(
                self.move(self.take_taps, self.rows(chan), self.core_s.at[3 + slot],
                          self.core_r.at[3 + slot], self.core))

    def take_done(self):
        for copy in self.core_take:
            copy.wait_recv()

    def drain(self):
        for copy in self.started + self.relays + self.gives + self.core_plane + self.core_take:
            copy.wait_send()


def front_kernel(
    img, tgt, steps, loss, embed, words, norm_gain, norm_bias, conv_bias, qv_bias, out_b,
    emb_w, emb_b, ctx_w, ctx_b, w1, w2, wq, wo,
    x_o, t_o, vec_o, st_o, a1_o, hid_o, a2_o, res_o, nrm_o, w1_o, w2_o, wq_o, wo_o, qkv_o,
    attn_o, p_o, ctx_o, pc_o, o_o, linv_o, feat, tokens,
    x_v, t_v, vec_v, st_v, a1_v, hid_v, a2_v, res_v, nrm_v, w1_v, w2_v, wq_v, wo_v, qkv_v,
    attn_v,
    msg, groups, slots, halo, vsrc, wide, cond, keys, ckeys, qs, vext, cvext, sbuf, mbuf, cbuf, pb, ob,
    vs, vr, ims, imr, tgs, tgr, own_sem, first_s, first_r, relay_s, relay_r, give_s, give_r,
    core_s, core_r, wos, wor, wofs, wofr, wol, sts, str_, hs, hr, qs_s, qs_r, lsem, osem, psem,
    as_, ar,
):
    me = Place()
    barrier = pltpu.get_barrier_semaphore()
    greet_plane(me, barrier)
    own_block = me.pair == me.z
    for chan in range(4):
        itself = jnp.logical_and(me.pair == me.z, me.c == chan)

        @pl.when(jnp.logical_not(itself))
        def _():
            pl.semaphore_signal(
                barrier, inc=1, device_id=(2 * me.pair + me.k, chan), device_id_type=MESH_ID
            )

    odd = lax.rem(me.z, 2)
    pl.semaphore_signal(
        barrier, inc=1, device_id=(2 * (me.z + 1 - 2 * odd) + me.k, me.c), device_id_type=MESH_ID
    )
    wide[...] = jnp.zeros((16, EMB), F32)
    wide[0:4, :] = embed[...].astype(F32)
    row = lax.broadcasted_iota(jnp.int32, (16, EMB // 2), 0)
    column = lax.broadcasted_iota(jnp.int32, (16, EMB // 2), 1).astype(F32)
    frequency = jnp.exp(-math.log(10000.0) * column / (EMB // 2))
    angle = jnp.zeros((16, EMB // 2), F32)
    for n in range(4):
        angle = jnp.where(row == n, steps[n].astype(F32) * frequency, angle)
    for start, wave in ((0, jnp.cos), (EMB // 2, jnp.sin)):
        value = wave(angle) + wide[:, start : start + EMB // 2]
        feat[:, start : start + EMB // 2] = jnp.where(row < 4, swish(value), 0.0).astype(BF)
    for n in range(4):
        wide[4 * n : 4 * n + 4, :] = words[n].astype(F32)
    tokens[...] = wide[...].astype(BF)
    for j in range(2):
        cond[j] = mm(feat[...], emb_w[j], NT) + emb_b[j : j + 1, :]
    vsrc[0:3, :] = norm_gain[...]
    vsrc[3:6, :] = norm_bias[...]
    vsrc[6:8, :] = conv_bias[...]
    vsrc[8:10, :] = qv_bias[...]
    vsrc[10:11, :] = out_b[...]
    vsrc[11:12, :] = cond[0, pl.ds(me.z, 1), :]
    vsrc[12:13, :] = cond[1, pl.ds(me.z, 1), :]
    vsrc[13:14, :] = jnp.full((1, 128), loss[me.z], F32)
    vsrc[14:16, :] = jnp.zeros((2, 128), F32)
    lane = lax.broadcasted_iota(jnp.int32, (16, 128), 1)
    for j in range(2):
        value = mm(tokens[...], ctx_w[j], NT) + ctx_b[j : j + 1, :]
        turned = pltpu.roll(value, HEAD, 1)
        first = lax.div(lane, HEAD) == me.k
        both = jnp.where(first, value, turned)
        ctx_o[j] = both.astype(BF)
        if j == 0:
            ckeys[...] = both.astype(BF)
        else:
            tall = jnp.concatenate([both, jnp.zeros((112, 128), F32)], axis=0)
            cvext[0:HEAD, :] = jnp.transpose(tall)[0:HEAD].astype(BF)
    row = lax.broadcasted_iota(jnp.int32, (16, H * W), 0)
    vext[HEAD:, :] = jnp.where(row == 0, 1.0, 0.0).astype(BF)
    cvext[HEAD:, :] = jnp.where(row[:, 0:128] == 0, 1.0, 0.0).astype(BF)
    pl.semaphore_wait(barrier, 8 + 4 - jnp.where(own_block, 1, 0))
    own_cols = pl.ds(pl.multiple_of(me.c * 128, 128), 128)

    vec_v[:, own_cols] = vsrc[...]
    vec_copies = [
        send(vsrc, vec_v.at[:, own_cols], vs.at[t], vr.at[t], (me.r, lax.rem(me.c + t, 4)))
        for t in range(1, 4)
    ]

    def image_send(src, dst, ssem, rsem):
        for n, device in image_targets(me):
            itself = jnp.logical_and(own_block, me.z == n)

            @pl.when(jnp.logical_not(itself))
            def _():
                send(src.at[n], dst.at[:, own_cols], ssem.at[n], rsem.at[me.c], device)

            @pl.when(itself)
            def _():
                local(src.at[n], dst.at[:, own_cols], rsem.at[me.c])

    def image_wait(src, dst, ssem, rsem):
        for chan in range(4):
            pltpu.make_async_copy(
                src.at[0], dst.at[:, pl.ds(chan * 128, 128)], rsem.at[chan]
            ).wait()

    def image_drain(src, dst, ssem, rsem):
        for n, device in image_targets(me):
            itself = jnp.logical_and(own_block, me.z == n)

            @pl.when(jnp.logical_not(itself))
            def _():
                pltpu.make_async_remote_copy(
                    src_ref=src.at[n], dst_ref=dst.at[:, own_cols], send_sem=ssem.at[n],
                    recv_sem=rsem.at[me.c], device_id=device, device_id_type=MESH_ID,
                ).wait_send()

    gather_sems = (own_sem, first_s, first_r, relay_s, relay_r, give_s, give_r, core_s, core_r)
    gather1 = Gather(me, 0, w1, w1_v, gather_sems)
    gather2 = Gather(me, 1, w2, w2_v, gather_sems)
    gather3 = Gather(me, 2, wq, wq_v, gather_sems)

    image_send(img, x_v, ims, imr)
    gather1.start()
    group_matrix(groups)
    col_zero = jnp.zeros((8, C), F32)
    for copy in vec_copies:
        copy.wait()
    outs = []

    def save(index, src, dst):
        outs.append(local(src, dst, osem.at[index]))

    def statistics(number, ref):
        def add(i, carry):
            value = ref[chunk_of(i), :].astype(F32)
            return (carry[0] + fold(value), carry[1] + fold(value * value))

        first, square = lax.fori_loop(0, CHUNKS, add, (col_zero, col_zero))
        store_rows(slots.at[number], me.d, [as_row(first), as_row(square)])
        return plane_exchange(me, slots.at[number], sts.at[number], str_.at[number])

    def finish_statistics(number, copies):
        for copy in copies:
            copy.wait()
        means = group_total(slots_total(slots.at[number]), groups) * (1.0 / (H * W * 16))
        center = means[0:1]
        inverse = lax.rsqrt(means[1:2] - center * center + EPSILON)
        st_v[2 * number : 2 * number + 1, :] = center
        st_v[2 * number + 1 : 2 * number + 2, :] = inverse
        return center, inverse

    image_wait(img, x_v, ims, imr)
    copies = statistics(0, x_v)
    save(0, x_v, x_o)
    save(2, vec_v, vec_o)
    gather1.relay()
    center, inverse = finish_statistics(0, copies)
    gain, bias = vec_v[0:1, :], vec_v[3:4, :]

    @pl.loop(0, CHUNKS)
    def _(i):
        value = (x_v[chunk_of(i), :].astype(F32) - center) * inverse
        put_shifted(a1_v, 64 + i * 64, swish(value * gain + bias))

    halo_send(me, a1_v, halo.at[0], hs.at[0], hr.at[0])
    gather1.relayed()
    gather2.start()
    hid_v[...] = jnp.broadcast_to(vec_v[6:7, :], (PIX, C))
    gather1.plane_done()
    conv_taps(hid_v, a1_v, w1_v, (1,), False, NT)
    halo_wait(me, a1_v, halo.at[0], hs.at[0], hr.at[0])
    save(4, a1_v, a1_o)
    gather1.take()
    conv_taps(hid_v, a1_v, w1_v, (2 * odd,), False, NT)
    gather1.take_done()
    conv_taps(hid_v, a1_v, w1_v, (2 - 2 * odd,), False, NT)
    copies = statistics(1, hid_v)
    save(9, w1_v, w1_o)
    save(5, hid_v, hid_o)
    gather2.relay()
    center, inverse = finish_statistics(1, copies)
    gain, bias = vec_v[1:2, :], vec_v[4:5, :]
    scale, shift = 1.0 + vec_v[11:12, :], vec_v[12:13, :]

    @pl.loop(0, CHUNKS)
    def _(i):
        value = (hid_v[chunk_of(i), :] - center) * inverse
        put_shifted(a2_v, 64 + i * 64, swish((value * gain + bias) * scale + shift))

    halo_send(me, a2_v, halo.at[1], hs.at[1], hr.at[1])
    gather2.relayed()
    gather3.start()
    res_v[...] = x_v[...].astype(F32) + vec_v[7:8, :]
    gather2.plane_done()
    conv_taps(res_v, a2_v, w2_v, (1,), False, NT)
    halo_wait(me, a2_v, halo.at[1], hs.at[1], hr.at[1])
    save(6, a2_v.at[1], a2_o)
    gather2.take()
    gather3.relay()
    conv_taps(res_v, a2_v, w2_v, (2 * odd,), False, NT)
    gather2.take_done()
    gather3.relayed()
    conv_taps(res_v, a2_v, w2_v, (2 - 2 * odd,), False, NT)
    copies = statistics(2, res_v)
    save(10, w2_v, w2_o)
    save(7, res_v, res_o)
    gather3.take()
    center, inverse = finish_statistics(2, copies)
    gain, bias = vec_v[2:3, :], vec_v[5:6, :]
    normed = (res_v[...] - center) * inverse * gain + bias
    nrm_v[...] = normed.astype(BF)
    st_v[6:8, :] = jnp.zeros((2, C), F32)
    save(8, nrm_v, nrm_o)
    save(3, st_v, st_o)
    turned = jnp.transpose(normed).astype(BF)
    gather3.plane_done()
    gather3.take_done()
    save(11, wq_v, wq_o)
    band_cols = pl.ds(pl.multiple_of(me.band * PIX, PIX), PIX)

    def head_rows(head):
        return pl.ds(pl.multiple_of(head * HEAD, HEAD), HEAD)

    owns = []
    qkv_copies = {}
    for j, bias_row in ((1, None), (2, 9), (0, 8)):
        value = mm(wq_v[j], turned)
        if bias_row is not None:
            tall = jnp.transpose(jnp.broadcast_to(vec_v[bias_row : bias_row + 1, :], (128, C)))
            value = value + jnp.concatenate([tall] * 4, axis=1)
        msg[j] = value.astype(BF)
        owns.append(local(msg.at[j, head_rows(me.d), :], qkv_v.at[j, :, band_cols], lsem.at[j]))
        qkv_copies[j] = []
        for step in range(1, 8):
            head = lax.rem(me.d + step, 8)
            qkv_copies[j].append(
                send(msg.at[j, head_rows(head), :], qkv_v.at[j, :, band_cols], qs_s.at[j, step],
                     qs_r.at[j, step], me.head_device(head)))

    for own in owns:
        own.wait()
    for copy in qkv_copies[1]:
        copy.wait()
    both = jnp.concatenate([qkv_v[1], qkv_v[1]], axis=0).astype(F32)
    keys[...] = jnp.transpose(both).astype(BF)

    def scale_queries(where):
        scaled = qkv_v[0, :, where].astype(F32) * (HEAD ** (-0.5) * LOG2E)
        top = scaled.astype(BF)
        qs[0:HEAD, where] = top
        qs[HEAD:, where] = (scaled - top.astype(F32)).astype(BF)

    scale_queries(band_cols)
    token = lax.broadcasted_iota(jnp.int32, (16, SUB), 0)
    valid = lax.div(token, CTX) == me.z
    chunks = H * W // KEYS

    def begin(slot, block):
        query = qs[:, pl.ds(pl.multiple_of(block * SUB, SUB), SUB)]
        score = jnp.where(valid, mm(ckeys[...], query), -1e30)
        cbuf[slot] = score
        return query, jnp.maximum(score[0:8], score[8:16])

    def score_chunk(slot, query, highest, chunk):
        value = mm(keys[chunk * KEYS : (chunk + 1) * KEYS, :], query)
        sbuf[slot, chunk * KEYS : (chunk + 1) * KEYS, :] = value
        return jnp.maximum(highest, jnp.max(value.reshape(KEYS // 8, 8, SUB), axis=0))

    query, highest = begin(0, 2 * me.band)
    for chunk in range(chunks):
        highest = score_chunk(0, query, highest, chunk)
    mbuf[0] = highest
    for copy in qkv_copies[2]:
        copy.wait()
    vext[0:HEAD, :] = qkv_v[2]
    for copy in qkv_copies[0]:
        copy.wait()
    scale_queries(pl.ds(0, H * W))
    save(13, qkv_v, qkv_o)
    image_send(tgt, t_v, tgs, tgr)
    half = pl.ds(pl.multiple_of(me.c * 128 + me.k * 64, 64), 64)
    my_half = pl.ds(pl.multiple_of(me.k * 64, 64), 64)
    wo_own = local(wo, wo_v.at[:, own_cols, :], wol.at[0])
    wo_copies = [
        send(wo.at[:, my_half, :], wo_v.at[:, half, :], wos.at[t], wor.at[t],
             (me.r, lax.rem(me.c + t, 4)))
        for t in range(1, 4)
    ]
    attn_rows = head_rows(me.d)

    def p_copy(block, slot):
        return pltpu.make_async_copy(
            pb.at[slot], p_o.at[:, pl.ds(pl.multiple_of(block * PIX, PIX), PIX)], psem.at[slot])

    @pl.loop(0, 8)
    def _(turn):
        block = lax.rem(me.band + turn, 8)
        slot = lax.rem(turn, 2)

        @pl.when(turn >= 2)
        def _():
            p_copy(block, slot).wait()

        for sub in range(2):
            cols = pl.ds(sub * SUB, SUB)
            place = pl.ds(pl.multiple_of(block * PIX + sub * SUB, SUB), SUB)
            following = lax.rem(2 * block + sub + 1, H * W // SUB)
            top = jnp.max(mbuf[sub], axis=0, keepdims=True)
            pc = jnp.exp2(cbuf[sub] - top).astype(BF)
            pc_o[:, place] = pc
            out = mm(cvext[:, 0:16], pc)
            query, highest = begin(1 - sub, following)
            for chunk in range(chunks):
                highest = score_chunk(1 - sub, query, highest, chunk)
                rows = slice(chunk * KEYS, (chunk + 1) * KEYS)
                probs = jnp.exp2(sbuf[sub, rows, :] - top).astype(BF)
                pb[slot, rows, cols] = probs
                out = out + mm(vext[:, rows], probs)
            mbuf[1 - sub] = highest
            linv = 1.0 / out[HEAD : HEAD + 1]
            out = out[0:HEAD] * linv
            o_o[:, place] = out
            ob[block, :, cols] = out.astype(BF)
            linv_o[:, place] = jnp.broadcast_to(linv, (8, SUB))
        p_copy(block, slot).start()

        @pl.when(block != me.band)
        def _():
            send(ob.at[block], attn_v.at[attn_rows, :], as_.at[block], ar.at[me.d],
                 me.band_device(block))

        @pl.when(block == me.band)
        def _():
            local(ob.at[block], attn_v.at[attn_rows, :], ar.at[me.d])

    wo_forward = []
    for t in range(1, 4):
        wo_copies[t - 1].wait()
        origin = lax.rem(me.c - t + 4, 4)
        rows = pl.ds(pl.multiple_of(origin * 128 + me.k * 64, 64), 64)
        wo_forward.append(
            send(wo_v.at[:, rows, :], wo_v.at[:, rows, :], wofs.at[t], wofr.at[t],
                 (me.r + 1 - 2 * me.k, me.c)))
    image_wait(tgt, t_v, tgs, tgr)
    save(1, t_v, t_o)
    for gather in (gather1, gather2, gather3):
        gather.drain()
    image_drain(img, x_v, ims, imr)
    image_drain(tgt, t_v, tgs, tgr)
    wo_own.wait()
    for copy in wo_forward:
        copy.wait()
    save(12, wo_v, wo_o)
    for block in range(8):

        @pl.when(block != me.band)
        def _():
            pltpu.make_async_remote_copy(
                src_ref=ob.at[block], dst_ref=attn_v.at[attn_rows, :], send_sem=as_.at[block],
                recv_sem=ar.at[me.d], device_id=me.band_device(block), device_id_type=MESH_ID,
            ).wait_send()

        pltpu.make_async_copy(
            ob.at[0], attn_v.at[pl.ds(block * HEAD, HEAD), :], ar.at[block]).wait()
    save(14, attn_v, attn_o)
    p_copy(0, 0).wait()
    p_copy(0, 1).wait()
    for copy in outs:
        copy.wait()


def front(*args):
    pixels = H * W
    saved = [
        ((PIX, C), BF), ((PIX, C), BF), ((16, C), F32), ((8, C), F32), ((3, PAD, C), BF),
        ((PIX, C), F32), ((3, PAD, C), BF), ((PIX, C), F32), ((PIX, C), BF), ((9, C, C), BF),
        ((9, C, C), BF), ((3, C, C), BF), ((1, C, C), BF), ((3, HEAD, pixels), BF), ((C, PIX), BF),
    ]
    more = [
        ((pixels, pixels), BF), ((2, 16, 128), BF), ((16, pixels), BF), ((HEAD, pixels), F32),
        ((8, pixels), F32), ((16, EMB), BF), ((16, CTXW), BF),
    ]
    return pl.pallas_call(
        front_kernel,
        name="front",
        out_shape=[
            jax.ShapeDtypeStruct(shape[1:] if j == 6 else shape, kind)
            for j, (shape, kind) in enumerate(saved + more)],
        in_specs=[ANY, ANY] + [SMEM] * 2 + [VMEM] * 11 + [ANY] * 4,
        out_specs=[ANY] * (len(saved) + 1) + [VMEM] * 6,
        scratch_shapes=[pltpu.VMEM(*one) for one in saved]
        + [
            pltpu.VMEM((3, C, C), BF), pltpu.VMEM((C, C), BF), pltpu.VMEM((3, 8, 8, C), F32),
            pltpu.VMEM((2, 2, 64, C), BF), pltpu.VMEM((16, 128), F32),
            pltpu.VMEM((16, EMB), F32),
            pltpu.VMEM((2, 16, 128), F32), pltpu.VMEM((pixels, 128), BF),
            pltpu.VMEM((16, 128), BF), pltpu.VMEM((128, pixels), BF),
            pltpu.VMEM((VROWS, pixels), BF), pltpu.VMEM((VROWS, 128), BF),
            pltpu.VMEM((2, pixels, SUB), F32), pltpu.VMEM((2, 8, SUB), F32),
            pltpu.VMEM((2, 16, SUB), F32), pltpu.VMEM((2, pixels, PIX), BF),
            pltpu.VMEM((8, HEAD, PIX), BF),
            DMA((4,)), DMA((4,)), DMA((4,)), DMA((4,)), DMA((4,)), DMA((4,)),
            DMA((3, 1)), DMA((3, 2)), DMA((3, 2)), DMA((3, 2)), DMA((3, 2)), DMA((3, 3)),
            DMA((3, 3)), DMA((3, 6)), DMA((3, 6)), DMA((4,)), DMA((4,)), DMA((4,)), DMA((4,)),
            DMA((1,)), DMA((3, 8)), DMA((3, 8)), DMA((2, 2)), DMA((2, 2)), DMA((3, 8)),
            DMA((3, 8)), DMA((3,)), DMA((15,)), DMA((2,)), DMA((8,)), DMA((8,)),
        ],
        compiler_params=pltpu.CompilerParams(
            collective_id=1, has_side_effects=True, vmem_limit_bytes=VMEM_LIMIT
        ),
    )(*args)


def band_back_send(me, src, dst, ssem, rsem):
    for chan in range(4):
        cols = pl.ds(chan * 128, 128)
        itself = jnp.logical_and(me.band == me.r, me.c == chan)

        @pl.when(jnp.logical_not(itself))
        def _():
            send(src.at[:, cols], dst.at[me.z], ssem.at[chan], rsem.at[me.z], (me.band, chan))

        @pl.when(itself)
        def _():
            local(src.at[:, cols], dst.at[me.z], rsem.at[me.z])


def band_back_wait(me, src, dst, ssem, rsem):
    for n in range(4):
        pltpu.make_async_copy(src.at[:, pl.ds(0, 128)], dst.at[n], rsem.at[n]).wait()
    for chan in range(4):
        itself = jnp.logical_and(me.band == me.r, me.c == chan)

        @pl.when(jnp.logical_not(itself))
        def _():
            pltpu.make_async_remote_copy(
                src_ref=src.at[:, pl.ds(chan * 128, 128)], dst_ref=dst.at[me.z],
                send_sem=ssem.at[chan], recv_sem=rsem.at[me.z], device_id=(me.band, chan),
                device_id_type=MESH_ID,
            ).wait_send()


def greet_back(me, barrier):
    own_block = me.pair == me.z
    for n in range(4):
        itself = jnp.logical_and(own_block, me.z == n)

        @pl.when(jnp.logical_not(itself))
        def _():
            pl.semaphore_signal(
                barrier, inc=1, device_id=(2 * n + me.k, mixed(me.z, jnp.int32(n))),
                device_id_type=MESH_ID,
            )

    return 4 - jnp.where(own_block, 1, 0)


def middle_kernel(
    attn, res, tgt, wo, vec, qkv, ctx, p, pc, o, linv, a2,
    out_o, cot_o, gwo_o, gob_o, dt_o, ctot_o, act_o,
    attn_v, res_v, tgt_v, wo_v, out_b, back, cot_v, dat, dot_v, qkv_v, o_v,
    vext, cvext, dos, dor, qrow, dq, pb, dkv, dqb, dt_v, dctx, cslots, act_v,
    bs, br, ds_, dr, cs, cr, ks, kr, q_s, q_r, lsem, osem, psem, acts, actr, es, er,
):
    me = Place()
    scaling = HEAD ** (-0.5)
    barrier = pltpu.get_barrier_semaphore()
    greet_plane(me, barrier)
    others = greet_back(me, barrier)
    for step in range(1, 8):
        pl.semaphore_signal(
            barrier, inc=1, device_id=(lax.rem(me.r + step, 8), me.c), device_id_type=MESH_ID
        )
    loads = [local(a, b, lsem.at[j]) for j, (a, b) in enumerate(
        ((attn, attn_v), (wo.at[0], wo_v), (res, res_v), (tgt, tgt_v), (qkv, qkv_v), (o, o_v)))]

    def p_copy(block, slot):
        return pltpu.make_async_copy(
            p.at[pl.ds(pl.multiple_of(block * PIX, PIX), PIX), :], pb.at[slot], psem.at[slot])

    p_copy(me.band, 0).start()

    def band_cols(band):
        return pl.ds(pl.multiple_of(band * PIX, PIX), PIX)

    def head_rows(head):
        return pl.ds(pl.multiple_of(head * HEAD, HEAD), HEAD)

    for load in loads[0:4]:
        load.wait()
    rows = jnp.transpose(attn_v[...].astype(F32)).astype(BF)
    result = res_v[...] + mm(rows, wo_v[...], NT) + vec[10:11, :]
    out_b[...] = result.astype(BF)
    cot = vec[13:14, :] * (result - tgt_v[...].astype(F32))
    cot_v[...] = cot
    low = cot.astype(BF)
    dat[...] = jnp.transpose(mm(low, wo_v[...])).astype(BF)
    pl.semaphore_wait(barrier, 14 + others)
    own = local(dat.at[head_rows(me.d), :], dot_v.at[:, band_cols(me.band)], lsem.at[6])
    copies = []
    for step in range(1, 8):
        head = lax.rem(me.d + step, 8)
        copies.append(
            send(dat.at[head_rows(head), :], dot_v.at[:, band_cols(me.band)], ds_.at[step],
                 dr.at[step], me.head_device(head)))
    piece = a2.at[pl.ds(64, PIX), :]
    x = me.c + 1 - 2 * lax.rem(me.c, 2)
    y = lax.rem(me.c + 2, 4)
    far = lax.rem(x + 2, 4)
    half, place = half_place(me)
    owner = half == me.k
    direct = [
        send(piece, act_v.at[act_rows(place), :], acts.at[j], actr.at[place],
             (2 * me.z + half, chan))
        for j, chan in enumerate((x, y))
    ]
    core_copy = pltpu.make_async_remote_copy(
        src_ref=piece, dst_ref=act_v.at[act_rows(place), :], send_sem=acts.at[2],
        recv_sem=actr.at[place], device_id=(2 * me.z + half, me.c), device_id_type=MESH_ID)
    pl.when(owner)(lambda: local(piece, act_v.at[act_rows(place), :], actr.at[place]) and None)
    pl.when(jnp.logical_not(owner))(lambda: core_copy.start())

    def places_of(chan):
        first = lax.rem(2 * mixed(chan, me.z), 4)
        return first, first + 1

    def act_wait(where):
        pltpu.make_async_copy(piece, act_v.at[act_rows(where), :], actr.at[where]).wait()

    def part_copy(slot, where, part, chan):
        rows = act_v.at[pl.ds(pl.multiple_of(64 + where * PIX + part * 256, 64), 256), :]
        return pltpu.make_async_remote_copy(
            src_ref=rows, dst_ref=rows, send_sem=acts.at[3 + slot],
            recv_sem=actr.at[4 + 4 * part + where], device_id=(2 * me.z + me.k, chan),
            device_id_type=MESH_ID)

    given = places_of(jnp.where(owner, x, y))
    given_part = jnp.where(owner, 0, 1)
    given_chan = jnp.where(owner, y, x)
    spread_edges(me, a2, act_v, es, er)
    saves = [local(cot_v, cot_o, osem.at[0])]
    lowf = low.astype(F32)
    gwo_o[...] = mm(jnp.transpose(lowf).astype(BF), rows).astype(BF)
    gob_o[...] = jnp.broadcast_to(as_row(lowf), (8, C))
    for load in loads[4:]:
        load.wait()
    row = lax.broadcasted_iota(jnp.int32, (HEAD, H * W), 0)
    ones = jnp.where(row < 3, 1.0, 0.0)
    vext[...] = jnp.transpose(jnp.concatenate([qkv_v[2].astype(F32), ones], axis=0)).astype(BF)
    lane = lax.broadcasted_iota(jnp.int32, (16, 128), 1)
    cvext[...] = jnp.where(
        lane < HEAD, ctx[1].astype(F32), jnp.where(lane < HEAD + 3, 1.0, 0.0)).astype(BF)
    queries = qkv_v[0].astype(F32) * scaling
    qrow[...] = jnp.transpose(
        jnp.concatenate([queries, jnp.zeros_like(queries)], axis=0)).astype(BF)
    own.wait()
    for copy in copies:
        copy.wait()
    band_back_send(me, out_b, back, bs, br)
    grad = (dot_v[...].astype(F32) * linv[0:1, :]).astype(BF)
    gradf = grad.astype(F32)
    delta = -jnp.sum(gradf * o_v[...], axis=0, keepdims=True)
    top = delta.astype(BF).astype(F32)
    mid = (delta - top).astype(BF).astype(F32)
    last = delta - top - mid
    dos[0:HEAD, :] = grad
    dos[HEAD:, :] = jnp.where(
        row == 0, top, jnp.where(row == 1, mid, jnp.where(row == 2, last, 0.0))).astype(BF)
    dor[...] = jnp.transpose(jnp.concatenate([gradf, jnp.zeros_like(gradf)], axis=0)).astype(BF)

    def score_grads(values, probs):
        return (probs.astype(F32) * mm(values, dos[...])).astype(BF)

    dsc = score_grads(cvext[...], pc[...])
    for j, (left, right) in enumerate(((dsc, qrow), (pc[...], dor))):
        value = mm(left, right[...])
        dctx[j] = jnp.where(me.k == 0, value, pltpu.roll(value, HEAD, 1))
    cslots[me.r] = dctx[...]
    ctx_copies = [
        send(cslots.at[me.r], cslots.at[me.r], cs.at[step], cr.at[step],
             (lax.rem(me.r + step, 8), me.c))
        for step in range(1, 8)
    ]
    wide = jnp.concatenate([ctx[0].astype(F32), jnp.zeros((112, 128), F32)], axis=0)
    dq[...] = mm(jnp.transpose(wide)[0:HEAD, 0:16].astype(BF), dsc)
    mine = head_rows(me.d)

    @pl.loop(0, 8)
    def _(turn):
        block = lax.rem(me.band + turn, 8)
        slot = lax.rem(turn, 2)

        @pl.when(turn < 7)
        def _():
            p_copy(lax.rem(block + 1, 8), 1 - slot).start()

        p_copy(block, slot).wait()

        @pl.when(turn == 3)
        def _():
            for j, where in enumerate(given):
                act_wait(where)
                part_copy(j, where, given_part, given_chan).start()

        grads = []
        for sub in range(2):
            part = pl.ds(pl.multiple_of(block * PIX + sub * SUB, SUB), SUB)
            probs = pb[slot, sub * SUB : (sub + 1) * SUB, :]
            grads.append(score_grads(vext[part, :], probs))
            dkv[block, 1, :, sub * SUB : (sub + 1) * SUB] = jnp.transpose(
                mm(probs, dor[...]))[0:HEAD].astype(BF)
        for sub in range(2):
            part = pl.ds(pl.multiple_of(block * PIX + sub * SUB, SUB), SUB)
            dkv[block, 0, :, sub * SUB : (sub + 1) * SUB] = jnp.transpose(
                mm(grads[sub], qrow[...]))[0:HEAD].astype(BF)
            dq[...] += mm(qkv_v[1, :, part], grads[sub])

        @pl.when(block != me.band)
        def _():
            send(dkv.at[block], dt_v.at[1:3, mine, :], ks.at[block], kr.at[me.d],
                 me.band_device(block))

        @pl.when(block == me.band)
        def _():
            local(dkv.at[block], dt_v.at[1:3, mine, :], kr.at[me.d])

    dqb[...] = (dq[...] * scaling).astype(BF)
    own = local(dqb.at[:, band_cols(me.band)], dt_v.at[0, mine, :], q_r.at[me.d])
    copies = []
    for step in range(1, 8):
        band = lax.rem(me.band + step, 8)
        copies.append(
            send(dqb.at[:, band_cols(band)], dt_v.at[0, mine, :], q_s.at[step], q_r.at[me.d],
                 me.band_device(band)))
    for copy in ctx_copies:
        copy.wait()
    for j in range(2):
        total = cslots[0, j]
        for slot in range(1, 8):
            total = total + cslots[slot, j]
        ctot_o[j] = total
    band_back_wait(me, out_b, back, bs, br)
    saves.append(local(back, out_o, osem.at[2]))
    for copy in copies:
        copy.wait_send()
    for block in range(8):

        @pl.when(block != me.band)
        def _():
            pltpu.make_async_remote_copy(
                src_ref=dkv.at[block], dst_ref=dt_v.at[1:3, mine, :], send_sem=ks.at[block],
                recv_sem=kr.at[me.d], device_id=me.band_device(block), device_id_type=MESH_ID,
            ).wait_send()

        pltpu.make_async_copy(
            dkv.at[0], dt_v.at[1:3, pl.ds(block * HEAD, HEAD), :], kr.at[block]).wait()
        pltpu.make_async_copy(
            dqb.at[:, pl.ds(0, PIX)], dt_v.at[0, pl.ds(block * HEAD, HEAD), :], q_r.at[block]
        ).wait()
    saves.append(local(dt_v, dt_o, osem.at[1]))
    spread_edges(me, a2, act_v, es, er, finish=True)
    for copy in direct:
        copy.wait_send()
    pl.when(jnp.logical_not(owner))(lambda: core_copy.wait_send())
    for j, where in enumerate(given):
        part_copy(j, where, given_part, given_chan).wait_send()

    @pl.when(owner)
    def _():
        for where in places_of(me.c):
            act_wait(where)

    @pl.when(jnp.logical_not(owner))
    def _():
        for where in places_of(far):
            for part in range(2):
                part_copy(0, where, part, x).wait_recv()

    saves.append(local(act_v, act_o, osem.at[3]))
    for copy in saves:
        copy.wait()


def middle(*args):
    pixels = H * W
    return pl.pallas_call(
        middle_kernel,
        name="middle",
        out_shape=[
            jax.ShapeDtypeStruct((4, PIX, 128), BF),
            jax.ShapeDtypeStruct((PIX, C), F32),
            jax.ShapeDtypeStruct((C, C), BF),
            jax.ShapeDtypeStruct((8, C), F32),
            jax.ShapeDtypeStruct((3, C, PIX), BF),
            jax.ShapeDtypeStruct((2, 16, 128), F32),
            jax.ShapeDtypeStruct((HALF_ROWS, C), BF),
        ],
        in_specs=[ANY] * 4 + [VMEM, ANY, VMEM, ANY, VMEM, ANY, VMEM, ANY],
        out_specs=[ANY, ANY, VMEM, VMEM, ANY, VMEM, ANY],
        scratch_shapes=[
            pltpu.VMEM((C, PIX), BF), pltpu.VMEM((PIX, C), F32), pltpu.VMEM((PIX, C), BF),
            pltpu.VMEM((C, C), BF), pltpu.VMEM((PIX, C), BF), pltpu.VMEM((4, PIX, 128), BF),
            pltpu.VMEM((PIX, C), F32), pltpu.VMEM((C, PIX), BF), pltpu.VMEM((HEAD, pixels), BF),
            pltpu.VMEM((3, HEAD, pixels), BF), pltpu.VMEM((HEAD, pixels), F32),
            pltpu.VMEM((pixels, 128), BF), pltpu.VMEM((16, 128), BF),
            pltpu.VMEM((128, pixels), BF), pltpu.VMEM((pixels, 128), BF),
            pltpu.VMEM((pixels, 128), BF), pltpu.VMEM((HEAD, pixels), F32),
            pltpu.VMEM((2, PIX, pixels), BF), pltpu.VMEM((8, 2, HEAD, PIX), BF),
            pltpu.VMEM((HEAD, pixels), BF), pltpu.VMEM((3, C, PIX), BF),
            pltpu.VMEM((2, 16, 128), F32), pltpu.VMEM((8, 2, 16, 128), F32),
            pltpu.VMEM((HALF_ROWS, C), BF),
            DMA((4,)), DMA((4,)), DMA((8,)), DMA((8,)), DMA((8,)), DMA((8,)), DMA((8,)),
            DMA((8,)), DMA((8,)), DMA((8,)), DMA((7,)), DMA((4,)), DMA((2,)),
            DMA((5,)), DMA((12,)), DMA((4,)), DMA((1,)),
        ],
        compiler_params=pltpu.CompilerParams(
            collective_id=2, has_side_effects=True, vmem_limit_bytes=VMEM_LIMIT
        ),
    )(*args)


TAPS = 22
WHOLE = 13
GROUP_TAPS = ((0, 1), (1, 3), (13, 3), (16, 3), (19, 3), (4, 3), (7, 3), (10, 3))
GROUPS_SENT = len(GROUP_TAPS)
STAGES = 9


def only(condition, action):
    if condition is None:
        action()
    else:
        pl.when(condition)(lambda: action() and None)


class Reduce:
    def __init__(self, me, part, quarter, bufs, total, sems):
        self.me, self.part, self.quarter, self.total = me, part, quarter, total
        (self.from_core, self.quarter_core, self.near_x, self.near_y, self.last_x, self.last_y, self.plane,
         self.plane_in, self.half_in) = bufs
        self.s, self.r = sems
        odd = lax.rem(me.z, 2)
        self.x = me.c + 1 - 2 * lax.rem(me.c, 2)
        self.y = lax.rem(me.c + 2, 4)
        self.far = lax.rem(self.x + 2, 4)
        self.core = (me.r + 1 - 2 * me.k, me.c)
        self.z1 = me.z + 1 - 2 * odd
        self.inner = jnp.logical_or(me.z == 1, me.z == 2)
        self.outer = jnp.logical_not(self.inner)
        self.half = lax.rem(me.z + 1, 2)
        self.copies = {}

    def plane_device(self, z):
        return (2 * z + self.me.k, self.me.c)

    def advance(self, group):
        stage, waiting = self.copies.get(group, (0, []))
        for copy, sends, takes in waiting:
            only(sends, copy.wait_send)
            only(takes, copy.wait_recv)
        start, count = GROUP_TAPS[group]
        first = ((self.core_send, self.first_send, self.second_send, self.inward)
                 if start < WHOLE else (self.conv_core_send, self.conv_inward))
        step = (first + (self.half_send, self.half_back, self.outward, self.core_back,
                         lambda *_: []))[stage]
        taps = pl.ds(start, count)
        self.conv = pl.ds(start - WHOLE, count)
        moves = step(taps, lambda body: pl.loop(start, start + count)(body))
        copies = []
        for j, (src, dst, device, *when) in enumerate(moves):
            copy = pltpu.make_async_remote_copy(
                src_ref=src, dst_ref=dst, send_sem=self.s.at[group, stage, j],
                recv_sem=self.r.at[group, stage, j], device_id=device, device_id_type=MESH_ID)
            sends, takes = when if when else (None, None)
            only(sends, copy.start)
            copies.append((copy, sends, takes))
        self.copies[group] = (stage + 1, copies)

    def core_send(self, taps, each):
        return [(self.part.at[taps, :, 1 - self.me.k], self.from_core.at[taps], self.core)]

    def first_send(self, taps, each):
        me, part = self.me, self.part

        @each
        def _(tap):
            own = part[tap, :, me.k].astype(F32) + self.from_core[tap].astype(F32)
            part[tap, :, me.k] = own.astype(BF)

        low, high = pl.ds(0, 32), pl.ds(32, 32)
        x, y = (me.r, self.x), (me.r, self.y)
        return [
            (part.at[taps, self.far, me.k, low, :], self.near_x.at[1, taps], x),
            (part.at[taps, self.far, me.k, high, :], self.near_y.at[1, taps], y),
            (part.at[taps, self.x, me.k, low, :], self.near_x.at[0, taps], x),
            (part.at[taps, self.y, me.k, high, :], self.near_y.at[0, taps], y),
        ]

    def conv_core_send(self, taps, each):
        return [(self.quarter.at[self.conv, 1 - self.me.k], self.quarter_core.at[self.conv], self.core)]

    def conv_inward(self, taps, each):
        @each
        def _(tap):
            value = (self.quarter[tap - WHOLE, self.me.k].astype(F32)
                     + self.quarter_core[tap - WHOLE].astype(F32))
            self.plane[tap] = value.astype(BF)

        return self.to_inner(taps)

    def second_send(self, taps, each):
        me, part = self.me, self.part
        low, high = pl.ds(0, 32), pl.ds(32, 32)

        @each
        def _(tap):
            for chan, rows, near in ((self.y, low, self.near_x), (self.x, high, self.near_y)):
                value = part[tap, chan, me.k, rows, :].astype(F32) + near[1, tap].astype(F32)
                part[tap, chan, me.k, rows, :] = value.astype(BF)

        return [
            (part.at[taps, self.y, me.k, low, :], self.last_y.at[taps], (me.r, self.y)),
            (part.at[taps, self.x, me.k, high, :], self.last_x.at[taps], (me.r, self.x)),
        ]

    def inward(self, taps, each):
        me, part = self.me, self.part

        @each
        def _(tap):
            for start, near, last in ((0, self.near_x, self.last_y), (32, self.near_y, self.last_x)):
                rows = pl.ds(start, 32)
                value = (part[tap, me.c, me.k, rows, :].astype(F32) + near[0, tap].astype(F32)
                         + last[tap].astype(F32))
                self.plane[tap, rows, :] = value.astype(BF)

        return self.to_inner(taps)

    def to_inner(self, taps):
        return [(self.plane.at[taps], self.plane_in.at[taps], self.plane_device(self.z1),
                 self.outer, self.inner)]

    def half_rows(self, half):
        return pl.ds(pl.multiple_of(half * 32, 32), 32)

    def half_send(self, taps, each):
        @pl.when(self.inner)
        def _():
            @each
            def _(tap):
                value = self.plane[tap].astype(F32) + self.plane_in[tap].astype(F32)
                self.plane[tap] = value.astype(BF)

        return [(self.plane.at[taps, self.half_rows(1 - self.half), :], self.half_in.at[taps],
                 self.plane_device(3 - self.me.z), self.inner, self.inner)]

    def half_back(self, taps, each):
        me = self.me

        @pl.when(self.inner)
        def _():
            @each
            def _(tap):
                value = (self.plane[tap, self.half_rows(self.half), :].astype(F32)
                         + self.half_in[tap].astype(F32))
                self.total[tap, me.k, self.half] = value.astype(BF)

        piece = self.total.at[taps, me.k, self.half]
        return [(piece, piece, self.plane_device(3 - me.z), self.inner, self.inner)]

    def outward(self, taps, each):
        piece = self.total.at[taps, self.me.k]
        return [(piece, piece, self.plane_device(self.z1), self.inner, self.outer)]

    def core_back(self, taps, each):
        piece = self.total.at[taps, self.me.k]
        return [(piece, piece, self.core)]


def back_kernel(
    dt, vec, st, x, a1, hid, act2, res, nrm, cot, w1, w2, wq, gwo, gob,
    gimg_o, zs_o, gw1_o, gw2_o, gqkv_o, gwo_o,
    dt_v, x_v, a1_v, hid_v, act2_v, res_v, nrm_v, drs_v, w1_v, w2_v, wq_v,
    cat, turned, turned1, acc, groups, slots, halo, keep, img_b, back, zsl, dquart,
    part, quarter, from_core, quarter_core, near_x, near_y, last_x, last_y, plane, plane_in, half_in, total,
    ss, sr, hs, hr, bs, br, zs, zr, red_s, red_r, lsem, osem, ds_, dr,
):
    me = Place()
    barrier = pltpu.get_barrier_semaphore()
    greet_plane(me, barrier)
    others = greet_back(me, barrier)
    for t in range(1, 4):
        pl.semaphore_signal(
            barrier, inc=1, device_id=(2 * lax.rem(me.z + t, 4) + me.k, me.c),
            device_id_type=MESH_ID,
        )
    loads = [local(a, b, lsem.at[j]) for j, (a, b) in enumerate((
        (dt, dt_v), (wq, wq_v), (res, res_v), (gwo, part.at[0]), (nrm, nrm_v), (cot, drs_v),
        (act2, act2_v), (w2, w2_v), (hid, hid_v), (a1, a1_v), (w1, w1_v), (x, x_v)))]
    reduce = Reduce(
        me, part, quarter, (from_core, quarter_core, near_x, near_y, last_x, last_y, plane, plane_in,
                            half_in), total, (red_s, red_r))

    def advance(*groups):
        for group in groups:
            reduce.advance(group)

    group_matrix(groups)
    zero8 = jnp.zeros((8, C), F32)
    members = 1.0 / (H * W * 16)
    loads[0].wait()
    loads[1].wait()
    for j in range(3):
        rows = jnp.transpose(dt_v[j].astype(F32))
        if j != 1:
            keep[j : j + 1, :] = as_row(rows)
        value = mm(rows.astype(BF), wq_v[j])
        if j == 0:
            acc[...] = value
        else:
            acc[...] += value
    loads[2].wait()

    def sums(scaled_of, upstream_of):
        def add(i, carry):
            upstream = upstream_of(i)
            return (carry[0] + fold(upstream), carry[1] + fold(upstream * scaled_of(i)))

        first, cross = lax.fori_loop(0, CHUNKS, add, (zero8, zero8))
        return [as_row(first), as_row(cross)]

    def scaled(ref, number):
        return lambda i: (ref[chunk_of(i), :].astype(F32) - st[2 * number : 2 * number + 1, :]) * st[
            2 * number + 1 : 2 * number + 2, :]

    def exchange(number, rows):
        store_rows(slots.at[number], me.d, rows)
        return plane_exchange(me, slots.at[number], ss.at[number], sr.at[number])

    scaled3, scaled2, scaled1 = scaled(res_v, 2), scaled(hid_v, 1), scaled(x_v, 0)
    rows3 = sums(scaled3, lambda i: acc[chunk_of(i), :])
    pl.semaphore_wait(barrier, 10 + others)
    copies = exchange(0, rows3)
    loads[3].wait()
    advance(0)
    loads[4].wait()

    @pl.loop(0, 3)
    def _(j):
        part[1 + j] = mm(dt_v[j], nrm_v[...]).astype(BF).reshape(4, 2, 64, C)

    advance(1)
    loads[5].wait()
    for copy in copies:
        copy.wait()

    def group_means(total_rows, factor):
        return group_total(total_rows * factor, groups) * members

    total3 = slots_total(slots.at[0])
    gain = vec[2:3, :]
    means = group_means(total3, gain)
    keep[8:16, :] = total3
    inverse = st[5:6, :]

    def resid_grad(i, carry):
        where = chunk_of(i)
        value = drs_v[where, :] + inverse * (
            acc[where, :] * gain - means[0:1] - scaled3(i) * means[1:2])
        drs_v[where, :] = value
        put_shifted(cat, 64 + i * 64, value)
        return carry + fold(value.astype(BF).astype(F32))

    keep[3:4, :] = as_row(lax.fori_loop(0, CHUNKS, resid_grad, zero8))
    def grad_of(chan):
        return cat.at[1, pl.ds(64, PIX), pl.ds(pl.multiple_of(chan * 128, 128), 128)]

    grads_sems = (ds_, dr)

    def half_weight_grads(act, groups_of):
        spread_received(grad_of, dquart, grad_rows, dr)
        value = dquart[...].astype(F32)
        col = lax.rem(lax.broadcasted_iota(jnp.int32, (4 * PIX, 128), 0), 64)
        moved = (jnp.where(col == 63, 0.0, pltpu.roll(value, 4 * PIX - 1, 0)), value,
                 jnp.where(col == 0, 0.0, pltpu.roll(value, 1, 0)))
        for j in range(3):
            turned[j * 128 : (j + 1) * 128, :] = jnp.transpose(moved[j]).astype(BF)
        for row, group in enumerate(groups_of):
            start = GROUP_TAPS[group][0]
            taps = mm(turned[...], act[row * 64 : row * 64 + 4 * PIX, :])
            for j in range(3):
                quarter[start - WHOLE + j] = taps[j * 128 : (j + 1) * 128].astype(BF).reshape(
                    2, 64, C)
            advance(group)

    def weight_grads(group, source):
        start, count = GROUP_TAPS[group]

        @pl.loop(0, count)
        def _(i):
            tap = start - 4 + i
            rows = pl.ds(pl.multiple_of(lax.div(tap, 3) * 64, 64), PIX)
            part[start + i] = mm(turned1[...], source[lax.rem(tap, 3), rows, :]).astype(
                BF).reshape(4, 2, 64, C)

        advance(group)

    halo_send(me, cat, halo.at[0], hs.at[0], hr.at[0])
    spread_rows(me, grad_of, dquart, grad_rows, *grads_sems, SPREAD)
    acc[...] = jnp.zeros((PIX, C), F32)
    loads[7].wait()
    conv_taps(acc, cat, w2_v, (1,), True, NN)
    halo_wait(me, cat, halo.at[0], hs.at[0], hr.at[0])
    conv_taps(acc, cat, w2_v, (0, 2), True, NN)
    loads[8].wait()
    gain2, bias2 = vec[1:2, :], vec[4:5, :]
    scale, shift = 1.0 + vec[11:12, :], vec[12:13, :]

    def mod_grad(i):
        where = chunk_of(i)
        mod = (scaled2(i) * gain2 + bias2) * scale + shift
        value = acc[where, :] * swish_slope(mod)
        acc[where, :] = value
        return value

    copies = exchange(1, sums(scaled2, mod_grad))
    advance(0, 1)
    loads[6].wait()
    half_weight_grads(act2_v, (2, 3, 4))
    spread_sent(me, grad_of, dquart, grad_rows, *grads_sems)
    for copy in copies:
        copy.wait()
    total2 = slots_total(slots.at[1])
    means2 = group_means(total2, gain2 * scale)
    keep[16:24, :] = total2
    inverse2 = st[3:4, :]

    def hidden_grad(i, carry):
        where = chunk_of(i)
        value = inverse2 * (
            acc[where, :] * (gain2 * scale) - means2[0:1] - scaled2(i) * means2[1:2])
        acc[where, :] = value
        put_shifted(cat, 64 + i * 64, value)
        return carry + fold(value.astype(BF).astype(F32))

    keep[1:2, :] = as_row(lax.fori_loop(0, CHUNKS, hidden_grad, zero8))
    halo_send(me, cat, halo.at[1], hs.at[1], hr.at[1])
    advance(2, 3, 4)
    turned1[...] = jnp.transpose(acc[...]).astype(BF)
    loads[9].wait()
    for group in (5, 6, 7):
        weight_grads(group, a1_v)
    advance(0, 1, 5)
    acc[...] = jnp.zeros((PIX, C), F32)
    loads[10].wait()
    conv_taps(acc, cat, w1_v, (1,), True, NN)
    halo_wait(me, cat, halo.at[1], hs.at[1], hr.at[1])
    conv_taps(acc, cat, w1_v, (0, 2), True, NN)
    loads[11].wait()
    gain1, bias1 = vec[0:1, :], vec[3:4, :]

    def pre_grad(i):
        where = chunk_of(i)
        value = acc[where, :] * swish_slope(scaled1(i) * gain1 + bias1)
        acc[where, :] = value
        return value

    first, cross = sums(scaled1, pre_grad)
    copies = exchange(2, [first, cross, keep[1:2, :], keep[3:4, :], keep[0:1, :], keep[2:3, :],
                          gob[0:1, :]])
    advance(6, 2, 3, 4)
    for copy in copies:
        copy.wait()
    total1 = slots_total(slots.at[2])
    means1 = group_means(total1, gain1)
    inverse1 = st[1:2, :]

    @pl.loop(0, CHUNKS)
    def _(i):
        where = chunk_of(i)
        value = drs_v[where, :] + inverse1 * (
            acc[where, :] * gain1 - means1[0:1] - scaled1(i) * means1[1:2])
        img_b[where, :] = value.astype(BF)

    band_back_send(me, img_b, back, bs, br)
    u2, v2 = keep[16:17, :], keep[17:18, :]
    keep[24:40, :] = jnp.concatenate(
        [total1[1:2], scale * v2, keep[9:10, :], total1[0:1], scale * u2, keep[8:9, :],
         total1[2:7], gain2 * v2 + bias2 * u2, u2, jnp.zeros((3, C), F32)], axis=0)
    own_cols = pl.ds(pl.multiple_of(me.c * 128, 128), 128)
    zsl[me.z] = keep[24:40, own_cols]
    zcopies = [
        send(zsl.at[me.z], zsl.at[me.z], zs.at[t], zr.at[t],
             (2 * lax.rem(me.z + t, 4) + me.k, me.c))
        for t in range(1, 4)
    ]
    advance(7, 5, 6, 0, 1, 2, 3, 4, 7, 5, 6, 2, 3, 4, 0, 1, 7, 5, 6, 2, 3, 4, 0, 1, 7, 5, 6)
    for copy in zcopies:
        copy.wait()
    zs_o[...] = zsl[...]
    advance(0, 1, 7, 5, 6, 7, 0, 1, 5, 6, 7)
    band_back_wait(me, img_b, back, bs, br)
    saves = [local(back, gimg_o, osem.at[0])]
    for _ in range(STAGES):
        for group in range(GROUPS_SENT):
            if reduce.copies[group][0] < (STAGES - 2 if 2 <= group < 5 else STAGES):
                reduce.advance(group)
    for j, (dst, start, count) in enumerate(
            ((gwo_o, 0, 1), (gqkv_o, 1, 3), (gw2_o, 13, 9), (gw1_o, 4, 9))):
        saves.append(local(total.at[pl.ds(start, count)], dst, osem.at[j + 1]))
    for copy in saves:
        copy.wait()


def back(*args):
    shared = [
        ((3, C, PIX), BF), ((PIX, C), BF), ((3, PAD, C), BF), ((PIX, C), F32),
        ((HALF_ROWS, C), BF), ((PIX, C), F32), ((PIX, C), BF), ((PIX, C), F32), ((9, C, C), BF),
        ((9, C, C), BF), ((3, C, C), BF), ((3, PAD, C), BF), ((384, 4 * PIX), BF), ((C, PIX), BF), ((PIX, C), F32),
        ((C, C), BF), ((3, 8, 8, C), F32), ((2, 2, 64, C), BF), ((40, C), F32), ((PIX, C), BF),
        ((4, PIX, 128), BF), ((4, 16, 128), F32), ((4 * PIX, 128), BF),
        ((WHOLE, 4, 2, 64, C), BF), ((TAPS - WHOLE, 2, 64, C), BF), ((WHOLE, 4, 64, C), BF),
        ((TAPS - WHOLE, 64, C), BF), ((2, WHOLE, 32, C), BF), ((2, WHOLE, 32, C), BF),
        ((WHOLE, 32, C), BF), ((WHOLE, 32, C), BF), ((TAPS, 64, C), BF), ((TAPS, 64, C), BF),
        ((TAPS, 32, C), BF), ((TAPS, 2, 2, 32, C), BF),
    ]
    return pl.pallas_call(
        back_kernel,
        name="back",
        out_shape=[
            jax.ShapeDtypeStruct((4, PIX, 128), BF),
            jax.ShapeDtypeStruct((4, 16, 128), F32),
            jax.ShapeDtypeStruct((9, 2, 2, 32, C), BF),
            jax.ShapeDtypeStruct((9, 2, 2, 32, C), BF),
            jax.ShapeDtypeStruct((3, 2, 2, 32, C), BF),
            jax.ShapeDtypeStruct((1, 2, 2, 32, C), BF),
        ],
        in_specs=[ANY, VMEM, VMEM] + [ANY] * 11 + [VMEM],
        out_specs=[ANY, VMEM, ANY, ANY, ANY, ANY],
        scratch_shapes=[pltpu.VMEM(*one) for one in shared]
        + [
            DMA((3, 8)), DMA((3, 8)), DMA((2, 2)), DMA((2, 2)), DMA((4,)), DMA((4,)), DMA((4,)),
            DMA((4,)), DMA((GROUPS_SENT, STAGES, 4)), DMA((GROUPS_SENT, STAGES, 4)), DMA((12,)),
            DMA((5,)), DMA((4,)), DMA((4,)),
        ],
        compiler_params=pltpu.CompilerParams(
            collective_id=3, has_side_effects=True, vmem_limit_bytes=VMEM_LIMIT
        ),
    )(*args)


def split_rows(rows):
    first = rows.astype(BF).astype(F32)
    second = (rows - first).astype(BF).astype(F32)
    stacked = jnp.concatenate([first, second, rows - first - second, jnp.zeros((80, 128), F32)],
                              axis=0)
    left = jnp.transpose(stacked).astype(BF)
    return left[:, 0:16], left[:, 16:32], left[:, 32:48]


def finish_kernel(
    res, gimg, gw1, gw2, gqkv, gwo, zs, ctot, feat, tokens,
    res_o, gimg_o, gain_o, bias_o, gw1_o, gw2_o, cb_o, gemb_o, gembb_o, gqkv_o, qvb_o, gctx_o,
    gctxb_o, gwo_o, ob_o,
    res_v, gimg_v, gw1_v, gw2_v, gqkv_v, gwo_v, res_f, gimg_f, gw1_f, gw2_f, gqkv_f, gwo_f,
    gemb_f, gctx_f, lsem, osem,
):
    pairs = (
        (gw1, gw1_v, gw1_f, gw1_o), (gw2, gw2_v, gw2_f, gw2_o), (res, res_v, res_f, res_o),
        (gimg, gimg_v, gimg_f, gimg_o), (gqkv, gqkv_v, gqkv_f, gqkv_o), (gwo, gwo_v, gwo_f, gwo_o))
    loads = [local(src, low, lsem.at[j]) for j, (src, low, _, _) in enumerate(pairs)]
    saves = []
    for j in range(2):
        rows = jnp.concatenate([zs[n, 11 + j : 12 + j, :] for n in range(4)]
                               + [jnp.zeros((12, 128), F32)], axis=0)
        gemb_f[j] = sum(mm(term, feat[...]) for term in split_rows(rows))
        saves.append(local(gemb_f.at[j], gemb_o.at[j], osem.at[6 + j]))
        gctx_f[j] = sum(mm(term, tokens[...]) for term in split_rows(ctot[j]))
        saves.append(local(gctx_f.at[j], gctx_o.at[j], osem.at[8 + j]))
        gctxb_o[j : j + 1, :] = as_row(ctot[j])
    total = (zs[0] + zs[1]) + (zs[2] + zs[3])
    gain_o[...] = total[0:3]
    bias_o[...] = total[3:6]
    cb_o[...] = total[6:8]
    qvb_o[...] = total[8:10]
    ob_o[...] = total[10:11]
    gembb_o[...] = total[11:13]
    for j, (_, low, high, dst) in enumerate(pairs):
        loads[j].wait()

        @pl.loop(0, high.shape[0])
        def _(i):
            high[i] = low[i].astype(F32)

        saves.append(local(high, dst, osem.at[j]))
    for copy in saves:
        copy.wait()


def finish(*args):
    wide = [((4, PIX, 128), F32)] * 2 + [((9, 128, C), F32)] * 2 + [((3, 128, C), F32),
                                                                    ((1, 128, C), F32)]
    res, gimg, gw1, gw2, gqkv, gwo = wide
    emb, ctx = ((2, 128, EMB), F32), ((2, 128, CTXW), F32)
    outs = [
        res, gimg, ((3, 128), F32), ((3, 128), F32), gw1, gw2, ((2, 128), F32), emb,
        ((2, 128), F32), gqkv, ((2, 128), F32), ctx, ((2, 128), F32), gwo, ((1, 128), F32)]
    return pl.pallas_call(
        finish_kernel,
        name="finish",
        out_shape=[jax.ShapeDtypeStruct(*one) for one in outs],
        in_specs=[ANY] * 6 + [VMEM] * 4,
        out_specs=[VMEM if len(one[0]) == 2 else ANY for one in outs],
        scratch_shapes=[pltpu.VMEM(shape, BF) for shape, _ in wide]
        + [pltpu.VMEM(*one) for one in wide + [emb, ctx]] + [DMA((6,)), DMA((10,))],
        compiler_params=pltpu.CompilerParams(vmem_limit_bytes=VMEM_LIMIT),
    )(*args)


def plane_body(
    image, target, time_index, loss_weight, clip_embed, clip_tokens, norm_gain, norm_bias,
    conv1_w, conv2_w, conv_bias, emb_w, emb_b, qkv_w, qv_bias, ctx_w, ctx_b, out_w, out_b,
):
    (x, tgt, vec, st, a1, hid, a2, res, nrm, w1, w2, wq, wo, qkv, attn, p, ctx, pc, o, linv, feat,
     tokens) = front(
        image.reshape(4, PIX, 128), target.reshape(4, PIX, 128), time_index, loss_weight,
        clip_embed, clip_tokens, norm_gain, norm_bias, conv_bias, qv_bias, out_b[None], emb_w,
        emb_b, ctx_w, ctx_b, conv1_w.reshape(9, 128, C), conv2_w.reshape(9, 128, C), qkv_w,
        out_w[None])
    result, cot, gwo, gob, dt, ctot, act2 = middle(
        attn, res, tgt, wo, vec, qkv, ctx, p, pc, o, linv, a2)
    gimg, zs, gw1, gw2, gqkv, gwo = back(
        dt, vec, st, x, a1, hid, act2, res, nrm, cot, w1, w2, wq, gwo.reshape(4, 2, 64, C), gob)
    taps = lambda value: value.reshape(value.shape[0], 128, C)
    outs = finish(result, gimg, taps(gw1), taps(gw2), taps(gqkv), taps(gwo), zs, ctot, feat, tokens)
    shapes = (
        image, image, norm_gain, norm_bias, conv1_w, conv2_w, conv_bias, emb_w, emb_b, qkv_w,
        qv_bias, ctx_w, ctx_b, out_w, out_b)
    return tuple(out.reshape(like.shape) for out, like in zip(outs, shapes))


def solution(mesh):
    sizes = dict(mesh.shape)
    planes = sizes["row"] == 8 and sizes["chan"] == 4
    return jax.shard_map(
        plane_body if planes else general_body,
        mesh=mesh,
        in_specs=(
            P(None, "row", None, "chan"), P(None, "row", None, "chan"), P(), P(), P(), P(),
            P(None, "chan"), P(None, "chan"), P(None, None, "chan", None),
            P(None, None, "chan", None), P(None, "chan"), P(None, "chan", None),
            P(None, "chan"), P(None, "chan", None), P(None, "chan"), P(None, "chan", None),
            P(None, "chan"), P("chan", None), P("chan"),
        ),
        out_specs=(
            P(None, "row", None, "chan"), P(None, "row", None, "chan"), P(None, "chan"),
            P(None, "chan"), P(None, None, "chan", None), P(None, None, "chan", None),
            P(None, "chan"), P(None, "chan", None), P(None, "chan"), P(None, "chan", None),
            P(None, "chan"), P(None, "chan", None), P(None, "chan"), P("chan", None), P("chan"),
        ),
        check_vma=False,
    )
```

```python
import math

import jax
import jax.numpy as jnp
from jax import lax
from jax.experimental import pallas as pl
from jax.experimental.pallas import tpu as pltpu
from jax.sharding import PartitionSpec as P

C = 512
GROUPS = 32
HEAD = 64
EMB = 2048
CTXW = 2048
CTX = 4
H = 64
W = 64
MB_IMG = 2


HIGH = lax.Precision.HIGHEST
EPSILON = 1e-05


def with_halo(cells, sides, width):
    for axis, dim in sides:
        count = lax.axis_size(axis)
        ends = count - 1
        head = lax.slice_in_dim(cells, 0, width, axis=dim)
        tail = lax.slice_in_dim(cells, cells.shape[dim] - width, cells.shape[dim], axis=dim)
        cells = jnp.concatenate(
            [
                lax.ppermute(tail, axis, [(i, (i + 1) % count) for i in range(ends)]),
                cells,
                lax.ppermute(head, axis, [((i + 1) % count, i) for i in range(ends)]),
            ],
            axis=dim,
        )
    return cells


def swish(source):
    return source * jax.nn.sigmoid(source)


def swish_slope(source):
    sigma = jax.nn.sigmoid(source)
    return sigma * (1.0 + source * (1.0 - sigma))


def time_features(time_index, width_all):
    half_width = width_all // 2
    frequency = jnp.exp(-math.log(10000.0) * jnp.arange(half_width, dtype=jnp.float32) / half_width)
    angles = time_index.astype(jnp.float32)[:, None] * frequency[None, :]
    return jnp.concatenate([jnp.cos(angles), jnp.sin(angles)], axis=1)


def rows_around(source):
    return with_halo(source, (("row", 1),), 1)


def all_channels(source):
    return lax.all_gather(source, "chan", axis=3, tiled=True)


def channel_total(source):
    return lax.psum_scatter(
        source.astype(jnp.bfloat16), "chan", scatter_dimension=3, tiled=True
    ).astype(jnp.float32)


def norm_forward(source, group_width, members):
    layout = source.shape
    grouped = source.reshape(layout[0], layout[1], layout[2], layout[3] // group_width, group_width)
    first_sum = jnp.sum(grouped, axis=(1, 2, 4))
    square_sum = jnp.sum(grouped * grouped, axis=(1, 2, 4))
    first_sum, square_sum = lax.psum((first_sum, square_sum), "row")
    center = first_sum / members
    spread = square_sum / members - center * center
    inverse_std = lax.rsqrt(spread + EPSILON)
    scaled = (grouped - center[:, None, None, :, None]) * inverse_std[:, None, None, :, None]
    return (scaled.reshape(layout), inverse_std)


def norm_backward(upstream, scaled, inverse_std, gain, group_width, members):
    layout = upstream.shape
    grouped_grad = (upstream * gain).reshape(
        layout[0], layout[1], layout[2], layout[3] // group_width, group_width
    )
    grouped_norm = scaled.reshape(grouped_grad.shape)
    grad_sum = jnp.sum(grouped_grad, axis=(1, 2, 4))
    cross_sum = jnp.sum(grouped_grad * grouped_norm, axis=(1, 2, 4))
    grad_sum, cross_sum = lax.psum((grad_sum, cross_sum), "row")
    result = inverse_std[:, None, None, :, None] * (
        grouped_grad
        - grad_sum[:, None, None, :, None] / members
        - grouped_norm * (cross_sum[:, None, None, :, None] / members)
    )
    gain_grad = jnp.sum(upstream * scaled, axis=(0, 1, 2))
    bias_grad = jnp.sum(upstream, axis=(0, 1, 2))
    return (result.reshape(layout), gain_grad, bias_grad)


def conv_apply(padded, weight):
    height = padded.shape[1] - 2
    width = padded.shape[2]
    widened = jnp.pad(padded, ((0, 0), (0, 0), (1, 1), (0, 0)))
    result = None
    for row_step in range(3):
        for col_step in range(3):
            partial_term = jnp.einsum(
                "nhwc,dc->nhwd",
                widened[:, row_step : row_step + height, col_step : col_step + width],
                weight[row_step, col_step],
                preferred_element_type=jnp.float32,
            )
            result = partial_term if result is None else result + partial_term
    return result


def conv_weight_grad(padded, upstream_low):
    height = upstream_low.shape[1]
    width = upstream_low.shape[2]
    widened = jnp.pad(padded, ((0, 0), (0, 0), (1, 1), (0, 0)))
    stacked = []
    for row_step in range(3):
        row_terms = []
        for col_step in range(3):
            row_terms.append(
                jnp.einsum(
                    "nhwc,nhwd->dc",
                    widened[:, row_step : row_step + height, col_step : col_step + width],
                    upstream_low,
                    preferred_element_type=jnp.float32,
                )
            )
        stacked.append(jnp.stack(row_terms))
    return jnp.stack(stacked)


def conv_input_grad(upstream_low, weight):
    height = upstream_low.shape[1]
    width = upstream_low.shape[2]
    widened = jnp.pad(rows_around(upstream_low), ((0, 0), (0, 0), (1, 1), (0, 0)))
    result = None
    for row_step in range(3):
        for col_step in range(3):
            partial_term = jnp.einsum(
                "nhwd,dc->nhwc",
                widened[
                    :, 2 - row_step : 2 - row_step + height, 2 - col_step : 2 - col_step + width
                ],
                weight[row_step, col_step],
                preferred_element_type=jnp.float32,
            )
            result = partial_term if result is None else result + partial_term
    return channel_total(result)


def general_body(
    image,
    target,
    time_index,
    loss_weight,
    clip_embed,
    clip_tokens,
    norm_gain,
    norm_bias,
    conv1_w,
    conv2_w,
    conv_bias,
    emb_w,
    emb_b,
    qkv_w,
    qv_bias,
    ctx_w,
    ctx_b,
    out_w,
    out_b,
):
    local_chan = conv1_w.shape[2]
    group_width = C // GROUPS
    members = H * W * group_width
    head_count = local_chan // HEAD
    scaling = HEAD ** (-0.5)
    batches = image.shape[0] // MB_IMG
    band_rows = image.shape[1]
    image_cols = image.shape[2]

    def heads_of(source):
        return source.reshape(source.shape[0], -1, head_count, HEAD)

    def one_batch(carry, items):
        picture, target_in, steps_in, weight_in, embed_in, tokens_in = items
        feat_low = swish(time_features(steps_in, EMB) + embed_in.astype(jnp.float32)).astype(
            jnp.bfloat16
        )
        cond = (
            jnp.einsum("ne,jde->njd", feat_low, emb_w, preferred_element_type=jnp.float32) + emb_b
        )
        scale_term = cond[:, 0][:, None, None, :]
        shift_term = cond[:, 1][:, None, None, :]
        picture_f = picture.astype(jnp.float32)
        scaled_one, inverse_one = norm_forward(picture_f, group_width, members)
        pre_one = scaled_one * norm_gain[0] + norm_bias[0]
        padded_one = all_channels(rows_around(swish(pre_one).astype(jnp.bfloat16)))
        hidden = conv_apply(padded_one, conv1_w) + conv_bias[0]
        scaled_two, inverse_two = norm_forward(hidden, group_width, members)
        normal_two = scaled_two * norm_gain[1] + norm_bias[1]
        modded = normal_two * (1.0 + scale_term) + shift_term
        padded_two = all_channels(rows_around(swish(modded).astype(jnp.bfloat16)))
        resid = picture_f + conv_apply(padded_two, conv2_w) + conv_bias[1]
        scaled_three, inverse_three = norm_forward(resid, group_width, members)
        normed_full = all_channels(
            (scaled_three * norm_gain[2] + norm_bias[2]).astype(jnp.bfloat16)
        )
        projected = jnp.einsum(
            "nhwc,tdc->nhwtd", normed_full, qkv_w, preferred_element_type=jnp.float32
        )
        query_own = heads_of((projected[..., 0, :] + qv_bias[0]).astype(jnp.bfloat16))
        key_own = heads_of(projected[..., 1, :].astype(jnp.bfloat16))
        value_own = heads_of((projected[..., 2, :] + qv_bias[1]).astype(jnp.bfloat16))
        context = (
            jnp.einsum("nte,jde->ntjd", tokens_in, ctx_w, preferred_element_type=jnp.float32)
            + ctx_b
        )
        ctx_key = heads_of(context[:, :, 0].astype(jnp.bfloat16))
        ctx_value = heads_of(context[:, :, 1].astype(jnp.bfloat16))
        key_rows, value_rows = (
            lax.all_gather(key_own, "row", axis=1, tiled=True),
            lax.all_gather(value_own, "row", axis=1, tiled=True),
        )
        score_image = (
            jnp.einsum("nqhd,nkhd->nhqk", query_own, key_rows, preferred_element_type=jnp.float32)
            * scaling
        )
        score_context = (
            jnp.einsum("nqhd,nkhd->nhqk", query_own, ctx_key, preferred_element_type=jnp.float32)
            * scaling
        )
        top_score = jnp.maximum(jnp.max(score_image, axis=3), jnp.max(score_context, axis=3))
        expo_image = jnp.exp(score_image - top_score[..., None])
        expo_context = jnp.exp(score_context - top_score[..., None])
        denom = jnp.sum(expo_image, axis=3) + jnp.sum(expo_context, axis=3)
        prob_image = expo_image / denom[..., None]
        prob_context = expo_context / denom[..., None]
        attended = jnp.einsum(
            "nhqk,nkhd->nqhd",
            prob_image.astype(jnp.bfloat16),
            value_rows,
            preferred_element_type=jnp.float32,
        ) + jnp.einsum(
            "nhqk,nkhd->nqhd",
            prob_context.astype(jnp.bfloat16),
            ctx_value,
            preferred_element_type=jnp.float32,
        )
        attn_full = all_channels(attended.astype(jnp.bfloat16).reshape(picture.shape))
        result = (
            resid
            + jnp.einsum("nhwc,dc->nhwd", attn_full, out_w, preferred_element_type=jnp.float32)
            + out_b
        )
        cotangent = weight_in[:, None, None, None] * (result - target_in.astype(jnp.float32))
        grad_proj = cotangent.astype(jnp.bfloat16)
        grad_outw = jnp.einsum(
            "nhwc,nhwd->dc", attn_full, grad_proj, preferred_element_type=jnp.float32
        )
        grad_outb = jnp.sum(grad_proj.astype(jnp.float32), axis=(0, 1, 2))
        grad_attn = heads_of(
            channel_total(
                jnp.einsum("nhwd,dc->nhwc", grad_proj, out_w, preferred_element_type=jnp.float32)
            ).astype(jnp.bfloat16)
        )
        dprob_image = jnp.einsum(
            "nqhd,nkhd->nhqk", grad_attn, value_rows, preferred_element_type=jnp.float32
        )
        dprob_context = jnp.einsum(
            "nqhd,nkhd->nhqk", grad_attn, ctx_value, preferred_element_type=jnp.float32
        )
        delta = jnp.sum(prob_image * dprob_image, axis=3) + jnp.sum(
            prob_context * dprob_context, axis=3
        )
        dscore_image = (prob_image * (dprob_image - delta[..., None])).astype(jnp.bfloat16)
        dscore_context = (prob_context * (dprob_context - delta[..., None])).astype(jnp.bfloat16)
        grad_query = (
            jnp.einsum(
                "nhqk,nkhd->nqhd", dscore_image, key_rows, preferred_element_type=jnp.float32
            )
            + jnp.einsum(
                "nhqk,nkhd->nqhd", dscore_context, ctx_key, preferred_element_type=jnp.float32
            )
        ) * scaling
        grad_ctx_key = (
            jnp.einsum(
                "nhqk,nqhd->nkhd", dscore_context, query_own, preferred_element_type=jnp.float32
            )
            * scaling
        )
        grad_ctx_value = jnp.einsum(
            "nhqk,nqhd->nkhd",
            prob_context.astype(jnp.bfloat16),
            grad_attn,
            preferred_element_type=jnp.float32,
        )
        key_terms = (
            jnp.einsum(
                "nhqk,nqhd->nkhd", dscore_image, query_own, preferred_element_type=jnp.float32
            )
            * scaling
        )
        value_terms = jnp.einsum(
            "nhqk,nqhd->nkhd",
            prob_image.astype(jnp.bfloat16),
            grad_attn,
            preferred_element_type=jnp.float32,
        )
        grad_key, grad_value = (
            lax.psum_scatter(
                key_terms.astype(jnp.bfloat16), "row", scatter_dimension=1, tiled=True
            ).astype(jnp.float32),
            lax.psum_scatter(
                value_terms.astype(jnp.bfloat16), "row", scatter_dimension=1, tiled=True
            ).astype(jnp.float32),
        )
        grad_stack = (
            jnp.stack([grad_query, grad_key, grad_value], axis=2)
            .reshape(picture.shape[0], band_rows, image_cols, 3, local_chan)
            .astype(jnp.bfloat16)
        )
        grad_qkvw = jnp.einsum(
            "nhwc,nhwtd->tdc", normed_full, grad_stack, preferred_element_type=jnp.float32
        )
        stack_sums = jnp.sum(grad_stack.astype(jnp.float32), axis=(0, 1, 2))
        grad_qvb = jnp.stack([stack_sums[0], stack_sums[2]])
        grad_context = jnp.stack(
            [
                grad_ctx_key.reshape(picture.shape[0], CTX, local_chan),
                grad_ctx_value.reshape(picture.shape[0], CTX, local_chan),
            ],
            axis=2,
        )
        grad_ctxw = jnp.einsum(
            "nte,ntjd->jde", tokens_in.astype(jnp.float32), grad_context, precision=HIGH
        )
        grad_ctxb = jnp.sum(grad_context, axis=(0, 1))
        grad_normed = channel_total(
            jnp.einsum("nhwtd,tdc->nhwc", grad_stack, qkv_w, preferred_element_type=jnp.float32)
        )
        grad_resid, gain_three, bias_three = norm_backward(
            grad_normed, scaled_three, inverse_three, norm_gain[2], group_width, members
        )
        grad_resid = cotangent + grad_resid
        grad_conv_two = grad_resid.astype(jnp.bfloat16)
        grad_w_two = conv_weight_grad(padded_two, grad_conv_two)
        grad_b_two = jnp.sum(grad_conv_two.astype(jnp.float32), axis=(0, 1, 2))
        grad_modded = conv_input_grad(grad_conv_two, conv2_w) * swish_slope(modded)
        grad_cond = jnp.stack(
            [jnp.sum(grad_modded * normal_two, axis=(1, 2)), jnp.sum(grad_modded, axis=(1, 2))],
            axis=1,
        )
        grad_embw = jnp.einsum(
            "ne,njd->jde", feat_low.astype(jnp.float32), grad_cond, precision=HIGH
        )
        grad_embb = jnp.sum(grad_cond, axis=0)
        grad_hidden, gain_two, bias_two = norm_backward(
            grad_modded * (1.0 + scale_term),
            scaled_two,
            inverse_two,
            norm_gain[1],
            group_width,
            members,
        )
        grad_conv_one = grad_hidden.astype(jnp.bfloat16)
        grad_w_one = conv_weight_grad(padded_one, grad_conv_one)
        grad_b_one = jnp.sum(grad_conv_one.astype(jnp.float32), axis=(0, 1, 2))
        grad_pre_one = conv_input_grad(grad_conv_one, conv1_w) * swish_slope(pre_one)
        grad_input, gain_one, bias_one = norm_backward(
            grad_pre_one, scaled_one, inverse_one, norm_gain[0], group_width, members
        )
        grad_picture = grad_resid + grad_input
        grad_gains = jnp.stack([gain_one, gain_two, gain_three])
        grad_biases = jnp.stack([bias_one, bias_two, bias_three])
        grad_convb = jnp.stack([grad_b_one, grad_b_two])
        batch_grads = (
            grad_gains,
            grad_biases,
            grad_w_one,
            grad_w_two,
            grad_convb,
            grad_embw,
            grad_embb,
            grad_qkvw,
            grad_qvb,
            grad_ctxw,
            grad_ctxb,
            grad_outw,
            grad_outb,
        )
        updated = tuple((running + update for running, update in zip(carry, batch_grads)))
        return (updated, (result, grad_picture))

    start = (
        jnp.zeros(norm_gain.shape, jnp.float32),
        jnp.zeros(norm_bias.shape, jnp.float32),
        jnp.zeros(conv1_w.shape, jnp.float32),
        jnp.zeros(conv2_w.shape, jnp.float32),
        jnp.zeros(conv_bias.shape, jnp.float32),
        jnp.zeros(emb_w.shape, jnp.float32),
        jnp.zeros(emb_b.shape, jnp.float32),
        jnp.zeros(qkv_w.shape, jnp.float32),
        jnp.zeros(qv_bias.shape, jnp.float32),
        jnp.zeros(ctx_w.shape, jnp.float32),
        jnp.zeros(ctx_b.shape, jnp.float32),
        jnp.zeros(out_w.shape, jnp.float32),
        jnp.zeros(out_b.shape, jnp.float32),
    )
    items = (
        image.reshape(batches, MB_IMG, band_rows, image_cols, local_chan),
        target.reshape(batches, MB_IMG, band_rows, image_cols, local_chan),
        time_index.reshape(batches, MB_IMG),
        loss_weight.reshape(batches, MB_IMG),
        clip_embed.reshape(batches, MB_IMG, EMB),
        clip_tokens.reshape(batches, MB_IMG, CTX, CTXW),
    )
    totals, (results, picture_grads) = lax.scan(one_batch, start, items)
    (
        sum_gain,
        sum_bias,
        sum_conv_one,
        sum_conv_two,
        sum_conv_bias,
        sum_emb_w,
        sum_emb_b,
        sum_qkv_w,
        sum_qv_bias,
        sum_ctx_w,
        sum_ctx_b,
        sum_out_w,
        sum_out_b,
    ) = totals
    (
        sum_gain,
        sum_bias,
        sum_conv_one,
        sum_conv_two,
        sum_conv_bias,
        sum_emb_w,
        sum_emb_b,
        sum_qkv_w,
        sum_qv_bias,
        sum_ctx_w,
        sum_ctx_b,
        sum_out_w,
        sum_out_b,
    ) = (
        lax.psum(sum_gain.astype(jnp.bfloat16), "row").astype(jnp.float32),
        lax.psum(sum_bias.astype(jnp.bfloat16), "row").astype(jnp.float32),
        lax.psum(sum_conv_one.astype(jnp.bfloat16), "row").astype(jnp.float32),
        lax.psum(sum_conv_two.astype(jnp.bfloat16), "row").astype(jnp.float32),
        lax.psum(sum_conv_bias.astype(jnp.bfloat16), "row").astype(jnp.float32),
        lax.psum(sum_emb_w.astype(jnp.bfloat16), "row").astype(jnp.float32),
        lax.psum(sum_emb_b.astype(jnp.bfloat16), "row").astype(jnp.float32),
        lax.psum(sum_qkv_w.astype(jnp.bfloat16), "row").astype(jnp.float32),
        lax.psum(sum_qv_bias.astype(jnp.bfloat16), "row").astype(jnp.float32),
        lax.psum(sum_ctx_w.astype(jnp.bfloat16), "row").astype(jnp.float32),
        lax.psum(sum_ctx_b.astype(jnp.bfloat16), "row").astype(jnp.float32),
        lax.psum(sum_out_w.astype(jnp.bfloat16), "row").astype(jnp.float32),
        lax.psum(sum_out_b.astype(jnp.bfloat16), "row").astype(jnp.float32),
    )
    return (
        results.reshape(image.shape),
        picture_grads.reshape(image.shape),
        sum_gain,
        sum_bias,
        sum_conv_one,
        sum_conv_two,
        sum_conv_bias,
        sum_emb_w,
        sum_emb_b,
        sum_qkv_w,
        sum_qv_bias,
        sum_ctx_w,
        sum_ctx_b,
        sum_out_w,
        sum_out_b,
    )


BF = jnp.bfloat16
F32 = jnp.float32
MESH_ID = pl.DeviceIdType.MESH
NN = (((1,), (0,)), ((), ()))
NT = (((1,), (1,)), ((), ()))
ANY = pl.BlockSpec(memory_space=pl.ANY)
VMEM = pl.BlockSpec(memory_space=pltpu.VMEM)
SMEM = pl.BlockSpec(memory_space=pltpu.SMEM)
PIX = 512
PAD = 640
CHUNKS = 8
VMEM_LIMIT = 60 * 2**20
DMA = pltpu.SemaphoreType.DMA


def mm(left, right, dims=NN):
    return lax.dot_general(left, right, dims, preferred_element_type=F32)


def mixed(chan, z):
    low = lax.rem(chan + lax.div(z, 2), 2)
    return low + 2 * lax.rem(lax.div(chan, 2) + lax.rem(z, 2), 2)


class Place:
    def __init__(self):
        self.r = lax.axis_index("row")
        self.c = lax.axis_index("chan")
        self.z = lax.div(self.r, 2)
        self.k = lax.rem(self.r, 2)
        self.d = 2 * self.c + self.k
        self.pair = mixed(self.c, self.z)
        self.band = 2 * self.pair + self.k

    def head_device(self, head):
        return (2 * self.z + lax.rem(head, 2), lax.div(head, 2))

    def band_device(self, band):
        return (2 * self.z + lax.rem(band, 2), mixed(lax.div(band, 2), self.z))


def send(src, dst, send_sem, recv_sem, device):
    copy = pltpu.make_async_remote_copy(
        src_ref=src,
        dst_ref=dst,
        send_sem=send_sem,
        recv_sem=recv_sem,
        device_id=device,
        device_id_type=MESH_ID,
    )
    copy.start()
    return copy


def local(src, dst, sem):
    copy = pltpu.make_async_copy(src, dst, sem)
    copy.start()
    return copy


def greet_plane(me, barrier):
    for step in range(1, 8):
        pl.semaphore_signal(
            barrier,
            inc=1,
            device_id=me.head_device(lax.rem(me.d + step, 8)),
            device_id_type=MESH_ID,
        )


def group_matrix(ref):
    rows = lax.broadcasted_iota(jnp.int32, (C, C), 0)
    cols = lax.broadcasted_iota(jnp.int32, (C, C), 1)
    ref[...] = jnp.where(lax.div(rows, 16) == lax.div(cols, 16), 1.0, 0.0).astype(BF)


def group_total(rows, groups_ref):
    top = rows.astype(BF)
    rest = rows - top.astype(F32)
    mid = rest.astype(BF)
    low = (rest - mid.astype(F32)).astype(BF)
    stacked = jnp.concatenate([top, mid, low, jnp.zeros_like(low)], axis=0)
    sums = mm(stacked, groups_ref[...])
    return sums[0:8] + sums[8:16] + sums[16:24]


def plane_exchange(me, slots, ssem, rsem):
    copies = []
    for step in range(1, 8):
        copies.append(
            send(
                slots.at[me.d],
                slots.at[me.d],
                ssem.at[step],
                rsem.at[step],
                me.head_device(lax.rem(me.d + step, 8)),
            )
        )
    return copies


def slots_total(slots):
    total = slots[0]
    for slot in range(1, 8):
        total = total + slots[slot]
    return total


def fold(value):
    return value.reshape(value.shape[0] // 8, 8, value.shape[1]).sum(axis=0)


def as_row(value):
    return jnp.sum(value, axis=0, keepdims=True)


def store_rows(slots, index, rows):
    filled = rows + [jnp.zeros((1, C), F32)] * (8 - len(rows))
    slots[index] = jnp.concatenate(filled, axis=0)


def chunk_of(i):
    return pl.ds(pl.multiple_of(i * 64, 64), 64)


def put_shifted(dst, start, value):
    col = lax.broadcasted_iota(jnp.int32, (64, C), 0)
    where = pl.ds(pl.multiple_of(start, 64), 64)
    dst[1, where, :] = value.astype(BF)
    dst[0, where, :] = jnp.where(col == 0, 0.0, pltpu.roll(value, 1, 0)).astype(BF)
    dst[2, where, :] = jnp.where(col == 63, 0.0, pltpu.roll(value, 63, 0)).astype(BF)


def halo_send(me, cat, halo, ssem, rsem):
    @pl.when(me.band > 0)
    def _():
        send(cat.at[1, pl.ds(64, 64), :], halo.at[1], ssem.at[0], rsem.at[1],
             me.band_device(me.band - 1))

    @pl.when(me.band < 7)
    def _():
        send(cat.at[1, pl.ds(512, 64), :], halo.at[0], ssem.at[1], rsem.at[0],
             me.band_device(me.band + 1))


def halo_wait(me, cat, halo, ssem, rsem):
    def pair(slot, ahead):
        return pltpu.make_async_remote_copy(
            src_ref=cat.at[1, pl.ds(64, 64), :], dst_ref=halo.at[slot],
            send_sem=ssem.at[slot], recv_sem=rsem.at[slot],
            device_id=me.band_device(ahead), device_id_type=MESH_ID)

    zero = jnp.zeros((64, C), F32)

    @pl.when(me.band > 0)
    def _():
        both = pair(0, me.band - 1)
        both.wait_send()
        both.wait_recv()
        put_shifted(cat, 0, halo[0].astype(F32))

    @pl.when(me.band == 0)
    def _():
        put_shifted(cat, 0, zero)

    @pl.when(me.band < 7)
    def _():
        both = pair(1, me.band + 1)
        both.wait_send()
        both.wait_recv()
        put_shifted(cat, 576, halo[1].astype(F32))

    @pl.when(me.band == 7)
    def _():
        put_shifted(cat, 576, zero)


def conv_taps(acc, cat, weight, order, flip, dims):
    @pl.loop(0, 3 * len(order))
    def _(i):
        step = lax.div(i, 3)
        col = lax.rem(i, 3)
        row = order[0] if len(order) == 1 else order[0] + step * (order[1] - order[0])
        tap = (2 - row) * 3 + (2 - col) if flip else row * 3 + col
        start = pl.multiple_of(row * 64, 64)
        acc[...] += mm(cat[col, pl.ds(start, PIX), :], weight[tap], dims)


HALF_ROWS = 34 * 64
SPREAD = (1, 2, 3, 0)


def half_place(me):
    return lax.div(me.pair, 2), lax.rem(me.band, 4)


def spread_rows(me, src_of, dst, place_rows, ssem, rsem, steps):
    core, place = half_place(me)
    for step in steps:
        chan = lax.rem(me.c + step, 4)
        args = (src_of(chan), dst.at[place_rows(place), :])
        if step == 0:

            @pl.when(core == me.k)
            def _():
                local(*args, rsem.at[place])

            @pl.when(core != me.k)
            def _():
                send(*args, ssem.at[step], rsem.at[place], (2 * me.z + core, chan))

        else:
            send(*args, ssem.at[step], rsem.at[place], (2 * me.z + core, chan))


def spread_sent(me, src_of, dst, place_rows, ssem, rsem):
    core, place = half_place(me)
    for step in range(4):
        chan = lax.rem(me.c + step, 4)

        def done():
            pltpu.make_async_remote_copy(
                src_ref=src_of(chan), dst_ref=dst.at[place_rows(place), :],
                send_sem=ssem.at[step], recv_sem=rsem.at[place],
                device_id=(2 * me.z + core, chan), device_id_type=MESH_ID).wait_send()

        if step == 0:
            pl.when(core != me.k)(done)
        else:
            done()


def spread_received(src_of, dst, place_rows, rsem):
    for place in range(4):
        pltpu.make_async_copy(src_of(0), dst.at[place_rows(place), :], rsem.at[place]).wait()


def act_rows(place):
    return pl.ds(pl.multiple_of(64 + place * PIX, 64), PIX)


def grad_rows(place):
    return pl.ds(place * PIX, PIX)


def spread_edges(me, act, dst, ssem, rsem, finish=False):
    for band, core, start, to in ((3, 1, 512, 0), (4, 0, 64, HALF_ROWS - 64)):

        @pl.when(me.band == band)
        def _():
            piece, there = act.at[pl.ds(start, 64), :], dst.at[pl.ds(to, 64), :]
            for step in range(4):
                chan = lax.rem(me.c + step, 4)
                if step == 0:
                    if not finish:
                        local(piece, there, rsem.at[0])
                else:
                    copy = pltpu.make_async_remote_copy(
                        src_ref=piece, dst_ref=there, send_sem=ssem.at[step], recv_sem=rsem.at[0],
                        device_id=(2 * me.z + core, chan), device_id_type=MESH_ID)
                    if finish:
                        copy.wait_send()
                    else:
                        copy.start()

    if finish:
        pltpu.make_async_copy(act.at[pl.ds(0, 64), :], dst.at[pl.ds(0, 64), :], rsem.at[0]).wait()
    else:
        empty = jnp.zeros((64, C), BF)

        @pl.when(me.k == 0)
        def _():
            dst[0:64, :] = empty

        @pl.when(me.k == 1)
        def _():
            dst[HALF_ROWS - 64 :, :] = empty


LOG2E = 1.4426950408889634
VROWS = 80
SUB = 256
KEYS = 256


def image_targets(me):
    return [(n, (2 * n + me.k, mixed(me.z, jnp.int32(n)))) for n in range(4)]


class Gather:
    def __init__(self, me, index, src, dst, sems):
        self.me, self.src, self.dst = me, src, dst
        third = src.shape[0] // 3
        odd = lax.rem(me.z, 2)
        self.plane_taps = pl.ds(third * odd, 2 * third)
        self.give_taps = pl.ds(2 * third * odd, third)
        self.take_taps = pl.ds(2 * third * (1 - odd), third)
        self.x = me.c + 1 - 2 * lax.rem(me.c, 2)
        self.y = lax.rem(me.c + 2, 4)
        self.far = lax.rem(self.x + 2, 4)
        self.core = (me.r + 1 - 2 * me.k, me.c)
        self.over = (2 * (me.z + 1 - 2 * odd) + me.k, me.c)
        (self.own, self.first_s, self.first_r, self.relay_s, self.relay_r, self.give_s,
         self.give_r, self.core_s, self.core_r) = [sem.at[index] for sem in sems]
        self.started = []
        self.core_plane = []
        self.core_take = []
        self.gives = []

    def rows(self, chan, start=0, size=64):
        return pl.ds(pl.multiple_of(chan * 128 + self.me.k * 64 + start, size), size)

    def move(self, taps, rows, s, r, device):
        piece = self.dst.at[taps, rows, :]
        return send(piece, piece, s, r, device)

    def start(self):
        me = self.me
        half = pl.ds(pl.multiple_of(me.k * 64, 64), 64)
        quarter = pl.ds(pl.multiple_of(me.c * 128, 128), 128)
        for j, chan in enumerate((self.x, self.y)):
            self.started.append(
                send(self.src.at[self.plane_taps, half, :],
                     self.dst.at[self.plane_taps, self.rows(me.c), :],
                     self.first_s.at[j], self.first_r.at[j], (me.r, chan)))
        self.kept = local(self.src, self.dst.at[:, quarter, :], self.own.at[0])

    def spread(self, slot, chan):
        self.core_plane.append(
            self.move(self.plane_taps, self.rows(chan), self.core_s.at[slot], self.core_r.at[slot],
                      self.core))
        self.gives.append(
            self.move(self.give_taps, self.rows(chan), self.give_s.at[slot], self.give_r.at[slot],
                      self.over))

    def relay(self):
        self.relays = []
        for j, (chan, onward) in enumerate(((self.x, self.y), (self.y, self.x))):
            self.started[j].wait_recv()
            self.relays.append(
                self.move(self.plane_taps, self.rows(chan, 32 * j, 32), self.relay_s.at[j],
                          self.relay_r.at[j], (self.me.r, onward)))
            self.spread(j, chan)

    def relayed(self):
        for copy in self.relays:
            copy.wait_recv()
        self.spread(2, self.far)

    def plane_done(self):
        self.kept.wait()
        for copy in self.core_plane:
            copy.wait_recv()

    def take(self):
        for slot, chan in enumerate((self.x, self.y, self.far)):
            self.gives[slot].wait_recv()
            self.core_take.append(
                self.move(self.take_taps, self.rows(chan), self.core_s.at[3 + slot],
                          self.core_r.at[3 + slot], self.core))

    def take_done(self):
        for copy in self.core_take:
            copy.wait_recv()

    def drain(self):
        for copy in self.started + self.relays + self.gives + self.core_plane + self.core_take:
            copy.wait_send()


def front_kernel(
    img, tgt, steps, loss, embed, words, norm_gain, norm_bias, conv_bias, qv_bias, out_b,
    emb_w, emb_b, ctx_w, ctx_b, w1, w2, wq, wo,
    x_o, t_o, vec_o, st_o, a1_o, hid_o, a2_o, res_o, nrm_o, w1_o, w2_o, wq_o, wo_o, qkv_o,
    attn_o, p_o, ctx_o, pc_o, o_o, linv_o, feat, tokens,
    x_v, t_v, vec_v, st_v, a1_v, hid_v, a2_v, res_v, nrm_v, w1_v, w2_v, wq_v, wo_v, qkv_v,
    attn_v,
    msg, groups, slots, halo, vsrc, wide, cond, keys, ckeys, qs, vext, cvext, sbuf, mbuf, cbuf, pb, ob,
    vs, vr, ims, imr, tgs, tgr, own_sem, first_s, first_r, relay_s, relay_r, give_s, give_r,
    core_s, core_r, wos, wor, wofs, wofr, wol, sts, str_, hs, hr, qs_s, qs_r, lsem, osem, psem,
    as_, ar,
):
    me = Place()
    barrier = pltpu.get_barrier_semaphore()
    greet_plane(me, barrier)
    own_block = me.pair == me.z
    for chan in range(4):
        itself = jnp.logical_and(me.pair == me.z, me.c == chan)

        @pl.when(jnp.logical_not(itself))
        def _():
            pl.semaphore_signal(
                barrier, inc=1, device_id=(2 * me.pair + me.k, chan), device_id_type=MESH_ID
            )

    odd = lax.rem(me.z, 2)
    pl.semaphore_signal(
        barrier, inc=1, device_id=(2 * (me.z + 1 - 2 * odd) + me.k, me.c), device_id_type=MESH_ID
    )
    wide[...] = jnp.zeros((16, EMB), F32)
    wide[0:4, :] = embed[...].astype(F32)
    row = lax.broadcasted_iota(jnp.int32, (16, EMB // 2), 0)
    column = lax.broadcasted_iota(jnp.int32, (16, EMB // 2), 1).astype(F32)
    frequency = jnp.exp(-math.log(10000.0) * column / (EMB // 2))
    angle = jnp.zeros((16, EMB // 2), F32)
    for n in range(4):
        angle = jnp.where(row == n, steps[n].astype(F32) * frequency, angle)
    for start, wave in ((0, jnp.cos), (EMB // 2, jnp.sin)):
        value = wave(angle) + wide[:, start : start + EMB // 2]
        feat[:, start : start + EMB // 2] = jnp.where(row < 4, swish(value), 0.0).astype(BF)
    for n in range(4):
        wide[4 * n : 4 * n + 4, :] = words[n].astype(F32)
    tokens[...] = wide[...].astype(BF)
    for j in range(2):
        cond[j] = mm(feat[...], emb_w[j], NT) + emb_b[j : j + 1, :]
    vsrc[0:3, :] = norm_gain[...]
    vsrc[3:6, :] = norm_bias[...]
    vsrc[6:8, :] = conv_bias[...]
    vsrc[8:10, :] = qv_bias[...]
    vsrc[10:11, :] = out_b[...]
    vsrc[11:12, :] = cond[0, pl.ds(me.z, 1), :]
    vsrc[12:13, :] = cond[1, pl.ds(me.z, 1), :]
    vsrc[13:14, :] = jnp.full((1, 128), loss[me.z], F32)
    vsrc[14:16, :] = jnp.zeros((2, 128), F32)
    lane = lax.broadcasted_iota(jnp.int32, (16, 128), 1)
    for j in range(2):
        value = mm(tokens[...], ctx_w[j], NT) + ctx_b[j : j + 1, :]
        turned = pltpu.roll(value, HEAD, 1)
        first = lax.div(lane, HEAD) == me.k
        both = jnp.where(first, value, turned)
        ctx_o[j] = both.astype(BF)
        if j == 0:
            ckeys[...] = both.astype(BF)
        else:
            tall = jnp.concatenate([both, jnp.zeros((112, 128), F32)], axis=0)
            cvext[0:HEAD, :] = jnp.transpose(tall)[0:HEAD].astype(BF)
    row = lax.broadcasted_iota(jnp.int32, (16, H * W), 0)
    vext[HEAD:, :] = jnp.where(row == 0, 1.0, 0.0).astype(BF)
    cvext[HEAD:, :] = jnp.where(row[:, 0:128] == 0, 1.0, 0.0).astype(BF)
    pl.semaphore_wait(barrier, 8 + 4 - jnp.where(own_block, 1, 0))
    own_cols = pl.ds(pl.multiple_of(me.c * 128, 128), 128)

    vec_v[:, own_cols] = vsrc[...]
    vec_copies = [
        send(vsrc, vec_v.at[:, own_cols], vs.at[t], vr.at[t], (me.r, lax.rem(me.c + t, 4)))
        for t in range(1, 4)
    ]

    def image_send(src, dst, ssem, rsem):
        for n, device in image_targets(me):
            itself = jnp.logical_and(own_block, me.z == n)

            @pl.when(jnp.logical_not(itself))
            def _():
                send(src.at[n], dst.at[:, own_cols], ssem.at[n], rsem.at[me.c], device)

            @pl.when(itself)
            def _():
                local(src.at[n], dst.at[:, own_cols], rsem.at[me.c])

    def image_wait(src, dst, ssem, rsem):
        for chan in range(4):
            pltpu.make_async_copy(
                src.at[0], dst.at[:, pl.ds(chan * 128, 128)], rsem.at[chan]
            ).wait()

    def image_drain(src, dst, ssem, rsem):
        for n, device in image_targets(me):
            itself = jnp.logical_and(own_block, me.z == n)

            @pl.when(jnp.logical_not(itself))
            def _():
                pltpu.make_async_remote_copy(
                    src_ref=src.at[n], dst_ref=dst.at[:, own_cols], send_sem=ssem.at[n],
                    recv_sem=rsem.at[me.c], device_id=device, device_id_type=MESH_ID,
                ).wait_send()

    gather_sems = (own_sem, first_s, first_r, relay_s, relay_r, give_s, give_r, core_s, core_r)
    gather1 = Gather(me, 0, w1, w1_v, gather_sems)
    gather2 = Gather(me, 1, w2, w2_v, gather_sems)
    gather3 = Gather(me, 2, wq, wq_v, gather_sems)

    image_send(img, x_v, ims, imr)
    gather1.start()
    group_matrix(groups)
    col_zero = jnp.zeros((8, C), F32)
    for copy in vec_copies:
        copy.wait()
    outs = []

    def save(index, src, dst):
        outs.append(local(src, dst, osem.at[index]))

    def statistics(number, ref):
        def add(i, carry):
            value = ref[chunk_of(i), :].astype(F32)
            return (carry[0] + fold(value), carry[1] + fold(value * value))

        first, square = lax.fori_loop(0, CHUNKS, add, (col_zero, col_zero))
        store_rows(slots.at[number], me.d, [as_row(first), as_row(square)])
        return plane_exchange(me, slots.at[number], sts.at[number], str_.at[number])

    def finish_statistics(number, copies):
        for copy in copies:
            copy.wait()
        means = group_total(slots_total(slots.at[number]), groups) * (1.0 / (H * W * 16))
        center = means[0:1]
        inverse = lax.rsqrt(means[1:2] - center * center + EPSILON)
        st_v[2 * number : 2 * number + 1, :] = center
        st_v[2 * number + 1 : 2 * number + 2, :] = inverse
        return center, inverse

    image_wait(img, x_v, ims, imr)
    copies = statistics(0, x_v)
    save(0, x_v, x_o)
    save(2, vec_v, vec_o)
    gather1.relay()
    center, inverse = finish_statistics(0, copies)
    gain, bias = vec_v[0:1, :], vec_v[3:4, :]

    @pl.loop(0, CHUNKS)
    def _(i):
        value = (x_v[chunk_of(i), :].astype(F32) - center) * inverse
        put_shifted(a1_v, 64 + i * 64, swish(value * gain + bias))

    halo_send(me, a1_v, halo.at[0], hs.at[0], hr.at[0])
    gather1.relayed()
    gather2.start()
    hid_v[...] = jnp.broadcast_to(vec_v[6:7, :], (PIX, C))
    gather1.plane_done()
    conv_taps(hid_v, a1_v, w1_v, (1,), False, NT)
    halo_wait(me, a1_v, halo.at[0], hs.at[0], hr.at[0])
    save(4, a1_v, a1_o)
    gather1.take()
    conv_taps(hid_v, a1_v, w1_v, (2 * odd,), False, NT)
    gather1.take_done()
    conv_taps(hid_v, a1_v, w1_v, (2 - 2 * odd,), False, NT)
    copies = statistics(1, hid_v)
    save(9, w1_v, w1_o)
    save(5, hid_v, hid_o)
    gather2.relay()
    center, inverse = finish_statistics(1, copies)
    gain, bias = vec_v[1:2, :], vec_v[4:5, :]
    scale, shift = 1.0 + vec_v[11:12, :], vec_v[12:13, :]

    @pl.loop(0, CHUNKS)
    def _(i):
        value = (hid_v[chunk_of(i), :] - center) * inverse
        put_shifted(a2_v, 64 + i * 64, swish((value * gain + bias) * scale + shift))

    halo_send(me, a2_v, halo.at[1], hs.at[1], hr.at[1])
    gather2.relayed()
    gather3.start()
    res_v[...] = x_v[...].astype(F32) + vec_v[7:8, :]
    gather2.plane_done()
    conv_taps(res_v, a2_v, w2_v, (1,), False, NT)
    halo_wait(me, a2_v, halo.at[1], hs.at[1], hr.at[1])
    save(6, a2_v.at[1], a2_o)
    gather2.take()
    gather3.relay()
    conv_taps(res_v, a2_v, w2_v, (2 * odd,), False, NT)
    gather2.take_done()
    gather3.relayed()
    conv_taps(res_v, a2_v, w2_v, (2 - 2 * odd,), False, NT)
    copies = statistics(2, res_v)
    save(10, w2_v, w2_o)
    save(7, res_v, res_o)
    gather3.take()
    center, inverse = finish_statistics(2, copies)
    gain, bias = vec_v[2:3, :], vec_v[5:6, :]
    normed = (res_v[...] - center) * inverse * gain + bias
    nrm_v[...] = normed.astype(BF)
    st_v[6:8, :] = jnp.zeros((2, C), F32)
    save(8, nrm_v, nrm_o)
    save(3, st_v, st_o)
    turned = jnp.transpose(normed).astype(BF)
    gather3.plane_done()
    gather3.take_done()
    save(11, wq_v, wq_o)
    band_cols = pl.ds(pl.multiple_of(me.band * PIX, PIX), PIX)

    def head_rows(head):
        return pl.ds(pl.multiple_of(head * HEAD, HEAD), HEAD)

    owns = []
    qkv_copies = {}
    for j, bias_row in ((1, None), (2, 9), (0, 8)):
        value = mm(wq_v[j], turned)
        if bias_row is not None:
            tall = jnp.transpose(jnp.broadcast_to(vec_v[bias_row : bias_row + 1, :], (128, C)))
            value = value + jnp.concatenate([tall] * 4, axis=1)
        msg[j] = value.astype(BF)
        owns.append(local(msg.at[j, head_rows(me.d), :], qkv_v.at[j, :, band_cols], lsem.at[j]))
        qkv_copies[j] = []
        for step in range(1, 8):
            head = lax.rem(me.d + step, 8)
            qkv_copies[j].append(
                send(msg.at[j, head_rows(head), :], qkv_v.at[j, :, band_cols], qs_s.at[j, step],
                     qs_r.at[j, step], me.head_device(head)))

    for own in owns:
        own.wait()
    for copy in qkv_copies[1]:
        copy.wait()
    both = jnp.concatenate([qkv_v[1], qkv_v[1]], axis=0).astype(F32)
    keys[...] = jnp.transpose(both).astype(BF)

    def scale_queries(where):
        scaled = qkv_v[0, :, where].astype(F32) * (HEAD ** (-0.5) * LOG2E)
        top = scaled.astype(BF)
        qs[0:HEAD, where] = top
        qs[HEAD:, where] = (scaled - top.astype(F32)).astype(BF)

    scale_queries(band_cols)
    token = lax.broadcasted_iota(jnp.int32, (16, SUB), 0)
    valid = lax.div(token, CTX) == me.z
    chunks = H * W // KEYS

    def begin(slot, block):
        query = qs[:, pl.ds(pl.multiple_of(block * SUB, SUB), SUB)]
        score = jnp.where(valid, mm(ckeys[...], query), -1e30)
        cbuf[slot] = score
        return query, jnp.maximum(score[0:8], score[8:16])

    def score_chunk(slot, query, highest, chunk):
        value = mm(keys[chunk * KEYS : (chunk + 1) * KEYS, :], query)
        sbuf[slot, chunk * KEYS : (chunk + 1) * KEYS, :] = value
        return jnp.maximum(highest, jnp.max(value.reshape(KEYS // 8, 8, SUB), axis=0))

    query, highest = begin(0, 2 * me.band)
    for chunk in range(chunks):
        highest = score_chunk(0, query, highest, chunk)
    mbuf[0] = highest
    for copy in qkv_copies[2]:
        copy.wait()
    vext[0:HEAD, :] = qkv_v[2]
    for copy in qkv_copies[0]:
        copy.wait()
    scale_queries(pl.ds(0, H * W))
    save(13, qkv_v, qkv_o)
    image_send(tgt, t_v, tgs, tgr)
    half = pl.ds(pl.multiple_of(me.c * 128 + me.k * 64, 64), 64)
    my_half = pl.ds(pl.multiple_of(me.k * 64, 64), 64)
    wo_own = local(wo, wo_v.at[:, own_cols, :], wol.at[0])
    wo_copies = [
        send(wo.at[:, my_half, :], wo_v.at[:, half, :], wos.at[t], wor.at[t],
             (me.r, lax.rem(me.c + t, 4)))
        for t in range(1, 4)
    ]
    attn_rows = head_rows(me.d)

    def p_copy(block, slot):
        return pltpu.make_async_copy(
            pb.at[slot], p_o.at[:, pl.ds(pl.multiple_of(block * PIX, PIX), PIX)], psem.at[slot])

    @pl.loop(0, 8)
    def _(turn):
        block = lax.rem(me.band + turn, 8)
        slot = lax.rem(turn, 2)

        @pl.when(turn >= 2)
        def _():
            p_copy(block, slot).wait()

        for sub in range(2):
            cols = pl.ds(sub * SUB, SUB)
            place = pl.ds(pl.multiple_of(block * PIX + sub * SUB, SUB), SUB)
            following = lax.rem(2 * block + sub + 1, H * W // SUB)
            top = jnp.max(mbuf[sub], axis=0, keepdims=True)
            pc = jnp.exp2(cbuf[sub] - top).astype(BF)
            pc_o[:, place] = pc
            out = mm(cvext[:, 0:16], pc)
            query, highest = begin(1 - sub, following)
            for chunk in range(chunks):
                highest = score_chunk(1 - sub, query, highest, chunk)
                rows = slice(chunk * KEYS, (chunk + 1) * KEYS)
                probs = jnp.exp2(sbuf[sub, rows, :] - top).astype(BF)
                pb[slot, rows, cols] = probs
                out = out + mm(vext[:, rows], probs)
            mbuf[1 - sub] = highest
            linv = 1.0 / out[HEAD : HEAD + 1]
            out = out[0:HEAD] * linv
            o_o[:, place] = out
            ob[block, :, cols] = out.astype(BF)
            linv_o[:, place] = jnp.broadcast_to(linv, (8, SUB))
        p_copy(block, slot).start()

        @pl.when(block != me.band)
        def _():
            send(ob.at[block], attn_v.at[attn_rows, :], as_.at[block], ar.at[me.d],
                 me.band_device(block))

        @pl.when(block == me.band)
        def _():
            local(ob.at[block], attn_v.at[attn_rows, :], ar.at[me.d])

    wo_forward = []
    for t in range(1, 4):
        wo_copies[t - 1].wait()
        origin = lax.rem(me.c - t + 4, 4)
        rows = pl.ds(pl.multiple_of(origin * 128 + me.k * 64, 64), 64)
        wo_forward.append(
            send(wo_v.at[:, rows, :], wo_v.at[:, rows, :], wofs.at[t], wofr.at[t],
                 (me.r + 1 - 2 * me.k, me.c)))
    image_wait(tgt, t_v, tgs, tgr)
    save(1, t_v, t_o)
    for gather in (gather1, gather2, gather3):
        gather.drain()
    image_drain(img, x_v, ims, imr)
    image_drain(tgt, t_v, tgs, tgr)
    wo_own.wait()
    for copy in wo_forward:
        copy.wait()
    save(12, wo_v, wo_o)
    for block in range(8):

        @pl.when(block != me.band)
        def _():
            pltpu.make_async_remote_copy(
                src_ref=ob.at[block], dst_ref=attn_v.at[attn_rows, :], send_sem=as_.at[block],
                recv_sem=ar.at[me.d], device_id=me.band_device(block), device_id_type=MESH_ID,
            ).wait_send()

        pltpu.make_async_copy(
            ob.at[0], attn_v.at[pl.ds(block * HEAD, HEAD), :], ar.at[block]).wait()
    save(14, attn_v, attn_o)
    p_copy(0, 0).wait()
    p_copy(0, 1).wait()
    for copy in outs:
        copy.wait()


def front(*args):
    pixels = H * W
    saved = [
        ((PIX, C), BF), ((PIX, C), BF), ((16, C), F32), ((8, C), F32), ((3, PAD, C), BF),
        ((PIX, C), F32), ((3, PAD, C), BF), ((PIX, C), F32), ((PIX, C), BF), ((9, C, C), BF),
        ((9, C, C), BF), ((3, C, C), BF), ((1, C, C), BF), ((3, HEAD, pixels), BF), ((C, PIX), BF),
    ]
    more = [
        ((pixels, pixels), BF), ((2, 16, 128), BF), ((16, pixels), BF), ((HEAD, pixels), F32),
        ((8, pixels), F32), ((16, EMB), BF), ((16, CTXW), BF),
    ]
    return pl.pallas_call(
        front_kernel,
        name="front",
        out_shape=[
            jax.ShapeDtypeStruct(shape[1:] if j == 6 else shape, kind)
            for j, (shape, kind) in enumerate(saved + more)],
        in_specs=[ANY, ANY] + [SMEM] * 2 + [VMEM] * 11 + [ANY] * 4,
        out_specs=[ANY] * (len(saved) + 1) + [VMEM] * 6,
        scratch_shapes=[pltpu.VMEM(*one) for one in saved]
        + [
            pltpu.VMEM((3, C, C), BF), pltpu.VMEM((C, C), BF), pltpu.VMEM((3, 8, 8, C), F32),
            pltpu.VMEM((2, 2, 64, C), BF), pltpu.VMEM((16, 128), F32),
            pltpu.VMEM((16, EMB), F32),
            pltpu.VMEM((2, 16, 128), F32), pltpu.VMEM((pixels, 128), BF),
            pltpu.VMEM((16, 128), BF), pltpu.VMEM((128, pixels), BF),
            pltpu.VMEM((VROWS, pixels), BF), pltpu.VMEM((VROWS, 128), BF),
            pltpu.VMEM((2, pixels, SUB), F32), pltpu.VMEM((2, 8, SUB), F32),
            pltpu.VMEM((2, 16, SUB), F32), pltpu.VMEM((2, pixels, PIX), BF),
            pltpu.VMEM((8, HEAD, PIX), BF),
            DMA((4,)), DMA((4,)), DMA((4,)), DMA((4,)), DMA((4,)), DMA((4,)),
            DMA((3, 1)), DMA((3, 2)), DMA((3, 2)), DMA((3, 2)), DMA((3, 2)), DMA((3, 3)),
            DMA((3, 3)), DMA((3, 6)), DMA((3, 6)), DMA((4,)), DMA((4,)), DMA((4,)), DMA((4,)),
            DMA((1,)), DMA((3, 8)), DMA((3, 8)), DMA((2, 2)), DMA((2, 2)), DMA((3, 8)),
            DMA((3, 8)), DMA((3,)), DMA((15,)), DMA((2,)), DMA((8,)), DMA((8,)),
        ],
        compiler_params=pltpu.CompilerParams(
            collective_id=1, has_side_effects=True, vmem_limit_bytes=VMEM_LIMIT
        ),
    )(*args)


def band_back_send(me, src, dst, ssem, rsem):
    for chan in range(4):
        cols = pl.ds(chan * 128, 128)
        itself = jnp.logical_and(me.band == me.r, me.c == chan)

        @pl.when(jnp.logical_not(itself))
        def _():
            send(src.at[:, cols], dst.at[me.z], ssem.at[chan], rsem.at[me.z], (me.band, chan))

        @pl.when(itself)
        def _():
            local(src.at[:, cols], dst.at[me.z], rsem.at[me.z])


def band_back_wait(me, src, dst, ssem, rsem):
    for n in range(4):
        pltpu.make_async_copy(src.at[:, pl.ds(0, 128)], dst.at[n], rsem.at[n]).wait()
    for chan in range(4):
        itself = jnp.logical_and(me.band == me.r, me.c == chan)

        @pl.when(jnp.logical_not(itself))
        def _():
            pltpu.make_async_remote_copy(
                src_ref=src.at[:, pl.ds(chan * 128, 128)], dst_ref=dst.at[me.z],
                send_sem=ssem.at[chan], recv_sem=rsem.at[me.z], device_id=(me.band, chan),
                device_id_type=MESH_ID,
            ).wait_send()


def greet_back(me, barrier):
    own_block = me.pair == me.z
    for n in range(4):
        itself = jnp.logical_and(own_block, me.z == n)

        @pl.when(jnp.logical_not(itself))
        def _():
            pl.semaphore_signal(
                barrier, inc=1, device_id=(2 * n + me.k, mixed(me.z, jnp.int32(n))),
                device_id_type=MESH_ID,
            )

    return 4 - jnp.where(own_block, 1, 0)


def middle_kernel(
    attn, res, tgt, wo, vec, qkv, ctx, p, pc, o, linv, a2,
    out_o, cot_o, gwo_o, gob_o, dt_o, ctot_o, act_o,
    attn_v, res_v, tgt_v, wo_v, out_b, back, cot_v, dat, dot_v, qkv_v, o_v,
    vext, cvext, dos, dor, qrow, dq, pb, dkv, dqb, dt_v, dctx, cslots, act_v,
    bs, br, ds_, dr, cs, cr, ks, kr, q_s, q_r, lsem, osem, psem, acts, actr, es, er,
):
    me = Place()
    scaling = HEAD ** (-0.5)
    barrier = pltpu.get_barrier_semaphore()
    greet_plane(me, barrier)
    others = greet_back(me, barrier)
    for step in range(1, 8):
        pl.semaphore_signal(
            barrier, inc=1, device_id=(lax.rem(me.r + step, 8), me.c), device_id_type=MESH_ID
        )
    loads = [local(a, b, lsem.at[j]) for j, (a, b) in enumerate(
        ((attn, attn_v), (wo.at[0], wo_v), (res, res_v), (tgt, tgt_v), (qkv, qkv_v), (o, o_v)))]

    def p_copy(block, slot):
        return pltpu.make_async_copy(
            p.at[pl.ds(pl.multiple_of(block * PIX, PIX), PIX), :], pb.at[slot], psem.at[slot])

    p_copy(me.band, 0).start()

    def band_cols(band):
        return pl.ds(pl.multiple_of(band * PIX, PIX), PIX)

    def head_rows(head):
        return pl.ds(pl.multiple_of(head * HEAD, HEAD), HEAD)

    for load in loads[0:4]:
        load.wait()
    rows = jnp.transpose(attn_v[...].astype(F32)).astype(BF)
    result = res_v[...] + mm(rows, wo_v[...], NT) + vec[10:11, :]
    out_b[...] = result.astype(BF)
    cot = vec[13:14, :] * (result - tgt_v[...].astype(F32))
    cot_v[...] = cot
    low = cot.astype(BF)
    dat[...] = jnp.transpose(mm(low, wo_v[...])).astype(BF)
    pl.semaphore_wait(barrier, 14 + others)
    own = local(dat.at[head_rows(me.d), :], dot_v.at[:, band_cols(me.band)], lsem.at[6])
    copies = []
    for step in range(1, 8):
        head = lax.rem(me.d + step, 8)
        copies.append(
            send(dat.at[head_rows(head), :], dot_v.at[:, band_cols(me.band)], ds_.at[step],
                 dr.at[step], me.head_device(head)))
    piece = a2.at[pl.ds(64, PIX), :]
    x = me.c + 1 - 2 * lax.rem(me.c, 2)
    y = lax.rem(me.c + 2, 4)
    far = lax.rem(x + 2, 4)
    half, place = half_place(me)
    owner = half == me.k
    direct = [
        send(piece, act_v.at[act_rows(place), :], acts.at[j], actr.at[place],
             (2 * me.z + half, chan))
        for j, chan in enumerate((x, y))
    ]
    core_copy = pltpu.make_async_remote_copy(
        src_ref=piece, dst_ref=act_v.at[act_rows(place), :], send_sem=acts.at[2],
        recv_sem=actr.at[place], device_id=(2 * me.z + half, me.c), device_id_type=MESH_ID)
    pl.when(owner)(lambda: local(piece, act_v.at[act_rows(place), :], actr.at[place]) and None)
    pl.when(jnp.logical_not(owner))(lambda: core_copy.start())

    def places_of(chan):
        first = lax.rem(2 * mixed(chan, me.z), 4)
        return first, first + 1

    def act_wait(where):
        pltpu.make_async_copy(piece, act_v.at[act_rows(where), :], actr.at[where]).wait()

    def part_copy(slot, where, part, chan):
        rows = act_v.at[pl.ds(pl.multiple_of(64 + where * PIX + part * 256, 64), 256), :]
        return pltpu.make_async_remote_copy(
            src_ref=rows, dst_ref=rows, send_sem=acts.at[3 + slot],
            recv_sem=actr.at[4 + 4 * part + where], device_id=(2 * me.z + me.k, chan),
            device_id_type=MESH_ID)

    given = places_of(jnp.where(owner, x, y))
    given_part = jnp.where(owner, 0, 1)
    given_chan = jnp.where(owner, y, x)
    spread_edges(me, a2, act_v, es, er)
    saves = [local(cot_v, cot_o, osem.at[0])]
    lowf = low.astype(F32)
    gwo_o[...] = mm(jnp.transpose(lowf).astype(BF), rows).astype(BF)
    gob_o[...] = jnp.broadcast_to(as_row(lowf), (8, C))
    for load in loads[4:]:
        load.wait()
    row = lax.broadcasted_iota(jnp.int32, (HEAD, H * W), 0)
    ones = jnp.where(row < 3, 1.0, 0.0)
    vext[...] = jnp.transpose(jnp.concatenate([qkv_v[2].astype(F32), ones], axis=0)).astype(BF)
    lane = lax.broadcasted_iota(jnp.int32, (16, 128), 1)
    cvext[...] = jnp.where(
        lane < HEAD, ctx[1].astype(F32), jnp.where(lane < HEAD + 3, 1.0, 0.0)).astype(BF)
    queries = qkv_v[0].astype(F32) * scaling
    qrow[...] = jnp.transpose(
        jnp.concatenate([queries, jnp.zeros_like(queries)], axis=0)).astype(BF)
    own.wait()
    for copy in copies:
        copy.wait()
    band_back_send(me, out_b, back, bs, br)
    grad = (dot_v[...].astype(F32) * linv[0:1, :]).astype(BF)
    gradf = grad.astype(F32)
    delta = -jnp.sum(gradf * o_v[...], axis=0, keepdims=True)
    top = delta.astype(BF).astype(F32)
    mid = (delta - top).astype(BF).astype(F32)
    last = delta - top - mid
    dos[0:HEAD, :] = grad
    dos[HEAD:, :] = jnp.where(
        row == 0, top, jnp.where(row == 1, mid, jnp.where(row == 2, last, 0.0))).astype(BF)
    dor[...] = jnp.transpose(jnp.concatenate([gradf, jnp.zeros_like(gradf)], axis=0)).astype(BF)

    def score_grads(values, probs):
        return (probs.astype(F32) * mm(values, dos[...])).astype(BF)

    dsc = score_grads(cvext[...], pc[...])
    for j, (left, right) in enumerate(((dsc, qrow), (pc[...], dor))):
        value = mm(left, right[...])
        dctx[j] = jnp.where(me.k == 0, value, pltpu.roll(value, HEAD, 1))
    cslots[me.r] = dctx[...]
    ctx_copies = [
        send(cslots.at[me.r], cslots.at[me.r], cs.at[step], cr.at[step],
             (lax.rem(me.r + step, 8), me.c))
        for step in range(1, 8)
    ]
    wide = jnp.concatenate([ctx[0].astype(F32), jnp.zeros((112, 128), F32)], axis=0)
    dq[...] = mm(jnp.transpose(wide)[0:HEAD, 0:16].astype(BF), dsc)
    mine = head_rows(me.d)

    @pl.loop(0, 8)
    def _(turn):
        block = lax.rem(me.band + turn, 8)
        slot = lax.rem(turn, 2)

        @pl.when(turn < 7)
        def _():
            p_copy(lax.rem(block + 1, 8), 1 - slot).start()

        p_copy(block, slot).wait()

        @pl.when(turn == 3)
        def _():
            for j, where in enumerate(given):
                act_wait(where)
                part_copy(j, where, given_part, given_chan).start()

        grads = []
        for sub in range(2):
            part = pl.ds(pl.multiple_of(block * PIX + sub * SUB, SUB), SUB)
            probs = pb[slot, sub * SUB : (sub + 1) * SUB, :]
            grads.append(score_grads(vext[part, :], probs))
            dkv[block, 1, :, sub * SUB : (sub + 1) * SUB] = jnp.transpose(
                mm(probs, dor[...]))[0:HEAD].astype(BF)
        for sub in range(2):
            part = pl.ds(pl.multiple_of(block * PIX + sub * SUB, SUB), SUB)
            dkv[block, 0, :, sub * SUB : (sub + 1) * SUB] = jnp.transpose(
                mm(grads[sub], qrow[...]))[0:HEAD].astype(BF)
            dq[...] += mm(qkv_v[1, :, part], grads[sub])

        @pl.when(block != me.band)
        def _():
            send(dkv.at[block], dt_v.at[1:3, mine, :], ks.at[block], kr.at[me.d],
                 me.band_device(block))

        @pl.when(block == me.band)
        def _():
            local(dkv.at[block], dt_v.at[1:3, mine, :], kr.at[me.d])

    dqb[...] = (dq[...] * scaling).astype(BF)
    own = local(dqb.at[:, band_cols(me.band)], dt_v.at[0, mine, :], q_r.at[me.d])
    copies = []
    for step in range(1, 8):
        band = lax.rem(me.band + step, 8)
        copies.append(
            send(dqb.at[:, band_cols(band)], dt_v.at[0, mine, :], q_s.at[step], q_r.at[me.d],
                 me.band_device(band)))
    for copy in ctx_copies:
        copy.wait()
    for j in range(2):
        total = cslots[0, j]
        for slot in range(1, 8):
            total = total + cslots[slot, j]
        ctot_o[j] = total
    band_back_wait(me, out_b, back, bs, br)
    saves.append(local(back, out_o, osem.at[2]))
    for copy in copies:
        copy.wait_send()
    for block in range(8):

        @pl.when(block != me.band)
        def _():
            pltpu.make_async_remote_copy(
                src_ref=dkv.at[block], dst_ref=dt_v.at[1:3, mine, :], send_sem=ks.at[block],
                recv_sem=kr.at[me.d], device_id=me.band_device(block), device_id_type=MESH_ID,
            ).wait_send()

        pltpu.make_async_copy(
            dkv.at[0], dt_v.at[1:3, pl.ds(block * HEAD, HEAD), :], kr.at[block]).wait()
        pltpu.make_async_copy(
            dqb.at[:, pl.ds(0, PIX)], dt_v.at[0, pl.ds(block * HEAD, HEAD), :], q_r.at[block]
        ).wait()
    saves.append(local(dt_v, dt_o, osem.at[1]))
    spread_edges(me, a2, act_v, es, er, finish=True)
    for copy in direct:
        copy.wait_send()
    pl.when(jnp.logical_not(owner))(lambda: core_copy.wait_send())
    for j, where in enumerate(given):
        part_copy(j, where, given_part, given_chan).wait_send()

    @pl.when(owner)
    def _():
        for where in places_of(me.c):
            act_wait(where)

    @pl.when(jnp.logical_not(owner))
    def _():
        for where in places_of(far):
            for part in range(2):
                part_copy(0, where, part, x).wait_recv()

    saves.append(local(act_v, act_o, osem.at[3]))
    for copy in saves:
        copy.wait()


def middle(*args):
    pixels = H * W
    return pl.pallas_call(
        middle_kernel,
        name="middle",
        out_shape=[
            jax.ShapeDtypeStruct((4, PIX, 128), BF),
            jax.ShapeDtypeStruct((PIX, C), F32),
            jax.ShapeDtypeStruct((C, C), BF),
            jax.ShapeDtypeStruct((8, C), F32),
            jax.ShapeDtypeStruct((3, C, PIX), BF),
            jax.ShapeDtypeStruct((2, 16, 128), F32),
            jax.ShapeDtypeStruct((HALF_ROWS, C), BF),
        ],
        in_specs=[ANY] * 4 + [VMEM, ANY, VMEM, ANY, VMEM, ANY, VMEM, ANY],
        out_specs=[ANY, ANY, VMEM, VMEM, ANY, VMEM, ANY],
        scratch_shapes=[
            pltpu.VMEM((C, PIX), BF), pltpu.VMEM((PIX, C), F32), pltpu.VMEM((PIX, C), BF),
            pltpu.VMEM((C, C), BF), pltpu.VMEM((PIX, C), BF), pltpu.VMEM((4, PIX, 128), BF),
            pltpu.VMEM((PIX, C), F32), pltpu.VMEM((C, PIX), BF), pltpu.VMEM((HEAD, pixels), BF),
            pltpu.VMEM((3, HEAD, pixels), BF), pltpu.VMEM((HEAD, pixels), F32),
            pltpu.VMEM((pixels, 128), BF), pltpu.VMEM((16, 128), BF),
            pltpu.VMEM((128, pixels), BF), pltpu.VMEM((pixels, 128), BF),
            pltpu.VMEM((pixels, 128), BF), pltpu.VMEM((HEAD, pixels), F32),
            pltpu.VMEM((2, PIX, pixels), BF), pltpu.VMEM((8, 2, HEAD, PIX), BF),
            pltpu.VMEM((HEAD, pixels), BF), pltpu.VMEM((3, C, PIX), BF),
            pltpu.VMEM((2, 16, 128), F32), pltpu.VMEM((8, 2, 16, 128), F32),
            pltpu.VMEM((HALF_ROWS, C), BF),
            DMA((4,)), DMA((4,)), DMA((8,)), DMA((8,)), DMA((8,)), DMA((8,)), DMA((8,)),
            DMA((8,)), DMA((8,)), DMA((8,)), DMA((7,)), DMA((4,)), DMA((2,)),
            DMA((5,)), DMA((12,)), DMA((4,)), DMA((1,)),
        ],
        compiler_params=pltpu.CompilerParams(
            collective_id=2, has_side_effects=True, vmem_limit_bytes=VMEM_LIMIT
        ),
    )(*args)


TAPS = 22
WHOLE = 13
GROUP_TAPS = ((0, 1), (1, 3), (13, 3), (16, 3), (19, 3), (4, 3), (7, 3), (10, 3))
GROUPS_SENT = len(GROUP_TAPS)
STAGES = 9


def only(condition, action):
    if condition is None:
        action()
    else:
        pl.when(condition)(lambda: action() and None)


class Reduce:
    def __init__(self, me, part, quarter, bufs, total, sems):
        self.me, self.part, self.quarter, self.total = me, part, quarter, total
        (self.from_core, self.quarter_core, self.near_x, self.near_y, self.last_x, self.last_y, self.plane,
         self.plane_in, self.half_in) = bufs
        self.s, self.r = sems
        odd = lax.rem(me.z, 2)
        self.x = me.c + 1 - 2 * lax.rem(me.c, 2)
        self.y = lax.rem(me.c + 2, 4)
        self.far = lax.rem(self.x + 2, 4)
        self.core = (me.r + 1 - 2 * me.k, me.c)
        self.z1 = me.z + 1 - 2 * odd
        self.inner = jnp.logical_or(me.z == 1, me.z == 2)
        self.outer = jnp.logical_not(self.inner)
        self.half = lax.rem(me.z + 1, 2)
        self.copies = {}

    def plane_device(self, z):
        return (2 * z + self.me.k, self.me.c)

    def advance(self, group):
        stage, waiting = self.copies.get(group, (0, []))
        for copy, sends, takes in waiting:
            only(sends, copy.wait_send)
            only(takes, copy.wait_recv)
        start, count = GROUP_TAPS[group]
        first = ((self.core_send, self.first_send, self.second_send, self.inward)
                 if start < WHOLE else (self.conv_core_send, self.conv_inward))
        step = (first + (self.half_send, self.half_back, self.outward, self.core_back,
                         lambda *_: []))[stage]
        taps = pl.ds(start, count)
        self.conv = pl.ds(start - WHOLE, count)
        moves = step(taps, lambda body: pl.loop(start, start + count)(body))
        copies = []
        for j, (src, dst, device, *when) in enumerate(moves):
            copy = pltpu.make_async_remote_copy(
                src_ref=src, dst_ref=dst, send_sem=self.s.at[group, stage, j],
                recv_sem=self.r.at[group, stage, j], device_id=device, device_id_type=MESH_ID)
            sends, takes = when if when else (None, None)
            only(sends, copy.start)
            copies.append((copy, sends, takes))
        self.copies[group] = (stage + 1, copies)

    def core_send(self, taps, each):
        return [(self.part.at[taps, :, 1 - self.me.k], self.from_core.at[taps], self.core)]

    def first_send(self, taps, each):
        me, part = self.me, self.part

        @each
        def _(tap):
            own = part[tap, :, me.k].astype(F32) + self.from_core[tap].astype(F32)
            part[tap, :, me.k] = own.astype(BF)

        low, high = pl.ds(0, 32), pl.ds(32, 32)
        x, y = (me.r, self.x), (me.r, self.y)
        return [
            (part.at[taps, self.far, me.k, low, :], self.near_x.at[1, taps], x),
            (part.at[taps, self.far, me.k, high, :], self.near_y.at[1, taps], y),
            (part.at[taps, self.x, me.k, low, :], self.near_x.at[0, taps], x),
            (part.at[taps, self.y, me.k, high, :], self.near_y.at[0, taps], y),
        ]

    def conv_core_send(self, taps, each):
        return [(self.quarter.at[self.conv, 1 - self.me.k], self.quarter_core.at[self.conv], self.core)]

    def conv_inward(self, taps, each):
        @each
        def _(tap):
            value = (self.quarter[tap - WHOLE, self.me.k].astype(F32)
                     + self.quarter_core[tap - WHOLE].astype(F32))
            self.plane[tap] = value.astype(BF)

        return self.to_inner(taps)

    def second_send(self, taps, each):
        me, part = self.me, self.part
        low, high = pl.ds(0, 32), pl.ds(32, 32)

        @each
        def _(tap):
            for chan, rows, near in ((self.y, low, self.near_x), (self.x, high, self.near_y)):
                value = part[tap, chan, me.k, rows, :].astype(F32) + near[1, tap].astype(F32)
                part[tap, chan, me.k, rows, :] = value.astype(BF)

        return [
            (part.at[taps, self.y, me.k, low, :], self.last_y.at[taps], (me.r, self.y)),
            (part.at[taps, self.x, me.k, high, :], self.last_x.at[taps], (me.r, self.x)),
        ]

    def inward(self, taps, each):
        me, part = self.me, self.part

        @each
        def _(tap):
            for start, near, last in ((0, self.near_x, self.last_y), (32, self.near_y, self.last_x)):
                rows = pl.ds(start, 32)
                value = (part[tap, me.c, me.k, rows, :].astype(F32) + near[0, tap].astype(F32)
                         + last[tap].astype(F32))
                self.plane[tap, rows, :] = value.astype(BF)

        return self.to_inner(taps)

    def to_inner(self, taps):
        return [(self.plane.at[taps], self.plane_in.at[taps], self.plane_device(self.z1),
                 self.outer, self.inner)]

    def half_rows(self, half):
        return pl.ds(pl.multiple_of(half * 32, 32), 32)

    def half_send(self, taps, each):
        @pl.when(self.inner)
        def _():
            @each
            def _(tap):
                value = self.plane[tap].astype(F32) + self.plane_in[tap].astype(F32)
                self.plane[tap] = value.astype(BF)

        return [(self.plane.at[taps, self.half_rows(1 - self.half), :], self.half_in.at[taps],
                 self.plane_device(3 - self.me.z), self.inner, self.inner)]

    def half_back(self, taps, each):
        me = self.me

        @pl.when(self.inner)
        def _():
            @each
            def _(tap):
                value = (self.plane[tap, self.half_rows(self.half), :].astype(F32)
                         + self.half_in[tap].astype(F32))
                self.total[tap, me.k, self.half] = value.astype(BF)

        piece = self.total.at[taps, me.k, self.half]
        return [(piece, piece, self.plane_device(3 - me.z), self.inner, self.inner)]

    def outward(self, taps, each):
        piece = self.total.at[taps, self.me.k]
        return [(piece, piece, self.plane_device(self.z1), self.inner, self.outer)]

    def core_back(self, taps, each):
        piece = self.total.at[taps, self.me.k]
        return [(piece, piece, self.core)]


def back_kernel(
    dt, vec, st, x, a1, hid, act2, res, nrm, cot, w1, w2, wq, gwo, gob,
    gimg_o, zs_o, gw1_o, gw2_o, gqkv_o, gwo_o,
    dt_v, x_v, a1_v, hid_v, act2_v, res_v, nrm_v, drs_v, w1_v, w2_v, wq_v,
    cat, turned, turned1, acc, groups, slots, halo, keep, img_b, back, zsl, dquart,
    part, quarter, from_core, quarter_core, near_x, near_y, last_x, last_y, plane, plane_in, half_in, total,
    ss, sr, hs, hr, bs, br, zs, zr, red_s, red_r, lsem, osem, ds_, dr,
):
    me = Place()
    barrier = pltpu.get_barrier_semaphore()
    greet_plane(me, barrier)
    others = greet_back(me, barrier)
    for t in range(1, 4):
        pl.semaphore_signal(
            barrier, inc=1, device_id=(2 * lax.rem(me.z + t, 4) + me.k, me.c),
            device_id_type=MESH_ID,
        )
    loads = [local(a, b, lsem.at[j]) for j, (a, b) in enumerate((
        (dt, dt_v), (wq, wq_v), (res, res_v), (gwo, part.at[0]), (nrm, nrm_v), (cot, drs_v),
        (act2, act2_v), (w2, w2_v), (hid, hid_v), (a1, a1_v), (w1, w1_v), (x, x_v)))]
    reduce = Reduce(
        me, part, quarter, (from_core, quarter_core, near_x, near_y, last_x, last_y, plane, plane_in,
                            half_in), total, (red_s, red_r))

    def advance(*groups):
        for group in groups:
            reduce.advance(group)

    group_matrix(groups)
    zero8 = jnp.zeros((8, C), F32)
    members = 1.0 / (H * W * 16)
    loads[0].wait()
    loads[1].wait()
    for j in range(3):
        rows = jnp.transpose(dt_v[j].astype(F32))
        if j != 1:
            keep[j : j + 1, :] = as_row(rows)
        value = mm(rows.astype(BF), wq_v[j])
        if j == 0:
            acc[...] = value
        else:
            acc[...] += value
    loads[2].wait()

    def sums(scaled_of, upstream_of):
        def add(i, carry):
            upstream = upstream_of(i)
            return (carry[0] + fold(upstream), carry[1] + fold(upstream * scaled_of(i)))

        first, cross = lax.fori_loop(0, CHUNKS, add, (zero8, zero8))
        return [as_row(first), as_row(cross)]

    def scaled(ref, number):
        return lambda i: (ref[chunk_of(i), :].astype(F32) - st[2 * number : 2 * number + 1, :]) * st[
            2 * number + 1 : 2 * number + 2, :]

    def exchange(number, rows):
        store_rows(slots.at[number], me.d, rows)
        return plane_exchange(me, slots.at[number], ss.at[number], sr.at[number])

    scaled3, scaled2, scaled1 = scaled(res_v, 2), scaled(hid_v, 1), scaled(x_v, 0)
    rows3 = sums(scaled3, lambda i: acc[chunk_of(i), :])
    pl.semaphore_wait(barrier, 10 + others)
    copies = exchange(0, rows3)
    loads[3].wait()
    advance(0)
    loads[4].wait()

    @pl.loop(0, 3)
    def _(j):
        part[1 + j] = mm(dt_v[j], nrm_v[...]).astype(BF).reshape(4, 2, 64, C)

    advance(1)
    loads[5].wait()
    for copy in copies:
        copy.wait()

    def group_means(total_rows, factor):
        return group_total(total_rows * factor, groups) * members

    total3 = slots_total(slots.at[0])
    gain = vec[2:3, :]
    means = group_means(total3, gain)
    keep[8:16, :] = total3
    inverse = st[5:6, :]

    def resid_grad(i, carry):
        where = chunk_of(i)
        value = drs_v[where, :] + inverse * (
            acc[where, :] * gain - means[0:1] - scaled3(i) * means[1:2])
        drs_v[where, :] = value
        put_shifted(cat, 64 + i * 64, value)
        return carry + fold(value.astype(BF).astype(F32))

    keep[3:4, :] = as_row(lax.fori_loop(0, CHUNKS, resid_grad, zero8))
    def grad_of(chan):
        return cat.at[1, pl.ds(64, PIX), pl.ds(pl.multiple_of(chan * 128, 128), 128)]

    grads_sems = (ds_, dr)

    def half_weight_grads(act, groups_of):
        spread_received(grad_of, dquart, grad_rows, dr)
        value = dquart[...].astype(F32)
        col = lax.rem(lax.broadcasted_iota(jnp.int32, (4 * PIX, 128), 0), 64)
        moved = (jnp.where(col == 63, 0.0, pltpu.roll(value, 4 * PIX - 1, 0)), value,
                 jnp.where(col == 0, 0.0, pltpu.roll(value, 1, 0)))
        for j in range(3):
            turned[j * 128 : (j + 1) * 128, :] = jnp.transpose(moved[j]).astype(BF)
        for row, group in enumerate(groups_of):
            start = GROUP_TAPS[group][0]
            taps = mm(turned[...], act[row * 64 : row * 64 + 4 * PIX, :])
            for j in range(3):
                quarter[start - WHOLE + j] = taps[j * 128 : (j + 1) * 128].astype(BF).reshape(
                    2, 64, C)
            advance(group)

    def weight_grads(group, source):
        start, count = GROUP_TAPS[group]

        @pl.loop(0, count)
        def _(i):
            tap = start - 4 + i
            rows = pl.ds(pl.multiple_of(lax.div(tap, 3) * 64, 64), PIX)
            part[start + i] = mm(turned1[...], source[lax.rem(tap, 3), rows, :]).astype(
                BF).reshape(4, 2, 64, C)

        advance(group)

    halo_send(me, cat, halo.at[0], hs.at[0], hr.at[0])
    spread_rows(me, grad_of, dquart, grad_rows, *grads_sems, SPREAD)
    acc[...] = jnp.zeros((PIX, C), F32)
    loads[7].wait()
    conv_taps(acc, cat, w2_v, (1,), True, NN)
    halo_wait(me, cat, halo.at[0], hs.at[0], hr.at[0])
    conv_taps(acc, cat, w2_v, (0, 2), True, NN)
    loads[8].wait()
    gain2, bias2 = vec[1:2, :], vec[4:5, :]
    scale, shift = 1.0 + vec[11:12, :], vec[12:13, :]

    def mod_grad(i):
        where = chunk_of(i)
        mod = (scaled2(i) * gain2 + bias2) * scale + shift
        value = acc[where, :] * swish_slope(mod)
        acc[where, :] = value
        return value

    copies = exchange(1, sums(scaled2, mod_grad))
    advance(0, 1)
    loads[6].wait()
    half_weight_grads(act2_v, (2, 3, 4))
    spread_sent(me, grad_of, dquart, grad_rows, *grads_sems)
    for copy in copies:
        copy.wait()
    total2 = slots_total(slots.at[1])
    means2 = group_means(total2, gain2 * scale)
    keep[16:24, :] = total2
    inverse2 = st[3:4, :]

    def hidden_grad(i, carry):
        where = chunk_of(i)
        value = inverse2 * (
            acc[where, :] * (gain2 * scale) - means2[0:1] - scaled2(i) * means2[1:2])
        acc[where, :] = value
        put_shifted(cat, 64 + i * 64, value)
        return carry + fold(value.astype(BF).astype(F32))

    keep[1:2, :] = as_row(lax.fori_loop(0, CHUNKS, hidden_grad, zero8))
    halo_send(me, cat, halo.at[1], hs.at[1], hr.at[1])
    advance(2, 3, 4)
    turned1[...] = jnp.transpose(acc[...]).astype(BF)
    loads[9].wait()
    for group in (5, 6, 7):
        weight_grads(group, a1_v)
    advance(0, 1, 5)
    acc[...] = jnp.zeros((PIX, C), F32)
    loads[10].wait()
    conv_taps(acc, cat, w1_v, (1,), True, NN)
    halo_wait(me, cat, halo.at[1], hs.at[1], hr.at[1])
    conv_taps(acc, cat, w1_v, (0, 2), True, NN)
    loads[11].wait()
    gain1, bias1 = vec[0:1, :], vec[3:4, :]

    def pre_grad(i):
        where = chunk_of(i)
        value = acc[where, :] * swish_slope(scaled1(i) * gain1 + bias1)
        acc[where, :] = value
        return value

    first, cross = sums(scaled1, pre_grad)
    copies = exchange(2, [first, cross, keep[1:2, :], keep[3:4, :], keep[0:1, :], keep[2:3, :],
                          gob[0:1, :]])
    advance(6, 2, 3, 4)
    for copy in copies:
        copy.wait()
    total1 = slots_total(slots.at[2])
    means1 = group_means(total1, gain1)
    inverse1 = st[1:2, :]

    @pl.loop(0, CHUNKS)
    def _(i):
        where = chunk_of(i)
        value = drs_v[where, :] + inverse1 * (
            acc[where, :] * gain1 - means1[0:1] - scaled1(i) * means1[1:2])
        img_b[where, :] = value.astype(BF)

    band_back_send(me, img_b, back, bs, br)
    u2, v2 = keep[16:17, :], keep[17:18, :]
    keep[24:40, :] = jnp.concatenate(
        [total1[1:2], scale * v2, keep[9:10, :], total1[0:1], scale * u2, keep[8:9, :],
         total1[2:7], gain2 * v2 + bias2 * u2, u2, jnp.zeros((3, C), F32)], axis=0)
    own_cols = pl.ds(pl.multiple_of(me.c * 128, 128), 128)
    zsl[me.z] = keep[24:40, own_cols]
    zcopies = [
        send(zsl.at[me.z], zsl.at[me.z], zs.at[t], zr.at[t],
             (2 * lax.rem(me.z + t, 4) + me.k, me.c))
        for t in range(1, 4)
    ]
    advance(7, 5, 6, 0, 1, 2, 3, 4, 7, 5, 6, 2, 3, 4, 0, 1, 7, 5, 6, 2, 3, 4, 0, 1, 7, 5, 6)
    for copy in zcopies:
        copy.wait()
    zs_o[...] = zsl[...]
    advance(0, 1, 7, 5, 6, 7, 0, 1, 5, 6, 7)
    band_back_wait(me, img_b, back, bs, br)
    saves = [local(back, gimg_o, osem.at[0])]
    for _ in range(STAGES):
        for group in range(GROUPS_SENT):
            if reduce.copies[group][0] < (STAGES - 2 if 2 <= group < 5 else STAGES):
                reduce.advance(group)
    for j, (dst, start, count) in enumerate(
            ((gwo_o, 0, 1), (gqkv_o, 1, 3), (gw2_o, 13, 9), (gw1_o, 4, 9))):
        saves.append(local(total.at[pl.ds(start, count)], dst, osem.at[j + 1]))
    for copy in saves:
        copy.wait()


def back(*args):
    shared = [
        ((3, C, PIX), BF), ((PIX, C), BF), ((3, PAD, C), BF), ((PIX, C), F32),
        ((HALF_ROWS, C), BF), ((PIX, C), F32), ((PIX, C), BF), ((PIX, C), F32), ((9, C, C), BF),
        ((9, C, C), BF), ((3, C, C), BF), ((3, PAD, C), BF), ((384, 4 * PIX), BF), ((C, PIX), BF), ((PIX, C), F32),
        ((C, C), BF), ((3, 8, 8, C), F32), ((2, 2, 64, C), BF), ((40, C), F32), ((PIX, C), BF),
        ((4, PIX, 128), BF), ((4, 16, 128), F32), ((4 * PIX, 128), BF),
        ((WHOLE, 4, 2, 64, C), BF), ((TAPS - WHOLE, 2, 64, C), BF), ((WHOLE, 4, 64, C), BF),
        ((TAPS - WHOLE, 64, C), BF), ((2, WHOLE, 32, C), BF), ((2, WHOLE, 32, C), BF),
        ((WHOLE, 32, C), BF), ((WHOLE, 32, C), BF), ((TAPS, 64, C), BF), ((TAPS, 64, C), BF),
        ((TAPS, 32, C), BF), ((TAPS, 2, 2, 32, C), BF),
    ]
    return pl.pallas_call(
        back_kernel,
        name="back",
        out_shape=[
            jax.ShapeDtypeStruct((4, PIX, 128), BF),
            jax.ShapeDtypeStruct((4, 16, 128), F32),
            jax.ShapeDtypeStruct((9, 2, 2, 32, C), BF),
            jax.ShapeDtypeStruct((9, 2, 2, 32, C), BF),
            jax.ShapeDtypeStruct((3, 2, 2, 32, C), BF),
            jax.ShapeDtypeStruct((1, 2, 2, 32, C), BF),
        ],
        in_specs=[ANY, VMEM, VMEM] + [ANY] * 11 + [VMEM],
        out_specs=[ANY, VMEM, ANY, ANY, ANY, ANY],
        scratch_shapes=[pltpu.VMEM(*one) for one in shared]
        + [
            DMA((3, 8)), DMA((3, 8)), DMA((2, 2)), DMA((2, 2)), DMA((4,)), DMA((4,)), DMA((4,)),
            DMA((4,)), DMA((GROUPS_SENT, STAGES, 4)), DMA((GROUPS_SENT, STAGES, 4)), DMA((12,)),
            DMA((5,)), DMA((4,)), DMA((4,)),
        ],
        compiler_params=pltpu.CompilerParams(
            collective_id=3, has_side_effects=True, vmem_limit_bytes=VMEM_LIMIT
        ),
    )(*args)


def split_rows(rows):
    first = rows.astype(BF).astype(F32)
    second = (rows - first).astype(BF).astype(F32)
    stacked = jnp.concatenate([first, second, rows - first - second, jnp.zeros((80, 128), F32)],
                              axis=0)
    left = jnp.transpose(stacked).astype(BF)
    return left[:, 0:16], left[:, 16:32], left[:, 32:48]


def finish_kernel(
    res, gimg, gw1, gw2, gqkv, gwo, zs, ctot, feat, tokens,
    res_o, gimg_o, gain_o, bias_o, gw1_o, gw2_o, cb_o, gemb_o, gembb_o, gqkv_o, qvb_o, gctx_o,
    gctxb_o, gwo_o, ob_o,
    res_v, gimg_v, gw1_v, gw2_v, gqkv_v, gwo_v, res_f, gimg_f, gw1_f, gw2_f, gqkv_f, gwo_f,
    gemb_f, gctx_f, lsem, osem,
):
    pairs = (
        (gw1, gw1_v, gw1_f, gw1_o), (gw2, gw2_v, gw2_f, gw2_o), (res, res_v, res_f, res_o),
        (gimg, gimg_v, gimg_f, gimg_o), (gqkv, gqkv_v, gqkv_f, gqkv_o), (gwo, gwo_v, gwo_f, gwo_o))
    loads = [local(src, low, lsem.at[j]) for j, (src, low, _, _) in enumerate(pairs)]
    saves = []
    for j in range(2):
        rows = jnp.concatenate([zs[n, 11 + j : 12 + j, :] for n in range(4)]
                               + [jnp.zeros((12, 128), F32)], axis=0)
        gemb_f[j] = sum(mm(term, feat[...]) for term in split_rows(rows))
        saves.append(local(gemb_f.at[j], gemb_o.at[j], osem.at[6 + j]))
        gctx_f[j] = sum(mm(term, tokens[...]) for term in split_rows(ctot[j]))
        saves.append(local(gctx_f.at[j], gctx_o.at[j], osem.at[8 + j]))
        gctxb_o[j : j + 1, :] = as_row(ctot[j])
    total = (zs[0] + zs[1]) + (zs[2] + zs[3])
    gain_o[...] = total[0:3]
    bias_o[...] = total[3:6]
    cb_o[...] = total[6:8]
    qvb_o[...] = total[8:10]
    ob_o[...] = total[10:11]
    gembb_o[...] = total[11:13]
    for j, (_, low, high, dst) in enumerate(pairs):
        loads[j].wait()

        @pl.loop(0, high.shape[0])
        def _(i):
            high[i] = low[i].astype(F32)

        saves.append(local(high, dst, osem.at[j]))
    for copy in saves:
        copy.wait()


def finish(*args):
    wide = [((4, PIX, 128), F32)] * 2 + [((9, 128, C), F32)] * 2 + [((3, 128, C), F32),
                                                                    ((1, 128, C), F32)]
    res, gimg, gw1, gw2, gqkv, gwo = wide
    emb, ctx = ((2, 128, EMB), F32), ((2, 128, CTXW), F32)
    outs = [
        res, gimg, ((3, 128), F32), ((3, 128), F32), gw1, gw2, ((2, 128), F32), emb,
        ((2, 128), F32), gqkv, ((2, 128), F32), ctx, ((2, 128), F32), gwo, ((1, 128), F32)]
    return pl.pallas_call(
        finish_kernel,
        name="finish",
        out_shape=[jax.ShapeDtypeStruct(*one) for one in outs],
        in_specs=[ANY] * 6 + [VMEM] * 4,
        out_specs=[VMEM if len(one[0]) == 2 else ANY for one in outs],
        scratch_shapes=[pltpu.VMEM(shape, BF) for shape, _ in wide]
        + [pltpu.VMEM(*one) for one in wide + [emb, ctx]] + [DMA((6,)), DMA((10,))],
        compiler_params=pltpu.CompilerParams(vmem_limit_bytes=VMEM_LIMIT),
    )(*args)


def plane_body(
    image, target, time_index, loss_weight, clip_embed, clip_tokens, norm_gain, norm_bias,
    conv1_w, conv2_w, conv_bias, emb_w, emb_b, qkv_w, qv_bias, ctx_w, ctx_b, out_w, out_b,
):
    (x, tgt, vec, st, a1, hid, a2, res, nrm, w1, w2, wq, wo, qkv, attn, p, ctx, pc, o, linv, feat,
     tokens) = front(
        image.reshape(4, PIX, 128), target.reshape(4, PIX, 128), time_index, loss_weight,
        clip_embed, clip_tokens, norm_gain, norm_bias, conv_bias, qv_bias, out_b[None], emb_w,
        emb_b, ctx_w, ctx_b, conv1_w.reshape(9, 128, C), conv2_w.reshape(9, 128, C), qkv_w,
        out_w[None])
    result, cot, gwo, gob, dt, ctot, act2 = middle(
        attn, res, tgt, wo, vec, qkv, ctx, p, pc, o, linv, a2)
    gimg, zs, gw1, gw2, gqkv, gwo = back(
        dt, vec, st, x, a1, hid, act2, res, nrm, cot, w1, w2, wq, gwo.reshape(4, 2, 64, C), gob)
    taps = lambda value: value.reshape(value.shape[0], 128, C)
    outs = finish(result, gimg, taps(gw1), taps(gw2), taps(gqkv), taps(gwo), zs, ctot, feat, tokens)
    shapes = (
        image, image, norm_gain, norm_bias, conv1_w, conv2_w, conv_bias, emb_w, emb_b, qkv_w,
        qv_bias, ctx_w, ctx_b, out_w, out_b)
    return tuple(out.reshape(like.shape) for out, like in zip(outs, shapes))


def solution(mesh):
    sizes = dict(mesh.shape)
    planes = sizes["row"] == 8 and sizes["chan"] == 4
    return jax.shard_map(
        plane_body if planes else general_body,
        mesh=mesh,
        in_specs=(
            P(None, "row", None, "chan"), P(None, "row", None, "chan"), P(), P(), P(), P(),
            P(None, "chan"), P(None, "chan"), P(None, None, "chan", None),
            P(None, None, "chan", None), P(None, "chan"), P(None, "chan", None),
            P(None, "chan"), P(None, "chan", None), P(None, "chan"), P(None, "chan", None),
            P(None, "chan"), P("chan", None), P("chan"),
        ),
        out_specs=(
            P(None, "row", None, "chan"), P(None, "row", None, "chan"), P(None, "chan"),
            P(None, "chan"), P(None, None, "chan", None), P(None, None, "chan", None),
            P(None, "chan"), P(None, "chan", None), P(None, "chan"), P(None, "chan", None),
            P(None, "chan"), P(None, "chan", None), P(None, "chan"), P("chan", None), P("chan"),
        ),
        check_vma=False,
    )
```
